32 devices in a mesh: dp: 2 (over x), expert: 4 (over z), tensor: 4 (over y, core).
Axes of the slice: x: 2, y: 2, z: 4, core: 2. Of those that a mesh axis runs over, the one named last changes fastest.
Arguments:
- grad_out: bfloat16 [1024, 4096], P(('dp', 'expert')), may hold values from -6 to 6
- expert_ids: int32 [1024, 8], P(('dp', 'expert')), may hold values from 0 to 127, all different within a row
- gate_values: bfloat16 [1024, 8], P(('dp', 'expert')), may hold values from 0.019897461 to 0.5
- saved_hidden: bfloat16 [2, 4, 16, 1536], P('dp', 'expert', None, 'tensor'), may hold values from -0.59765625 to 0.59765625
- down_weight: bfloat16 [4, 1536, 4096], P('expert', 'tensor'), may hold values from -0.15625 to 0.15625
Outputs:
- gate_grad: float32 [1024, 8], P(('dp', 'expert'))
- hidden_grad: bfloat16 [2, 4, 16, 1536], P('dp', 'expert', None, 'tensor')
- down_grad: float32 [4, 1536, 4096], P('expert', 'tensor', 'dp')
The draws below stay inside these ranges and needn't reach their ends.
Inputs may be any that keep to these rules, and one draw needn't show every extreme that they name: `expert_ids`: the 8 experts of a row differ.
All inputs are finite; a program needn't handle non-finite values.
Results may differ from the reference program's by a relative error of at most 0.0085.
Values may be sent and summed in bfloat16 or wider, within the bound.
No kernel may reach another device: no remote copies, remote signals or barrier semaphores. Data moves between devices by JAX's collectives and lax.ppermute only.
A program may use at most 64 MiB of HBM per device.

```python
import math
from functools import partial
import jax
import jax.numpy as jnp
from jax import lax

D = 4096
EXPERTS = 128
TOP = 8
FF = 1536
CAP = 4
TOK = 128
TOKENS = 1024
SLOTS = 16
N_DP = 2
N_EXPERT = 4


def block_scale(key, shape, shards, low, high):
    def one(position, shards_of):
        draws = jax.random.uniform(jax.random.fold_in(jax.random.fold_in(key, 6), position), (shards_of,), jnp.float32, low / len(shards), high / len(shards))
        return jnp.repeat(jnp.exp(draws), shape[position] // shards_of).reshape((-1,) + (1,) * (len(shape) - position - 1))

    loudness = one(*shards[0])
    for cut in shards[1:]:
        loudness = loudness * one(*cut)
    return loudness


def picks_of(stream_key, rows, number_of, top, lift):
    order = jax.random.permutation(jax.random.fold_in(stream_key, 1), number_of)
    boost = order
    for power in range(3):
        boost = boost * boost // number_of
    boost = boost * lift // number_of
    tickets = jax.random.randint(jax.random.fold_in(stream_key, 2), (rows, number_of), 0, 4096) + boost
    fixed_rows = jax.random.permutation(jax.random.fold_in(stream_key, 3), rows)[jnp.arange(number_of) % rows]
    tickets = jnp.where(jnp.arange(rows)[:, None] == fixed_rows[None, :], 1 << 14, tickets)
    priority = tickets * number_of + jnp.arange(number_of)
    return lax.top_k(priority.astype(jnp.int32), top)[1].astype(jnp.int32)


def normal_values(key, dims, scale, most, split=(), kind=jnp.bfloat16):
    result = jax.random.normal(key, dims, jnp.float32) * scale
    if len(split) > 0:
        result = block_scale(key, dims, split, -0.22, 0.18) * result
    return jnp.clip(result, min=-most, max=most).astype(kind)


def setup_inputs(seed: int = 0) -> dict:
    keys = jax.random.split(jax.random.key(seed), 6)
    grad_out = normal_values(keys[0], (TOKENS, D), 1.0, 6.0, ((0, 8),))
    expert_ids = picks_of(keys[1], TOKENS, EXPERTS, TOP, 1024)
    gate_values = jnp.clip(jnp.exp(math.log(0.5) - 3.224016 * jax.random.uniform(keys[2], (TOKENS, TOP), jnp.float32) ** block_scale(keys[2], (TOKENS, TOP), ((0, 8),), -0.2, 0.2)), 0.019897461, 0.5).astype(jnp.bfloat16)
    saved_hidden = normal_values(keys[3], (N_DP, N_EXPERT, SLOTS, FF), 0.1, 0.59765625, ((0, 2), (1, 4), (3, 4)))
    down_weight = normal_values(keys[4], (N_EXPERT, FF, D), FF ** -0.5, 0.15625, ((0, 4), (1, 4)))
    return dict(grad_out=grad_out, expert_ids=expert_ids, gate_values=gate_values, saved_hidden=saved_hidden, down_weight=down_weight)


def slot_table(route_ids, gate_rows, count):
    experts = jnp.arange(count, dtype=jnp.int32)
    hits = (route_ids[:, :, None] == experts[None, None, :]).astype(jnp.int32)
    member = lax.optimization_barrier(jnp.sum(hits, axis=1))
    gate_expert = lax.optimization_barrier(jnp.sum(jnp.where(hits > 0, gate_rows.astype(jnp.float32)[:, :, None], 0.0), axis=1))
    before = jnp.cumsum(member, axis=0) - member
    kept = member * (before < CAP).astype(jnp.int32)
    places = jnp.arange(CAP, dtype=jnp.int32)
    match = kept.T[:, None, :] * (before.T[:, None, :] == places[None, :, None]).astype(jnp.int32)
    positions = jnp.arange(route_ids.shape[0], dtype=jnp.int32)
    source_row = lax.optimization_barrier(jnp.sum(match * positions[None, None, :], axis=2)).astype(jnp.int32)
    filled = lax.optimization_barrier(jnp.sum(match, axis=2))
    slot_gate = lax.optimization_barrier(jnp.sum(match.astype(jnp.float32) * gate_expert.T[:, None, :], axis=2)).astype(jnp.bfloat16)
    return (source_row, filled, slot_gate, hits, kept, before)

def returned_grad(back, hits, kept, before):
    count = back.shape[0]
    spots = jnp.minimum(before, CAP - 1)
    picked = back[jnp.arange(count, dtype=jnp.int32)[None, :], spots]
    picked = jnp.where(kept > 0, picked, jnp.zeros((), picked.dtype))
    return lax.optimization_barrier(jnp.sum(hits.astype(picked.dtype) * picked[:, None, :], axis=2))

def pick_rows(grad_rows, source_row, filled):
    return jnp.where(filled[:, :, None] > 0, grad_rows[source_row], jnp.zeros((), grad_rows.dtype))

def reference(grad_out, expert_ids, gate_values, saved_hidden, down_weight):
    grads = grad_out.reshape(N_DP, N_EXPERT, TOK, D)
    routes = expert_ids.reshape(N_DP, N_EXPERT, TOK, TOP)
    gates = gate_values.reshape(N_DP, N_EXPERT, TOK, TOP)
    weight_wide = down_weight.astype(jnp.float32)
    table = partial(slot_table, count=N_EXPERT)

    def group(total, inputs):
        grad_group, route_group, gate_group, hidden_group = inputs
        source_row, filled, slot_gate, hits, kept, before = jax.vmap(table)(route_group, gate_group)
        outgoing = jax.vmap(pick_rows)(grad_group, source_row, filled)
        received = jnp.swapaxes(outgoing, 0, 1).reshape(N_EXPERT, N_EXPERT * CAP, D)
        gate_in = jnp.swapaxes(slot_gate, 0, 1).reshape(N_EXPERT, N_EXPERT * CAP).astype(jnp.float32)
        upstream = jnp.einsum('esd,efd->esf', received.astype(jnp.float32), weight_wide)
        hidden_grad = (gate_in[:, :, None] * upstream).astype(jnp.bfloat16)
        gate_part = lax.optimization_barrier(jnp.sum(hidden_group.astype(jnp.float32) * upstream, axis=2))
        weighted = (gate_in[:, :, None] * received.astype(jnp.float32)).astype(jnp.bfloat16)
        partial_grad = jnp.einsum('esf,esd->efd', hidden_group.astype(jnp.float32), weighted.astype(jnp.float32)).astype(jnp.bfloat16)
        back = jnp.swapaxes(gate_part.reshape(N_EXPERT, N_EXPERT, CAP), 0, 1)
        gate_grad = jax.vmap(returned_grad)(back, hits, kept, before)
        return (total + partial_grad.astype(jnp.float32), (gate_grad, hidden_grad))
    begin = jnp.zeros((N_EXPERT, FF, D), jnp.float32)
    total, (gate_grad, hidden_grad) = lax.scan(group, begin, (grads, routes, gates, saved_hidden))
    return (gate_grad.reshape(N_DP * N_EXPERT * TOK, TOP), hidden_grad, total)
```

```python
import functools

import jax
import jax.numpy as jnp
from jax import lax
from jax.experimental import pallas as pl
from jax.experimental.pallas import tpu as pltpu
from jax.sharding import PartitionSpec as P

CAP = 4
LANES = 128
PAD = 8
VMEM = pl.BlockSpec(memory_space=pltpu.VMEM)


def dot(a, b, dims):
    return lax.dot_general(a, b, (dims, ((), ())), preferred_element_type=jnp.float32)


def route_kernel(count, ids_ref, gates_ref, grad_ref, match_ref, *sends):
    me = lax.axis_index("expert")
    top, tokens = ids_ref.shape
    width = grad_ref.shape[1]
    rows = count * PAD
    row = lax.broadcasted_iota(jnp.int32, (rows, tokens), 0)
    expert = me + row // PAD
    expert = jnp.where(expert >= count, expert - count, expert)
    place = row % PAD
    ids = ids_ref[...]
    gates = gates_ref[...].astype(jnp.float32)
    member = jnp.zeros((rows, tokens), jnp.float32)
    gate = jnp.zeros((rows, tokens), jnp.float32)
    for k in range(top):
        hit = ids[k : k + 1, :] == expert
        member = jnp.where(hit, 1.0, member)
        gate = jnp.where(hit, gates[k : k + 1, :], gate)
    earlier = lax.broadcasted_iota(jnp.int32, (tokens, tokens), 0)
    later = lax.broadcasted_iota(jnp.int32, (tokens, tokens), 1)
    before = dot(
        member.astype(jnp.bfloat16), (earlier < later).astype(jnp.bfloat16), ((1,), (0,))
    )
    taken = (member > 0) & (before == place.astype(jnp.float32)) & (place < CAP)
    match = taken.astype(jnp.float32)
    match_ref[...] = match
    slot_gate = jnp.sum(match * gate, axis=1, keepdims=True)
    picked = dot(match.astype(jnp.bfloat16), grad_ref[...], ((1,), (0,)))
    for r in range(count):
        part = slice(r * PAD, r * PAD + CAP)
        sends[r][:, :width] = picked[part].astype(jnp.bfloat16)
        sends[r][:, width:] = jnp.broadcast_to(slot_gate[part], (CAP, LANES)).astype(jnp.bfloat16)


def slot_order(count):
    me = lax.axis_index("expert")
    slots = count * CAP
    here = lax.broadcasted_iota(jnp.int32, (slots, slots), 0)
    saved = lax.broadcasted_iota(jnp.int32, (slots, slots), 1)
    block = me - here // CAP
    block = jnp.where(block < 0, block + count, block)
    return (saved == block * CAP + here % CAP).astype(jnp.bfloat16)


def expert_kernel(count, groups, hidden_ref, weight_ref, *refs):
    received = refs[:count]
    hidden_grad_ref, back_ref = refs[count : count + 2]
    pays = refs[count + 2 : count + 2 + groups]
    rows_ref, weighted_ref = refs[count + 2 + groups :]
    width = weight_ref.shape[2]
    units = weight_ref.shape[1]
    for r in range(count):
        rows_ref[r * CAP : (r + 1) * CAP, :] = received[r][...].astype(jnp.float32)
    rows = rows_ref[:, :width]
    gate = rows_ref[:, width : width + 1]
    order = slot_order(count)
    hidden = dot(order, hidden_ref[0, 0], ((1,), (0,)))
    upstream = dot(rows.astype(jnp.bfloat16), weight_ref[0], ((1,), (1,)))
    back = jnp.sum(hidden * upstream, axis=1, keepdims=True)
    back_ref[...] = jnp.broadcast_to(back, back_ref.shape)
    scaled = (gate * upstream).astype(jnp.bfloat16)
    hidden_grad_ref[0, 0] = dot(order, scaled, ((0,), (0,))).astype(jnp.bfloat16)
    weighted_ref[...] = (gate * rows).astype(jnp.bfloat16)
    share = width // groups
    me = lax.axis_index("dp")
    for r in range(groups):
        group = me + r
        group = jnp.where(group >= groups, group - groups, group)
        pays[r][:, :share] = weighted_ref[:, pl.ds(pl.multiple_of(group * share, share), share)]
        pays[r][:, share:] = hidden.astype(jnp.bfloat16)


def down_kernel(groups, *refs):
    out_ref = refs[groups]
    step = pl.program_id(0)
    block, share = out_ref.shape[1:]
    total = None
    for r in range(groups):
        start = pl.multiple_of(share + step * block, LANES)
        hidden = refs[r][:, pl.ds(start, block)]
        term = dot(hidden, refs[r][:, :share], ((0,), (0,)))
        term = term.astype(jnp.bfloat16).astype(jnp.float32)
        total = term if total is None else total + term
    out_ref[0] = total


def gate_kernel(count, parts, ids_ref, match_ref, *refs):
    out_ref = refs[-1]
    me = lax.axis_index("expert")
    ids = ids_ref[...]
    total = jnp.zeros(out_ref.shape, jnp.float32)
    for r in range(count):
        expert = me + r
        expert = jnp.where(expert >= count, expert - count, expert)
        value = refs[0][r * CAP : (r + 1) * CAP, :]
        for part in range(1, parts):
            value = value + refs[part][r * CAP : (r + 1) * CAP, :]
        match = match_ref[r * PAD : r * PAD + CAP, :]
        chosen = jnp.sum(jnp.where(match > 0, value, 0.0), axis=0, keepdims=True)
        total = total + jnp.where(ids == expert, chosen, 0.0)
    out_ref[...] = total


def rotate(value, axis, by):
    size = lax.axis_size(axis)
    return lax.ppermute(value, axis, [(i, (i + by) % size) for i in range(size)])


def on_device(grad_out, expert_ids, gate_values, saved_hidden, down_weight):
    count = lax.axis_size("expert")
    groups = lax.axis_size("dp")
    tensors = lax.axis_size("tensor")
    tokens, width = grad_out.shape
    units = down_weight.shape[1]
    slots = count * CAP
    share = width // groups
    ids = expert_ids.T
    params = pltpu.CompilerParams(vmem_limit_bytes=24 * 2**20)

    match, *sends = pl.pallas_call(
        functools.partial(route_kernel, count),
        out_shape=[jax.ShapeDtypeStruct((count * PAD, tokens), jnp.float32)]
        + [jax.ShapeDtypeStruct((CAP, width + LANES), jnp.bfloat16)] * count,
        in_specs=[VMEM] * 3,
        out_specs=[VMEM] * (1 + count),
        compiler_params=params,
        name="route",
    )(ids, gate_values.T, grad_out)

    received = [sends[0]] + [rotate(sends[r], "expert", r) for r in range(1, count)]

    hidden_grad, back, *pays = pl.pallas_call(
        functools.partial(expert_kernel, count, groups),
        out_shape=[
            jax.ShapeDtypeStruct(saved_hidden.shape, jnp.bfloat16),
            jax.ShapeDtypeStruct((slots, LANES), jnp.float32),
        ]
        + [jax.ShapeDtypeStruct((slots, share + units), jnp.bfloat16)] * groups,
        in_specs=[VMEM] * (2 + count),
        out_specs=[VMEM] * (2 + groups),
        scratch_shapes=[
            pltpu.VMEM((slots, width + LANES), jnp.float32),
            pltpu.VMEM((slots, width), jnp.bfloat16),
        ],
        compiler_params=params,
        name="expert",
    )(saved_hidden, down_weight, *received)

    pays = [pays[0]] + [rotate(pays[r], "dp", r) for r in range(1, groups)]
    chunks = [back[r * CAP : (r + 1) * CAP] for r in range(count)]
    chunks = [chunks[0]] + [rotate(chunks[r], "expert", -r) for r in range(1, count)]
    back = jnp.concatenate(chunks, axis=0)
    backs = [back] + [rotate(back, "tensor", r) for r in range(1, tensors)]

    block = LANES
    down_grad = pl.pallas_call(
        functools.partial(down_kernel, groups),
        grid=(units // block,),
        out_shape=jax.ShapeDtypeStruct((1, units, share), jnp.float32),
        in_specs=[VMEM] * groups,
        out_specs=pl.BlockSpec((1, block, share), lambda i: (0, i, 0)),
        compiler_params=params,
        name="down",
    )(*pays)

    gate_grad = pl.pallas_call(
        functools.partial(gate_kernel, count, tensors),
        out_shape=jax.ShapeDtypeStruct(ids.shape, jnp.float32),
        in_specs=[VMEM] * (2 + tensors),
        out_specs=VMEM,
        compiler_params=params,
        name="gates",
    )(ids, match, *backs)
    return (gate_grad.T, hidden_grad, down_grad)


def solution(mesh):
    return jax.shard_map(
        on_device,
        mesh=mesh,
        in_specs=(
            P(("dp", "expert"), None),
            P(("dp", "expert"), None),
            P(("dp", "expert"), None),
            P("dp", "expert", None, "tensor"),
            P("expert", "tensor", None),
        ),
        out_specs=(
            P(("dp", "expert"), None),
            P("dp", "expert", None, "tensor"),
            P("expert", "tensor", "dp"),
        ),
        check_vma=False,
    )
```

```python
import functools

import jax
import jax.numpy as jnp
from jax import lax
from jax.experimental import pallas as pl
from jax.experimental.pallas import tpu as pltpu
from jax.sharding import PartitionSpec as P

CAP = 4
LANES = 128
PAD = 8
VMEM = pl.BlockSpec(memory_space=pltpu.VMEM)
HBM = pl.BlockSpec(memory_space=pltpu.HBM)
PARAMS = pltpu.CompilerParams(vmem_limit_bytes=32 * 2**20)


def dot(a, b, dims):
    return lax.dot_general(a, b, (dims, ((), ())), preferred_element_type=jnp.float32)


def in_hbm(*arrays):
    return [pltpu.with_memory_space_constraint(x, pltpu.HBM) for x in arrays]


def cost(flops, nbytes):
    return pl.CostEstimate(flops=flops, bytes_accessed=nbytes, transcendentals=0)


def paired(size):
    return size & (size - 1) == 0


def target(me, step, size):
    if paired(size):
        return me ^ step
    after = me + step
    return after % size if isinstance(me, int) else jnp.where(after >= size, after - size, after)


def source(me, step, size):
    if paired(size):
        return me ^ step
    before = me - step
    return before % size if isinstance(me, int) else jnp.where(before < 0, before + size, before)


def send(value, axis, step, give=target):
    size = lax.axis_size(axis)
    return lax.ppermute(value, axis, [(i, give(i, step, size)) for i in range(size)])


def route_kernel(count, ids_hbm, gates_hbm, grad_hbm, ids_out, match_ref, *refs):
    sends = refs[:count]
    ids_ref, gates_ref, grad_ref, sems = refs[count:]
    small = [
        pltpu.make_async_copy(ids_hbm, ids_ref, sems.at[0]),
        pltpu.make_async_copy(gates_hbm, gates_ref, sems.at[1]),
    ]
    large = pltpu.make_async_copy(grad_hbm, grad_ref, sems.at[2])
    for copy in small:
        copy.start()
    large.start()
    me = lax.axis_index("expert")
    top, tokens = ids_ref.shape
    width = grad_ref.shape[1]
    rows = count * PAD
    row = lax.broadcasted_iota(jnp.int32, (rows, tokens), 0)
    expert = target(me, row // PAD, count)
    place = row % PAD
    earlier = lax.broadcasted_iota(jnp.int32, (tokens, tokens), 0)
    later = lax.broadcasted_iota(jnp.int32, (tokens, tokens), 1)
    order = (earlier < later).astype(jnp.bfloat16)
    for copy in small:
        copy.wait()
    ids = ids_ref[...]
    ids_out[...] = ids
    gates = gates_ref[...].astype(jnp.float32)
    member = jnp.zeros((rows, tokens), jnp.float32)
    gate = jnp.zeros((rows, tokens), jnp.float32)
    for k in range(top):
        hit = ids[k : k + 1, :] == expert
        member = jnp.where(hit, 1.0, member)
        gate = jnp.where(hit, gates[k : k + 1, :], gate)
    before = dot(member.astype(jnp.bfloat16), order, ((1,), (0,)))
    taken = (member > 0) & (before == place.astype(jnp.float32)) & (place < CAP)
    match = taken.astype(jnp.float32)
    match_ref[...] = match
    slot_gate = jnp.sum(match * gate, axis=1, keepdims=True)
    match = match.astype(jnp.bfloat16)
    large.wait()
    picked = dot(match, grad_ref[...], ((1,), (0,)))
    for r in range(count):
        part = slice(r * PAD, r * PAD + CAP)
        sends[r][:, :width] = picked[part].astype(jnp.bfloat16)
        sends[r][:, width:] = jnp.broadcast_to(slot_gate[part], (CAP, LANES)).astype(jnp.bfloat16)


def slot_order(count):
    me = lax.axis_index("expert")
    slots = count * CAP
    here = lax.broadcasted_iota(jnp.int32, (slots, slots), 0)
    saved = lax.broadcasted_iota(jnp.int32, (slots, slots), 1)
    return (saved == source(me, here // CAP, count) * CAP + here % CAP).astype(jnp.bfloat16)


def forward_kernel(count, pieces, match_ref, hidden_hbm, weight_hbm, weight_ref, hidden_ref, y_ref, *refs):
    saved_ref, sems = refs
    units = weight_ref.shape[0]
    block = units // pieces
    first = pltpu.make_async_copy(hidden_hbm.at[0, 0], saved_ref, sems.at[pieces])
    first.start()
    loads = []
    for p in range(pieces):
        rows = pl.ds(p * block, block)
        loads.append(pltpu.make_async_copy(weight_hbm.at[0, rows], weight_ref.at[rows], sems.at[p]))
        loads[-1].start()
    first.wait()
    hidden = dot(slot_order(count), saved_ref[...], ((1,), (0,))).astype(jnp.bfloat16)
    hidden_ref[...] = hidden
    for p in range(pieces):
        loads[p].wait()
        rows = slice(p * block, (p + 1) * block)
        term = dot(hidden[:, rows], weight_ref[rows, :], ((1,), (0,)))
        if p == 0:
            y_ref[...] = term
        else:
            y_ref[...] += term


def slot_kernel(count, groups, y_ref, hidden_ref, *refs):
    received = refs[:count]
    rows_ref, gate_ref = refs[count : count + 2]
    backs = refs[count + 2 : 2 * count + 2]
    pays = refs[2 * count + 2 : 2 * count + 2 + groups]
    wide_ref, weighted_ref = refs[2 * count + 2 + groups :]
    width = y_ref.shape[1]
    for r in range(count):
        wide_ref[r * CAP : (r + 1) * CAP, :] = received[r][...].astype(jnp.float32)
    rows = wide_ref[:, :width]
    back = jnp.sum(rows * y_ref[...], axis=1, keepdims=True)
    for r in range(count):
        backs[r][...] = jnp.broadcast_to(back[r * CAP : (r + 1) * CAP], backs[r].shape)
    gate = wide_ref[:, width:]
    gate_ref[...] = gate
    rows_ref[...] = rows.astype(jnp.bfloat16)
    weighted_ref[...] = (gate[:, :1] * rows).astype(jnp.bfloat16)
    share = width // groups
    me = lax.axis_index("dp")
    for r in range(groups):
        group = target(me, r, groups)
        pays[r][:, :share] = weighted_ref[:, pl.ds(pl.multiple_of(group * share, share), share)]
        pays[r][:, share:] = hidden_ref[...]


def down_term(pay_ref, share, start, block):
    hidden = pay_ref[:, pl.ds(start, block)]
    return dot(hidden, pay_ref[:, :share], ((0,), (0,))).astype(jnp.bfloat16)


def upstream_kernel(count, pieces, rows_ref, gate_ref, weight_ref, pay_ref, hidden_grad_ref, own_ref):
    units = weight_ref.shape[0]
    share = own_ref.shape[1]
    upstream = dot(rows_ref[...], weight_ref[...], ((1,), (1,)))
    scaled = (gate_ref[:, :1] * upstream).astype(jnp.bfloat16)
    hidden_grad_ref[0, 0] = dot(slot_order(count), scaled, ((0,), (0,))).astype(jnp.bfloat16)
    block = units // pieces
    for p in range(pieces):
        own_ref[p * block : (p + 1) * block, :] = down_term(pay_ref, share, share + p * block, block)


def down_kernel(others, own_ref, *refs):
    out_ref = refs[others]
    block, share = out_ref.shape[1:]
    step = pl.program_id(0)
    total = own_ref[...].astype(jnp.float32)
    for r in range(others):
        start = pl.multiple_of(share + step * block, LANES)
        total = total + down_term(refs[r], share, start, block).astype(jnp.float32)
    out_ref[0] = total


def gate_kernel(count, parts, ids_ref, match_ref, *refs):
    out_ref = refs[-1]
    me = lax.axis_index("expert")
    ids = ids_ref[...]
    total = jnp.zeros(out_ref.shape, jnp.float32)
    for r in range(count):
        value = refs[0][r * CAP : (r + 1) * CAP, :]
        for part in range(1, parts):
            value = value + refs[part][r * CAP : (r + 1) * CAP, :]
        match = match_ref[r * PAD : r * PAD + CAP, :]
        chosen = jnp.sum(jnp.where(match > 0, value, 0.0), axis=0, keepdims=True)
        total = total + jnp.where(ids == target(me, r, count), chosen, 0.0)
    out_ref[...] = total


def on_device(grad_out, expert_ids, gate_values, saved_hidden, down_weight):
    count = lax.axis_size("expert")
    groups = lax.axis_size("dp")
    tensors = lax.axis_size("tensor")
    tokens, width = grad_out.shape
    top = expert_ids.shape[1]
    units = down_weight.shape[1]
    slots = count * CAP
    share = width // groups
    pieces = units // LANES

    ids, match, *sends = pl.pallas_call(
        functools.partial(route_kernel, count),
        out_shape=[
            jax.ShapeDtypeStruct((top, tokens), jnp.int32),
            jax.ShapeDtypeStruct((count * PAD, tokens), jnp.float32),
        ]
        + [jax.ShapeDtypeStruct((CAP, width + LANES), jnp.bfloat16)] * count,
        in_specs=[HBM] * 3,
        out_specs=[VMEM] * (2 + count),
        scratch_shapes=[
            pltpu.VMEM((top, tokens), jnp.int32),
            pltpu.VMEM((top, tokens), jnp.bfloat16),
            pltpu.VMEM((tokens, width), jnp.bfloat16),
            pltpu.SemaphoreType.DMA((3,)),
        ],
        compiler_params=PARAMS,
        cost_estimate=cost(2 * count * PAD * tokens * width, 2 * tokens * width),
        name="route",
    )(*in_hbm(expert_ids.T, gate_values.T, grad_out))

    received = [sends[0]] + [send(sends[r], "expert", r) for r in range(1, count)]

    weight, hidden, y = pl.pallas_call(
        functools.partial(forward_kernel, count, pieces),
        out_shape=[
            jax.ShapeDtypeStruct((units, width), jnp.bfloat16),
            jax.ShapeDtypeStruct((slots, units), jnp.bfloat16),
            jax.ShapeDtypeStruct((slots, width), jnp.float32),
        ],
        in_specs=[VMEM, HBM, HBM],
        out_specs=[VMEM] * 3,
        scratch_shapes=[
            pltpu.VMEM((slots, units), jnp.bfloat16),
            pltpu.SemaphoreType.DMA((pieces + 1,)),
        ],
        compiler_params=PARAMS,
        cost_estimate=cost(2 * slots * units * width, 2 * units * width),
        name="forward",
    )(match, *in_hbm(saved_hidden, down_weight))

    rows, gate, *rest = pl.pallas_call(
        functools.partial(slot_kernel, count, groups),
        out_shape=[
            jax.ShapeDtypeStruct((slots, width), jnp.bfloat16),
            jax.ShapeDtypeStruct((slots, LANES), jnp.float32),
        ]
        + [jax.ShapeDtypeStruct((CAP, LANES), jnp.float32)] * count
        + [jax.ShapeDtypeStruct((slots, share + units), jnp.bfloat16)] * groups,
        in_specs=[VMEM] * (2 + count),
        out_specs=[VMEM] * (2 + count + groups),
        scratch_shapes=[
            pltpu.VMEM((slots, width + LANES), jnp.float32),
            pltpu.VMEM((slots, width), jnp.bfloat16),
        ],
        compiler_params=PARAMS,
        cost_estimate=cost(4 * slots * width, 16 * slots * width),
        name="slots",
    )(y, hidden, *received)
    backs, pays = rest[:count], rest[count:]

    backs = [backs[0]] + [send(backs[r], "expert", r, source) for r in range(1, count)]
    others = [send(pays[r], "dp", r) for r in range(1, groups)]
    back = jnp.concatenate(backs, axis=0)
    backs = [back] + [send(back, "tensor", r) for r in range(1, tensors)]

    hidden_grad, own = pl.pallas_call(
        functools.partial(upstream_kernel, count, pieces),
        out_shape=[
            jax.ShapeDtypeStruct(saved_hidden.shape, jnp.bfloat16),
            jax.ShapeDtypeStruct((units, share), jnp.bfloat16),
        ],
        in_specs=[VMEM] * 4,
        out_specs=[VMEM] * 2,
        compiler_params=PARAMS,
        cost_estimate=cost(2 * slots * units * (width + share), 2 * units * width),
        name="upstream",
    )(rows, gate, weight, pays[0])

    down_grad = pl.pallas_call(
        functools.partial(down_kernel, groups - 1),
        grid=(pieces,),
        out_shape=jax.ShapeDtypeStruct((1, units, share), jnp.float32),
        in_specs=[pl.BlockSpec((LANES, share), lambda i: (i, 0))] + [VMEM] * (groups - 1),
        out_specs=pl.BlockSpec((1, LANES, share), lambda i: (0, i, 0)),
        compiler_params=PARAMS,
        cost_estimate=cost(2 * slots * units * share, 4 * units * share),
        name="down",
    )(own, *others)

    gate_grad = pl.pallas_call(
        functools.partial(gate_kernel, count, tensors),
        out_shape=jax.ShapeDtypeStruct(ids.shape, jnp.float32),
        in_specs=[VMEM] * (2 + tensors),
        out_specs=VMEM,
        compiler_params=PARAMS,
        cost_estimate=cost(tensors * slots * tokens, 4 * tensors * slots * tokens),
        name="gates",
    )(ids, match, *backs)
    return (gate_grad.T, hidden_grad, down_grad)


def solution(mesh):
    return jax.shard_map(
        on_device,
        mesh=mesh,
        in_specs=(
            P(("dp", "expert"), None),
            P(("dp", "expert"), None),
            P(("dp", "expert"), None),
            P("dp", "expert", None, "tensor"),
            P("expert", "tensor", None),
        ),
        out_specs=(
            P(("dp", "expert"), None),
            P("dp", "expert", None, "tensor"),
            P("expert", "tensor", "dp"),
        ),
        check_vma=False,
    )
```

```python
import functools

import jax
import jax.numpy as jnp
from jax import lax
from jax.experimental import pallas as pl
from jax.experimental.pallas import tpu as pltpu
from jax.sharding import PartitionSpec as P

CAP = 4
LANES = 128
PAD = 8
VMEM = pl.BlockSpec(memory_space=pltpu.VMEM)
HBM = pl.BlockSpec(memory_space=pltpu.HBM)
PARAMS = pltpu.CompilerParams(vmem_limit_bytes=32 * 2**20)


def dot(a, b, dims):
    return lax.dot_general(a, b, (dims, ((), ())), preferred_element_type=jnp.float32)


def in_hbm(*arrays):
    return [pltpu.with_memory_space_constraint(x, pltpu.HBM) for x in arrays]


def cost(flops, nbytes):
    return pl.CostEstimate(flops=flops, bytes_accessed=nbytes, transcendentals=0)


def paired(size):
    return size & (size - 1) == 0


def target(me, step, size):
    if paired(size):
        return me ^ step
    after = me + step
    return after % size if isinstance(me, int) else jnp.where(after >= size, after - size, after)


def source(me, step, size):
    if paired(size):
        return me ^ step
    before = me - step
    return before % size if isinstance(me, int) else jnp.where(before < 0, before + size, before)


def reply(step, size):
    return step if paired(size) else -step % size


def send(value, axis, step, give=target):
    size = lax.axis_size(axis)
    return lax.ppermute(value, axis, [(i, give(i, step, size)) for i in range(size)])


def front_kernel(count, pieces, *refs):
    ids_hbm, gates_hbm, grad_hbm, hidden_hbm, weight_hbm = refs[:5]
    ids_ref, match_ref, weight_ref, hidden_ref = refs[5:9]
    sends = refs[9 : 9 + count]
    gates_ref, grad_ref, saved_ref, both_ref, sems = refs[9 + count :]
    units, width = weight_ref.shape
    block = units // pieces
    top, tokens = ids_ref.shape
    pairs = [(ids_hbm, ids_ref), (gates_hbm, gates_ref), (hidden_hbm.at[0, 0], saved_ref), (grad_hbm, grad_ref)]
    for p in range(pieces):
        part = pl.ds(p * block, block)
        pairs.append((weight_hbm.at[0, part], weight_ref.at[part]))
    copies = [pltpu.make_async_copy(*pair, sems.at[n]) for n, pair in enumerate(pairs)]
    for copy in copies:
        copy.start()
    me = lax.axis_index("expert")
    rows = count * PAD
    row = lax.broadcasted_iota(jnp.int32, (rows, tokens), 0)
    expert = target(me, row // PAD, count)
    place = row % PAD
    earlier = lax.broadcasted_iota(jnp.int32, (tokens, tokens), 0)
    later = lax.broadcasted_iota(jnp.int32, (tokens, tokens), 1)
    order = (earlier < later).astype(jnp.bfloat16)
    for copy in copies[:3]:
        copy.wait()
    ids = ids_ref[...]
    gates = gates_ref[...].astype(jnp.float32)
    member = jnp.zeros((rows, tokens), jnp.float32)
    gate = jnp.zeros((rows, tokens), jnp.float32)
    for k in range(top):
        hit = ids[k : k + 1, :] == expert
        member = jnp.where(hit, 1.0, member)
        gate = jnp.where(hit, gates[k : k + 1, :], gate)
    before = dot(member.astype(jnp.bfloat16), order, ((1,), (0,)))
    taken = (member > 0) & (before == place.astype(jnp.float32)) & (place < CAP)
    match = taken.astype(jnp.float32)
    match_ref[...] = match
    slot_gate = jnp.sum(match * gate, axis=1, keepdims=True)
    match = match.astype(jnp.bfloat16)

    slots = count * CAP
    saved = saved_ref[...]
    hidden_ref[...] = dot(slot_order(count), saved, ((1,), (0,))).astype(jnp.bfloat16)
    here = lax.broadcasted_iota(jnp.int32, (rows, slots), 0)
    there = lax.broadcasted_iota(jnp.int32, (rows, slots), 1)
    chosen = (here % PAD >= CAP) & (there == target(me, here // PAD, count) * CAP + here % PAD - CAP)
    hidden = dot(chosen.astype(jnp.bfloat16), saved, ((1,), (0,))).astype(jnp.bfloat16)

    copies[3].wait()
    both_ref[...] = dot(match, grad_ref[...], ((1,), (0,)))
    for p in range(pieces):
        copies[4 + p].wait()
        part = slice(p * block, (p + 1) * block)
        both_ref[...] += dot(hidden[:, part], weight_ref[part, :], ((1,), (0,)))
    for r in range(count):
        part = slice(r * PAD, (r + 1) * PAD)
        sends[r][:, :width] = both_ref[part, :].astype(jnp.bfloat16)
        sends[r][:, width:] = jnp.broadcast_to(slot_gate[part], (PAD, LANES)).astype(jnp.bfloat16)


def slot_order(count):
    me = lax.axis_index("expert")
    slots = count * CAP
    here = lax.broadcasted_iota(jnp.int32, (slots, slots), 0)
    saved = lax.broadcasted_iota(jnp.int32, (slots, slots), 1)
    return (saved == source(me, here // CAP, count) * CAP + here % CAP).astype(jnp.bfloat16)


def slot_kernel(count, groups, hidden_ref, *refs):
    sent = refs[:count]
    received = refs[count : 2 * count]
    back_ref, rows_ref, gate_ref = refs[2 * count : 2 * count + 3]
    pays = refs[2 * count + 3 : 2 * count + 3 + groups]
    wide_ref, weighted_ref = refs[2 * count + 3 + groups :]
    width = rows_ref.shape[1]
    for r in range(count):
        mine = sent[r][...].astype(jnp.float32)[:CAP, :width]
        theirs = received[reply(r, count)][...].astype(jnp.float32)[CAP:, :width]
        back = jnp.sum(mine * theirs, axis=1, keepdims=True)
        back_ref[r * CAP : (r + 1) * CAP, :] = jnp.broadcast_to(back, (CAP, LANES))
        wide_ref[r * CAP : (r + 1) * CAP, :] = received[r][...].astype(jnp.float32)[:CAP]
    rows = wide_ref[:, :width]
    gate = wide_ref[:, width:]
    gate_ref[...] = gate
    rows_ref[...] = rows.astype(jnp.bfloat16)
    weighted_ref[...] = (gate[:, :1] * rows).astype(jnp.bfloat16)
    share = width // groups
    me = lax.axis_index("dp")
    for r in range(groups):
        group = target(me, r, groups)
        pays[r][:, :share] = weighted_ref[:, pl.ds(pl.multiple_of(group * share, share), share)]
        pays[r][:, share:] = hidden_ref[...]


def down_term(pay_ref, share, start, block):
    hidden = pay_ref[:, pl.ds(start, block)]
    return dot(hidden, pay_ref[:, :share], ((0,), (0,))).astype(jnp.bfloat16)


def upstream_kernel(count, pieces, rows_ref, gate_ref, weight_ref, pay_ref, hidden_grad_ref, own_ref):
    units = weight_ref.shape[0]
    share = own_ref.shape[1]
    upstream = dot(weight_ref[...], rows_ref[...], ((1,), (1,))).T
    scaled = (gate_ref[:, :1] * upstream).astype(jnp.bfloat16)
    hidden_grad_ref[0, 0] = dot(slot_order(count), scaled, ((0,), (0,))).astype(jnp.bfloat16)
    block = units // pieces
    for p in range(pieces):
        own_ref[p * block : (p + 1) * block, :] = down_term(pay_ref, share, share + p * block, block)


def down_kernel(others, pieces, own_ref, *refs):
    out_hbm, total_ref, sems = refs[others:]
    units, share = own_ref.shape
    block = units // pieces
    copies = []
    for p in range(pieces):
        part = slice(p * block, (p + 1) * block)
        total = own_ref[part, :].astype(jnp.float32)
        for r in range(others):
            total = total + down_term(refs[r], share, share + p * block, block).astype(jnp.float32)
        total_ref[part, :] = total
        part = pl.ds(p * block, block)
        copies.append(pltpu.make_async_copy(total_ref.at[part], out_hbm.at[0, part], sems.at[p]))
        copies[-1].start()
    for copy in copies:
        copy.wait()


def gate_kernel(count, ids_ref, match_ref, back_ref, out_ref):
    me = lax.axis_index("expert")
    ids = ids_ref[...]
    total = jnp.zeros(out_ref.shape, jnp.float32)
    for r in range(count):
        value = back_ref[r * CAP : (r + 1) * CAP, :]
        match = match_ref[r * PAD : r * PAD + CAP, :]
        chosen = jnp.sum(jnp.where(match > 0, value, 0.0), axis=0, keepdims=True)
        total = total + jnp.where(ids == target(me, r, count), chosen, 0.0)
    out_ref[...] = total


def total_over(value, axis):
    size = lax.axis_size(axis)
    if not paired(size):
        return sum([send(value, axis, r) for r in range(1, size)], value)
    step = 1
    while step < size:
        value = value + send(value, axis, step)
        step *= 2
    return value


def on_device(grad_out, expert_ids, gate_values, saved_hidden, down_weight):
    count = lax.axis_size("expert")
    groups = lax.axis_size("dp")
    tokens, width = grad_out.shape
    top = expert_ids.shape[1]
    units = down_weight.shape[1]
    slots = count * CAP
    share = width // groups
    pieces = units // LANES

    payload = jax.ShapeDtypeStruct((PAD, width + LANES), jnp.bfloat16)
    ids, match, weight, hidden, *sends = pl.pallas_call(
        functools.partial(front_kernel, count, pieces),
        out_shape=[
            jax.ShapeDtypeStruct((top, tokens), jnp.int32),
            jax.ShapeDtypeStruct((count * PAD, tokens), jnp.float32),
            jax.ShapeDtypeStruct((units, width), jnp.bfloat16),
            jax.ShapeDtypeStruct((slots, units), jnp.bfloat16),
        ]
        + [payload] * count,
        in_specs=[HBM] * 5,
        out_specs=[VMEM] * (4 + count),
        scratch_shapes=[
            pltpu.VMEM((top, tokens), jnp.bfloat16),
            pltpu.VMEM((tokens, width), jnp.bfloat16),
            pltpu.VMEM((slots, units), jnp.bfloat16),
            pltpu.VMEM((count * PAD, width), jnp.float32),
            pltpu.SemaphoreType.DMA((4 + pieces,)),
        ],
        compiler_params=PARAMS,
        cost_estimate=cost(2 * count * PAD * (tokens + units) * width, 2 * (tokens + units) * width),
        name="front",
    )(*in_hbm(expert_ids.T, gate_values.T, grad_out, saved_hidden, down_weight))

    received = [sends[0]] + [send(sends[r], "expert", r) for r in range(1, count)]

    back, rows, gate, *pays = pl.pallas_call(
        functools.partial(slot_kernel, count, groups),
        out_shape=[
            jax.ShapeDtypeStruct((slots, LANES), jnp.float32),
            jax.ShapeDtypeStruct((slots, width), jnp.bfloat16),
            jax.ShapeDtypeStruct((slots, LANES), jnp.float32),
        ]
        + [jax.ShapeDtypeStruct((slots, share + units), jnp.bfloat16)] * groups,
        in_specs=[VMEM] * (1 + 2 * count),
        out_specs=[VMEM] * (3 + groups),
        scratch_shapes=[
            pltpu.VMEM((slots, width + LANES), jnp.float32),
            pltpu.VMEM((slots, width), jnp.bfloat16),
        ],
        compiler_params=PARAMS,
        cost_estimate=cost(4 * slots * width, 16 * slots * width),
        name="slots",
    )(hidden, *sends, *received)

    others = [send(pays[r], "dp", r) for r in range(1, groups)]
    back = total_over(back, "tensor")

    hidden_grad, own = pl.pallas_call(
        functools.partial(upstream_kernel, count, pieces),
        out_shape=[
            jax.ShapeDtypeStruct(saved_hidden.shape, jnp.bfloat16),
            jax.ShapeDtypeStruct((units, share), jnp.bfloat16),
        ],
        in_specs=[VMEM] * 4,
        out_specs=[VMEM] * 2,
        compiler_params=PARAMS,
        cost_estimate=cost(2 * slots * units * (width + share), 2 * units * width),
        name="upstream",
    )(rows, gate, weight, pays[0])

    down_grad = pl.pallas_call(
        functools.partial(down_kernel, groups - 1, pieces),
        out_shape=jax.ShapeDtypeStruct((1, units, share), jnp.float32),
        in_specs=[VMEM] * groups,
        out_specs=HBM,
        scratch_shapes=[
            pltpu.VMEM((units, share), jnp.float32),
            pltpu.SemaphoreType.DMA((pieces,)),
        ],
        compiler_params=PARAMS,
        cost_estimate=cost(2 * slots * units * share, 4 * units * share),
        name="down",
    )(own, *others)

    gate_grad = pl.pallas_call(
        functools.partial(gate_kernel, count),
        out_shape=jax.ShapeDtypeStruct(ids.shape, jnp.float32),
        in_specs=[VMEM] * 3,
        out_specs=VMEM,
        compiler_params=PARAMS,
        cost_estimate=cost(slots * tokens, 4 * slots * tokens),
        name="gates",
    )(ids, match, back)
    return (gate_grad.T, hidden_grad, down_grad)


def solution(mesh):
    return jax.shard_map(
        on_device,
        mesh=mesh,
        in_specs=(
            P(("dp", "expert"), None),
            P(("dp", "expert"), None),
            P(("dp", "expert"), None),
            P("dp", "expert", None, "tensor"),
            P("expert", "tensor", None),
        ),
        out_specs=(
            P(("dp", "expert"), None),
            P("dp", "expert", None, "tensor"),
            P("expert", "tensor", "dp"),
        ),
        check_vma=False,
    )
```

```python
import functools

import jax
import jax.numpy as jnp
from jax import lax
from jax.experimental import pallas as pl
from jax.experimental.pallas import tpu as pltpu
from jax.sharding import PartitionSpec as P

CAP = 4
LANES = 128
PAD = 8
VMEM = pl.BlockSpec(memory_space=pltpu.VMEM)
HBM = pl.BlockSpec(memory_space=pltpu.HBM)
PARAMS = pltpu.CompilerParams(vmem_limit_bytes=32 * 2**20)


def dot(a, b, dims):
    return lax.dot_general(a, b, (dims, ((), ())), preferred_element_type=jnp.float32)


def in_hbm(*arrays):
    return [pltpu.with_memory_space_constraint(x, pltpu.HBM) for x in arrays]


def cost(flops, nbytes):
    return pl.CostEstimate(flops=flops, bytes_accessed=nbytes, transcendentals=0)


def paired(size):
    return size & (size - 1) == 0


def target(me, step, size):
    if paired(size):
        return me ^ step
    after = me + step
    return after % size if isinstance(me, int) else jnp.where(after >= size, after - size, after)


def source(me, step, size):
    if paired(size):
        return me ^ step
    before = me - step
    return before % size if isinstance(me, int) else jnp.where(before < 0, before + size, before)


def reply(step, size):
    return step if paired(size) else -step % size


def send(value, axis, step, give=target):
    size = lax.axis_size(axis)
    return lax.ppermute(value, axis, [(i, give(i, step, size)) for i in range(size)])


def front_kernel(count, pieces, *refs):
    ids_hbm, gates_hbm, grad_hbm, hidden_hbm, weight_hbm = refs[:5]
    ids_ref, match_ref, weight_ref, hidden_ref = refs[5:9]
    sends = refs[9 : 9 + count]
    gates_ref, grad_ref, saved_ref, sems = refs[9 + count :]
    units, width = weight_ref.shape
    block = width // pieces
    top, tokens = ids_ref.shape
    pairs = [(ids_hbm, ids_ref), (gates_hbm, gates_ref), (hidden_hbm.at[0, 0], saved_ref)]
    for p in range(pieces):
        part = pl.ds(p * block, block)
        pairs.append((grad_hbm.at[:, part], grad_ref.at[:, part]))
        pairs.append((weight_hbm.at[0, :, part], weight_ref.at[:, part]))
    copies = [pltpu.make_async_copy(*pair, sems.at[n]) for n, pair in enumerate(pairs)]
    for copy in copies:
        copy.start()
    me = lax.axis_index("expert")
    rows = count * PAD
    row = lax.broadcasted_iota(jnp.int32, (rows, tokens), 0)
    expert = target(me, row // PAD, count)
    place = row % PAD
    earlier = lax.broadcasted_iota(jnp.int32, (tokens, tokens), 0)
    later = lax.broadcasted_iota(jnp.int32, (tokens, tokens), 1)
    order = (earlier < later).astype(jnp.bfloat16)
    for copy in copies[:3]:
        copy.wait()
    ids = ids_ref[...]
    gates = gates_ref[...].astype(jnp.float32)
    member = jnp.zeros((rows, tokens), jnp.float32)
    gate = jnp.zeros((rows, tokens), jnp.float32)
    for k in range(top):
        hit = ids[k : k + 1, :] == expert
        member = jnp.where(hit, 1.0, member)
        gate = jnp.where(hit, gates[k : k + 1, :], gate)
    before = dot(member.astype(jnp.bfloat16), order, ((1,), (0,)))
    taken = (member > 0) & (before == place.astype(jnp.float32)) & (place < CAP)
    match = taken.astype(jnp.float32)
    match_ref[...] = match
    slot_gate = jnp.sum(match * gate, axis=1, keepdims=True)
    match = match.astype(jnp.bfloat16)

    slots = count * CAP
    saved = saved_ref[...]
    hidden_ref[...] = dot(slot_order(count), saved, ((1,), (0,))).astype(jnp.bfloat16)
    here = lax.broadcasted_iota(jnp.int32, (rows, slots), 0)
    there = lax.broadcasted_iota(jnp.int32, (rows, slots), 1)
    chosen = (here % PAD >= CAP) & (there == target(me, here // PAD, count) * CAP + here % PAD - CAP)
    hidden = dot(chosen.astype(jnp.bfloat16), saved, ((1,), (0,))).astype(jnp.bfloat16)

    for r in range(count):
        part = slice(r * PAD, (r + 1) * PAD)
        sends[r][:, width:] = jnp.broadcast_to(slot_gate[part], (PAD, LANES)).astype(jnp.bfloat16)
    for p in range(pieces):
        part = slice(p * block, (p + 1) * block)
        copies[3 + 2 * p].wait()
        both = dot(match, grad_ref[:, part], ((1,), (0,)))
        copies[4 + 2 * p].wait()
        both = both + dot(hidden, weight_ref[:, part], ((1,), (0,)))
        for r in range(count):
            sends[r][:, part] = both[r * PAD : (r + 1) * PAD].astype(jnp.bfloat16)


def slot_order(count):
    me = lax.axis_index("expert")
    slots = count * CAP
    here = lax.broadcasted_iota(jnp.int32, (slots, slots), 0)
    saved = lax.broadcasted_iota(jnp.int32, (slots, slots), 1)
    return (saved == source(me, here // CAP, count) * CAP + here % CAP).astype(jnp.bfloat16)


def slot_kernel(count, groups, hidden_ref, *refs):
    sent = refs[:count]
    received = refs[count : 2 * count]
    back_ref, rows_ref, gate_ref = refs[2 * count : 2 * count + 3]
    pays = refs[2 * count + 3 : 2 * count + 3 + groups]
    wide_ref, weighted_ref = refs[2 * count + 3 + groups :]
    width = rows_ref.shape[1]
    for r in range(count):
        mine = sent[r][...].astype(jnp.float32)[:CAP, :width]
        theirs = received[reply(r, count)][...].astype(jnp.float32)[CAP:, :width]
        back = jnp.sum(mine * theirs, axis=1, keepdims=True)
        back_ref[r * CAP : (r + 1) * CAP, :] = jnp.broadcast_to(back, (CAP, LANES))
        wide_ref[r * CAP : (r + 1) * CAP, :] = received[r][...].astype(jnp.float32)[:CAP]
    rows = wide_ref[:, :width]
    gate = wide_ref[:, width:]
    gate_ref[...] = gate
    rows_ref[...] = rows.astype(jnp.bfloat16)
    weighted_ref[...] = (gate[:, :1] * rows).astype(jnp.bfloat16)
    share = width // groups
    me = lax.axis_index("dp")
    for r in range(groups):
        group = target(me, r, groups)
        pays[r][:, :share] = weighted_ref[:, pl.ds(pl.multiple_of(group * share, share), share)]
        pays[r][:, share:] = hidden_ref[...]


def down_term(pay_ref, share, start, block):
    hidden = pay_ref[:, pl.ds(start, block)]
    return dot(hidden, pay_ref[:, :share], ((0,), (0,))).astype(jnp.bfloat16)


def own_kernel(pieces, pay_ref, own_ref):
    units, share = own_ref.shape
    block = units // pieces
    for p in range(pieces):
        own_ref[p * block : (p + 1) * block, :] = down_term(pay_ref, share, share + p * block, block)


def last_kernel(count, others, parts, pieces, *refs):
    own_ref = refs[0]
    pays = refs[1 : 1 + others]
    backs = refs[1 + others : 1 + others + parts]
    ids_ref, match_ref, rows_ref, gate_ref, weight_ref = refs[1 + others + parts : 6 + others + parts]
    gate_hbm, hidden_hbm, down_hbm, gate_out, hidden_out, down_out, sems = refs[6 + others + parts :]
    units, share = own_ref.shape
    block = units // pieces
    copies = []

    def write(n, values, destination):
        copies.append(pltpu.make_async_copy(values, destination, sems.at[n]))
        copies[-1].start()

    for p in range(pieces):
        part = slice(p * block, (p + 1) * block)
        total = own_ref[part, :].astype(jnp.float32)
        for pay_ref in pays:
            total = total + down_term(pay_ref, share, share + p * block, block).astype(jnp.float32)
        down_out[part, :] = total
        part = pl.ds(p * block, block)
        write(p, down_out.at[part], down_hbm.at[0, part])

    me = lax.axis_index("expert")
    ids = ids_ref[...]
    back = backs[0][...]
    for ref in backs[1:]:
        back = back + ref[...]
    total = jnp.zeros(gate_out.shape, jnp.float32)
    for r in range(count):
        value = back[r * CAP : (r + 1) * CAP, :]
        match = match_ref[r * PAD : r * PAD + CAP, :]
        chosen = jnp.sum(jnp.where(match > 0, value, 0.0), axis=0, keepdims=True)
        total = total + jnp.where(ids == target(me, r, count), chosen, 0.0)
    gate_out[...] = total
    write(pieces, gate_out, gate_hbm)

    upstream = dot(rows_ref[...], weight_ref[...], ((1,), (1,)))
    scaled = (gate_ref[:, :1] * upstream).astype(jnp.bfloat16)
    hidden_out[...] = dot(slot_order(count), scaled, ((0,), (0,))).astype(jnp.bfloat16)
    write(pieces + 1, hidden_out, hidden_hbm.at[0, 0])
    for copy in copies:
        copy.wait()


def on_device(grad_out, expert_ids, gate_values, saved_hidden, down_weight):
    count = lax.axis_size("expert")
    groups = lax.axis_size("dp")
    tensors = lax.axis_size("tensor")
    tokens, width = grad_out.shape
    top = expert_ids.shape[1]
    units = down_weight.shape[1]
    slots = count * CAP
    share = width // groups
    pieces = units // LANES
    columns = width // 512

    payload = jax.ShapeDtypeStruct((PAD, width + LANES), jnp.bfloat16)
    ids, match, weight, hidden, *sends = pl.pallas_call(
        functools.partial(front_kernel, count, columns),
        out_shape=[
            jax.ShapeDtypeStruct((top, tokens), jnp.int32),
            jax.ShapeDtypeStruct((count * PAD, tokens), jnp.float32),
            jax.ShapeDtypeStruct((units, width), jnp.bfloat16),
            jax.ShapeDtypeStruct((slots, units), jnp.bfloat16),
        ]
        + [payload] * count,
        in_specs=[HBM] * 5,
        out_specs=[VMEM] * (4 + count),
        scratch_shapes=[
            pltpu.VMEM((top, tokens), jnp.bfloat16),
            pltpu.VMEM((tokens, width), jnp.bfloat16),
            pltpu.VMEM((slots, units), jnp.bfloat16),
            pltpu.SemaphoreType.DMA((3 + 2 * columns,)),
        ],
        compiler_params=PARAMS,
        cost_estimate=cost(2 * count * PAD * (tokens + units) * width, 2 * (tokens + units) * width),
        name="front",
    )(*in_hbm(expert_ids.T, gate_values.T, grad_out, saved_hidden, down_weight))

    received = [sends[0]] + [send(sends[r], "expert", r) for r in reversed(range(1, count))][::-1]

    back, rows, gate, *pays = pl.pallas_call(
        functools.partial(slot_kernel, count, groups),
        out_shape=[
            jax.ShapeDtypeStruct((slots, LANES), jnp.float32),
            jax.ShapeDtypeStruct((slots, width), jnp.bfloat16),
            jax.ShapeDtypeStruct((slots, LANES), jnp.float32),
        ]
        + [jax.ShapeDtypeStruct((slots, share + units), jnp.bfloat16)] * groups,
        in_specs=[VMEM] * (1 + 2 * count),
        out_specs=[VMEM] * (3 + groups),
        scratch_shapes=[
            pltpu.VMEM((slots, width + LANES), jnp.float32),
            pltpu.VMEM((slots, width), jnp.bfloat16),
        ],
        compiler_params=PARAMS,
        cost_estimate=cost(4 * slots * width, 16 * slots * width),
        name="slots",
    )(hidden, *sends, *received)

    others = [send(pays[r], "dp", r) for r in range(1, groups)]
    backs = [back] + [send(back, "tensor", r) for r in range(1, tensors)]

    own = pl.pallas_call(
        functools.partial(own_kernel, pieces),
        out_shape=jax.ShapeDtypeStruct((units, share), jnp.bfloat16),
        in_specs=[VMEM],
        out_specs=VMEM,
        compiler_params=PARAMS,
        cost_estimate=cost(2 * slots * units * share, 2 * units * share),
        name="own",
    )(pays[0])

    gate_grad, hidden_grad, down_grad = pl.pallas_call(
        functools.partial(last_kernel, count, groups - 1, tensors, pieces),
        out_shape=[
            jax.ShapeDtypeStruct(ids.shape, jnp.float32),
            jax.ShapeDtypeStruct(saved_hidden.shape, jnp.bfloat16),
            jax.ShapeDtypeStruct((1, units, share), jnp.float32),
        ],
        in_specs=[VMEM] * (5 + groups + tensors),
        out_specs=[HBM] * 3,
        scratch_shapes=[
            pltpu.VMEM(ids.shape, jnp.float32),
            pltpu.VMEM((slots, units), jnp.bfloat16),
            pltpu.VMEM((units, share), jnp.float32),
            pltpu.SemaphoreType.DMA((pieces + 2,)),
        ],
        compiler_params=PARAMS,
        cost_estimate=cost(2 * slots * units * (width + share), 4 * units * share),
        name="last",
    )(own, *others, *backs, ids, match, rows, gate, weight)
    return (gate_grad.T, hidden_grad, down_grad)


def solution(mesh):
    return jax.shard_map(
        on_device,
        mesh=mesh,
        in_specs=(
            P(("dp", "expert"), None),
            P(("dp", "expert"), None),
            P(("dp", "expert"), None),
            P("dp", "expert", None, "tensor"),
            P("expert", "tensor", None),
        ),
        out_specs=(
            P(("dp", "expert"), None),
            P("dp", "expert", None, "tensor"),
            P("expert", "tensor", "dp"),
        ),
        check_vma=False,
    )
```

```python
import functools

import jax
import jax.numpy as jnp
from jax import lax
from jax.experimental import pallas as pl
from jax.experimental.pallas import tpu as pltpu
from jax.sharding import PartitionSpec as P

CAP = 4
LANES = 128
JOINT = 1
AFTER_WAIT = (10**9, 10**7)
PAD = 8
VMEM = pl.BlockSpec(memory_space=pltpu.VMEM)
HBM = pl.BlockSpec(memory_space=pltpu.HBM)
PARAMS = pltpu.CompilerParams(vmem_limit_bytes=32 * 2**20)


def dot(a, b, dims):
    return lax.dot_general(a, b, (dims, ((), ())), preferred_element_type=jnp.float32)


def in_hbm(*arrays):
    return [pltpu.with_memory_space_constraint(x, pltpu.HBM) for x in arrays]


def cost(flops, nbytes):
    return pl.CostEstimate(flops=flops, bytes_accessed=nbytes, transcendentals=0)


def paired(size):
    return size & (size - 1) == 0


def target(me, step, size):
    if paired(size):
        return me ^ ((size - step) % size)
    after = me + step
    return after % size if isinstance(me, int) else jnp.where(after >= size, after - size, after)


def source(me, step, size):
    if paired(size):
        return target(me, step, size)
    before = me - step
    return before % size if isinstance(me, int) else jnp.where(before < 0, before + size, before)


def reply(step, size):
    return step if paired(size) else -step % size


def apart(size):
    return [r for r in range(size) if r != JOINT]


def send(value, axis, step, give=target):
    size = lax.axis_size(axis)
    return lax.ppermute(value, axis, [(i, give(i, step, size)) for i in range(size)])


def front_kernel(count, pieces, *refs):
    ids_hbm, gates_hbm, grad_hbm, hidden_hbm, weight_hbm = refs[:5]
    ids_ref, match_ref, weight_ref, hidden_ref = refs[5:9]
    sends = refs[9 : 9 + count]
    products = refs[9 + count : 8 + 2 * count]
    gates_ref, grad_ref, saved_ref, picked_ref, total_ref, sems = refs[8 + 2 * count :]
    units, width = weight_ref.shape
    top, tokens = ids_ref.shape
    pairs = [(ids_hbm, ids_ref), (gates_hbm, gates_ref), (hidden_hbm.at[0, 0], saved_ref)]
    half = tokens // 2
    for p in range(2):
        part = pl.ds(p * half, half)
        pairs.append((grad_hbm.at[part], grad_ref.at[part]))
    half = units // (2 * pieces)
    for p in range(2 * pieces):
        part = pl.ds(p * half, half)
        pairs.append((weight_hbm.at[0, part], weight_ref.at[part]))
    copies = [pltpu.make_async_copy(*pair, sems.at[n]) for n, pair in enumerate(pairs)]
    for copy in copies:
        copy.start()
    me = lax.axis_index("expert")
    rows = count * PAD
    row = lax.broadcasted_iota(jnp.int32, (rows, tokens), 0)
    expert = target(me, row // PAD, count)
    place = row % PAD
    earlier = lax.broadcasted_iota(jnp.int32, (tokens, tokens), 0)
    later = lax.broadcasted_iota(jnp.int32, (tokens, tokens), 1)
    order = (earlier < later).astype(jnp.bfloat16)
    for copy in copies[:3]:
        copy.wait()
    ids = ids_ref[...]
    gates = gates_ref[...].astype(jnp.float32)
    member = jnp.zeros((rows, tokens), jnp.float32)
    gate = jnp.zeros((rows, tokens), jnp.float32)
    for k in range(top):
        hit = ids[k : k + 1, :] == expert
        member = jnp.where(hit, 1.0, member)
        gate = jnp.where(hit, gates[k : k + 1, :], gate)
    before = dot(member.astype(jnp.bfloat16), order, ((1,), (0,)))
    taken = (member > 0) & (before == place.astype(jnp.float32)) & (place < CAP)
    match = taken.astype(jnp.float32)
    match_ref[...] = match
    slot_gate = jnp.sum(match * gate, axis=1, keepdims=True)
    match = match.astype(jnp.bfloat16)

    slots = count * CAP
    saved = saved_ref[...]
    hidden_ref[...] = dot(slot_order(count), saved, ((1,), (0,))).astype(jnp.bfloat16)
    here = lax.broadcasted_iota(jnp.int32, (rows, slots), 0)
    there = lax.broadcasted_iota(jnp.int32, (rows, slots), 1)
    place = here % PAD - jnp.where(here // PAD == JOINT, CAP, 0)
    chosen = (place >= 0) & (place < CAP) & (there == target(me, here // PAD, count) * CAP + place)
    hidden = dot(chosen.astype(jnp.bfloat16), saved, ((1,), (0,))).astype(jnp.bfloat16)

    for copy in copies[3:5]:
        copy.wait()
    picked_ref[...] = dot(match, grad_ref[...], ((1,), (0,)))
    for r in range(count):
        part = slice(r * PAD, r * PAD + sends[r].shape[0])
        gate = jnp.broadcast_to(slot_gate[part], (sends[r].shape[0], LANES))
        sends[r][:, width:] = gate.astype(jnp.bfloat16)
        if r != JOINT:
            sends[r][:, :width] = picked_ref[part, :].astype(jnp.bfloat16)
    block = units // pieces
    for p in range(pieces):
        for copy in copies[5 + 2 * p : 7 + 2 * p]:
            copy.wait()
        part = slice(p * block, (p + 1) * block)
        term = dot(hidden[:, part], weight_ref[part, :], ((1,), (0,)))
        total_ref[...] = term if p == 0 else total_ref[...] + term
    for product, r in zip(products, apart(count)):
        product[...] = total_ref[r * PAD : r * PAD + CAP, :].astype(jnp.bfloat16)
    part = slice(JOINT * PAD, (JOINT + 1) * PAD)
    sends[JOINT][:, :width] = (picked_ref[part, :] + total_ref[part, :]).astype(jnp.bfloat16)


def slot_order(count):
    me = lax.axis_index("expert")
    slots = count * CAP
    here = lax.broadcasted_iota(jnp.int32, (slots, slots), 0)
    saved = lax.broadcasted_iota(jnp.int32, (slots, slots), 1)
    return (saved == source(me, here // CAP, count) * CAP + here % CAP).astype(jnp.bfloat16)


def slot_kernel(count, groups, hidden_ref, *refs):
    received = refs[:count]
    rows_ref, gate_ref = refs[count : count + 2]
    pays = refs[count + 2 : count + 2 + groups]
    wide_ref, weighted_ref = refs[count + 2 + groups :]
    width = rows_ref.shape[1]
    for r in range(count):
        wide_ref[r * CAP : (r + 1) * CAP, :] = received[r][...].astype(jnp.float32)[:CAP]
    rows = wide_ref[:, :width]
    gate = wide_ref[:, width:]
    gate_ref[...] = gate
    rows_ref[...] = rows.astype(jnp.bfloat16)
    weighted_ref[...] = (gate[:, :1] * rows).astype(jnp.bfloat16)
    share = width // groups
    me = lax.axis_index("dp")
    for r in range(groups):
        group = target(me, r, groups)
        pays[r][:, :share] = weighted_ref[:, pl.ds(pl.multiple_of(group * share, share), share)]
        pays[r][:, share:] = hidden_ref[...]


def back_kernel(count, *refs):
    sent = refs[:count]
    joint_ref = refs[count]
    products = dict(zip(apart(count), refs[count + 1 : 2 * count]))
    back_ref = refs[2 * count]
    width = products[0].shape[1]
    for r in range(count):
        step = reply(r, count)
        if step != JOINT:
            theirs = products[step][...].astype(jnp.float32)
        else:
            theirs = joint_ref[:, :width].astype(jnp.float32)[CAP:]
        mine = sent[r][:, :width].astype(jnp.float32)[:CAP]
        back = jnp.sum(mine * theirs, axis=1, keepdims=True)
        back_ref[r * CAP : (r + 1) * CAP, :] = jnp.broadcast_to(back, (CAP, LANES))


def down_term(pay_ref, share, start, block):
    hidden = pay_ref[:, pl.ds(start, block)]
    return dot(hidden, pay_ref[:, :share], ((0,), (0,))).astype(jnp.bfloat16)


def own_kernel(pieces, pay_ref, own_ref):
    units, share = own_ref.shape
    block = units // pieces
    for p in range(pieces):
        own_ref[p * block : (p + 1) * block, :] = down_term(pay_ref, share, share + p * block, block)


def last_kernel(count, others, parts, pieces, *refs):
    own_ref = refs[0]
    pays = refs[1 : 1 + others]
    backs = refs[1 + others : 1 + others + parts]
    ids_ref, match_ref, rows_ref, gate_ref, weight_ref = refs[1 + others + parts : 6 + others + parts]
    gate_hbm, hidden_hbm, down_hbm, gate_out, hidden_out, down_out, sems = refs[6 + others + parts :]
    units, share = own_ref.shape
    block = units // pieces
    copies = []

    def write(n, values, destination):
        copies.append(pltpu.make_async_copy(values, destination, sems.at[n]))
        copies[-1].start()

    for p in range(pieces):
        part = slice(p * block, (p + 1) * block)
        total = own_ref[part, :].astype(jnp.float32)
        for pay_ref in pays:
            total = total + down_term(pay_ref, share, share + p * block, block).astype(jnp.float32)
        down_out[part, :] = total
        part = pl.ds(p * block, block)
        write(p, down_out.at[part], down_hbm.at[0, part])

    me = lax.axis_index("expert")
    ids = ids_ref[...]
    back = backs[0][...]
    for ref in backs[1:]:
        back = back + ref[...]
    total = jnp.zeros(gate_out.shape, jnp.float32)
    for r in range(count):
        value = back[r * CAP : (r + 1) * CAP, :]
        match = match_ref[r * PAD : r * PAD + CAP, :]
        chosen = jnp.sum(jnp.where(match > 0, value, 0.0), axis=0, keepdims=True)
        total = total + jnp.where(ids == target(me, r, count), chosen, 0.0)
    gate_out[...] = total
    write(pieces, gate_out, gate_hbm)

    upstream = dot(rows_ref[...], weight_ref[...], ((1,), (1,)))
    scaled = (gate_ref[:, :1] * upstream).astype(jnp.bfloat16)
    hidden_out[...] = dot(slot_order(count), scaled, ((0,), (0,))).astype(jnp.bfloat16)
    write(pieces + 1, hidden_out, hidden_hbm.at[0, 0])
    for copy in copies:
        copy.wait()


def on_device(grad_out, expert_ids, gate_values, saved_hidden, down_weight):
    count = lax.axis_size("expert")
    groups = lax.axis_size("dp")
    tensors = lax.axis_size("tensor")
    tokens, width = grad_out.shape
    top = expert_ids.shape[1]
    units = down_weight.shape[1]
    slots = count * CAP
    share = width // groups
    pieces = units // LANES

    ids, match, weight, hidden, *rest = pl.pallas_call(
        functools.partial(front_kernel, count, pieces),
        out_shape=[
            jax.ShapeDtypeStruct((top, tokens), jnp.int32),
            jax.ShapeDtypeStruct((count * PAD, tokens), jnp.float32),
            jax.ShapeDtypeStruct((units, width), jnp.bfloat16),
            jax.ShapeDtypeStruct((slots, units), jnp.bfloat16),
        ]
        + [
            jax.ShapeDtypeStruct((PAD if r == JOINT else CAP, width + LANES), jnp.bfloat16)
            for r in range(count)
        ]
        + [jax.ShapeDtypeStruct((CAP, width), jnp.bfloat16)] * (count - 1),
        in_specs=[HBM] * 5,
        out_specs=[VMEM] * (3 + 2 * count),
        scratch_shapes=[
            pltpu.VMEM((top, tokens), jnp.bfloat16),
            pltpu.VMEM((tokens, width), jnp.bfloat16),
            pltpu.VMEM((slots, units), jnp.bfloat16),
            pltpu.VMEM((count * PAD, width), jnp.float32),
            pltpu.VMEM((count * PAD, width), jnp.float32),
            pltpu.SemaphoreType.DMA((5 + 2 * pieces,)),
        ],
        compiler_params=PARAMS,
        cost_estimate=cost(2 * count * PAD * (tokens + units) * width, 2 * (tokens + units) * width),
        name="front",
    )(*in_hbm(expert_ids.T, gate_values.T, grad_out, saved_hidden, down_weight))
    sends, products = rest[:count], rest[count:]

    received = [sends[0]] + [send(sends[r], "expert", r) for r in range(1, count)]
    theirs = [products[0]] + [send(products[r - 1], "expert", r) for r in range(JOINT + 1, count)]

    rows, gate, *pays = pl.pallas_call(
        functools.partial(slot_kernel, count, groups),
        out_shape=[
            jax.ShapeDtypeStruct((slots, width), jnp.bfloat16),
            jax.ShapeDtypeStruct((slots, LANES), jnp.float32),
        ]
        + [jax.ShapeDtypeStruct((slots, share + units), jnp.bfloat16)] * groups,
        in_specs=[VMEM] * (1 + count),
        out_specs=[VMEM] * (2 + groups),
        scratch_shapes=[
            pltpu.VMEM((slots, width + LANES), jnp.float32),
            pltpu.VMEM((slots, width), jnp.bfloat16),
        ],
        compiler_params=PARAMS,
        cost_estimate=cost(4 * slots * width, 8 * slots * width),
        name="slots",
    )(hidden, *received)

    back = pl.pallas_call(
        functools.partial(back_kernel, count),
        out_shape=jax.ShapeDtypeStruct((slots, LANES), jnp.float32),
        in_specs=[VMEM] * (2 * count),
        out_specs=VMEM,
        compiler_params=PARAMS,
        cost_estimate=cost(*AFTER_WAIT),
        name="backs",
    )(*sends, received[JOINT], *theirs)

    others = [send(pays[r], "dp", r) for r in range(1, groups)]
    backs = [back] + [send(back, "tensor", r) for r in range(1, tensors)]

    own = pl.pallas_call(
        functools.partial(own_kernel, pieces),
        out_shape=jax.ShapeDtypeStruct((units, share), jnp.bfloat16),
        in_specs=[VMEM],
        out_specs=VMEM,
        compiler_params=PARAMS,
        cost_estimate=cost(2 * slots * units * share, 2 * units * share),
        name="own",
    )(pays[0])

    gate_grad, hidden_grad, down_grad = pl.pallas_call(
        functools.partial(last_kernel, count, groups - 1, tensors, pieces),
        out_shape=[
            jax.ShapeDtypeStruct(ids.shape, jnp.float32),
            jax.ShapeDtypeStruct(saved_hidden.shape, jnp.bfloat16),
            jax.ShapeDtypeStruct((1, units, share), jnp.float32),
        ],
        in_specs=[VMEM] * (5 + groups + tensors),
        out_specs=[HBM] * 3,
        scratch_shapes=[
            pltpu.VMEM(ids.shape, jnp.float32),
            pltpu.VMEM((slots, units), jnp.bfloat16),
            pltpu.VMEM((units, share), jnp.float32),
            pltpu.SemaphoreType.DMA((pieces + 2,)),
        ],
        compiler_params=PARAMS,
        cost_estimate=cost(2 * slots * units * (width + share), 4 * units * share),
        name="last",
    )(own, *others, *backs, ids, match, rows, gate, weight)
    return (gate_grad.T, hidden_grad, down_grad)


def solution(mesh):
    return jax.shard_map(
        on_device,
        mesh=mesh,
        in_specs=(
            P(("dp", "expert"), None),
            P(("dp", "expert"), None),
            P(("dp", "expert"), None),
            P("dp", "expert", None, "tensor"),
            P("expert", "tensor", None),
        ),
        out_specs=(
            P(("dp", "expert"), None),
            P("dp", "expert", None, "tensor"),
            P("expert", "tensor", "dp"),
        ),
        check_vma=False,
    )
```

```python
import functools

import jax
import jax.numpy as jnp
from jax import lax
from jax.experimental import pallas as pl
from jax.experimental.pallas import tpu as pltpu
from jax.sharding import PartitionSpec as P

CAP = 4
LANES = 128
JOINT = 1
AFTER_WAIT = (10**9, 10**7)
PAD = 8
VMEM = pl.BlockSpec(memory_space=pltpu.VMEM)
HBM = pl.BlockSpec(memory_space=pltpu.HBM)
PARAMS = pltpu.CompilerParams(vmem_limit_bytes=32 * 2**20)


def dot(a, b, dims):
    return lax.dot_general(a, b, (dims, ((), ())), preferred_element_type=jnp.float32)


def in_hbm(*arrays):
    return [pltpu.with_memory_space_constraint(x, pltpu.HBM) for x in arrays]


def cost(flops, nbytes):
    return pl.CostEstimate(flops=flops, bytes_accessed=nbytes, transcendentals=0)


def paired(size):
    return size & (size - 1) == 0


def target(me, step, size):
    if paired(size):
        return me ^ ((size - step) % size)
    after = me + step
    return after % size if isinstance(me, int) else jnp.where(after >= size, after - size, after)


def source(me, step, size):
    if paired(size):
        return target(me, step, size)
    before = me - step
    return before % size if isinstance(me, int) else jnp.where(before < 0, before + size, before)


def reply(step, size):
    return step if paired(size) else -step % size


def apart(size):
    return [r for r in range(1, size) if r != JOINT]


def halves():
    return 2 - lax.axis_size("tensor") % 2


def half_of(width):
    size = width // halves()
    return size, pl.multiple_of(lax.axis_index("tensor") % halves() * size, LANES)


def send(value, axis, step, give=target):
    size = lax.axis_size(axis)
    return lax.ppermute(value, axis, [(i, give(i, step, size)) for i in range(size)])


def front_kernel(count, pieces, *refs):
    ids_hbm, gates_hbm, grad_hbm, hidden_hbm, weight_hbm = refs[:5]
    ids_ref, match_ref, weight_ref, hidden_ref, picked_ref, gate_ref, total_ref = refs[5:12]
    sends = dict(zip(range(1, count), refs[12 : 11 + count]))
    products = dict(zip(apart(count), refs[11 + count : 9 + 2 * count]))
    gates_ref, grad_ref, saved_ref, sems = refs[9 + 2 * count :]
    units, width = weight_ref.shape
    top, tokens = ids_ref.shape
    pairs = [(ids_hbm, ids_ref), (gates_hbm, gates_ref), (hidden_hbm.at[0, 0], saved_ref)]
    half = tokens // 2
    for p in range(2):
        part = pl.ds(p * half, half)
        pairs.append((grad_hbm.at[part], grad_ref.at[part]))
    half = units // (2 * pieces)
    for p in range(2 * pieces):
        part = pl.ds(p * half, half)
        pairs.append((weight_hbm.at[0, part], weight_ref.at[part]))
    copies = [pltpu.make_async_copy(*pair, sems.at[n]) for n, pair in enumerate(pairs)]
    for copy in copies:
        copy.start()
    me = lax.axis_index("expert")
    rows = count * PAD
    row = lax.broadcasted_iota(jnp.int32, (rows, tokens), 0)
    expert = target(me, row // PAD, count)
    place = row % PAD
    earlier = lax.broadcasted_iota(jnp.int32, (tokens, tokens), 0)
    later = lax.broadcasted_iota(jnp.int32, (tokens, tokens), 1)
    order = (earlier < later).astype(jnp.bfloat16)
    for copy in copies[:3]:
        copy.wait()
    ids = ids_ref[...]
    gates = gates_ref[...].astype(jnp.float32)
    member = jnp.zeros((rows, tokens), jnp.float32)
    gate = jnp.zeros((rows, tokens), jnp.float32)
    for k in range(top):
        hit = ids[k : k + 1, :] == expert
        member = jnp.where(hit, 1.0, member)
        gate = jnp.where(hit, gates[k : k + 1, :], gate)
    before = dot(member.astype(jnp.bfloat16), order, ((1,), (0,)))
    taken = (member > 0) & (before == place.astype(jnp.float32)) & (place < CAP)
    match = taken.astype(jnp.float32)
    match_ref[...] = match
    slot_gate = jnp.sum(match * gate, axis=1, keepdims=True)
    match = match.astype(jnp.bfloat16)

    slots = count * CAP
    saved = saved_ref[...]
    hidden_ref[...] = dot(slot_order(count), saved, ((1,), (0,))).astype(jnp.bfloat16)
    here = lax.broadcasted_iota(jnp.int32, (rows, slots), 0)
    there = lax.broadcasted_iota(jnp.int32, (rows, slots), 1)
    chosen = (here % PAD < CAP) & (there == target(me, here // PAD, count) * CAP + here % PAD)
    hidden = dot(chosen.astype(jnp.bfloat16), saved, ((1,), (0,))).astype(jnp.bfloat16)

    for copy in copies[3:5]:
        copy.wait()
    gate_ref[...] = jnp.broadcast_to(slot_gate, gate_ref.shape)
    picked_ref[...] = dot(match, grad_ref[...], ((1,), (0,)))
    half, begin = half_of(width)
    for r, ref in sends.items():
        part = slice(r * PAD, r * PAD + CAP)
        ref[:, :half] = picked_ref[part, pl.ds(begin, half)].astype(jnp.bfloat16)
        ref[:, half : half + LANES] = gate_ref[part, :].astype(jnp.bfloat16)
    block = units // pieces
    for p in range(pieces):
        for copy in copies[5 + 2 * p : 7 + 2 * p]:
            copy.wait()
        part = slice(p * block, (p + 1) * block)
        term = dot(hidden[:, part], weight_ref[part, :], ((1,), (0,)))
        total_ref[...] = term if p == 0 else total_ref[...] + term
    for r, ref in products.items():
        ref[...] = total_ref[r * PAD : r * PAD + CAP, :].astype(jnp.bfloat16)
    product = total_ref[JOINT * PAD : JOINT * PAD + CAP, :].astype(jnp.bfloat16)
    sends[JOINT][:, half + LANES :] = product


def slot_order(count):
    me = lax.axis_index("expert")
    slots = count * CAP
    here = lax.broadcasted_iota(jnp.int32, (slots, slots), 0)
    saved = lax.broadcasted_iota(jnp.int32, (slots, slots), 1)
    return (saved == source(me, here // CAP, count) * CAP + here % CAP).astype(jnp.bfloat16)


def pack_kernel(count, *refs):
    packed_ref, wide_ref = refs[count - 1 :]
    for r in range(1, count):
        half = refs[r - 1][:, : packed_ref.shape[1]]
        wide_ref[(r - 1) * CAP : r * CAP, :] = half.astype(jnp.float32)
    packed_ref[...] = wide_ref[...].astype(jnp.bfloat16)


def slot_kernel(count, groups, hidden_ref, picked_ref, sent_gate_ref, *refs):
    received = refs[: count - 1]
    others = refs[count - 1 : -4 - groups]
    rows_ref, gate_ref = refs[-4 - groups : -2 - groups]
    pays = refs[-2 - groups : -2]
    wide_ref, weighted_ref = refs[-2:]
    width = rows_ref.shape[1]
    half, begin = half_of(width)
    wide_ref[:CAP, :] = picked_ref[:CAP, :]
    gate_ref[:CAP, :] = sent_gate_ref[:CAP, :]
    for r in range(1, count):
        part = slice(r * CAP, (r + 1) * CAP)
        wide_ref[part, pl.ds(begin, half)] = received[r - 1][:, :half].astype(jnp.float32)
        gate_ref[part, :] = received[r - 1][:, half : half + LANES].astype(jnp.float32)
    for other in others:
        begin = pl.multiple_of(width - half - begin, LANES)
        wide_ref[CAP:, pl.ds(begin, half)] = other[...].astype(jnp.float32)
    rows = wide_ref[...]
    rows_ref[...] = rows.astype(jnp.bfloat16)
    weighted_ref[...] = (gate_ref[:, :1] * rows).astype(jnp.bfloat16)
    share = width // groups
    me = lax.axis_index("dp")
    for r in range(groups):
        group = target(me, r, groups)
        pays[r][:, :share] = weighted_ref[:, pl.ds(pl.multiple_of(group * share, share), share)]
        pays[r][:, share:] = hidden_ref[...]


def back_kernel(count, picked_ref, total_ref, joint_ref, *refs):
    products = dict(zip(apart(count), refs[: count - 2]))
    back_ref = refs[count - 2]
    width = picked_ref.shape[1]
    for r in range(count):
        step = reply(r, count)
        if step == 0:
            theirs = total_ref[:CAP, :]
        elif step == JOINT:
            theirs = joint_ref[:, joint_ref.shape[1] - width :].astype(jnp.float32)
        else:
            theirs = products[step][...].astype(jnp.float32)
        mine = picked_ref[r * PAD : r * PAD + CAP, :]
        back = jnp.sum(mine * theirs, axis=1, keepdims=True)
        back_ref[r * CAP : (r + 1) * CAP, :] = jnp.broadcast_to(back, (CAP, LANES))


def down_term(pay_ref, share, start, block):
    hidden = pay_ref[:, pl.ds(start, block)]
    return dot(hidden, pay_ref[:, :share], ((0,), (0,))).astype(jnp.bfloat16)


def own_kernel(pieces, pay_ref, own_ref):
    units, share = own_ref.shape
    block = units // pieces
    for p in range(pieces):
        own_ref[p * block : (p + 1) * block, :] = down_term(pay_ref, share, share + p * block, block)


def last_kernel(count, others, parts, pieces, *refs):
    own_ref = refs[0]
    pays = refs[1 : 1 + others]
    backs = refs[1 + others : 1 + others + parts]
    ids_ref, match_ref, rows_ref, gate_ref, weight_ref = refs[1 + others + parts : 6 + others + parts]
    gate_hbm, hidden_hbm, down_hbm, gate_out, hidden_out, down_out, sems = refs[6 + others + parts :]
    units, share = own_ref.shape
    block = units // pieces
    copies = []

    def write(n, values, destination):
        copies.append(pltpu.make_async_copy(values, destination, sems.at[n]))
        copies[-1].start()

    for p in range(pieces):
        part = slice(p * block, (p + 1) * block)
        total = own_ref[part, :].astype(jnp.float32)
        for pay_ref in pays:
            total = total + down_term(pay_ref, share, share + p * block, block).astype(jnp.float32)
        down_out[part, :] = total
        part = pl.ds(p * block, block)
        write(p, down_out.at[part], down_hbm.at[0, part])

    me = lax.axis_index("expert")
    ids = ids_ref[...]
    back = backs[0][...]
    for ref in backs[1:]:
        back = back + ref[...]
    total = jnp.zeros(gate_out.shape, jnp.float32)
    for r in range(count):
        value = back[r * CAP : (r + 1) * CAP, :]
        match = match_ref[r * PAD : r * PAD + CAP, :]
        chosen = jnp.sum(jnp.where(match > 0, value, 0.0), axis=0, keepdims=True)
        total = total + jnp.where(ids == target(me, r, count), chosen, 0.0)
    gate_out[...] = total
    write(pieces, gate_out, gate_hbm)

    upstream = dot(rows_ref[...], weight_ref[...], ((1,), (1,)))
    scaled = (gate_ref[:, :1] * upstream).astype(jnp.bfloat16)
    hidden_out[...] = dot(slot_order(count), scaled, ((0,), (0,))).astype(jnp.bfloat16)
    write(pieces + 1, hidden_out, hidden_hbm.at[0, 0])
    for copy in copies:
        copy.wait()


def on_device(grad_out, expert_ids, gate_values, saved_hidden, down_weight):
    count = lax.axis_size("expert")
    groups = lax.axis_size("dp")
    tensors = lax.axis_size("tensor")
    tokens, width = grad_out.shape
    top = expert_ids.shape[1]
    units = down_weight.shape[1]
    slots = count * CAP
    share = width // groups
    pieces = units // LANES
    half = width // halves()

    ids, match, weight, hidden, picked, sent_gate, total, *rest = pl.pallas_call(
        functools.partial(front_kernel, count, pieces),
        out_shape=[
            jax.ShapeDtypeStruct((top, tokens), jnp.int32),
            jax.ShapeDtypeStruct((count * PAD, tokens), jnp.float32),
            jax.ShapeDtypeStruct((units, width), jnp.bfloat16),
            jax.ShapeDtypeStruct((slots, units), jnp.bfloat16),
            jax.ShapeDtypeStruct((count * PAD, width), jnp.float32),
            jax.ShapeDtypeStruct((count * PAD, LANES), jnp.float32),
            jax.ShapeDtypeStruct((count * PAD, width), jnp.float32),
        ]
        + [
            jax.ShapeDtypeStruct((CAP, half + LANES + width * (r == JOINT)), jnp.bfloat16)
            for r in range(1, count)
        ]
        + [jax.ShapeDtypeStruct((CAP, width), jnp.bfloat16)] * (count - 2),
        in_specs=[HBM] * 5,
        out_specs=[VMEM] * (4 + 2 * count),
        scratch_shapes=[
            pltpu.VMEM((top, tokens), jnp.bfloat16),
            pltpu.VMEM((tokens, width), jnp.bfloat16),
            pltpu.VMEM((slots, units), jnp.bfloat16),
            pltpu.SemaphoreType.DMA((5 + 2 * pieces,)),
        ],
        compiler_params=PARAMS,
        cost_estimate=cost(2 * count * PAD * (tokens + units) * width, 2 * (tokens + units) * width),
        name="front",
    )(*in_hbm(expert_ids.T, gate_values.T, grad_out, saved_hidden, down_weight))
    sends, products = rest[: count - 1], rest[count - 1 :]

    received = [send(x, "expert", r) for r, x in zip(range(1, count), sends)]
    theirs = [send(x, "expert", r) for r, x in zip(apart(count), products)]

    halved = []
    if halves() > 1:
        packed = pl.pallas_call(
            functools.partial(pack_kernel, count),
            out_shape=jax.ShapeDtypeStruct((slots - CAP, half), jnp.bfloat16),
            in_specs=[VMEM] * (count - 1),
            out_specs=VMEM,
            scratch_shapes=[pltpu.VMEM((slots - CAP, half), jnp.float32)],
            compiler_params=PARAMS,
            cost_estimate=cost(slots * width, 4 * slots * width),
            name="pack",
        )(*received)
        halved = [lax.ppermute(packed, "tensor", [(i, i ^ 1) for i in range(tensors)])]

    rows, gate, *pays = pl.pallas_call(
        functools.partial(slot_kernel, count, groups),
        out_shape=[
            jax.ShapeDtypeStruct((slots, width), jnp.bfloat16),
            jax.ShapeDtypeStruct((slots, LANES), jnp.float32),
        ]
        + [jax.ShapeDtypeStruct((slots, share + units), jnp.bfloat16)] * groups,
        in_specs=[VMEM] * (2 + count + len(halved)),
        out_specs=[VMEM] * (2 + groups),
        scratch_shapes=[
            pltpu.VMEM((slots, width), jnp.float32),
            pltpu.VMEM((slots, width), jnp.bfloat16),
        ],
        compiler_params=PARAMS,
        cost_estimate=cost(4 * slots * width, 8 * slots * width),
        name="slots",
    )(hidden, picked, sent_gate, *received, *halved)

    back = pl.pallas_call(
        functools.partial(back_kernel, count),
        out_shape=jax.ShapeDtypeStruct((slots, LANES), jnp.float32),
        in_specs=[VMEM] * (1 + count),
        out_specs=VMEM,
        compiler_params=PARAMS,
        cost_estimate=cost(*AFTER_WAIT),
        name="backs",
    )(picked, total, received[JOINT - 1], *theirs)

    others = [send(pays[r], "dp", r) for r in range(1, groups)]
    backs = [back] + [send(back, "tensor", r) for r in reversed(range(1, tensors))]

    own = pl.pallas_call(
        functools.partial(own_kernel, pieces),
        out_shape=jax.ShapeDtypeStruct((units, share), jnp.bfloat16),
        in_specs=[VMEM],
        out_specs=VMEM,
        compiler_params=PARAMS,
        cost_estimate=cost(2 * slots * units * share, 2 * units * share),
        name="own",
    )(pays[0])

    gate_grad, hidden_grad, down_grad = pl.pallas_call(
        functools.partial(last_kernel, count, groups - 1, tensors, pieces),
        out_shape=[
            jax.ShapeDtypeStruct(ids.shape, jnp.float32),
            jax.ShapeDtypeStruct(saved_hidden.shape, jnp.bfloat16),
            jax.ShapeDtypeStruct((1, units, share), jnp.float32),
        ],
        in_specs=[VMEM] * (5 + groups + tensors),
        out_specs=[HBM] * 3,
        scratch_shapes=[
            pltpu.VMEM(ids.shape, jnp.float32),
            pltpu.VMEM((slots, units), jnp.bfloat16),
            pltpu.VMEM((units, share), jnp.float32),
            pltpu.SemaphoreType.DMA((pieces + 2,)),
        ],
        compiler_params=PARAMS,
        cost_estimate=cost(2 * slots * units * (width + share), 4 * units * share),
        name="last",
    )(own, *others, *backs, ids, match, rows, gate, weight)
    return (gate_grad.T, hidden_grad, down_grad)


def solution(mesh):
    return jax.shard_map(
        on_device,
        mesh=mesh,
        in_specs=(
            P(("dp", "expert"), None),
            P(("dp", "expert"), None),
            P(("dp", "expert"), None),
            P("dp", "expert", None, "tensor"),
            P("expert", "tensor", None),
        ),
        out_specs=(
            P(("dp", "expert"), None),
            P("dp", "expert", None, "tensor"),
            P("expert", "tensor", "dp"),
        ),
        check_vma=False,
    )
```

```python
import functools

import jax
import jax.numpy as jnp
from jax import lax
from jax.experimental import pallas as pl
from jax.experimental.pallas import tpu as pltpu
from jax.sharding import PartitionSpec as P

CAP = 4
LANES = 128
JOINT = 1
AFTER_WAIT = (10**9, 10**7)
PAD = 8
VMEM = pl.BlockSpec(memory_space=pltpu.VMEM)
HBM = pl.BlockSpec(memory_space=pltpu.HBM)
PARAMS = pltpu.CompilerParams(vmem_limit_bytes=32 * 2**20)


def dot(a, b, dims):
    return lax.dot_general(a, b, (dims, ((), ())), preferred_element_type=jnp.float32)


def in_hbm(*arrays):
    return [pltpu.with_memory_space_constraint(x, pltpu.HBM) for x in arrays]


def cost(flops, nbytes):
    return pl.CostEstimate(flops=flops, bytes_accessed=nbytes, transcendentals=0)


def paired(size):
    return size & (size - 1) == 0


def target(me, step, size):
    if paired(size):
        return me ^ ((size - step) % size)
    after = me + step
    return after % size if isinstance(me, int) else jnp.where(after >= size, after - size, after)


def source(me, step, size):
    if paired(size):
        return target(me, step, size)
    before = me - step
    return before % size if isinstance(me, int) else jnp.where(before < 0, before + size, before)


def reply(step, size):
    return step if paired(size) else -step % size


def apart(size):
    return [r for r in range(size) if r != JOINT]


def send(value, axis, step, give=target):
    size = lax.axis_size(axis)
    return lax.ppermute(value, axis, [(i, give(i, step, size)) for i in range(size)])


def front_kernel(count, pieces, *refs):
    ids_hbm, gates_hbm, grad_hbm, hidden_hbm, weight_hbm = refs[:5]
    ids_ref, match_ref, weight_ref, hidden_ref = refs[5:9]
    sends = refs[9 : 9 + count]
    products = refs[9 + count : 8 + 2 * count]
    gates_ref, grad_ref, saved_ref, picked_ref, total_ref, sems = refs[8 + 2 * count :]
    units, width = weight_ref.shape
    top, tokens = ids_ref.shape
    pairs = [(ids_hbm, ids_ref), (gates_hbm, gates_ref), (hidden_hbm.at[0, 0], saved_ref)]
    half = tokens // 2
    for p in range(2):
        part = pl.ds(p * half, half)
        pairs.append((grad_hbm.at[part], grad_ref.at[part]))
    half = units // (2 * pieces)
    for p in range(2 * pieces):
        part = pl.ds(p * half, half)
        pairs.append((weight_hbm.at[0, part], weight_ref.at[part]))
    copies = [pltpu.make_async_copy(*pair, sems.at[n]) for n, pair in enumerate(pairs)]
    for copy in copies:
        copy.start()
    me = lax.axis_index("expert")
    rows = count * PAD
    row = lax.broadcasted_iota(jnp.int32, (rows, tokens), 0)
    expert = target(me, row // PAD, count)
    place = row % PAD
    earlier = lax.broadcasted_iota(jnp.int32, (tokens, tokens), 0)
    later = lax.broadcasted_iota(jnp.int32, (tokens, tokens), 1)
    order = (earlier < later).astype(jnp.bfloat16)
    for copy in copies[:3]:
        copy.wait()
    ids = ids_ref[...]
    gates = gates_ref[...].astype(jnp.float32)
    member = jnp.zeros((rows, tokens), jnp.float32)
    gate = jnp.zeros((rows, tokens), jnp.float32)
    for k in range(top):
        hit = ids[k : k + 1, :] == expert
        member = jnp.where(hit, 1.0, member)
        gate = jnp.where(hit, gates[k : k + 1, :], gate)
    before = dot(member.astype(jnp.bfloat16), order, ((1,), (0,)))
    taken = (member > 0) & (before == place.astype(jnp.float32)) & (place < CAP)
    match = taken.astype(jnp.float32)
    match_ref[...] = match
    slot_gate = jnp.sum(match * gate, axis=1, keepdims=True)
    match = match.astype(jnp.bfloat16)

    slots = count * CAP
    saved = saved_ref[...]
    hidden_ref[...] = dot(slot_order(count), saved, ((1,), (0,))).astype(jnp.bfloat16)
    here = lax.broadcasted_iota(jnp.int32, (rows, slots), 0)
    there = lax.broadcasted_iota(jnp.int32, (rows, slots), 1)
    place = here % PAD - jnp.where(here // PAD == JOINT, CAP, 0)
    chosen = (place >= 0) & (place < CAP) & (there == target(me, here // PAD, count) * CAP + place)
    hidden = dot(chosen.astype(jnp.bfloat16), saved, ((1,), (0,))).astype(jnp.bfloat16)

    for copy in copies[3:5]:
        copy.wait()
    picked_ref[...] = dot(match, grad_ref[...], ((1,), (0,)))
    for r in range(count):
        part = slice(r * PAD, r * PAD + sends[r].shape[0])
        gate = jnp.broadcast_to(slot_gate[part], (sends[r].shape[0], LANES))
        sends[r][:, width:] = gate.astype(jnp.bfloat16)
        if r != JOINT:
            sends[r][:, :width] = picked_ref[part, :].astype(jnp.bfloat16)
    block = units // pieces
    for p in range(pieces):
        for copy in copies[5 + 2 * p : 7 + 2 * p]:
            copy.wait()
        part = slice(p * block, (p + 1) * block)
        term = dot(hidden[:, part], weight_ref[part, :], ((1,), (0,)))
        total_ref[...] = term if p == 0 else total_ref[...] + term
    for product, r in zip(products, apart(count)):
        product[...] = total_ref[r * PAD : r * PAD + CAP, :].astype(jnp.bfloat16)
    part = slice(JOINT * PAD, (JOINT + 1) * PAD)
    sends[JOINT][:, :width] = (picked_ref[part, :] + total_ref[part, :]).astype(jnp.bfloat16)


def slot_order(count):
    me = lax.axis_index("expert")
    slots = count * CAP
    here = lax.broadcasted_iota(jnp.int32, (slots, slots), 0)
    saved = lax.broadcasted_iota(jnp.int32, (slots, slots), 1)
    return (saved == source(me, here // CAP, count) * CAP + here % CAP).astype(jnp.bfloat16)


def slot_kernel(count, groups, hidden_ref, *refs):
    received = refs[:count]
    rows_ref, gate_ref = refs[count : count + 2]
    pays = refs[count + 2 : count + 2 + groups]
    wide_ref, weighted_ref = refs[count + 2 + groups :]
    width = rows_ref.shape[1]
    for r in range(count):
        wide_ref[r * CAP : (r + 1) * CAP, :] = received[r][...].astype(jnp.float32)[:CAP]
    rows = wide_ref[:, :width]
    gate = wide_ref[:, width:]
    gate_ref[...] = gate
    rows_ref[...] = rows.astype(jnp.bfloat16)
    weighted_ref[...] = (gate[:, :1] * rows).astype(jnp.bfloat16)
    share = width // groups
    me = lax.axis_index("dp")
    for r in range(groups):
        group = target(me, r, groups)
        pays[r][:, :share] = weighted_ref[:, pl.ds(pl.multiple_of(group * share, share), share)]
        pays[r][:, share:] = hidden_ref[...]


def back_kernel(count, *refs):
    sent = refs[:count]
    joint_ref = refs[count]
    products = dict(zip(apart(count), refs[count + 1 : 2 * count]))
    back_ref = refs[2 * count]
    width = products[0].shape[1]
    for r in range(count):
        step = reply(r, count)
        if step != JOINT:
            theirs = products[step][...].astype(jnp.float32)
        else:
            theirs = joint_ref[:, :width].astype(jnp.float32)[CAP:]
        mine = sent[r][:, :width].astype(jnp.float32)[:CAP]
        back = jnp.sum(mine * theirs, axis=1, keepdims=True)
        back_ref[r * CAP : (r + 1) * CAP, :] = jnp.broadcast_to(back, (CAP, LANES))


def down_term(pay_ref, share, start, block):
    hidden = pay_ref[:, pl.ds(start, block)]
    return dot(hidden, pay_ref[:, :share], ((0,), (0,))).astype(jnp.bfloat16)


def own_kernel(pieces, pay_ref, own_ref):
    units, share = own_ref.shape
    block = units // pieces
    for p in range(pieces):
        own_ref[p * block : (p + 1) * block, :] = down_term(pay_ref, share, share + p * block, block)


def down_kernel(count, others, pieces, *refs):
    own_ref = refs[0]
    pays = refs[1 : 1 + others]
    rows_ref, gate_ref, weight_ref, match_ref = refs[1 + others : 5 + others]
    hidden_hbm, down_hbm, match_out, hidden_out, down_out, sems = refs[5 + others :]
    units, share = own_ref.shape
    block = units // pieces
    copies = []

    def write(n, values, destination):
        copies.append(pltpu.make_async_copy(values, destination, sems.at[n]))
        copies[-1].start()

    for p in range(pieces):
        part = slice(p * block, (p + 1) * block)
        total = own_ref[part, :].astype(jnp.float32)
        for pay_ref in pays:
            total = total + down_term(pay_ref, share, share + p * block, block).astype(jnp.float32)
        down_out[part, :] = total
        part = pl.ds(p * block, block)
        write(p, down_out.at[part], down_hbm.at[0, part])

    match_out[...] = match_ref[...]
    upstream = dot(rows_ref[...], weight_ref[...], ((1,), (1,)))
    scaled = (gate_ref[:, :1] * upstream).astype(jnp.bfloat16)
    hidden_out[...] = dot(slot_order(count), scaled, ((0,), (0,))).astype(jnp.bfloat16)
    write(pieces, hidden_out, hidden_hbm.at[0, 0])
    for copy in copies:
        copy.wait()


def gate_kernel(count, ids_ref, match_ref, *refs):
    backs, out_ref = refs[:-1], refs[-1]
    me = lax.axis_index("expert")
    ids = ids_ref[...]
    back = backs[0][...]
    for ref in backs[1:]:
        back = back + ref[...]
    total = jnp.zeros(out_ref.shape, jnp.float32)
    for r in range(count):
        value = back[r * CAP : (r + 1) * CAP, :]
        match = match_ref[r * PAD : r * PAD + CAP, :]
        chosen = jnp.sum(jnp.where(match > 0, value, 0.0), axis=0, keepdims=True)
        total = total + jnp.where(ids == target(me, r, count), chosen, 0.0)
    out_ref[...] = total


def on_device(grad_out, expert_ids, gate_values, saved_hidden, down_weight):
    count = lax.axis_size("expert")
    groups = lax.axis_size("dp")
    tensors = lax.axis_size("tensor")
    tokens, width = grad_out.shape
    top = expert_ids.shape[1]
    units = down_weight.shape[1]
    slots = count * CAP
    share = width // groups
    pieces = units // LANES

    ids, match, weight, hidden, *rest = pl.pallas_call(
        functools.partial(front_kernel, count, pieces),
        out_shape=[
            jax.ShapeDtypeStruct((top, tokens), jnp.int32),
            jax.ShapeDtypeStruct((count * PAD, tokens), jnp.float32),
            jax.ShapeDtypeStruct((units, width), jnp.bfloat16),
            jax.ShapeDtypeStruct((slots, units), jnp.bfloat16),
        ]
        + [
            jax.ShapeDtypeStruct((PAD if r == JOINT else CAP, width + LANES), jnp.bfloat16)
            for r in range(count)
        ]
        + [jax.ShapeDtypeStruct((CAP, width), jnp.bfloat16)] * (count - 1),
        in_specs=[HBM] * 5,
        out_specs=[VMEM] * (3 + 2 * count),
        scratch_shapes=[
            pltpu.VMEM((top, tokens), jnp.bfloat16),
            pltpu.VMEM((tokens, width), jnp.bfloat16),
            pltpu.VMEM((slots, units), jnp.bfloat16),
            pltpu.VMEM((count * PAD, width), jnp.float32),
            pltpu.VMEM((count * PAD, width), jnp.float32),
            pltpu.SemaphoreType.DMA((5 + 2 * pieces,)),
        ],
        compiler_params=PARAMS,
        cost_estimate=cost(2 * count * PAD * (tokens + units) * width, 2 * (tokens + units) * width),
        name="front",
    )(*in_hbm(expert_ids.T, gate_values.T, grad_out, saved_hidden, down_weight))
    sends, products = rest[:count], rest[count:]

    received = [sends[0]] + [send(sends[r], "expert", r) for r in range(1, count)]
    theirs = [products[0]] + [send(products[r - 1], "expert", r) for r in range(JOINT + 1, count)]

    rows, gate, *pays = pl.pallas_call(
        functools.partial(slot_kernel, count, groups),
        out_shape=[
            jax.ShapeDtypeStruct((slots, width), jnp.bfloat16),
            jax.ShapeDtypeStruct((slots, LANES), jnp.float32),
        ]
        + [jax.ShapeDtypeStruct((slots, share + units), jnp.bfloat16)] * groups,
        in_specs=[VMEM] * (1 + count),
        out_specs=[VMEM] * (2 + groups),
        scratch_shapes=[
            pltpu.VMEM((slots, width + LANES), jnp.float32),
            pltpu.VMEM((slots, width), jnp.bfloat16),
        ],
        compiler_params=PARAMS,
        cost_estimate=cost(4 * slots * width, 8 * slots * width),
        name="slots",
    )(hidden, *received)

    back = pl.pallas_call(
        functools.partial(back_kernel, count),
        out_shape=jax.ShapeDtypeStruct((slots, LANES), jnp.float32),
        in_specs=[VMEM] * (2 * count),
        out_specs=VMEM,
        compiler_params=PARAMS,
        cost_estimate=cost(*AFTER_WAIT),
        name="backs",
    )(*sends, received[JOINT], *theirs)

    others = [send(pays[r], "dp", r) for r in range(1, groups)]
    backs = [back] + [send(back, "tensor", r) for r in reversed(range(1, tensors))]

    own = pl.pallas_call(
        functools.partial(own_kernel, pieces),
        out_shape=jax.ShapeDtypeStruct((units, share), jnp.bfloat16),
        in_specs=[VMEM],
        out_specs=VMEM,
        compiler_params=PARAMS,
        cost_estimate=cost(2 * slots * units * share, 2 * units * share),
        name="own",
    )(pays[0])

    hidden_grad, down_grad, match = pl.pallas_call(
        functools.partial(down_kernel, count, groups - 1, pieces),
        out_shape=[
            jax.ShapeDtypeStruct(saved_hidden.shape, jnp.bfloat16),
            jax.ShapeDtypeStruct((1, units, share), jnp.float32),
            jax.ShapeDtypeStruct(match.shape, jnp.float32),
        ],
        in_specs=[VMEM] * (4 + groups),
        out_specs=[HBM, HBM, VMEM],
        scratch_shapes=[
            pltpu.VMEM((slots, units), jnp.bfloat16),
            pltpu.VMEM((units, share), jnp.float32),
            pltpu.SemaphoreType.DMA((pieces + 1,)),
        ],
        compiler_params=PARAMS,
        cost_estimate=cost(2 * slots * units * (width + share), 4 * units * share),
        name="down",
    )(own, *others, rows, gate, weight, match)

    gate_grad = pl.pallas_call(
        functools.partial(gate_kernel, count),
        out_shape=jax.ShapeDtypeStruct(ids.shape, jnp.float32),
        in_specs=[VMEM] * (2 + tensors),
        out_specs=VMEM,
        compiler_params=PARAMS,
        cost_estimate=cost(slots * tokens, 4 * slots * tokens),
        name="gates",
    )(ids, match, *backs)
    return (gate_grad.T, hidden_grad, down_grad)


def solution(mesh):
    return jax.shard_map(
        on_device,
        mesh=mesh,
        in_specs=(
            P(("dp", "expert"), None),
            P(("dp", "expert"), None),
            P(("dp", "expert"), None),
            P("dp", "expert", None, "tensor"),
            P("expert", "tensor", None),
        ),
        out_specs=(
            P(("dp", "expert"), None),
            P("dp", "expert", None, "tensor"),
            P("expert", "tensor", "dp"),
        ),
        check_vma=False,
    )
```

```python
import functools

import jax
import jax.numpy as jnp
from jax import lax
from jax.experimental import pallas as pl
from jax.experimental.pallas import tpu as pltpu
from jax.sharding import PartitionSpec as P

CAP = 4
LANES = 128
AFTER_WAIT = (10**9, 10**7)
PAD = 8
VMEM = pl.BlockSpec(memory_space=pltpu.VMEM)
HBM = pl.BlockSpec(memory_space=pltpu.HBM)
PARAMS = pltpu.CompilerParams(vmem_limit_bytes=32 * 2**20)


def dot(a, b, dims):
    return lax.dot_general(a, b, (dims, ((), ())), preferred_element_type=jnp.float32)


def in_hbm(*arrays):
    return [pltpu.with_memory_space_constraint(x, pltpu.HBM) for x in arrays]


def cost(flops, nbytes):
    return pl.CostEstimate(flops=flops, bytes_accessed=nbytes, transcendentals=0)


def paired(size):
    return size & (size - 1) == 0


def target(me, step, size):
    if paired(size):
        return me ^ ((size - step) % size)
    after = me + step
    return after % size if isinstance(me, int) else jnp.where(after >= size, after - size, after)


def source(me, step, size):
    if paired(size):
        return target(me, step, size)
    before = me - step
    return before % size if isinstance(me, int) else jnp.where(before < 0, before + size, before)


def reply(step, size):
    return step if paired(size) else -step % size


def send(value, axis, step, give=target):
    size = lax.axis_size(axis)
    return lax.ppermute(value, axis, [(i, give(i, step, size)) for i in range(size)])


def front_kernel(count, pieces, *refs):
    ids_hbm, gates_hbm, grad_hbm, hidden_hbm, weight_hbm = refs[:5]
    ids_ref, match_ref, weight_ref, hidden_ref = refs[5:9]
    sends = refs[9 : 9 + count]
    products = refs[9 + count : 8 + 2 * count]
    gates_ref, grad_ref, saved_ref, picked_ref, total_ref, sems = refs[8 + 2 * count :]
    units, width = weight_ref.shape
    top, tokens = ids_ref.shape
    pairs = [(ids_hbm, ids_ref), (gates_hbm, gates_ref), (hidden_hbm.at[0, 0], saved_ref)]
    half = tokens // 2
    for p in range(2):
        part = pl.ds(p * half, half)
        pairs.append((grad_hbm.at[part], grad_ref.at[part]))
    half = units // (2 * pieces)
    for p in range(2 * pieces):
        part = pl.ds(p * half, half)
        pairs.append((weight_hbm.at[0, part], weight_ref.at[part]))
    copies = [pltpu.make_async_copy(*pair, sems.at[n]) for n, pair in enumerate(pairs)]
    for copy in copies:
        copy.start()
    me = lax.axis_index("expert")
    rows = count * PAD
    row = lax.broadcasted_iota(jnp.int32, (rows, tokens), 0)
    expert = target(me, row // PAD, count)
    place = row % PAD
    earlier = lax.broadcasted_iota(jnp.int32, (tokens, tokens), 0)
    later = lax.broadcasted_iota(jnp.int32, (tokens, tokens), 1)
    order = (earlier < later).astype(jnp.bfloat16)
    for copy in copies[:3]:
        copy.wait()
    ids = ids_ref[...]
    gates = gates_ref[...].astype(jnp.float32)
    member = jnp.zeros((rows, tokens), jnp.float32)
    gate = jnp.zeros((rows, tokens), jnp.float32)
    for k in range(top):
        hit = ids[k : k + 1, :] == expert
        member = jnp.where(hit, 1.0, member)
        gate = jnp.where(hit, gates[k : k + 1, :], gate)
    before = dot(member.astype(jnp.bfloat16), order, ((1,), (0,)))
    taken = (member > 0) & (before == place.astype(jnp.float32)) & (place < CAP)
    match = taken.astype(jnp.float32)
    match_ref[...] = match
    slot_gate = jnp.sum(match * gate, axis=1, keepdims=True)
    match = match.astype(jnp.bfloat16)

    slots = count * CAP
    saved = saved_ref[...]
    hidden_ref[...] = dot(slot_order(count), saved, ((1,), (0,))).astype(jnp.bfloat16)
    here = lax.broadcasted_iota(jnp.int32, (rows, slots), 0)
    there = lax.broadcasted_iota(jnp.int32, (rows, slots), 1)
    place = here % PAD - jnp.where(here // PAD == count - 1, CAP, 0)
    chosen = (place >= 0) & (place < CAP) & (there == target(me, here // PAD, count) * CAP + place)
    hidden = dot(chosen.astype(jnp.bfloat16), saved, ((1,), (0,))).astype(jnp.bfloat16)

    for copy in copies[3:5]:
        copy.wait()
    picked_ref[...] = dot(match, grad_ref[...], ((1,), (0,)))
    for r in range(count):
        part = slice(r * PAD, r * PAD + sends[r].shape[0])
        gate = jnp.broadcast_to(slot_gate[part], (sends[r].shape[0], LANES))
        sends[r][:, width:] = gate.astype(jnp.bfloat16)
        if r != count - 1:
            sends[r][:, :width] = picked_ref[part, :].astype(jnp.bfloat16)
    block = units // pieces
    for p in range(pieces):
        for copy in copies[5 + 2 * p : 7 + 2 * p]:
            copy.wait()
        part = slice(p * block, (p + 1) * block)
        term = dot(hidden[:, part], weight_ref[part, :], ((1,), (0,)))
        total_ref[...] = term if p == 0 else total_ref[...] + term
    for r, product in enumerate(products):
        product[...] = total_ref[r * PAD : r * PAD + CAP, :].astype(jnp.bfloat16)
    part = slice((count - 1) * PAD, count * PAD)
    sends[-1][:, :width] = (picked_ref[part, :] + total_ref[part, :]).astype(jnp.bfloat16)


def slot_order(count):
    me = lax.axis_index("expert")
    slots = count * CAP
    here = lax.broadcasted_iota(jnp.int32, (slots, slots), 0)
    saved = lax.broadcasted_iota(jnp.int32, (slots, slots), 1)
    return (saved == source(me, here // CAP, count) * CAP + here % CAP).astype(jnp.bfloat16)


def slot_kernel(count, groups, hidden_ref, *refs):
    received = refs[:count]
    rows_ref, gate_ref = refs[count : count + 2]
    pays = refs[count + 2 : count + 2 + groups]
    wide_ref, weighted_ref = refs[count + 2 + groups :]
    width = rows_ref.shape[1]
    for r in range(count):
        wide_ref[r * CAP : (r + 1) * CAP, :] = received[r][...].astype(jnp.float32)[:CAP]
    rows = wide_ref[:, :width]
    gate = wide_ref[:, width:]
    gate_ref[...] = gate
    rows_ref[...] = rows.astype(jnp.bfloat16)
    weighted_ref[...] = (gate[:, :1] * rows).astype(jnp.bfloat16)
    share = width // groups
    me = lax.axis_index("dp")
    for r in range(groups):
        group = target(me, r, groups)
        pays[r][:, :share] = weighted_ref[:, pl.ds(pl.multiple_of(group * share, share), share)]
        pays[r][:, share:] = hidden_ref[...]


def back_kernel(count, *refs):
    sent = refs[:count]
    joint_ref = refs[count]
    products = refs[count + 1 : 2 * count]
    back_ref = refs[2 * count]
    width = products[0].shape[1]
    for r in range(count):
        step = reply(r, count)
        if step != count - 1:
            theirs = products[step][...].astype(jnp.float32)
        else:
            theirs = joint_ref[:, :width].astype(jnp.float32)[CAP:]
        mine = sent[r][:, :width].astype(jnp.float32)[:CAP]
        back = jnp.sum(mine * theirs, axis=1, keepdims=True)
        back_ref[r * CAP : (r + 1) * CAP, :] = jnp.broadcast_to(back, (CAP, LANES))


def down_term(pay_ref, share, start, block):
    hidden = pay_ref[:, pl.ds(start, block)]
    return dot(hidden, pay_ref[:, :share], ((0,), (0,))).astype(jnp.bfloat16)


def upstream_kernel(count, pieces, rows_ref, gate_ref, weight_ref, pay_ref, product_ref, *refs):
    hidden_hbm, own_ref, product_out, hidden_out, sem = refs
    product_out[...] = product_ref[...]
    upstream = dot(rows_ref[...], weight_ref[...], ((1,), (1,)))
    scaled = (gate_ref[:, :1] * upstream).astype(jnp.bfloat16)
    hidden_out[...] = dot(slot_order(count), scaled, ((0,), (0,))).astype(jnp.bfloat16)
    write = pltpu.make_async_copy(hidden_out, hidden_hbm.at[0, 0], sem)
    write.start()
    units, share = own_ref.shape
    block = units // pieces
    for p in range(pieces):
        own_ref[p * block : (p + 1) * block, :] = down_term(pay_ref, share, share + p * block, block)
    write.wait()


def down_kernel(others, pieces, *refs):
    own_ref, match_ref = refs[:2]
    pays = refs[2 : 2 + others]
    down_hbm, match_out, down_out, sems = refs[2 + others :]
    match_out[...] = match_ref[...]
    units, share = own_ref.shape
    block = units // pieces
    copies = []
    for p in range(pieces):
        part = slice(p * block, (p + 1) * block)
        total = own_ref[part, :].astype(jnp.float32)
        for pay_ref in pays:
            total = total + down_term(pay_ref, share, share + p * block, block).astype(jnp.float32)
        down_out[part, :] = total
        part = pl.ds(p * block, block)
        copies.append(pltpu.make_async_copy(down_out.at[part], down_hbm.at[0, part], sems.at[p]))
        copies[-1].start()
    for copy in copies:
        copy.wait()


def gate_kernel(count, ids_ref, match_ref, *refs):
    backs, out_ref = refs[:-1], refs[-1]
    me = lax.axis_index("expert")
    ids = ids_ref[...]
    back = backs[0][...]
    for ref in backs[1:]:
        back = back + ref[...]
    total = jnp.zeros(out_ref.shape, jnp.float32)
    for r in range(count):
        value = back[r * CAP : (r + 1) * CAP, :]
        match = match_ref[r * PAD : r * PAD + CAP, :]
        chosen = jnp.sum(jnp.where(match > 0, value, 0.0), axis=0, keepdims=True)
        total = total + jnp.where(ids == target(me, r, count), chosen, 0.0)
    out_ref[...] = total


def on_device(grad_out, expert_ids, gate_values, saved_hidden, down_weight):
    count = lax.axis_size("expert")
    groups = lax.axis_size("dp")
    tensors = lax.axis_size("tensor")
    tokens, width = grad_out.shape
    top = expert_ids.shape[1]
    units = down_weight.shape[1]
    slots = count * CAP
    share = width // groups
    pieces = units // LANES

    ids, match, weight, hidden, *rest = pl.pallas_call(
        functools.partial(front_kernel, count, pieces),
        out_shape=[
            jax.ShapeDtypeStruct((top, tokens), jnp.int32),
            jax.ShapeDtypeStruct((count * PAD, tokens), jnp.float32),
            jax.ShapeDtypeStruct((units, width), jnp.bfloat16),
            jax.ShapeDtypeStruct((slots, units), jnp.bfloat16),
        ]
        + [
            jax.ShapeDtypeStruct((PAD if r == count - 1 else CAP, width + LANES), jnp.bfloat16)
            for r in range(count)
        ]
        + [jax.ShapeDtypeStruct((CAP, width), jnp.bfloat16)] * (count - 1),
        in_specs=[HBM] * 5,
        out_specs=[VMEM] * (3 + 2 * count),
        scratch_shapes=[
            pltpu.VMEM((top, tokens), jnp.bfloat16),
            pltpu.VMEM((tokens, width), jnp.bfloat16),
            pltpu.VMEM((slots, units), jnp.bfloat16),
            pltpu.VMEM((count * PAD, width), jnp.float32),
            pltpu.VMEM((count * PAD, width), jnp.float32),
            pltpu.SemaphoreType.DMA((5 + 2 * pieces,)),
        ],
        compiler_params=PARAMS,
        cost_estimate=cost(2 * count * PAD * (tokens + units) * width, 2 * (tokens + units) * width),
        name="front",
    )(*in_hbm(expert_ids.T, gate_values.T, grad_out, saved_hidden, down_weight))
    sends, products = rest[:count], rest[count:]

    received = [sends[0]] + [send(sends[r], "expert", r) for r in range(1, count)]
    theirs = [products[0]] + [send(products[r], "expert", r) for r in range(1, count - 1)]

    rows, gate, *pays = pl.pallas_call(
        functools.partial(slot_kernel, count, groups),
        out_shape=[
            jax.ShapeDtypeStruct((slots, width), jnp.bfloat16),
            jax.ShapeDtypeStruct((slots, LANES), jnp.float32),
        ]
        + [jax.ShapeDtypeStruct((slots, share + units), jnp.bfloat16)] * groups,
        in_specs=[VMEM] * (1 + count),
        out_specs=[VMEM] * (2 + groups),
        scratch_shapes=[
            pltpu.VMEM((slots, width + LANES), jnp.float32),
            pltpu.VMEM((slots, width), jnp.bfloat16),
        ],
        compiler_params=PARAMS,
        cost_estimate=cost(4 * slots * width, 8 * slots * width),
        name="slots",
    )(hidden, *received)

    others = [send(pays[r], "dp", r) for r in range(1, groups)]

    hidden_grad, own, theirs[0] = pl.pallas_call(
        functools.partial(upstream_kernel, count, pieces),
        out_shape=[
            jax.ShapeDtypeStruct(saved_hidden.shape, jnp.bfloat16),
            jax.ShapeDtypeStruct((units, share), jnp.bfloat16),
            jax.ShapeDtypeStruct((CAP, width), jnp.bfloat16),
        ],
        in_specs=[VMEM] * 5,
        out_specs=[HBM, VMEM, VMEM],
        scratch_shapes=[pltpu.VMEM((slots, units), jnp.bfloat16), pltpu.SemaphoreType.DMA(())],
        compiler_params=PARAMS,
        cost_estimate=cost(2 * slots * units * (width + share), 2 * units * width),
        name="upstream",
    )(rows, gate, weight, pays[0], theirs[0])

    back = pl.pallas_call(
        functools.partial(back_kernel, count),
        out_shape=jax.ShapeDtypeStruct((slots, LANES), jnp.float32),
        in_specs=[VMEM] * (2 * count),
        out_specs=VMEM,
        compiler_params=PARAMS,
        cost_estimate=cost(*AFTER_WAIT),
        name="backs",
    )(*sends, received[-1], *theirs)

    backs = [back] + [send(back, "tensor", r) for r in reversed(range(1, tensors))]

    down_grad, match = pl.pallas_call(
        functools.partial(down_kernel, groups - 1, pieces),
        out_shape=[
            jax.ShapeDtypeStruct((1, units, share), jnp.float32),
            jax.ShapeDtypeStruct(match.shape, jnp.float32),
        ],
        in_specs=[VMEM] * (1 + groups),
        out_specs=[HBM, VMEM],
        scratch_shapes=[
            pltpu.VMEM((units, share), jnp.float32),
            pltpu.SemaphoreType.DMA((pieces,)),
        ],
        compiler_params=PARAMS,
        cost_estimate=cost(2 * slots * units * share, 4 * units * share),
        name="down",
    )(own, match, *others)

    gate_grad = pl.pallas_call(
        functools.partial(gate_kernel, count),
        out_shape=jax.ShapeDtypeStruct(ids.shape, jnp.float32),
        in_specs=[VMEM] * (2 + tensors),
        out_specs=VMEM,
        compiler_params=PARAMS,
        cost_estimate=cost(slots * tokens, 4 * slots * tokens),
        name="gates",
    )(ids, match, *backs)
    return (gate_grad.T, hidden_grad, down_grad)


def solution(mesh):
    return jax.shard_map(
        on_device,
        mesh=mesh,
        in_specs=(
            P(("dp", "expert"), None),
            P(("dp", "expert"), None),
            P(("dp", "expert"), None),
            P("dp", "expert", None, "tensor"),
            P("expert", "tensor", None),
        ),
        out_specs=(
            P(("dp", "expert"), None),
            P("dp", "expert", None, "tensor"),
            P("expert", "tensor", "dp"),
        ),
        check_vma=False,
    )
```

```python
import functools

import jax
import jax.numpy as jnp
from jax import lax
from jax.experimental import pallas as pl
from jax.experimental.pallas import tpu as pltpu
from jax.sharding import PartitionSpec as P

CAP = 4
LANES = 128
AFTER_WAIT = (10**9, 10**7)
PAD = 8
VMEM = pl.BlockSpec(memory_space=pltpu.VMEM)
HBM = pl.BlockSpec(memory_space=pltpu.HBM)
PARAMS = pltpu.CompilerParams(vmem_limit_bytes=32 * 2**20)


def dot(a, b, dims):
    return lax.dot_general(a, b, (dims, ((), ())), preferred_element_type=jnp.float32)


def in_hbm(*arrays):
    return [pltpu.with_memory_space_constraint(x, pltpu.HBM) for x in arrays]


def cost(flops, nbytes):
    return pl.CostEstimate(flops=flops, bytes_accessed=nbytes, transcendentals=0)


def paired(size):
    return size & (size - 1) == 0


def target(me, step, size):
    if paired(size):
        return me ^ ((size - step) % size)
    after = me + step
    return after % size if isinstance(me, int) else jnp.where(after >= size, after - size, after)


def source(me, step, size):
    if paired(size):
        return target(me, step, size)
    before = me - step
    return before % size if isinstance(me, int) else jnp.where(before < 0, before + size, before)


def reply(step, size):
    return step if paired(size) else -step % size


def apart(size):
    return range(2, size - 1)


def send(value, axis, step, give=target):
    size = lax.axis_size(axis)
    return lax.ppermute(value, axis, [(i, give(i, step, size)) for i in range(size)])


def front_kernel(count, pieces, *refs):
    ids_hbm, gates_hbm, grad_hbm, hidden_hbm, weight_hbm = refs[:5]
    ids_ref, match_ref, weight_ref, hidden_ref, picked_ref, gate_ref, total_ref = refs[5:12]
    sends = dict(zip(range(1, count), refs[12 : 11 + count]))
    products = dict(zip(apart(count), refs[11 + count : 11 + count + len(apart(count))]))
    gates_ref, grad_ref, saved_ref, sems = refs[-4:]
    units, width = weight_ref.shape
    top, tokens = ids_ref.shape
    pairs = [(ids_hbm, ids_ref), (gates_hbm, gates_ref), (hidden_hbm.at[0, 0], saved_ref)]
    half = tokens // 2
    for p in range(2):
        part = pl.ds(p * half, half)
        pairs.append((grad_hbm.at[part], grad_ref.at[part]))
    half = units // (2 * pieces)
    for p in range(2 * pieces):
        part = pl.ds(p * half, half)
        pairs.append((weight_hbm.at[0, part], weight_ref.at[part]))
    copies = [pltpu.make_async_copy(*pair, sems.at[n]) for n, pair in enumerate(pairs)]
    for copy in copies:
        copy.start()
    me = lax.axis_index("expert")
    rows = count * PAD
    row = lax.broadcasted_iota(jnp.int32, (rows, tokens), 0)
    expert = target(me, row // PAD, count)
    place = row % PAD
    earlier = lax.broadcasted_iota(jnp.int32, (tokens, tokens), 0)
    later = lax.broadcasted_iota(jnp.int32, (tokens, tokens), 1)
    order = (earlier < later).astype(jnp.bfloat16)
    for copy in copies[:3]:
        copy.wait()
    ids = ids_ref[...]
    gates = gates_ref[...].astype(jnp.float32)
    member = jnp.zeros((rows, tokens), jnp.float32)
    gate = jnp.zeros((rows, tokens), jnp.float32)
    for k in range(top):
        hit = ids[k : k + 1, :] == expert
        member = jnp.where(hit, 1.0, member)
        gate = jnp.where(hit, gates[k : k + 1, :], gate)
    before = dot(member.astype(jnp.bfloat16), order, ((1,), (0,)))
    taken = (member > 0) & (before == place.astype(jnp.float32)) & (place < CAP)
    match = taken.astype(jnp.float32)
    match_ref[...] = match
    slot_gate = jnp.sum(match * gate, axis=1, keepdims=True)
    match = match.astype(jnp.bfloat16)

    slots = count * CAP
    saved = saved_ref[...]
    hidden_ref[...] = dot(slot_order(count), saved, ((1,), (0,))).astype(jnp.bfloat16)
    here = lax.broadcasted_iota(jnp.int32, (rows, slots), 0)
    there = lax.broadcasted_iota(jnp.int32, (rows, slots), 1)
    chosen = (here % PAD < CAP) & (there == target(me, here // PAD, count) * CAP + here % PAD)
    hidden = dot(chosen.astype(jnp.bfloat16), saved, ((1,), (0,))).astype(jnp.bfloat16)

    for copy in copies[3:5]:
        copy.wait()
    gate_ref[...] = jnp.broadcast_to(slot_gate, gate_ref.shape)
    picked_ref[...] = dot(match, grad_ref[...], ((1,), (0,)))
    for r, send_ref in sends.items():
        part = slice(r * PAD, r * PAD + CAP)
        send_ref[:, :width] = picked_ref[part, :].astype(jnp.bfloat16)
        send_ref[:, width : width + LANES] = gate_ref[part, :].astype(jnp.bfloat16)
    block = units // pieces
    for p in range(pieces):
        for copy in copies[5 + 2 * p : 7 + 2 * p]:
            copy.wait()
        part = slice(p * block, (p + 1) * block)
        term = dot(hidden[:, part], weight_ref[part, :], ((1,), (0,)))
        total_ref[...] = term if p == 0 else total_ref[...] + term
    for r, send_ref in sends.items():
        product = total_ref[r * PAD : r * PAD + CAP, :].astype(jnp.bfloat16)
        if r in products:
            products[r][...] = product
        else:
            send_ref[:, width + LANES :] = product


def slot_order(count):
    me = lax.axis_index("expert")
    slots = count * CAP
    here = lax.broadcasted_iota(jnp.int32, (slots, slots), 0)
    saved = lax.broadcasted_iota(jnp.int32, (slots, slots), 1)
    return (saved == source(me, (here // CAP + 1) % count, count) * CAP + here % CAP).astype(jnp.bfloat16)


def slot_kernel(count, groups, hidden_ref, picked_ref, sent_gate_ref, *refs):
    received, refs = refs[: count - 1], refs[count - 1 :]
    rows_ref, gate_ref = refs[:2]
    pays = refs[2 : 2 + groups]
    wide_ref, weighted_ref = refs[2 + groups :]
    width = rows_ref.shape[1]
    share = width // groups
    slots = count * CAP
    wide_ref[slots - CAP : slots, :] = picked_ref[:CAP, :]
    gates = sent_gate_ref[:CAP, :].astype(jnp.bfloat16).astype(jnp.float32)
    gate_ref[slots - CAP :, :] = gates
    for r in range(1, count):
        part = slice((r - 1) * CAP, r * CAP)
        wide_ref[part, :] = received[r - 1][:, :width].astype(jnp.float32)
        gate_ref[part, :] = received[r - 1][:, width : width + LANES].astype(jnp.float32)
    rows = wide_ref[:slots, :]
    rows_ref[...] = rows.astype(jnp.bfloat16)
    weighted_ref[...] = (gate_ref[:, :1] * rows).astype(jnp.bfloat16)
    me = lax.axis_index("dp")
    for r in range(groups):
        begin = pl.multiple_of(target(me, r, groups) * share, share)
        pays[r][:, :share] = weighted_ref[:, pl.ds(begin, share)]
        pays[r][:, share:] = hidden_ref[...]


def back_kernel(count, picked_ref, total_ref, *refs):
    received = refs[: count - 1]
    products = dict(zip(apart(count), refs[count - 1 : -1]))
    back_ref = refs[-1]
    width = picked_ref.shape[1]
    for r in range(count):
        step = reply(r, count)
        if step == 0:
            theirs = total_ref[:CAP, :]
        else:
            ref = products[step] if step in products else received[step - 1]
            theirs = ref[:, ref.shape[1] - width :].astype(jnp.float32)
        mine = picked_ref[r * PAD : r * PAD + CAP, :]
        back = jnp.sum(mine * theirs, axis=1, keepdims=True)
        back_ref[r * CAP : (r + 1) * CAP, :] = jnp.broadcast_to(back, (CAP, LANES))


def down_kernel(count, groups, pieces, rows_ref, gate_ref, weight_ref, match_ref, *refs):
    pays = refs[:groups]
    hidden_hbm, down_hbm, match_out, hidden_out, down_out, sems = refs[groups:]
    units, share = down_out.shape
    block = units // pieces
    copies = []

    def write(n, values, destination):
        copies.append(pltpu.make_async_copy(values, destination, sems.at[n]))
        copies[-1].start()

    for p in range(pieces):
        part = slice(p * block, (p + 1) * block)
        total = None
        for pay_ref in pays:
            hidden = pay_ref[:, share + p * block : share + (p + 1) * block]
            term = dot(hidden, pay_ref[:, :share], ((0,), (0,)))
            term = term.astype(jnp.bfloat16).astype(jnp.float32)
            total = term if total is None else total + term
        down_out[part, :] = total
        part = pl.ds(p * block, block)
        write(p, down_out.at[part], down_hbm.at[0, part])

    match_out[...] = match_ref[...]
    upstream = dot(rows_ref[...], weight_ref[...], ((1,), (1,)))
    scaled = (gate_ref[:, :1] * upstream).astype(jnp.bfloat16)
    hidden_out[...] = dot(slot_order(count), scaled, ((0,), (0,))).astype(jnp.bfloat16)
    write(pieces, hidden_out, hidden_hbm.at[0, 0])
    for copy in copies:
        copy.wait()


def gate_kernel(count, ids_ref, match_ref, *refs):
    backs, out_ref = refs[:-1], refs[-1]
    me = lax.axis_index("expert")
    ids = ids_ref[...]
    back = backs[0][...]
    for ref in backs[1:]:
        back = back + ref[...]
    total = jnp.zeros(out_ref.shape, jnp.float32)
    for r in range(count):
        value = back[r * CAP : (r + 1) * CAP, :]
        match = match_ref[r * PAD : r * PAD + CAP, :]
        chosen = jnp.sum(jnp.where(match > 0, value, 0.0), axis=0, keepdims=True)
        total = total + jnp.where(ids == target(me, r, count), chosen, 0.0)
    out_ref[...] = total


def on_device(grad_out, expert_ids, gate_values, saved_hidden, down_weight):
    count = lax.axis_size("expert")
    groups = lax.axis_size("dp")
    tensors = lax.axis_size("tensor")
    tokens, width = grad_out.shape
    top = expert_ids.shape[1]
    units = down_weight.shape[1]
    slots = count * CAP
    share = width // groups
    pieces = units // LANES

    joined = [width + LANES if r in apart(count) else 2 * width + LANES for r in range(1, count)]
    ids, match, weight, hidden, picked, sent_gate, total, *rest = pl.pallas_call(
        functools.partial(front_kernel, count, pieces),
        out_shape=[
            jax.ShapeDtypeStruct((top, tokens), jnp.int32),
            jax.ShapeDtypeStruct((count * PAD, tokens), jnp.float32),
            jax.ShapeDtypeStruct((units, width), jnp.bfloat16),
            jax.ShapeDtypeStruct((slots, units), jnp.bfloat16),
            jax.ShapeDtypeStruct((count * PAD, width), jnp.float32),
            jax.ShapeDtypeStruct((count * PAD, LANES), jnp.float32),
            jax.ShapeDtypeStruct((count * PAD, width), jnp.float32),
        ]
        + [jax.ShapeDtypeStruct((CAP, size), jnp.bfloat16) for size in joined]
        + [jax.ShapeDtypeStruct((CAP, width), jnp.bfloat16)] * len(apart(count)),
        in_specs=[HBM] * 5,
        out_specs=[VMEM] * (6 + count + len(apart(count))),
        scratch_shapes=[
            pltpu.VMEM((top, tokens), jnp.bfloat16),
            pltpu.VMEM((tokens, width), jnp.bfloat16),
            pltpu.VMEM((slots, units), jnp.bfloat16),
            pltpu.SemaphoreType.DMA((5 + 2 * pieces,)),
        ],
        compiler_params=PARAMS,
        cost_estimate=cost(2 * count * PAD * (tokens + units) * width, 2 * (tokens + units) * width),
        name="front",
    )(*in_hbm(expert_ids.T, gate_values.T, grad_out, saved_hidden, down_weight))
    sends, products = rest[: count - 1], rest[count - 1 :]

    received = [send(x, "expert", r) for r, x in enumerate(sends, 1)]
    theirs = [send(x, "expert", r) for r, x in zip(apart(count), products)]

    rows, gate, *pays = pl.pallas_call(
        functools.partial(slot_kernel, count, groups),
        out_shape=[
            jax.ShapeDtypeStruct((slots, width), jnp.bfloat16),
            jax.ShapeDtypeStruct((slots, LANES), jnp.float32),
        ]
        + [jax.ShapeDtypeStruct((slots, share + units), jnp.bfloat16)] * groups,
        in_specs=[VMEM] * (2 + count),
        out_specs=[VMEM] * (2 + groups),
        scratch_shapes=[
            pltpu.VMEM((slots + PAD, width), jnp.float32),
            pltpu.VMEM((slots, width), jnp.bfloat16),
        ],
        compiler_params=PARAMS,
        cost_estimate=cost(4 * slots * width, 8 * slots * width),
        name="slots",
    )(hidden, picked, sent_gate, *received)

    back = pl.pallas_call(
        functools.partial(back_kernel, count),
        out_shape=jax.ShapeDtypeStruct((slots, LANES), jnp.float32),
        in_specs=[VMEM] * (1 + count + len(theirs)),
        out_specs=VMEM,
        compiler_params=PARAMS,
        cost_estimate=cost(*AFTER_WAIT),
        name="backs",
    )(picked, total, *received, *theirs)

    pays = [pays[0]] + [send(pays[r], "dp", r) for r in range(1, groups)]
    backs = [back] + [send(back, "tensor", r) for r in reversed(range(1, tensors))]

    hidden_grad, down_grad, match = pl.pallas_call(
        functools.partial(down_kernel, count, groups, pieces),
        out_shape=[
            jax.ShapeDtypeStruct(saved_hidden.shape, jnp.bfloat16),
            jax.ShapeDtypeStruct((1, units, share), jnp.float32),
            jax.ShapeDtypeStruct(match.shape, jnp.float32),
        ],
        in_specs=[VMEM] * (4 + groups),
        out_specs=[HBM, HBM, VMEM],
        scratch_shapes=[
            pltpu.VMEM((slots, units), jnp.bfloat16),
            pltpu.VMEM((units, share), jnp.float32),
            pltpu.SemaphoreType.DMA((pieces + 1,)),
        ],
        compiler_params=PARAMS,
        cost_estimate=cost(2 * slots * units * (width + 2 * share), 4 * units * share),
        name="down",
    )(rows, gate, weight, match, *pays)

    gate_grad = pl.pallas_call(
        functools.partial(gate_kernel, count),
        out_shape=jax.ShapeDtypeStruct(ids.shape, jnp.float32),
        in_specs=[VMEM] * (2 + tensors),
        out_specs=VMEM,
        compiler_params=PARAMS,
        cost_estimate=cost(slots * tokens, 4 * slots * tokens),
        name="gates",
    )(ids, match, *backs)
    return (gate_grad.T, hidden_grad, down_grad)


def solution(mesh):
    return jax.shard_map(
        on_device,
        mesh=mesh,
        in_specs=(
            P(("dp", "expert"), None),
            P(("dp", "expert"), None),
            P(("dp", "expert"), None),
            P("dp", "expert", None, "tensor"),
            P("expert", "tensor", None),
        ),
        out_specs=(
            P(("dp", "expert"), None),
            P("dp", "expert", None, "tensor"),
            P("expert", "tensor", "dp"),
        ),
        check_vma=False,
    )
```

```python
import functools

import jax
import jax.numpy as jnp
from jax import lax
from jax.experimental import pallas as pl
from jax.experimental.pallas import tpu as pltpu
from jax.sharding import PartitionSpec as P

CAP = 4
LANES = 128
AFTER_WAIT = (10**9, 10**7)
PAD = 8
VMEM = pl.BlockSpec(memory_space=pltpu.VMEM)
HBM = pl.BlockSpec(memory_space=pltpu.HBM)
PARAMS = pltpu.CompilerParams(vmem_limit_bytes=32 * 2**20)


def dot(a, b, dims):
    return lax.dot_general(a, b, (dims, ((), ())), preferred_element_type=jnp.float32)


def in_hbm(*arrays):
    return [pltpu.with_memory_space_constraint(x, pltpu.HBM) for x in arrays]


def cost(flops, nbytes):
    return pl.CostEstimate(flops=flops, bytes_accessed=nbytes, transcendentals=0)


def paired(size):
    return size & (size - 1) == 0


def target(me, step, size):
    if paired(size):
        return me ^ ((size - step) % size)
    after = me + step
    return after % size if isinstance(me, int) else jnp.where(after >= size, after - size, after)


def source(me, step, size):
    if paired(size):
        return target(me, step, size)
    before = me - step
    return before % size if isinstance(me, int) else jnp.where(before < 0, before + size, before)


def reply(step, size):
    return step if paired(size) else -step % size


def apart(size):
    return range(2, size - 1)


def send(value, axis, step, give=target):
    size = lax.axis_size(axis)
    return lax.ppermute(value, axis, [(i, give(i, step, size)) for i in range(size)])


def front_kernel(count, groups, pieces, *refs):
    ids_hbm, gates_hbm, grad_hbm, hidden_hbm, weight_hbm = refs[:5]
    ids_ref, match_ref, weight_ref, hidden_ref, picked_ref, gate_ref, total_ref = refs[5:12]
    sends = dict(zip(range(1, count), refs[12 : 11 + count]))
    products = dict(zip(apart(count), refs[11 + count : 11 + count + len(apart(count))]))
    early = refs[-3 - groups : -4]
    gates_ref, grad_ref, saved_ref, sems = refs[-4:]
    units, width = weight_ref.shape
    top, tokens = ids_ref.shape
    pairs = [(ids_hbm, ids_ref), (gates_hbm, gates_ref), (hidden_hbm.at[0, 0], saved_ref)]
    half = tokens // 2
    for p in range(2):
        part = pl.ds(p * half, half)
        pairs.append((grad_hbm.at[part], grad_ref.at[part]))
    half = units // (2 * pieces)
    for p in range(2 * pieces):
        part = pl.ds(p * half, half)
        pairs.append((weight_hbm.at[0, part], weight_ref.at[part]))
    copies = [pltpu.make_async_copy(*pair, sems.at[n]) for n, pair in enumerate(pairs)]
    for copy in copies:
        copy.start()
    me = lax.axis_index("expert")
    rows = count * PAD
    row = lax.broadcasted_iota(jnp.int32, (rows, tokens), 0)
    expert = target(me, row // PAD, count)
    place = row % PAD
    earlier = lax.broadcasted_iota(jnp.int32, (tokens, tokens), 0)
    later = lax.broadcasted_iota(jnp.int32, (tokens, tokens), 1)
    order = (earlier < later).astype(jnp.bfloat16)
    for copy in copies[:3]:
        copy.wait()
    ids = ids_ref[...]
    gates = gates_ref[...].astype(jnp.float32)
    member = jnp.zeros((rows, tokens), jnp.float32)
    gate = jnp.zeros((rows, tokens), jnp.float32)
    for k in range(top):
        hit = ids[k : k + 1, :] == expert
        member = jnp.where(hit, 1.0, member)
        gate = jnp.where(hit, gates[k : k + 1, :], gate)
    before = dot(member.astype(jnp.bfloat16), order, ((1,), (0,)))
    taken = (member > 0) & (before == place.astype(jnp.float32)) & (place < CAP)
    match = taken.astype(jnp.float32)
    match_ref[...] = match
    slot_gate = jnp.sum(match * gate, axis=1, keepdims=True)
    match = match.astype(jnp.bfloat16)

    slots = count * CAP
    saved = saved_ref[...]
    hidden_ref[...] = dot(slot_order(count), saved, ((1,), (0,))).astype(jnp.bfloat16)
    spread = dot(slot_order(count, PAD), saved, ((1,), (0,)))
    here = lax.broadcasted_iota(jnp.int32, (rows, slots), 0)
    there = lax.broadcasted_iota(jnp.int32, (rows, slots), 1)
    chosen = (here % PAD < CAP) & (there == target(me, here // PAD, count) * CAP + here % PAD)
    hidden = dot(chosen.astype(jnp.bfloat16), saved, ((1,), (0,))).astype(jnp.bfloat16)

    for copy in copies[3:5]:
        copy.wait()
    gate_ref[...] = jnp.broadcast_to(slot_gate, gate_ref.shape)
    picked_ref[...] = dot(match, grad_ref[...], ((1,), (0,)))
    for r, send_ref in sends.items():
        part = slice(r * PAD, r * PAD + CAP)
        send_ref[:, :width] = picked_ref[part, :].astype(jnp.bfloat16)
        send_ref[:, width : width + LANES] = gate_ref[part, :].astype(jnp.bfloat16)
    share = width // groups
    group = lax.axis_index("dp")
    for r, early_ref in enumerate(early, 1):
        begin = pl.multiple_of(target(group, r, groups) * share, share)
        weighted = gate_ref[:CAP, :1] * picked_ref[:CAP, pl.ds(begin, share)]
        early_ref[:, :share] = weighted.astype(jnp.bfloat16)
        for k in range(count):
            part = slice(share + k * units, share + (k + 1) * units)
            early_ref[:, part] = spread[k * PAD : k * PAD + CAP].astype(jnp.bfloat16)
    block = units // pieces
    for p in range(pieces):
        for copy in copies[5 + 2 * p : 7 + 2 * p]:
            copy.wait()
        part = slice(p * block, (p + 1) * block)
        term = dot(hidden[:, part], weight_ref[part, :], ((1,), (0,)))
        total_ref[...] = term if p == 0 else total_ref[...] + term
    for r, send_ref in sends.items():
        product = total_ref[r * PAD : r * PAD + CAP, :].astype(jnp.bfloat16)
        if r in products:
            products[r][...] = product
        else:
            send_ref[:, width + LANES :] = product


def slot_order(count, lines=CAP):
    me = lax.axis_index("expert")
    here = lax.broadcasted_iota(jnp.int32, (count * lines, count * CAP), 0)
    saved = lax.broadcasted_iota(jnp.int32, (count * lines, count * CAP), 1)
    place = here % lines
    block = source(me, (here // lines + 1) % count, count)
    return ((saved == block * CAP + place) & (place < CAP)).astype(jnp.bfloat16)


def slot_kernel(count, groups, hidden_ref, picked_ref, sent_gate_ref, *refs):
    received, refs = refs[: count - 1], refs[count - 1 :]
    early, refs = refs[: groups - 1], refs[groups - 1 :]
    rows_ref, gate_ref, own_ref = refs[:3]
    lates, others = refs[3 : 2 + groups], refs[2 + groups : 1 + 2 * groups]
    wide_ref, spread_ref, units_ref = refs[1 + 2 * groups :]
    width = rows_ref.shape[1]
    share = width // groups
    slots = count * CAP
    wide_ref[slots - CAP : slots, :] = picked_ref[:CAP, :]
    gate_ref[slots - CAP :, :] = sent_gate_ref[:CAP, :]
    for r in range(1, count):
        part = slice((r - 1) * CAP, r * CAP)
        rows = received[r - 1][:, :width].astype(jnp.float32)
        gate = received[r - 1][:, width : width + LANES].astype(jnp.float32)
        wide_ref[part, :] = rows
        gate_ref[part, :] = gate
        spread_ref[r * PAD : r * PAD + CAP, :] = gate[:, :1] * rows
    rows = wide_ref[:slots, :]
    rows_ref[...] = rows.astype(jnp.bfloat16)
    me = lax.axis_index("dp")
    for r, late_ref in enumerate(lates, 1):
        begin = pl.multiple_of(target(me, r, groups) * share, share)
        for k in range(1, count):
            late = spread_ref[k * PAD : k * PAD + CAP, pl.ds(begin, share)]
            late_ref[:, (k - 1) * share : k * share] = late.astype(jnp.bfloat16)
    begin = pl.multiple_of(me * share, share)
    weighted = gate_ref[:, :1] * wide_ref[:slots, pl.ds(begin, share)]
    own_ref[:, :share] = weighted.astype(jnp.bfloat16)
    own_ref[:, share:] = hidden_ref[...]
    units = hidden_ref.shape[1]
    for early_ref, other_ref in zip(early, others):
        for k in range(count):
            part = early_ref[:, share + k * units : share + (k + 1) * units]
            units_ref[k * CAP : (k + 1) * CAP, :] = part.astype(jnp.float32)
        other_ref[...] = units_ref[:slots, :].astype(jnp.bfloat16)


def back_kernel(count, picked_ref, total_ref, *refs):
    received = refs[: count - 1]
    products = dict(zip(apart(count), refs[count - 1 : -1]))
    back_ref = refs[-1]
    width = picked_ref.shape[1]
    for r in range(count):
        step = reply(r, count)
        if step == 0:
            theirs = total_ref[:CAP, :]
        else:
            ref = products[step] if step in products else received[step - 1]
            theirs = ref[:, ref.shape[1] - width :].astype(jnp.float32)
        mine = picked_ref[r * PAD : r * PAD + CAP, :]
        back = jnp.sum(mine * theirs, axis=1, keepdims=True)
        back_ref[r * CAP : (r + 1) * CAP, :] = jnp.broadcast_to(back, (CAP, LANES))


def down_term(hidden, rows):
    return dot(hidden, rows, ((0,), (0,))).astype(jnp.bfloat16)


def own_kernel(pieces, pay_ref, own_ref):
    units, share = own_ref.shape
    block = units // pieces
    for p in range(pieces):
        hidden = pay_ref[:, share + p * block : share + (p + 1) * block]
        own_ref[p * block : (p + 1) * block, :] = down_term(hidden, pay_ref[:, :share])


def down_kernel(count, others, pieces, own_ref, rows_ref, gate_ref, weight_ref, match_ref, *refs):
    early, lates, hiddens = refs[:others], refs[others : 2 * others], refs[2 * others : 3 * others]
    hidden_hbm, down_hbm, match_out, hidden_out, down_out, wide_ref, sems = refs[3 * others :]
    units, share = down_out.shape
    slots = count * CAP
    terms = []
    for early_ref, late_ref, hidden_ref in zip(early, lates, hiddens):
        for k in range(count - 1):
            late = late_ref[:, k * share : (k + 1) * share].astype(jnp.float32)
            wide_ref[k * CAP : (k + 1) * CAP, :] = late
        wide_ref[slots - CAP : slots, :] = early_ref[:, :share].astype(jnp.float32)
        terms.append((hidden_ref, wide_ref[:slots, :].astype(jnp.bfloat16)))
    block = units // pieces
    copies = []

    def write(n, values, destination):
        copies.append(pltpu.make_async_copy(values, destination, sems.at[n]))
        copies[-1].start()

    for p in range(pieces):
        part = slice(p * block, (p + 1) * block)
        total = own_ref[part, :].astype(jnp.float32)
        for hidden_ref, rows in terms:
            total = total + down_term(hidden_ref[:, part], rows).astype(jnp.float32)
        down_out[part, :] = total
        part = pl.ds(p * block, block)
        write(p, down_out.at[part], down_hbm.at[0, part])

    match_out[...] = match_ref[...]
    upstream = dot(rows_ref[...], weight_ref[...], ((1,), (1,)))
    scaled = (gate_ref[:, :1] * upstream).astype(jnp.bfloat16)
    hidden_out[...] = dot(slot_order(count), scaled, ((0,), (0,))).astype(jnp.bfloat16)
    write(pieces, hidden_out, hidden_hbm.at[0, 0])
    for copy in copies:
        copy.wait()


def gate_kernel(count, ids_ref, match_ref, *refs):
    backs, out_ref = refs[:-1], refs[-1]
    me = lax.axis_index("expert")
    ids = ids_ref[...]
    back = backs[0][...]
    for ref in backs[1:]:
        back = back + ref[...]
    total = jnp.zeros(out_ref.shape, jnp.float32)
    for r in range(count):
        value = back[r * CAP : (r + 1) * CAP, :]
        match = match_ref[r * PAD : r * PAD + CAP, :]
        chosen = jnp.sum(jnp.where(match > 0, value, 0.0), axis=0, keepdims=True)
        total = total + jnp.where(ids == target(me, r, count), chosen, 0.0)
    out_ref[...] = total


def on_device(grad_out, expert_ids, gate_values, saved_hidden, down_weight):
    count = lax.axis_size("expert")
    groups = lax.axis_size("dp")
    tensors = lax.axis_size("tensor")
    tokens, width = grad_out.shape
    top = expert_ids.shape[1]
    units = down_weight.shape[1]
    slots = count * CAP
    share = width // groups
    pieces = units // LANES

    joined = [width + LANES if r in apart(count) else 2 * width + LANES for r in range(1, count)]
    early = jax.ShapeDtypeStruct((CAP, share + count * units), jnp.bfloat16)
    ids, match, weight, hidden, picked, sent_gate, total, *rest = pl.pallas_call(
        functools.partial(front_kernel, count, groups, pieces),
        out_shape=[
            jax.ShapeDtypeStruct((top, tokens), jnp.int32),
            jax.ShapeDtypeStruct((count * PAD, tokens), jnp.float32),
            jax.ShapeDtypeStruct((units, width), jnp.bfloat16),
            jax.ShapeDtypeStruct((slots, units), jnp.bfloat16),
            jax.ShapeDtypeStruct((count * PAD, width), jnp.float32),
            jax.ShapeDtypeStruct((count * PAD, LANES), jnp.float32),
            jax.ShapeDtypeStruct((count * PAD, width), jnp.float32),
        ]
        + [jax.ShapeDtypeStruct((CAP, size), jnp.bfloat16) for size in joined]
        + [jax.ShapeDtypeStruct((CAP, width), jnp.bfloat16)] * len(apart(count))
        + [early] * (groups - 1),
        in_specs=[HBM] * 5,
        out_specs=[VMEM] * (5 + count + len(apart(count)) + groups),
        scratch_shapes=[
            pltpu.VMEM((top, tokens), jnp.bfloat16),
            pltpu.VMEM((tokens, width), jnp.bfloat16),
            pltpu.VMEM((slots, units), jnp.bfloat16),
            pltpu.SemaphoreType.DMA((5 + 2 * pieces,)),
        ],
        compiler_params=PARAMS,
        cost_estimate=cost(2 * count * PAD * (tokens + units) * width, 2 * (tokens + units) * width),
        name="front",
    )(*in_hbm(expert_ids.T, gate_values.T, grad_out, saved_hidden, down_weight))
    sends, rest = rest[: count - 1], rest[count - 1 :]
    products, early = rest[: len(apart(count))], rest[len(apart(count)) :]

    received = [send(x, "expert", r) for r, x in enumerate(sends, 1)]
    theirs = [send(x, "expert", r) for r, x in zip(apart(count), products)]
    early = [send(x, "dp", r) for r, x in enumerate(early, 1)]

    rows, gate, own, *rest = pl.pallas_call(
        functools.partial(slot_kernel, count, groups),
        out_shape=[
            jax.ShapeDtypeStruct((slots, width), jnp.bfloat16),
            jax.ShapeDtypeStruct((slots, LANES), jnp.float32),
            jax.ShapeDtypeStruct((slots, share + units), jnp.bfloat16),
        ]
        + [jax.ShapeDtypeStruct((CAP, (count - 1) * share), jnp.bfloat16)] * (groups - 1)
        + [jax.ShapeDtypeStruct((slots, units), jnp.bfloat16)] * (groups - 1),
        in_specs=[VMEM] * (1 + count + groups),
        out_specs=[VMEM] * (1 + 2 * groups),
        scratch_shapes=[
            pltpu.VMEM((slots + PAD, width), jnp.float32),
            pltpu.VMEM((count * PAD, width), jnp.float32),
            pltpu.VMEM((slots + PAD, units), jnp.float32),
        ],
        compiler_params=PARAMS,
        cost_estimate=cost(4 * slots * width, 8 * slots * width),
        name="slots",
    )(hidden, picked, sent_gate, *received, *early)
    lates, others = rest[: groups - 1], rest[groups - 1 :]

    back = pl.pallas_call(
        functools.partial(back_kernel, count),
        out_shape=jax.ShapeDtypeStruct((slots, LANES), jnp.float32),
        in_specs=[VMEM] * (1 + count + len(theirs)),
        out_specs=VMEM,
        compiler_params=PARAMS,
        cost_estimate=cost(*AFTER_WAIT),
        name="backs",
    )(picked, total, *received, *theirs)

    lates = [send(x, "dp", r) for r, x in enumerate(lates, 1)]
    backs = [back] + [send(back, "tensor", r) for r in reversed(range(1, tensors))]

    own = pl.pallas_call(
        functools.partial(own_kernel, pieces),
        out_shape=jax.ShapeDtypeStruct((units, share), jnp.bfloat16),
        in_specs=[VMEM],
        out_specs=VMEM,
        compiler_params=PARAMS,
        cost_estimate=cost(2 * slots * units * share, 2 * units * share),
        name="own",
    )(own)

    hidden_grad, down_grad, match = pl.pallas_call(
        functools.partial(down_kernel, count, groups - 1, pieces),
        out_shape=[
            jax.ShapeDtypeStruct(saved_hidden.shape, jnp.bfloat16),
            jax.ShapeDtypeStruct((1, units, share), jnp.float32),
            jax.ShapeDtypeStruct(match.shape, jnp.float32),
        ],
        in_specs=[VMEM] * (2 + 3 * groups),
        out_specs=[HBM, HBM, VMEM],
        scratch_shapes=[
            pltpu.VMEM((slots, units), jnp.bfloat16),
            pltpu.VMEM((units, share), jnp.float32),
            pltpu.VMEM((slots + PAD, share), jnp.float32),
            pltpu.SemaphoreType.DMA((pieces + 1,)),
        ],
        compiler_params=PARAMS,
        cost_estimate=cost(2 * slots * units * (width + share), 4 * units * share),
        name="down",
    )(own, rows, gate, weight, match, *early, *lates, *others)

    gate_grad = pl.pallas_call(
        functools.partial(gate_kernel, count),
        out_shape=jax.ShapeDtypeStruct(ids.shape, jnp.float32),
        in_specs=[VMEM] * (2 + tensors),
        out_specs=VMEM,
        compiler_params=PARAMS,
        cost_estimate=cost(slots * tokens, 4 * slots * tokens),
        name="gates",
    )(ids, match, *backs)
    return (gate_grad.T, hidden_grad, down_grad)


def solution(mesh):
    return jax.shard_map(
        on_device,
        mesh=mesh,
        in_specs=(
            P(("dp", "expert"), None),
            P(("dp", "expert"), None),
            P(("dp", "expert"), None),
            P("dp", "expert", None, "tensor"),
            P("expert", "tensor", None),
        ),
        out_specs=(
            P(("dp", "expert"), None),
            P("dp", "expert", None, "tensor"),
            P("expert", "tensor", "dp"),
        ),
        check_vma=False,
    )
```

```python
import functools

import jax
import jax.numpy as jnp
from jax import lax
from jax.experimental import pallas as pl
from jax.experimental.pallas import tpu as pltpu
from jax.sharding import PartitionSpec as P

CAP = 4
LANES = 128
JOINT = 1
AFTER_WAIT = (10**9, 10**7)
SPLIT = 4
PAD = 8
VMEM = pl.BlockSpec(memory_space=pltpu.VMEM)
HBM = pl.BlockSpec(memory_space=pltpu.HBM)
PARAMS = pltpu.CompilerParams(vmem_limit_bytes=32 * 2**20)


def dot(a, b, dims):
    return lax.dot_general(a, b, (dims, ((), ())), preferred_element_type=jnp.float32)


def in_hbm(*arrays):
    return [pltpu.with_memory_space_constraint(x, pltpu.HBM) for x in arrays]


def cost(flops, nbytes):
    return pl.CostEstimate(flops=flops, bytes_accessed=nbytes, transcendentals=0)


def paired(size):
    return size & (size - 1) == 0


def target(me, step, size):
    if paired(size):
        return me ^ ((size - step) % size)
    after = me + step
    return after % size if isinstance(me, int) else jnp.where(after >= size, after - size, after)


def source(me, step, size):
    if paired(size):
        return target(me, step, size)
    before = me - step
    return before % size if isinstance(me, int) else jnp.where(before < 0, before + size, before)


def reply(step, size):
    return step if paired(size) else -step % size


def apart(size):
    return [r for r in range(size) if r != JOINT]


def send(value, axis, step, give=target):
    size = lax.axis_size(axis)
    return lax.ppermute(value, axis, [(i, give(i, step, size)) for i in range(size)])


def front_kernel(count, pieces, *refs):
    ids_hbm, gates_hbm, grad_hbm, hidden_hbm, weight_hbm = refs[:5]
    ids_ref, match_ref, weight_ref, hidden_ref = refs[5:9]
    sends = refs[9 : 9 + count]
    products = refs[9 + count : 8 + 2 * count]
    gates_ref, grad_ref, saved_ref, picked_ref, total_ref, sems = refs[8 + 2 * count :]
    units, width = weight_ref.shape
    top, tokens = ids_ref.shape
    pairs = [(ids_hbm, ids_ref), (gates_hbm, gates_ref), (hidden_hbm.at[0, 0], saved_ref)]
    lines = tokens // SPLIT
    for p in range(SPLIT):
        part = pl.ds(p * lines, lines)
        pairs.append((grad_hbm.at[part], grad_ref.at[part]))
    lines = units // (SPLIT * pieces)
    for p in range(SPLIT * pieces):
        part = pl.ds(p * lines, lines)
        pairs.append((weight_hbm.at[0, part], weight_ref.at[part]))
    copies = [pltpu.make_async_copy(*pair, sems.at[n]) for n, pair in enumerate(pairs)]
    for copy in copies:
        copy.start()
    me = lax.axis_index("expert")
    rows = count * PAD
    row = lax.broadcasted_iota(jnp.int32, (rows, tokens), 0)
    expert = target(me, row // PAD, count)
    place = row % PAD
    earlier = lax.broadcasted_iota(jnp.int32, (tokens, tokens), 0)
    later = lax.broadcasted_iota(jnp.int32, (tokens, tokens), 1)
    order = (earlier < later).astype(jnp.bfloat16)
    for copy in copies[:3]:
        copy.wait()
    ids = ids_ref[...]
    gates = gates_ref[...].astype(jnp.float32)
    member = jnp.zeros((rows, tokens), jnp.float32)
    gate = jnp.zeros((rows, tokens), jnp.float32)
    for k in range(top):
        hit = ids[k : k + 1, :] == expert
        member = jnp.where(hit, 1.0, member)
        gate = jnp.where(hit, gates[k : k + 1, :], gate)
    before = dot(member.astype(jnp.bfloat16), order, ((1,), (0,)))
    taken = (member > 0) & (before == place.astype(jnp.float32)) & (place < CAP)
    match = taken.astype(jnp.float32)
    match_ref[...] = match
    slot_gate = jnp.sum(match * gate, axis=1, keepdims=True)
    match = match.astype(jnp.bfloat16)

    slots = count * CAP
    saved = saved_ref[...]
    hidden_ref[...] = dot(slot_order(count), saved, ((1,), (0,))).astype(jnp.bfloat16)
    here = lax.broadcasted_iota(jnp.int32, (rows, slots), 0)
    there = lax.broadcasted_iota(jnp.int32, (rows, slots), 1)
    place = here % PAD - jnp.where(here // PAD == JOINT, CAP, 0)
    chosen = (place >= 0) & (place < CAP) & (there == target(me, here // PAD, count) * CAP + place)
    hidden = dot(chosen.astype(jnp.bfloat16), saved, ((1,), (0,))).astype(jnp.bfloat16)

    for copy in copies[3 : 3 + SPLIT]:
        copy.wait()
    picked_ref[...] = dot(match, grad_ref[...], ((1,), (0,)))
    for r in range(count):
        part = slice(r * PAD, r * PAD + sends[r].shape[0])
        gate = jnp.broadcast_to(slot_gate[part], (sends[r].shape[0], LANES))
        sends[r][:, width:] = gate.astype(jnp.bfloat16)
        if r != JOINT:
            sends[r][:, :width] = picked_ref[part, :].astype(jnp.bfloat16)
    block = units // pieces
    for p in range(pieces):
        for copy in copies[3 + SPLIT * (p + 1) : 3 + SPLIT * (p + 2)]:
            copy.wait()
        part = slice(p * block, (p + 1) * block)
        term = dot(hidden[:, part], weight_ref[part, :], ((1,), (0,)))
        total_ref[...] = term if p == 0 else total_ref[...] + term
    for product, r in zip(products, apart(count)):
        product[...] = total_ref[r * PAD : r * PAD + CAP, :].astype(jnp.bfloat16)
    part = slice(JOINT * PAD, (JOINT + 1) * PAD)
    sends[JOINT][:, :width] = (picked_ref[part, :] + total_ref[part, :]).astype(jnp.bfloat16)


def slot_order(count):
    me = lax.axis_index("expert")
    slots = count * CAP
    here = lax.broadcasted_iota(jnp.int32, (slots, slots), 0)
    saved = lax.broadcasted_iota(jnp.int32, (slots, slots), 1)
    return (saved == source(me, here // CAP, count) * CAP + here % CAP).astype(jnp.bfloat16)


def slot_kernel(count, groups, hidden_ref, *refs):
    received = refs[:count]
    rows_ref, gate_ref = refs[count : count + 2]
    pays = refs[count + 2 : count + 2 + groups]
    wide_ref, weighted_ref = refs[count + 2 + groups :]
    width = rows_ref.shape[1]
    for r in range(count):
        wide_ref[r * CAP : (r + 1) * CAP, :] = received[r][...].astype(jnp.float32)[:CAP]
    rows = wide_ref[:, :width]
    gate = wide_ref[:, width:]
    gate_ref[...] = gate
    rows_ref[...] = rows.astype(jnp.bfloat16)
    weighted_ref[...] = (gate[:, :1] * rows).astype(jnp.bfloat16)
    share = width // groups
    me = lax.axis_index("dp")
    for r in range(groups):
        group = target(me, r, groups)
        pays[r][:, :share] = weighted_ref[:, pl.ds(pl.multiple_of(group * share, share), share)]
        pays[r][:, share:] = hidden_ref[...]


def back_kernel(count, *refs):
    sent = refs[:count]
    joint_ref = refs[count]
    products = dict(zip(apart(count), refs[count + 1 : 2 * count]))
    back_ref = refs[2 * count]
    width = products[0].shape[1]
    for r in range(count):
        step = reply(r, count)
        if step != JOINT:
            theirs = products[step][...].astype(jnp.float32)
        else:
            theirs = joint_ref[:, :width].astype(jnp.float32)[CAP:]
        mine = sent[r][:, :width].astype(jnp.float32)[:CAP]
        back = jnp.sum(mine * theirs, axis=1, keepdims=True)
        back_ref[r * CAP : (r + 1) * CAP, :] = jnp.broadcast_to(back, (CAP, LANES))


def down_term(pay_ref, share, start, block):
    hidden = pay_ref[:, pl.ds(start, block)]
    return dot(hidden, pay_ref[:, :share], ((0,), (0,))).astype(jnp.bfloat16)


def own_kernel(pieces, pay_ref, own_ref):
    units, share = own_ref.shape
    block = units // pieces
    for p in range(pieces):
        own_ref[p * block : (p + 1) * block, :] = down_term(pay_ref, share, share + p * block, block)


def down_kernel(count, others, pieces, *refs):
    own_ref = refs[0]
    pays = refs[1 : 1 + others]
    rows_ref, gate_ref, weight_ref, match_ref = refs[1 + others : 5 + others]
    hidden_hbm, down_hbm, match_out, hidden_out, down_out, sems = refs[5 + others :]
    units, share = own_ref.shape
    block = units // pieces
    copies = []

    def write(n, values, destination):
        copies.append(pltpu.make_async_copy(values, destination, sems.at[n]))
        copies[-1].start()

    for p in range(pieces):
        part = slice(p * block, (p + 1) * block)
        total = own_ref[part, :].astype(jnp.float32)
        for pay_ref in pays:
            total = total + down_term(pay_ref, share, share + p * block, block).astype(jnp.float32)
        down_out[part, :] = total
        lines = block // SPLIT
        for n in range(SPLIT * p, SPLIT * (p + 1)):
            part = pl.ds(n * lines, lines)
            write(n, down_out.at[part], down_hbm.at[0, part])

    match_out[...] = match_ref[...]
    upstream = dot(rows_ref[...], weight_ref[...], ((1,), (1,)))
    scaled = (gate_ref[:, :1] * upstream).astype(jnp.bfloat16)
    hidden_out[...] = dot(slot_order(count), scaled, ((0,), (0,))).astype(jnp.bfloat16)
    write(SPLIT * pieces, hidden_out, hidden_hbm.at[0, 0])
    for copy in copies:
        copy.wait()


def gate_kernel(count, ids_ref, match_ref, *refs):
    backs, out_ref = refs[:-1], refs[-1]
    me = lax.axis_index("expert")
    ids = ids_ref[...]
    back = backs[0][...]
    for ref in backs[1:]:
        back = back + ref[...]
    total = jnp.zeros(out_ref.shape, jnp.float32)
    for r in range(count):
        value = back[r * CAP : (r + 1) * CAP, :]
        match = match_ref[r * PAD : r * PAD + CAP, :]
        chosen = jnp.sum(jnp.where(match > 0, value, 0.0), axis=0, keepdims=True)
        total = total + jnp.where(ids == target(me, r, count), chosen, 0.0)
    out_ref[...] = total


def on_device(grad_out, expert_ids, gate_values, saved_hidden, down_weight):
    count = lax.axis_size("expert")
    groups = lax.axis_size("dp")
    tensors = lax.axis_size("tensor")
    tokens, width = grad_out.shape
    top = expert_ids.shape[1]
    units = down_weight.shape[1]
    slots = count * CAP
    share = width // groups
    pieces = units // LANES

    ids, match, weight, hidden, *rest = pl.pallas_call(
        functools.partial(front_kernel, count, pieces),
        out_shape=[
            jax.ShapeDtypeStruct((top, tokens), jnp.int32),
            jax.ShapeDtypeStruct((count * PAD, tokens), jnp.float32),
            jax.ShapeDtypeStruct((units, width), jnp.bfloat16),
            jax.ShapeDtypeStruct((slots, units), jnp.bfloat16),
        ]
        + [
            jax.ShapeDtypeStruct((PAD if r == JOINT else CAP, width + LANES), jnp.bfloat16)
            for r in range(count)
        ]
        + [jax.ShapeDtypeStruct((CAP, width), jnp.bfloat16)] * (count - 1),
        in_specs=[HBM] * 5,
        out_specs=[VMEM] * (3 + 2 * count),
        scratch_shapes=[
            pltpu.VMEM((top, tokens), jnp.bfloat16),
            pltpu.VMEM((tokens, width), jnp.bfloat16),
            pltpu.VMEM((slots, units), jnp.bfloat16),
            pltpu.VMEM((count * PAD, width), jnp.float32),
            pltpu.VMEM((count * PAD, width), jnp.float32),
            pltpu.SemaphoreType.DMA((3 + SPLIT * (pieces + 1),)),
        ],
        compiler_params=PARAMS,
        cost_estimate=cost(2 * count * PAD * (tokens + units) * width, 2 * (tokens + units) * width),
        name="front",
    )(*in_hbm(expert_ids.T, gate_values.T, grad_out, saved_hidden, down_weight))
    sends, products = rest[:count], rest[count:]

    received = [sends[0]] + [send(sends[r], "expert", r) for r in range(1, count)]
    theirs = [products[0]] + [send(products[r - 1], "expert", r) for r in range(JOINT + 1, count)]

    rows, gate, *pays = pl.pallas_call(
        functools.partial(slot_kernel, count, groups),
        out_shape=[
            jax.ShapeDtypeStruct((slots, width), jnp.bfloat16),
            jax.ShapeDtypeStruct((slots, LANES), jnp.float32),
        ]
        + [jax.ShapeDtypeStruct((slots, share + units), jnp.bfloat16)] * groups,
        in_specs=[VMEM] * (1 + count),
        out_specs=[VMEM] * (2 + groups),
        scratch_shapes=[
            pltpu.VMEM((slots, width + LANES), jnp.float32),
            pltpu.VMEM((slots, width), jnp.bfloat16),
        ],
        compiler_params=PARAMS,
        cost_estimate=cost(4 * slots * width, 8 * slots * width),
        name="slots",
    )(hidden, *received)

    back = pl.pallas_call(
        functools.partial(back_kernel, count),
        out_shape=jax.ShapeDtypeStruct((slots, LANES), jnp.float32),
        in_specs=[VMEM] * (2 * count),
        out_specs=VMEM,
        compiler_params=PARAMS,
        cost_estimate=cost(*AFTER_WAIT),
        name="backs",
    )(*sends, received[JOINT], *theirs)

    others = [send(pays[r], "dp", r) for r in range(1, groups)]
    backs = [back] + [send(back, "tensor", r) for r in reversed(range(1, tensors))]

    own = pl.pallas_call(
        functools.partial(own_kernel, pieces),
        out_shape=jax.ShapeDtypeStruct((units, share), jnp.bfloat16),
        in_specs=[VMEM],
        out_specs=VMEM,
        compiler_params=PARAMS,
        cost_estimate=cost(2 * slots * units * share, 2 * units * share),
        name="own",
    )(pays[0])

    hidden_grad, down_grad, match = pl.pallas_call(
        functools.partial(down_kernel, count, groups - 1, pieces),
        out_shape=[
            jax.ShapeDtypeStruct(saved_hidden.shape, jnp.bfloat16),
            jax.ShapeDtypeStruct((1, units, share), jnp.float32),
            jax.ShapeDtypeStruct(match.shape, jnp.float32),
        ],
        in_specs=[VMEM] * (4 + groups),
        out_specs=[HBM, HBM, VMEM],
        scratch_shapes=[
            pltpu.VMEM((slots, units), jnp.bfloat16),
            pltpu.VMEM((units, share), jnp.float32),
            pltpu.SemaphoreType.DMA((SPLIT * pieces + 1,)),
        ],
        compiler_params=PARAMS,
        cost_estimate=cost(2 * slots * units * (width + share), 4 * units * share),
        name="down",
    )(own, *others, rows, gate, weight, match)

    gate_grad = pl.pallas_call(
        functools.partial(gate_kernel, count),
        out_shape=jax.ShapeDtypeStruct(ids.shape, jnp.float32),
        in_specs=[VMEM] * (2 + tensors),
        out_specs=VMEM,
        compiler_params=PARAMS,
        cost_estimate=cost(slots * tokens, 4 * slots * tokens),
        name="gates",
    )(ids, match, *backs)
    return (gate_grad.T, hidden_grad, down_grad)


def solution(mesh):
    return jax.shard_map(
        on_device,
        mesh=mesh,
        in_specs=(
            P(("dp", "expert"), None),
            P(("dp", "expert"), None),
            P(("dp", "expert"), None),
            P("dp", "expert", None, "tensor"),
            P("expert", "tensor", None),
        ),
        out_specs=(
            P(("dp", "expert"), None),
            P("dp", "expert", None, "tensor"),
            P("expert", "tensor", "dp"),
        ),
        check_vma=False,
    )
```

```python
import functools

import jax
import jax.numpy as jnp
from jax import lax
from jax.experimental import pallas as pl
from jax.experimental.pallas import tpu as pltpu
from jax.sharding import PartitionSpec as P

CAP = 4
LANES = 128
JOINT = 1
AFTER_WAIT = (10**9, 10**7)
PAD = 8
VMEM = pl.BlockSpec(memory_space=pltpu.VMEM)
HBM = pl.BlockSpec(memory_space=pltpu.HBM)
PARAMS = pltpu.CompilerParams(vmem_limit_bytes=32 * 2**20)


def dot(a, b, dims):
    return lax.dot_general(a, b, (dims, ((), ())), preferred_element_type=jnp.float32)


def in_hbm(*arrays):
    return [pltpu.with_memory_space_constraint(x, pltpu.HBM) for x in arrays]


def cost(flops, nbytes):
    return pl.CostEstimate(flops=flops, bytes_accessed=nbytes, transcendentals=0)


def paired(size):
    return size & (size - 1) == 0


def target(me, step, size):
    if paired(size):
        return me ^ ((size - step) % size)
    after = me + step
    return after % size if isinstance(me, int) else jnp.where(after >= size, after - size, after)


def source(me, step, size):
    if paired(size):
        return target(me, step, size)
    before = me - step
    return before % size if isinstance(me, int) else jnp.where(before < 0, before + size, before)


def reply(step, size):
    return step if paired(size) else -step % size


def apart(size):
    return [r for r in range(size) if r != JOINT]


def send(value, axis, step, give=target):
    size = lax.axis_size(axis)
    return lax.ppermute(value, axis, [(i, give(i, step, size)) for i in range(size)])


def front_kernel(count, pieces, *refs):
    ids_hbm, gates_hbm, grad_hbm, hidden_hbm, weight_hbm = refs[:5]
    ids_ref, match_ref, weight_ref, hidden_ref = refs[5:9]
    sends = refs[9 : 9 + count]
    products = refs[9 + count : 8 + 2 * count]
    gates_ref, grad_ref, saved_ref, picked_ref, total_ref, chosen_ref, sems = refs[8 + 2 * count :]
    units, width = weight_ref.shape
    top, tokens = ids_ref.shape
    pairs = [(ids_hbm, ids_ref), (gates_hbm, gates_ref), (hidden_hbm.at[0, 0], saved_ref)]
    half = tokens // 2
    for p in range(2):
        part = pl.ds(p * half, half)
        pairs.append((grad_hbm.at[part], grad_ref.at[part]))
    half = units // (2 * pieces)
    for p in range(2 * pieces):
        part = pl.ds(p * half, half)
        pairs.append((weight_hbm.at[0, part], weight_ref.at[part]))
    copies = [pltpu.make_async_copy(*pair, sems.at[n]) for n, pair in enumerate(pairs)]
    for copy in copies:
        copy.start()
    me = lax.axis_index("expert")
    rows = count * PAD
    row = lax.broadcasted_iota(jnp.int32, (rows, tokens), 0)
    expert = target(me, row // PAD, count)
    place = row % PAD
    earlier = lax.broadcasted_iota(jnp.int32, (tokens, tokens), 0)
    later = lax.broadcasted_iota(jnp.int32, (tokens, tokens), 1)
    order = (earlier < later).astype(jnp.bfloat16)
    for copy in copies[:3]:
        copy.wait()
    ids = ids_ref[...]
    gates = gates_ref[...].astype(jnp.float32)
    member = jnp.zeros((rows, tokens), jnp.float32)
    gate = jnp.zeros((rows, tokens), jnp.float32)
    for k in range(top):
        hit = ids[k : k + 1, :] == expert
        member = jnp.where(hit, 1.0, member)
        gate = jnp.where(hit, gates[k : k + 1, :], gate)
    before = dot(member.astype(jnp.bfloat16), order, ((1,), (0,)))
    taken = (member > 0) & (before == place.astype(jnp.float32)) & (place < CAP)
    match = taken.astype(jnp.float32)
    match_ref[...] = match
    slot_gate = jnp.sum(match * gate, axis=1, keepdims=True)
    match = match.astype(jnp.bfloat16)

    slots = count * CAP
    saved = saved_ref[...]
    hidden_ref[...] = dot(slot_order(count), saved, ((1,), (0,))).astype(jnp.bfloat16)
    here = lax.broadcasted_iota(jnp.int32, (rows, slots), 0)
    there = lax.broadcasted_iota(jnp.int32, (rows, slots), 1)
    place = here % PAD - jnp.where(here // PAD == JOINT, CAP, 0)
    chosen = (place >= 0) & (place < CAP) & (there == target(me, here // PAD, count) * CAP + place)
    hidden = dot(chosen.astype(jnp.bfloat16), saved, ((1,), (0,))).astype(jnp.bfloat16)

    for copy in copies[3:5]:
        copy.wait()
    picked_ref[...] = dot(match, grad_ref[...], ((1,), (0,)))
    for r in range(count):
        part = slice(r * PAD, r * PAD + sends[r].shape[0])
        gate = jnp.broadcast_to(slot_gate[part], (sends[r].shape[0], LANES))
        sends[r][:, width:] = gate.astype(jnp.bfloat16)
        if r != JOINT:
            sends[r][:, :width] = picked_ref[part, :].astype(jnp.bfloat16)
    block = units // pieces
    chosen_ref[...] = hidden
    total_ref[...] = jnp.zeros(total_ref.shape, jnp.float32)

    @pl.loop(0, pieces)
    def _(p):
        for n in range(2):
            part = pl.ds(pl.multiple_of((2 * p + n) * half, half), half)
            load = (weight_hbm.at[0, part], weight_ref.at[part])
            pltpu.make_async_copy(*load, sems.at[5 + 2 * p + n]).wait()
        part = pl.ds(pl.multiple_of(p * block, block), block)
        total_ref[...] += dot(chosen_ref[:, part], weight_ref[part, :], ((1,), (0,)))

    for product, r in zip(products, apart(count)):
        product[...] = total_ref[r * PAD : r * PAD + CAP, :].astype(jnp.bfloat16)
    part = slice(JOINT * PAD, (JOINT + 1) * PAD)
    sends[JOINT][:, :width] = (picked_ref[part, :] + total_ref[part, :]).astype(jnp.bfloat16)


def slot_order(count):
    me = lax.axis_index("expert")
    slots = count * CAP
    here = lax.broadcasted_iota(jnp.int32, (slots, slots), 0)
    saved = lax.broadcasted_iota(jnp.int32, (slots, slots), 1)
    return (saved == source(me, here // CAP, count) * CAP + here % CAP).astype(jnp.bfloat16)


def slot_kernel(count, groups, hidden_ref, *refs):
    received = refs[:count]
    rows_ref, gate_ref = refs[count : count + 2]
    pays = refs[count + 2 : count + 2 + groups]
    wide_ref, weighted_ref = refs[count + 2 + groups :]
    width = rows_ref.shape[1]
    for r in range(count):
        wide_ref[r * CAP : (r + 1) * CAP, :] = received[r][...].astype(jnp.float32)[:CAP]
    rows = wide_ref[:, :width]
    gate = wide_ref[:, width:]
    gate_ref[...] = gate
    rows_ref[...] = rows.astype(jnp.bfloat16)
    weighted_ref[...] = (gate[:, :1] * rows).astype(jnp.bfloat16)
    share = width // groups
    me = lax.axis_index("dp")
    for r in range(groups):
        group = target(me, r, groups)
        pays[r][:, :share] = weighted_ref[:, pl.ds(pl.multiple_of(group * share, share), share)]
        pays[r][:, share:] = hidden_ref[...]


def back_kernel(count, *refs):
    sent = refs[:count]
    joint_ref = refs[count]
    products = dict(zip(apart(count), refs[count + 1 : 2 * count]))
    back_ref = refs[2 * count]
    width = products[0].shape[1]
    for r in range(count):
        step = reply(r, count)
        if step != JOINT:
            theirs = products[step][...].astype(jnp.float32)
        else:
            theirs = joint_ref[:, :width].astype(jnp.float32)[CAP:]
        mine = sent[r][:, :width].astype(jnp.float32)[:CAP]
        back = jnp.sum(mine * theirs, axis=1, keepdims=True)
        back_ref[r * CAP : (r + 1) * CAP, :] = jnp.broadcast_to(back, (CAP, LANES))


def down_term(pay_ref, share, start, block):
    hidden = pay_ref[:, pl.ds(start, block)]
    return dot(hidden, pay_ref[:, :share], ((0,), (0,))).astype(jnp.bfloat16)


def own_kernel(pieces, pay_ref, own_ref):
    units, share = own_ref.shape
    block = units // pieces

    @pl.loop(0, pieces)
    def _(p):
        start = pl.multiple_of(p * block, block)
        own_ref[pl.ds(start, block), :] = down_term(pay_ref, share, share + start, block)


def down_kernel(count, others, pieces, *refs):
    own_ref = refs[0]
    pays = refs[1 : 1 + others]
    rows_ref, gate_ref, weight_ref, match_ref = refs[1 + others : 5 + others]
    hidden_hbm, down_hbm, match_out, hidden_out, down_out, sems = refs[5 + others :]
    units, share = own_ref.shape
    block = units // pieces

    def write(p):
        part = pl.ds(pl.multiple_of(p * block, block), block)
        return pltpu.make_async_copy(down_out.at[part], down_hbm.at[0, part], sems.at[p])

    @pl.loop(0, pieces)
    def _(p):
        start = pl.multiple_of(p * block, block)
        part = pl.ds(start, block)
        total = own_ref[part, :].astype(jnp.float32)
        for pay_ref in pays:
            total = total + down_term(pay_ref, share, share + start, block).astype(jnp.float32)
        down_out[part, :] = total
        write(p).start()

    match_out[...] = match_ref[...]
    half = weight_ref.shape[1] // 2

    def product(n):
        part = pl.ds(pl.multiple_of(n * half, half), half)
        return dot(rows_ref[:, part], weight_ref[:, part], ((1,), (1,)))

    upstream = lax.fori_loop(0, 2, lambda n, total: total + product(n), jnp.zeros((rows_ref.shape[0], units), jnp.float32))
    scaled = (gate_ref[:, :1] * upstream).astype(jnp.bfloat16)
    hidden_out[...] = dot(slot_order(count), scaled, ((0,), (0,))).astype(jnp.bfloat16)
    last = pltpu.make_async_copy(hidden_out, hidden_hbm.at[0, 0], sems.at[pieces])
    last.start()
    for p in range(pieces):
        write(p).wait()
    last.wait()


def gate_kernel(count, ids_ref, match_ref, *refs):
    backs, out_ref = refs[:-1], refs[-1]
    me = lax.axis_index("expert")
    ids = ids_ref[...]
    back = backs[0][...]
    for ref in backs[1:]:
        back = back + ref[...]
    total = jnp.zeros(out_ref.shape, jnp.float32)
    for r in range(count):
        value = back[r * CAP : (r + 1) * CAP, :]
        match = match_ref[r * PAD : r * PAD + CAP, :]
        chosen = jnp.sum(jnp.where(match > 0, value, 0.0), axis=0, keepdims=True)
        total = total + jnp.where(ids == target(me, r, count), chosen, 0.0)
    out_ref[...] = total


def on_device(grad_out, expert_ids, gate_values, saved_hidden, down_weight):
    count = lax.axis_size("expert")
    groups = lax.axis_size("dp")
    tensors = lax.axis_size("tensor")
    tokens, width = grad_out.shape
    top = expert_ids.shape[1]
    units = down_weight.shape[1]
    slots = count * CAP
    share = width // groups
    pieces = units // LANES

    ids, match, weight, hidden, *rest = pl.pallas_call(
        functools.partial(front_kernel, count, pieces),
        out_shape=[
            jax.ShapeDtypeStruct((top, tokens), jnp.int32),
            jax.ShapeDtypeStruct((count * PAD, tokens), jnp.float32),
            jax.ShapeDtypeStruct((units, width), jnp.bfloat16),
            jax.ShapeDtypeStruct((slots, units), jnp.bfloat16),
        ]
        + [
            jax.ShapeDtypeStruct((PAD if r == JOINT else CAP, width + LANES), jnp.bfloat16)
            for r in range(count)
        ]
        + [jax.ShapeDtypeStruct((CAP, width), jnp.bfloat16)] * (count - 1),
        in_specs=[HBM] * 5,
        out_specs=[VMEM] * (3 + 2 * count),
        scratch_shapes=[
            pltpu.VMEM((top, tokens), jnp.bfloat16),
            pltpu.VMEM((tokens, width), jnp.bfloat16),
            pltpu.VMEM((slots, units), jnp.bfloat16),
            pltpu.VMEM((count * PAD, width), jnp.float32),
            pltpu.VMEM((count * PAD, width), jnp.float32),
            pltpu.VMEM((count * PAD, units), jnp.bfloat16),
            pltpu.SemaphoreType.DMA((5 + 2 * pieces,)),
        ],
        compiler_params=PARAMS,
        cost_estimate=cost(2 * count * PAD * (tokens + units) * width, 2 * (tokens + units) * width),
        name="front",
    )(*in_hbm(expert_ids.T, gate_values.T, grad_out, saved_hidden, down_weight))
    sends, products = rest[:count], rest[count:]

    received = [sends[0]] + [send(sends[r], "expert", r) for r in range(1, count)]
    theirs = [products[0]] + [send(products[r - 1], "expert", r) for r in range(JOINT + 1, count)]

    rows, gate, *pays = pl.pallas_call(
        functools.partial(slot_kernel, count, groups),
        out_shape=[
            jax.ShapeDtypeStruct((slots, width), jnp.bfloat16),
            jax.ShapeDtypeStruct((slots, LANES), jnp.float32),
        ]
        + [jax.ShapeDtypeStruct((slots, share + units), jnp.bfloat16)] * groups,
        in_specs=[VMEM] * (1 + count),
        out_specs=[VMEM] * (2 + groups),
        scratch_shapes=[
            pltpu.VMEM((slots, width + LANES), jnp.float32),
            pltpu.VMEM((slots, width), jnp.bfloat16),
        ],
        compiler_params=PARAMS,
        cost_estimate=cost(4 * slots * width, 8 * slots * width),
        name="slots",
    )(hidden, *received)

    back = pl.pallas_call(
        functools.partial(back_kernel, count),
        out_shape=jax.ShapeDtypeStruct((slots, LANES), jnp.float32),
        in_specs=[VMEM] * (2 * count),
        out_specs=VMEM,
        compiler_params=PARAMS,
        cost_estimate=cost(*AFTER_WAIT),
        name="backs",
    )(*sends, received[JOINT], *theirs)

    others = [send(pays[r], "dp", r) for r in range(1, groups)]
    backs = [back] + [send(back, "tensor", r) for r in reversed(range(1, tensors))]

    own = pl.pallas_call(
        functools.partial(own_kernel, pieces),
        out_shape=jax.ShapeDtypeStruct((units, share), jnp.bfloat16),
        in_specs=[VMEM],
        out_specs=VMEM,
        compiler_params=PARAMS,
        cost_estimate=cost(2 * slots * units * share, 2 * units * share),
        name="own",
    )(pays[0])

    hidden_grad, down_grad, match = pl.pallas_call(
        functools.partial(down_kernel, count, groups - 1, pieces),
        out_shape=[
            jax.ShapeDtypeStruct(saved_hidden.shape, jnp.bfloat16),
            jax.ShapeDtypeStruct((1, units, share), jnp.float32),
            jax.ShapeDtypeStruct(match.shape, jnp.float32),
        ],
        in_specs=[VMEM] * (4 + groups),
        out_specs=[HBM, HBM, VMEM],
        scratch_shapes=[
            pltpu.VMEM((slots, units), jnp.bfloat16),
            pltpu.VMEM((units, share), jnp.float32),
            pltpu.SemaphoreType.DMA((pieces + 1,)),
        ],
        compiler_params=PARAMS,
        cost_estimate=cost(2 * slots * units * (width + share), 4 * units * share),
        name="down",
    )(own, *others, rows, gate, weight, match)

    gate_grad = pl.pallas_call(
        functools.partial(gate_kernel, count),
        out_shape=jax.ShapeDtypeStruct(ids.shape, jnp.float32),
        in_specs=[VMEM] * (2 + tensors),
        out_specs=VMEM,
        compiler_params=PARAMS,
        cost_estimate=cost(slots * tokens, 4 * slots * tokens),
        name="gates",
    )(ids, match, *backs)
    return (gate_grad.T, hidden_grad, down_grad)


def solution(mesh):
    return jax.shard_map(
        on_device,
        mesh=mesh,
        in_specs=(
            P(("dp", "expert"), None),
            P(("dp", "expert"), None),
            P(("dp", "expert"), None),
            P("dp", "expert", None, "tensor"),
            P("expert", "tensor", None),
        ),
        out_specs=(
            P(("dp", "expert"), None),
            P("dp", "expert", None, "tensor"),
            P("expert", "tensor", "dp"),
        ),
        check_vma=False,
    )
```

```python
import functools

import jax
import jax.numpy as jnp
from jax import lax
from jax.experimental import pallas as pl
from jax.experimental.pallas import tpu as pltpu
from jax.sharding import PartitionSpec as P

CAP = 4
LANES = 128
JOINT = 1
AFTER_WAIT = (10**9, 10**7)
PAD = 8
VMEM = pl.BlockSpec(memory_space=pltpu.VMEM)
HBM = pl.BlockSpec(memory_space=pltpu.HBM)
PARAMS = pltpu.CompilerParams(vmem_limit_bytes=32 * 2**20)


def dot(a, b, dims):
    return lax.dot_general(a, b, (dims, ((), ())), preferred_element_type=jnp.float32)


def in_hbm(*arrays):
    return [pltpu.with_memory_space_constraint(x, pltpu.HBM) for x in arrays]


def cost(flops, nbytes):
    return pl.CostEstimate(flops=flops, bytes_accessed=nbytes, transcendentals=0)


def paired(size):
    return size & (size - 1) == 0


def target(me, step, size):
    if paired(size):
        return me ^ ((size - step) % size)
    after = me + step
    return after % size if isinstance(me, int) else jnp.where(after >= size, after - size, after)


def source(me, step, size):
    if paired(size):
        return target(me, step, size)
    before = me - step
    return before % size if isinstance(me, int) else jnp.where(before < 0, before + size, before)


def reply(step, size):
    return step if paired(size) else -step % size


def apart(size):
    return [r for r in range(size) if r != JOINT]


def send(value, axis, step, give=target):
    size = lax.axis_size(axis)
    return lax.ppermute(value, axis, [(i, give(i, step, size)) for i in range(size)])


def front_kernel(count, pieces, *refs):
    ids_hbm, gates_hbm, grad_hbm, hidden_hbm, weight_hbm = refs[:5]
    ids_ref, match_ref, weight_ref, hidden_ref = refs[5:9]
    sends = refs[9 : 9 + count]
    products = refs[9 + count : 8 + 2 * count]
    gates_ref, grad_ref, saved_ref, picked_ref, total_ref, sems = refs[8 + 2 * count :]
    units, width = weight_ref.shape
    top, tokens = ids_ref.shape
    pairs = [(ids_hbm, ids_ref), (gates_hbm, gates_ref), (hidden_hbm.at[0, 0], saved_ref)]
    half = tokens // 2
    for p in range(2):
        part = pl.ds(p * half, half)
        pairs.append((grad_hbm.at[part], grad_ref.at[part]))
    half = units // (2 * pieces)
    for p in range(2 * pieces):
        part = pl.ds(p * half, half)
        pairs.append((weight_hbm.at[0, part], weight_ref.at[part]))
    copies = [pltpu.make_async_copy(*pair, sems.at[n]) for n, pair in enumerate(pairs)]
    for copy in copies:
        copy.start()
    me = lax.axis_index("expert")
    rows = count * PAD
    row = lax.broadcasted_iota(jnp.int32, (rows, tokens), 0)
    expert = target(me, row // PAD, count)
    place = row % PAD
    earlier = lax.broadcasted_iota(jnp.int32, (tokens, tokens), 0)
    later = lax.broadcasted_iota(jnp.int32, (tokens, tokens), 1)
    order = (earlier < later).astype(jnp.bfloat16)
    for copy in copies[:3]:
        copy.wait()
    ids = ids_ref[...]
    gates = gates_ref[...].astype(jnp.float32)
    member = jnp.zeros((rows, tokens), jnp.float32)
    gate = jnp.zeros((rows, tokens), jnp.float32)
    for k in range(top):
        hit = ids[k : k + 1, :] == expert
        member = jnp.where(hit, 1.0, member)
        gate = jnp.where(hit, gates[k : k + 1, :], gate)
    before = dot(member.astype(jnp.bfloat16), order, ((1,), (0,)))
    taken = (member > 0) & (before == place.astype(jnp.float32)) & (place < CAP)
    match = taken.astype(jnp.float32)
    match_ref[...] = match
    slot_gate = jnp.sum(match * gate, axis=1, keepdims=True)
    match = match.astype(jnp.bfloat16)

    slots = count * CAP
    saved = saved_ref[...]
    hidden_ref[...] = dot(slot_order(count), saved, ((1,), (0,))).astype(jnp.bfloat16)
    here = lax.broadcasted_iota(jnp.int32, (rows, slots), 0)
    there = lax.broadcasted_iota(jnp.int32, (rows, slots), 1)
    place = here % PAD - jnp.where(here // PAD == JOINT, CAP, 0)
    chosen = (place >= 0) & (place < CAP) & (there == target(me, here // PAD, count) * CAP + place)
    hidden = dot(chosen.astype(jnp.bfloat16), saved, ((1,), (0,))).astype(jnp.bfloat16)

    for copy in copies[3:5]:
        copy.wait()
    picked_ref[...] = dot(match, grad_ref[...], ((1,), (0,)))
    for r in range(count):
        part = slice(r * PAD, r * PAD + sends[r].shape[0])
        gate = jnp.broadcast_to(slot_gate[part], (sends[r].shape[0], LANES))
        sends[r][:, width:] = gate.astype(jnp.bfloat16)
        if r != JOINT:
            sends[r][:, :width] = picked_ref[part, :].astype(jnp.bfloat16)
    block = units // pieces
    for p in range(pieces):
        for copy in copies[5 + 2 * p : 7 + 2 * p]:
            copy.wait()
        part = slice(p * block, (p + 1) * block)
        term = dot(hidden[:, part], weight_ref[part, :], ((1,), (0,)))
        total_ref[...] = term if p == 0 else total_ref[...] + term
    for product, r in zip(products, apart(count)):
        product[...] = total_ref[r * PAD : r * PAD + CAP, :].astype(jnp.bfloat16)
    part = slice(JOINT * PAD, (JOINT + 1) * PAD)
    sends[JOINT][:, :width] = (picked_ref[part, :] + total_ref[part, :]).astype(jnp.bfloat16)


def slot_order(count):
    me = lax.axis_index("expert")
    slots = count * CAP
    here = lax.broadcasted_iota(jnp.int32, (slots, slots), 0)
    saved = lax.broadcasted_iota(jnp.int32, (slots, slots), 1)
    return (saved == source(me, here // CAP, count) * CAP + here % CAP).astype(jnp.bfloat16)


def slot_kernel(count, groups, hidden_ref, *refs):
    received = refs[:count]
    rows_ref, gate_ref = refs[count : count + 2]
    pays = refs[count + 2 : count + 2 + groups]
    wide_ref, weighted_ref = refs[count + 2 + groups :]
    width = rows_ref.shape[1]
    for r in range(count):
        wide_ref[r * CAP : (r + 1) * CAP, :] = received[r][...].astype(jnp.float32)[:CAP]
    rows = wide_ref[:, :width]
    gate = wide_ref[:, width:]
    gate_ref[...] = gate
    rows_ref[...] = rows.astype(jnp.bfloat16)
    weighted_ref[...] = (gate[:, :1] * rows).astype(jnp.bfloat16)
    share = width // groups
    me = lax.axis_index("dp")
    for r in range(groups):
        group = target(me, r, groups)
        pays[r][:, :share] = weighted_ref[:, pl.ds(pl.multiple_of(group * share, share), share)]
        pays[r][:, share:] = hidden_ref[...]


def back_kernel(count, *refs):
    sent = refs[:count]
    joint_ref = refs[count]
    products = dict(zip(apart(count), refs[count + 1 : 2 * count]))
    back_ref = refs[2 * count]
    width = products[0].shape[1]
    for r in range(count):
        step = reply(r, count)
        if step != JOINT:
            theirs = products[step][...].astype(jnp.float32)
        else:
            theirs = joint_ref[:, :width].astype(jnp.float32)[CAP:]
        mine = sent[r][:, :width].astype(jnp.float32)[:CAP]
        back = jnp.sum(mine * theirs, axis=1, keepdims=True)
        back_ref[r * CAP : (r + 1) * CAP, :] = jnp.broadcast_to(back, (CAP, LANES))


def down_kernel(count, groups, pieces, rows_ref, gate_ref, weight_ref, match_ref, *refs):
    pays = refs[:groups]
    hidden_hbm, down_hbm, match_out, hidden_out, down_out, sems = refs[groups:]
    units, share = down_out.shape
    block = units // pieces
    slots = jnp.concatenate([pay_ref[...] for pay_ref in pays], axis=0)
    copies = []

    def write(n, values, destination):
        copies.append(pltpu.make_async_copy(values, destination, sems.at[n]))
        copies[-1].start()

    for p in range(pieces):
        part = slice(p * block, (p + 1) * block)
        hidden = slots[:, share + p * block : share + (p + 1) * block]
        down_out[part, :] = dot(hidden, slots[:, :share], ((0,), (0,)))
        part = pl.ds(p * block, block)
        write(p, down_out.at[part], down_hbm.at[0, part])

    match_out[...] = match_ref[...]
    upstream = dot(rows_ref[...], weight_ref[...], ((1,), (1,)))
    scaled = (gate_ref[:, :1] * upstream).astype(jnp.bfloat16)
    hidden_out[...] = dot(slot_order(count), scaled, ((0,), (0,))).astype(jnp.bfloat16)
    write(pieces, hidden_out, hidden_hbm.at[0, 0])
    for copy in copies:
        copy.wait()


def gate_kernel(count, ids_ref, match_ref, *refs):
    backs, out_ref = refs[:-1], refs[-1]
    me = lax.axis_index("expert")
    ids = ids_ref[...]
    back = backs[0][...]
    for ref in backs[1:]:
        back = back + ref[...]
    total = jnp.zeros(out_ref.shape, jnp.float32)
    for r in range(count):
        value = back[r * CAP : (r + 1) * CAP, :]
        match = match_ref[r * PAD : r * PAD + CAP, :]
        chosen = jnp.sum(jnp.where(match > 0, value, 0.0), axis=0, keepdims=True)
        total = total + jnp.where(ids == target(me, r, count), chosen, 0.0)
    out_ref[...] = total


def on_device(grad_out, expert_ids, gate_values, saved_hidden, down_weight):
    count = lax.axis_size("expert")
    groups = lax.axis_size("dp")
    tensors = lax.axis_size("tensor")
    tokens, width = grad_out.shape
    top = expert_ids.shape[1]
    units = down_weight.shape[1]
    slots = count * CAP
    share = width // groups
    pieces = units // LANES

    ids, match, weight, hidden, *rest = pl.pallas_call(
        functools.partial(front_kernel, count, pieces),
        out_shape=[
            jax.ShapeDtypeStruct((top, tokens), jnp.int32),
            jax.ShapeDtypeStruct((count * PAD, tokens), jnp.float32),
            jax.ShapeDtypeStruct((units, width), jnp.bfloat16),
            jax.ShapeDtypeStruct((slots, units), jnp.bfloat16),
        ]
        + [
            jax.ShapeDtypeStruct((PAD if r == JOINT else CAP, width + LANES), jnp.bfloat16)
            for r in range(count)
        ]
        + [jax.ShapeDtypeStruct((CAP, width), jnp.bfloat16)] * (count - 1),
        in_specs=[HBM] * 5,
        out_specs=[VMEM] * (3 + 2 * count),
        scratch_shapes=[
            pltpu.VMEM((top, tokens), jnp.bfloat16),
            pltpu.VMEM((tokens, width), jnp.bfloat16),
            pltpu.VMEM((slots, units), jnp.bfloat16),
            pltpu.VMEM((count * PAD, width), jnp.float32),
            pltpu.VMEM((count * PAD, width), jnp.float32),
            pltpu.SemaphoreType.DMA((5 + 2 * pieces,)),
        ],
        compiler_params=PARAMS,
        cost_estimate=cost(2 * count * PAD * (tokens + units) * width, 2 * (tokens + units) * width),
        name="front",
    )(*in_hbm(expert_ids.T, gate_values.T, grad_out, saved_hidden, down_weight))
    sends, products = rest[:count], rest[count:]

    received = [sends[0]] + [send(sends[r], "expert", r) for r in range(1, count)]
    theirs = [products[0]] + [send(products[r - 1], "expert", r) for r in range(JOINT + 1, count)]

    rows, gate, *pays = pl.pallas_call(
        functools.partial(slot_kernel, count, groups),
        out_shape=[
            jax.ShapeDtypeStruct((slots, width), jnp.bfloat16),
            jax.ShapeDtypeStruct((slots, LANES), jnp.float32),
        ]
        + [jax.ShapeDtypeStruct((slots, share + units), jnp.bfloat16)] * groups,
        in_specs=[VMEM] * (1 + count),
        out_specs=[VMEM] * (2 + groups),
        scratch_shapes=[
            pltpu.VMEM((slots, width + LANES), jnp.float32),
            pltpu.VMEM((slots, width), jnp.bfloat16),
        ],
        compiler_params=PARAMS,
        cost_estimate=cost(4 * slots * width, 8 * slots * width),
        name="slots",
    )(hidden, *received)

    back = pl.pallas_call(
        functools.partial(back_kernel, count),
        out_shape=jax.ShapeDtypeStruct((slots, LANES), jnp.float32),
        in_specs=[VMEM] * (2 * count),
        out_specs=VMEM,
        compiler_params=PARAMS,
        cost_estimate=cost(*AFTER_WAIT),
        name="backs",
    )(*sends, received[JOINT], *theirs)

    others = [send(pays[r], "dp", r) for r in range(1, groups)]
    backs = [back] + [send(back, "tensor", r) for r in reversed(range(1, tensors))]

    hidden_grad, down_grad, match = pl.pallas_call(
        functools.partial(down_kernel, count, groups, pieces),
        out_shape=[
            jax.ShapeDtypeStruct(saved_hidden.shape, jnp.bfloat16),
            jax.ShapeDtypeStruct((1, units, share), jnp.float32),
            jax.ShapeDtypeStruct(match.shape, jnp.float32),
        ],
        in_specs=[VMEM] * (4 + groups),
        out_specs=[HBM, HBM, VMEM],
        scratch_shapes=[
            pltpu.VMEM((slots, units), jnp.bfloat16),
            pltpu.VMEM((units, share), jnp.float32),
            pltpu.SemaphoreType.DMA((pieces + 1,)),
        ],
        compiler_params=PARAMS,
        cost_estimate=cost(2 * slots * units * (width + share), 4 * units * share),
        name="down",
    )(rows, gate, weight, match, pays[0], *others)

    gate_grad = pl.pallas_call(
        functools.partial(gate_kernel, count),
        out_shape=jax.ShapeDtypeStruct(ids.shape, jnp.float32),
        in_specs=[VMEM] * (2 + tensors),
        out_specs=VMEM,
        compiler_params=PARAMS,
        cost_estimate=cost(slots * tokens, 4 * slots * tokens),
        name="gates",
    )(ids, match, *backs)
    return (gate_grad.T, hidden_grad, down_grad)


def solution(mesh):
    return jax.shard_map(
        on_device,
        mesh=mesh,
        in_specs=(
            P(("dp", "expert"), None),
            P(("dp", "expert"), None),
            P(("dp", "expert"), None),
            P("dp", "expert", None, "tensor"),
            P("expert", "tensor", None),
        ),
        out_specs=(
            P(("dp", "expert"), None),
            P("dp", "expert", None, "tensor"),
            P("expert", "tensor", "dp"),
        ),
        check_vma=False,
    )
```

```python
import functools

import jax
import jax.numpy as jnp
from jax import lax
from jax.experimental import pallas as pl
from jax.experimental.pallas import tpu as pltpu
from jax.sharding import PartitionSpec as P

CAP = 4
LANES = 128
JOINT = 1
AFTER_WAIT = (10**9, 10**7)
PAD = 8
VMEM = pl.BlockSpec(memory_space=pltpu.VMEM)
HBM = pl.BlockSpec(memory_space=pltpu.HBM)
PARAMS = pltpu.CompilerParams(vmem_limit_bytes=32 * 2**20)


def dot(a, b, dims):
    return lax.dot_general(a, b, (dims, ((), ())), preferred_element_type=jnp.float32)


def in_hbm(*arrays):
    return [pltpu.with_memory_space_constraint(x, pltpu.HBM) for x in arrays]


def cost(flops, nbytes):
    return pl.CostEstimate(flops=flops, bytes_accessed=nbytes, transcendentals=0)


def paired(size):
    return size & (size - 1) == 0


def target(me, step, size):
    if paired(size):
        return me ^ ((size - step) % size)
    after = me + step
    return after % size if isinstance(me, int) else jnp.where(after >= size, after - size, after)


def source(me, step, size):
    if paired(size):
        return target(me, step, size)
    before = me - step
    return before % size if isinstance(me, int) else jnp.where(before < 0, before + size, before)


def reply(step, size):
    return step if paired(size) else -step % size


def apart(size):
    return [r for r in range(size) if r != JOINT]


def send(value, axis, step, give=target):
    size = lax.axis_size(axis)
    return lax.ppermute(value, axis, [(i, give(i, step, size)) for i in range(size)])


def front_kernel(count, pieces, *refs):
    ids_hbm, gates_hbm, grad_hbm, hidden_hbm, weight_hbm = refs[:5]
    ids_ref, match_ref, weight_ref, hidden_ref = refs[5:9]
    sends = refs[9 : 9 + count]
    products = refs[9 + count : 8 + 2 * count]
    gates_ref, grad_ref, saved_ref, picked_ref, total_ref, sems = refs[8 + 2 * count :]
    units, width = weight_ref.shape
    top, tokens = ids_ref.shape
    pairs = [(ids_hbm, ids_ref), (gates_hbm, gates_ref), (hidden_hbm.at[0, 0], saved_ref)]
    half = tokens // 2
    for p in range(2):
        part = pl.ds(p * half, half)
        pairs.append((grad_hbm.at[part], grad_ref.at[part]))
    half = units // (2 * pieces)
    for p in range(2 * pieces):
        part = pl.ds(p * half, half)
        pairs.append((weight_hbm.at[0, part], weight_ref.at[part]))
    copies = [pltpu.make_async_copy(*pair, sems.at[n]) for n, pair in enumerate(pairs)]
    for copy in copies:
        copy.start()
    me = lax.axis_index("expert")
    rows = count * PAD
    row = lax.broadcasted_iota(jnp.int32, (rows, tokens), 0)
    expert = target(me, row // PAD, count)
    place = row % PAD
    earlier = lax.broadcasted_iota(jnp.int32, (tokens, tokens), 0)
    later = lax.broadcasted_iota(jnp.int32, (tokens, tokens), 1)
    order = (earlier < later).astype(jnp.bfloat16)
    for copy in copies[:3]:
        copy.wait()
    ids = ids_ref[...]
    gates = gates_ref[...].astype(jnp.float32)
    member = jnp.zeros((rows, tokens), jnp.float32)
    gate = jnp.zeros((rows, tokens), jnp.float32)
    for k in range(top):
        hit = ids[k : k + 1, :] == expert
        member = jnp.where(hit, 1.0, member)
        gate = jnp.where(hit, gates[k : k + 1, :], gate)
    before = dot(member.astype(jnp.bfloat16), order, ((1,), (0,)))
    taken = (member > 0) & (before == place.astype(jnp.float32)) & (place < CAP)
    match = taken.astype(jnp.float32)
    match_ref[...] = match
    slot_gate = jnp.sum(match * gate, axis=1, keepdims=True)
    match = match.astype(jnp.bfloat16)

    slots = count * CAP
    saved = saved_ref[...]
    hidden_ref[...] = dot(slot_order(count), saved, ((1,), (0,))).astype(jnp.bfloat16)
    here = lax.broadcasted_iota(jnp.int32, (rows, slots), 0)
    there = lax.broadcasted_iota(jnp.int32, (rows, slots), 1)
    place = here % PAD - jnp.where(here // PAD == JOINT, CAP, 0)
    chosen = (place >= 0) & (place < CAP) & (there == target(me, here // PAD, count) * CAP + place)
    hidden = dot(chosen.astype(jnp.bfloat16), saved, ((1,), (0,))).astype(jnp.bfloat16)

    for copy in copies[3:5]:
        copy.wait()
    picked_ref[...] = dot(match, grad_ref[...], ((1,), (0,)))
    for r in range(count):
        part = slice(r * PAD, r * PAD + sends[r].shape[0])
        gate = jnp.broadcast_to(slot_gate[part], (sends[r].shape[0], LANES))
        sends[r][:, width:] = gate.astype(jnp.bfloat16)
        if r != JOINT:
            sends[r][:, :width] = picked_ref[part, :].astype(jnp.bfloat16)
    block = units // pieces
    for p in range(pieces):
        for copy in copies[5 + 2 * p : 7 + 2 * p]:
            copy.wait()
        part = slice(p * block, (p + 1) * block)
        term = dot(hidden[:, part], weight_ref[part, :], ((1,), (0,)))
        total_ref[...] = term if p == 0 else total_ref[...] + term
    for product, r in zip(products, apart(count)):
        product[...] = total_ref[r * PAD : r * PAD + CAP, :].astype(jnp.bfloat16)
    part = slice(JOINT * PAD, (JOINT + 1) * PAD)
    sends[JOINT][:, :width] = (picked_ref[part, :] + total_ref[part, :]).astype(jnp.bfloat16)


def slot_order(count):
    me = lax.axis_index("expert")
    slots = count * CAP
    here = lax.broadcasted_iota(jnp.int32, (slots, slots), 0)
    saved = lax.broadcasted_iota(jnp.int32, (slots, slots), 1)
    return (saved == source(me, here // CAP, count) * CAP + here % CAP).astype(jnp.bfloat16)


def slot_kernel(count, groups, hidden_ref, *refs):
    received = refs[:count]
    rows_ref, gate_ref = refs[count : count + 2]
    pays = refs[count + 2 : count + 2 + groups]
    wide_ref, weighted_ref = refs[count + 2 + groups :]
    width = rows_ref.shape[1]
    for r in range(count):
        wide_ref[r * CAP : (r + 1) * CAP, :] = received[r][...].astype(jnp.float32)[:CAP]
    rows = wide_ref[:, :width]
    gate = wide_ref[:, width:]
    gate_ref[...] = gate
    rows_ref[...] = rows.astype(jnp.bfloat16)
    weighted_ref[...] = (gate[:, :1] * rows).astype(jnp.bfloat16)
    share = width // groups
    me = lax.axis_index("dp")
    for r in range(groups):
        group = target(me, r, groups)
        pays[r][:, :share] = weighted_ref[:, pl.ds(pl.multiple_of(group * share, share), share)]
        pays[r][:, share:] = hidden_ref[...]


def back_kernel(count, *refs):
    sent = refs[:count]
    joint_ref = refs[count]
    products = dict(zip(apart(count), refs[count + 1 : 2 * count]))
    back_ref = refs[2 * count]
    width = products[0].shape[1]
    for r in range(count):
        step = reply(r, count)
        if step != JOINT:
            theirs = products[step][...].astype(jnp.float32)
        else:
            theirs = joint_ref[:, :width].astype(jnp.float32)[CAP:]
        mine = sent[r][:, :width].astype(jnp.float32)[:CAP]
        back = jnp.sum(mine * theirs, axis=1, keepdims=True)
        back_ref[r * CAP : (r + 1) * CAP, :] = jnp.broadcast_to(back, (CAP, LANES))


def upstream_part(rows_ref, weight_ref, begin, end):
    return dot(rows_ref[:, begin:end], weight_ref[:, begin:end], ((1,), (1,)))


def upstream_kernel(split, rows_ref, weight_ref, out_ref):
    out_ref[...] = upstream_part(rows_ref, weight_ref, 0, split)


def down_kernel(count, groups, pieces, split, part_ref, rows_ref, gate_ref, weight_ref, match_ref, *refs):
    pays = refs[:groups]
    hidden_hbm, down_hbm, match_out, hidden_out, down_out, sems = refs[groups:]
    units, share = down_out.shape
    block = units // pieces
    slots = jnp.concatenate([pay_ref[...] for pay_ref in pays], axis=0)
    copies = []

    def write(n, values, destination):
        copies.append(pltpu.make_async_copy(values, destination, sems.at[n]))
        copies[-1].start()

    for p in range(pieces):
        part = slice(p * block, (p + 1) * block)
        hidden = slots[:, share + p * block : share + (p + 1) * block]
        down_out[part, :] = dot(hidden, slots[:, :share], ((0,), (0,)))
        part = pl.ds(p * block, block)
        write(p, down_out.at[part], down_hbm.at[0, part])

    match_out[...] = match_ref[...]
    upstream = part_ref[...] + upstream_part(rows_ref, weight_ref, split, weight_ref.shape[1])
    scaled = (gate_ref[:, :1] * upstream).astype(jnp.bfloat16)
    hidden_out[...] = dot(slot_order(count), scaled, ((0,), (0,))).astype(jnp.bfloat16)
    write(pieces, hidden_out, hidden_hbm.at[0, 0])
    for copy in copies:
        copy.wait()


def gate_kernel(count, ids_ref, match_ref, *refs):
    backs, out_ref = refs[:-1], refs[-1]
    me = lax.axis_index("expert")
    ids = ids_ref[...]
    back = backs[0][...]
    for ref in backs[1:]:
        back = back + ref[...]
    total = jnp.zeros(out_ref.shape, jnp.float32)
    for r in range(count):
        value = back[r * CAP : (r + 1) * CAP, :]
        match = match_ref[r * PAD : r * PAD + CAP, :]
        chosen = jnp.sum(jnp.where(match > 0, value, 0.0), axis=0, keepdims=True)
        total = total + jnp.where(ids == target(me, r, count), chosen, 0.0)
    out_ref[...] = total


def on_device(grad_out, expert_ids, gate_values, saved_hidden, down_weight):
    count = lax.axis_size("expert")
    groups = lax.axis_size("dp")
    tensors = lax.axis_size("tensor")
    tokens, width = grad_out.shape
    top = expert_ids.shape[1]
    units = down_weight.shape[1]
    slots = count * CAP
    share = width // groups
    pieces = units // LANES

    ids, match, weight, hidden, *rest = pl.pallas_call(
        functools.partial(front_kernel, count, pieces),
        out_shape=[
            jax.ShapeDtypeStruct((top, tokens), jnp.int32),
            jax.ShapeDtypeStruct((count * PAD, tokens), jnp.float32),
            jax.ShapeDtypeStruct((units, width), jnp.bfloat16),
            jax.ShapeDtypeStruct((slots, units), jnp.bfloat16),
        ]
        + [
            jax.ShapeDtypeStruct((PAD if r == JOINT else CAP, width + LANES), jnp.bfloat16)
            for r in range(count)
        ]
        + [jax.ShapeDtypeStruct((CAP, width), jnp.bfloat16)] * (count - 1),
        in_specs=[HBM] * 5,
        out_specs=[VMEM] * (3 + 2 * count),
        scratch_shapes=[
            pltpu.VMEM((top, tokens), jnp.bfloat16),
            pltpu.VMEM((tokens, width), jnp.bfloat16),
            pltpu.VMEM((slots, units), jnp.bfloat16),
            pltpu.VMEM((count * PAD, width), jnp.float32),
            pltpu.VMEM((count * PAD, width), jnp.float32),
            pltpu.SemaphoreType.DMA((5 + 2 * pieces,)),
        ],
        compiler_params=PARAMS,
        cost_estimate=cost(2 * count * PAD * (tokens + units) * width, 2 * (tokens + units) * width),
        name="front",
    )(*in_hbm(expert_ids.T, gate_values.T, grad_out, saved_hidden, down_weight))
    sends, products = rest[:count], rest[count:]

    received = [sends[0]] + [send(sends[r], "expert", r) for r in range(1, count)]
    theirs = [products[0]] + [send(products[r - 1], "expert", r) for r in range(JOINT + 1, count)]

    rows, gate, *pays = pl.pallas_call(
        functools.partial(slot_kernel, count, groups),
        out_shape=[
            jax.ShapeDtypeStruct((slots, width), jnp.bfloat16),
            jax.ShapeDtypeStruct((slots, LANES), jnp.float32),
        ]
        + [jax.ShapeDtypeStruct((slots, share + units), jnp.bfloat16)] * groups,
        in_specs=[VMEM] * (1 + count),
        out_specs=[VMEM] * (2 + groups),
        scratch_shapes=[
            pltpu.VMEM((slots, width + LANES), jnp.float32),
            pltpu.VMEM((slots, width), jnp.bfloat16),
        ],
        compiler_params=PARAMS,
        cost_estimate=cost(4 * slots * width, 8 * slots * width),
        name="slots",
    )(hidden, *received)

    back = pl.pallas_call(
        functools.partial(back_kernel, count),
        out_shape=jax.ShapeDtypeStruct((slots, LANES), jnp.float32),
        in_specs=[VMEM] * (2 * count),
        out_specs=VMEM,
        compiler_params=PARAMS,
        cost_estimate=cost(*AFTER_WAIT),
        name="backs",
    )(*sends, received[JOINT], *theirs)

    others = [send(pays[r], "dp", r) for r in range(1, groups)]
    backs = [back] + [send(back, "tensor", r) for r in reversed(range(1, tensors))]

    split = width * 5 // 8
    upstream = pl.pallas_call(
        functools.partial(upstream_kernel, split),
        out_shape=jax.ShapeDtypeStruct((slots, units), jnp.float32),
        in_specs=[VMEM] * 2,
        out_specs=VMEM,
        compiler_params=PARAMS,
        cost_estimate=cost(2 * slots * units * split, 2 * units * split),
        name="upstream",
    )(rows, weight)

    hidden_grad, down_grad, match = pl.pallas_call(
        functools.partial(down_kernel, count, groups, pieces, split),
        out_shape=[
            jax.ShapeDtypeStruct(saved_hidden.shape, jnp.bfloat16),
            jax.ShapeDtypeStruct((1, units, share), jnp.float32),
            jax.ShapeDtypeStruct(match.shape, jnp.float32),
        ],
        in_specs=[VMEM] * (5 + groups),
        out_specs=[HBM, HBM, VMEM],
        scratch_shapes=[
            pltpu.VMEM((slots, units), jnp.bfloat16),
            pltpu.VMEM((units, share), jnp.float32),
            pltpu.SemaphoreType.DMA((pieces + 1,)),
        ],
        compiler_params=PARAMS,
        cost_estimate=cost(2 * slots * units * (width + share), 4 * units * share),
        name="down",
    )(upstream, rows, gate, weight, match, pays[0], *others)

    gate_grad = pl.pallas_call(
        functools.partial(gate_kernel, count),
        out_shape=jax.ShapeDtypeStruct(ids.shape, jnp.float32),
        in_specs=[VMEM] * (2 + tensors),
        out_specs=VMEM,
        compiler_params=PARAMS,
        cost_estimate=cost(slots * tokens, 4 * slots * tokens),
        name="gates",
    )(ids, match, *backs)
    return (gate_grad.T, hidden_grad, down_grad)


def solution(mesh):
    return jax.shard_map(
        on_device,
        mesh=mesh,
        in_specs=(
            P(("dp", "expert"), None),
            P(("dp", "expert"), None),
            P(("dp", "expert"), None),
            P("dp", "expert", None, "tensor"),
            P("expert", "tensor", None),
        ),
        out_specs=(
            P(("dp", "expert"), None),
            P("dp", "expert", None, "tensor"),
            P("expert", "tensor", "dp"),
        ),
        check_vma=False,
    )
```

```python
import functools

import jax
import jax.numpy as jnp
from jax import lax
from jax.experimental import pallas as pl
from jax.experimental.pallas import tpu as pltpu
from jax.sharding import PartitionSpec as P

CAP = 4
LANES = 128
JOINT = 1
AFTER_WAIT = (10**9, 10**7)
PAD = 8
VMEM = pl.BlockSpec(memory_space=pltpu.VMEM)
HBM = pl.BlockSpec(memory_space=pltpu.HBM)
PARAMS = pltpu.CompilerParams(vmem_limit_bytes=32 * 2**20)


def dot(a, b, dims):
    return lax.dot_general(a, b, (dims, ((), ())), preferred_element_type=jnp.float32)


def in_hbm(*arrays):
    return [pltpu.with_memory_space_constraint(x, pltpu.HBM) for x in arrays]


def cost(flops, nbytes):
    return pl.CostEstimate(flops=flops, bytes_accessed=nbytes, transcendentals=0)


def paired(size):
    return size & (size - 1) == 0


def target(me, step, size):
    if paired(size):
        return me ^ ((size - step) % size)
    after = me + step
    return after % size if isinstance(me, int) else jnp.where(after >= size, after - size, after)


def source(me, step, size):
    if paired(size):
        return target(me, step, size)
    before = me - step
    return before % size if isinstance(me, int) else jnp.where(before < 0, before + size, before)


def reply(step, size):
    return step if paired(size) else -step % size


def apart(size):
    return [r for r in range(size) if r != JOINT]


def send(value, axis, step, give=target):
    size = lax.axis_size(axis)
    return lax.ppermute(value, axis, [(i, give(i, step, size)) for i in range(size)])


def front_kernel(count, pieces, *refs):
    ids_hbm, gates_hbm, grad_hbm, hidden_hbm, weight_hbm = refs[:5]
    ids_ref, match_ref, weight_ref, hidden_ref = refs[5:9]
    sends = refs[9 : 9 + count]
    products = refs[9 + count : 8 + 2 * count]
    gates_ref, grad_ref, saved_ref, picked_ref, total_ref, sems = refs[8 + 2 * count :]
    units, width = weight_ref.shape
    top, tokens = ids_ref.shape
    pairs = [(ids_hbm, ids_ref), (gates_hbm, gates_ref), (hidden_hbm.at[0, 0], saved_ref)]
    half = tokens // 2
    for p in range(2):
        part = pl.ds(p * half, half)
        pairs.append((grad_hbm.at[part], grad_ref.at[part]))
    half = units // (2 * pieces)
    for p in range(2 * pieces):
        part = pl.ds(p * half, half)
        pairs.append((weight_hbm.at[0, part], weight_ref.at[part]))
    copies = [pltpu.make_async_copy(*pair, sems.at[n]) for n, pair in enumerate(pairs)]
    for copy in copies:
        copy.start()
    me = lax.axis_index("expert")
    rows = count * PAD
    row = lax.broadcasted_iota(jnp.int32, (rows, tokens), 0)
    expert = target(me, row // PAD, count)
    place = row % PAD
    earlier = lax.broadcasted_iota(jnp.int32, (tokens, tokens), 0)
    later = lax.broadcasted_iota(jnp.int32, (tokens, tokens), 1)
    order = (earlier < later).astype(jnp.bfloat16)
    for copy in copies[:3]:
        copy.wait()
    ids = ids_ref[...]
    gates = gates_ref[...].astype(jnp.float32)
    member = jnp.zeros((rows, tokens), jnp.float32)
    gate = jnp.zeros((rows, tokens), jnp.float32)
    for k in range(top):
        hit = ids[k : k + 1, :] == expert
        member = jnp.where(hit, 1.0, member)
        gate = jnp.where(hit, gates[k : k + 1, :], gate)
    before = dot(member.astype(jnp.bfloat16), order, ((1,), (0,)))
    taken = (member > 0) & (before == place.astype(jnp.float32)) & (place < CAP)
    match = taken.astype(jnp.float32)
    match_ref[...] = match
    slot_gate = jnp.sum(match * gate, axis=1, keepdims=True)
    match = match.astype(jnp.bfloat16)

    slots = count * CAP
    saved = saved_ref[...]
    hidden_ref[...] = dot(slot_order(count), saved, ((1,), (0,))).astype(jnp.bfloat16)
    here = lax.broadcasted_iota(jnp.int32, (rows, slots), 0)
    there = lax.broadcasted_iota(jnp.int32, (rows, slots), 1)
    place = here % PAD - jnp.where(here // PAD == JOINT, CAP, 0)
    chosen = (place >= 0) & (place < CAP) & (there == target(me, here // PAD, count) * CAP + place)
    hidden = dot(chosen.astype(jnp.bfloat16), saved, ((1,), (0,))).astype(jnp.bfloat16)

    for copy in copies[3:5]:
        copy.wait()
    picked_ref[...] = dot(match, grad_ref[...], ((1,), (0,)))
    for r in range(count):
        part = slice(r * PAD, r * PAD + sends[r].shape[0])
        gate = jnp.broadcast_to(slot_gate[part], (sends[r].shape[0], LANES))
        sends[r][:, width:] = gate.astype(jnp.bfloat16)
        if r != JOINT:
            sends[r][:, :width] = picked_ref[part, :].astype(jnp.bfloat16)
    block = units // pieces
    for p in range(pieces):
        for copy in copies[5 + 2 * p : 7 + 2 * p]:
            copy.wait()
        part = slice(p * block, (p + 1) * block)
        term = dot(hidden[:, part], weight_ref[part, :], ((1,), (0,)))
        total_ref[...] = term if p == 0 else total_ref[...] + term
    for product, r in zip(products, apart(count)):
        product[...] = total_ref[r * PAD : r * PAD + CAP, :].astype(jnp.bfloat16)
    part = slice(JOINT * PAD, (JOINT + 1) * PAD)
    sends[JOINT][:, :width] = (picked_ref[part, :] + total_ref[part, :]).astype(jnp.bfloat16)


def slot_order(count):
    me = lax.axis_index("expert")
    slots = count * CAP
    here = lax.broadcasted_iota(jnp.int32, (slots, slots), 0)
    saved = lax.broadcasted_iota(jnp.int32, (slots, slots), 1)
    return (saved == source(me, here // CAP, count) * CAP + here % CAP).astype(jnp.bfloat16)


def slot_kernel(count, groups, hidden_ref, *refs):
    received = refs[:count]
    rows_ref, gate_ref = refs[count : count + 2]
    pays = refs[count + 2 : count + 2 + groups]
    wide_ref, weighted_ref = refs[count + 2 + groups :]
    width = rows_ref.shape[1]
    for r in range(count):
        wide_ref[r * CAP : (r + 1) * CAP, :] = received[r][...].astype(jnp.float32)[:CAP]
    rows = wide_ref[:, :width]
    gate = wide_ref[:, width:]
    gate_ref[...] = gate
    rows_ref[...] = rows.astype(jnp.bfloat16)
    weighted_ref[...] = (gate[:, :1] * rows).astype(jnp.bfloat16)
    share = width // groups
    me = lax.axis_index("dp")
    for r in range(groups):
        group = target(me, r, groups)
        pays[r][:, :share] = weighted_ref[:, pl.ds(pl.multiple_of(group * share, share), share)]
        pays[r][:, share:] = hidden_ref[...]


def back_kernel(count, *refs):
    sent = refs[:count]
    joint_ref = refs[count]
    products = dict(zip(apart(count), refs[count + 1 : 2 * count]))
    back_ref = refs[2 * count]
    width = products[0].shape[1]
    for r in range(count):
        step = reply(r, count)
        if step != JOINT:
            theirs = products[step][...].astype(jnp.float32)
        else:
            theirs = joint_ref[:, :width].astype(jnp.float32)[CAP:]
        mine = sent[r][:, :width].astype(jnp.float32)[:CAP]
        back = jnp.sum(mine * theirs, axis=1, keepdims=True)
        back_ref[r * CAP : (r + 1) * CAP, :] = jnp.broadcast_to(back, (CAP, LANES))


def upstream_kernel(count, rows_ref, gate_ref, weight_ref, out_ref):
    upstream = dot(rows_ref[...], weight_ref[...], ((1,), (1,)))
    scaled = (gate_ref[:, :1] * upstream).astype(jnp.bfloat16)
    out_ref[...] = dot(slot_order(count), scaled, ((0,), (0,))).astype(jnp.bfloat16)


def last_kernel(count, groups, parts, pieces, ids_ref, match_ref, hidden_ref, *refs):
    pays, refs = refs[:groups], refs[groups:]
    backs, refs = refs[:parts], refs[parts:]
    gate_hbm, hidden_hbm, down_hbm, gate_out, down_out, sems = refs
    units, share = down_out.shape
    block = units // pieces
    slots = jnp.concatenate([pay_ref[...] for pay_ref in pays], axis=0)
    copies = []

    def write(values, destination):
        copies.append(pltpu.make_async_copy(values, destination, sems.at[len(copies)]))
        copies[-1].start()

    for p in range(pieces):
        part = slice(p * block, (p + 1) * block)
        hidden = slots[:, share + p * block : share + (p + 1) * block]
        down_out[part, :] = dot(hidden, slots[:, :share], ((0,), (0,)))
        part = pl.ds(p * block, block)
        write(down_out.at[part], down_hbm.at[0, part])
    write(hidden_ref, hidden_hbm.at[0, 0])

    me = lax.axis_index("expert")
    ids = ids_ref[...]
    back = backs[0][...]
    for ref in backs[1:]:
        back = back + ref[...]
    total = jnp.zeros(gate_out.shape, jnp.float32)
    for r in range(count):
        value = back[r * CAP : (r + 1) * CAP, :]
        match = match_ref[r * PAD : r * PAD + CAP, :]
        chosen = jnp.sum(jnp.where(match > 0, value, 0.0), axis=0, keepdims=True)
        total = total + jnp.where(ids == target(me, r, count), chosen, 0.0)
    gate_out[...] = total
    write(gate_out, gate_hbm)
    for copy in copies:
        copy.wait()


def on_device(grad_out, expert_ids, gate_values, saved_hidden, down_weight):
    count = lax.axis_size("expert")
    groups = lax.axis_size("dp")
    tensors = lax.axis_size("tensor")
    tokens, width = grad_out.shape
    top = expert_ids.shape[1]
    units = down_weight.shape[1]
    slots = count * CAP
    share = width // groups
    pieces = units // LANES

    ids, match, weight, hidden, *rest = pl.pallas_call(
        functools.partial(front_kernel, count, pieces),
        out_shape=[
            jax.ShapeDtypeStruct((top, tokens), jnp.int32),
            jax.ShapeDtypeStruct((count * PAD, tokens), jnp.float32),
            jax.ShapeDtypeStruct((units, width), jnp.bfloat16),
            jax.ShapeDtypeStruct((slots, units), jnp.bfloat16),
        ]
        + [
            jax.ShapeDtypeStruct((PAD if r == JOINT else CAP, width + LANES), jnp.bfloat16)
            for r in range(count)
        ]
        + [jax.ShapeDtypeStruct((CAP, width), jnp.bfloat16)] * (count - 1),
        in_specs=[HBM] * 5,
        out_specs=[VMEM] * (3 + 2 * count),
        scratch_shapes=[
            pltpu.VMEM((top, tokens), jnp.bfloat16),
            pltpu.VMEM((tokens, width), jnp.bfloat16),
            pltpu.VMEM((slots, units), jnp.bfloat16),
            pltpu.VMEM((count * PAD, width), jnp.float32),
            pltpu.VMEM((count * PAD, width), jnp.float32),
            pltpu.SemaphoreType.DMA((5 + 2 * pieces,)),
        ],
        compiler_params=PARAMS,
        cost_estimate=cost(2 * count * PAD * (tokens + units) * width, 2 * (tokens + units) * width),
        name="front",
    )(*in_hbm(expert_ids.T, gate_values.T, grad_out, saved_hidden, down_weight))
    sends, products = rest[:count], rest[count:]

    received = [sends[0]] + [send(sends[r], "expert", r) for r in range(1, count)]
    theirs = [products[0]] + [send(products[r - 1], "expert", r) for r in range(JOINT + 1, count)]

    rows, gate, *pays = pl.pallas_call(
        functools.partial(slot_kernel, count, groups),
        out_shape=[
            jax.ShapeDtypeStruct((slots, width), jnp.bfloat16),
            jax.ShapeDtypeStruct((slots, LANES), jnp.float32),
        ]
        + [jax.ShapeDtypeStruct((slots, share + units), jnp.bfloat16)] * groups,
        in_specs=[VMEM] * (1 + count),
        out_specs=[VMEM] * (2 + groups),
        scratch_shapes=[
            pltpu.VMEM((slots, width + LANES), jnp.float32),
            pltpu.VMEM((slots, width), jnp.bfloat16),
        ],
        compiler_params=PARAMS,
        cost_estimate=cost(4 * slots * width, 8 * slots * width),
        name="slots",
    )(hidden, *received)

    back = pl.pallas_call(
        functools.partial(back_kernel, count),
        out_shape=jax.ShapeDtypeStruct((slots, LANES), jnp.float32),
        in_specs=[VMEM] * (2 * count),
        out_specs=VMEM,
        compiler_params=PARAMS,
        cost_estimate=cost(*AFTER_WAIT),
        name="backs",
    )(*sends, received[JOINT], *theirs)

    others = [send(pays[r], "dp", r) for r in range(1, groups)]
    backs = [back] + [send(back, "tensor", r) for r in reversed(range(1, tensors))]

    hidden_grad = pl.pallas_call(
        functools.partial(upstream_kernel, count),
        out_shape=jax.ShapeDtypeStruct((slots, units), jnp.bfloat16),
        in_specs=[VMEM] * 3,
        out_specs=VMEM,
        compiler_params=PARAMS,
        cost_estimate=cost(2 * slots * units * width, 2 * units * width),
        name="upstream",
    )(rows, gate, weight)

    gate_grad, hidden_grad, down_grad = pl.pallas_call(
        functools.partial(last_kernel, count, groups, tensors, pieces),
        out_shape=[
            jax.ShapeDtypeStruct(ids.shape, jnp.float32),
            jax.ShapeDtypeStruct(saved_hidden.shape, jnp.bfloat16),
            jax.ShapeDtypeStruct((1, units, share), jnp.float32),
        ],
        in_specs=[VMEM] * (3 + groups + tensors),
        out_specs=[HBM] * 3,
        scratch_shapes=[
            pltpu.VMEM(ids.shape, jnp.float32),
            pltpu.VMEM((units, share), jnp.float32),
            pltpu.SemaphoreType.DMA((pieces + 2,)),
        ],
        compiler_params=PARAMS,
        cost_estimate=cost(2 * slots * units * share, 4 * units * share),
        name="last",
    )(ids, match, hidden_grad, pays[0], *others, *backs)
    return (gate_grad.T, hidden_grad, down_grad)


def solution(mesh):
    return jax.shard_map(
        on_device,
        mesh=mesh,
        in_specs=(
            P(("dp", "expert"), None),
            P(("dp", "expert"), None),
            P(("dp", "expert"), None),
            P("dp", "expert", None, "tensor"),
            P("expert", "tensor", None),
        ),
        out_specs=(
            P(("dp", "expert"), None),
            P("dp", "expert", None, "tensor"),
            P("expert", "tensor", "dp"),
        ),
        check_vma=False,
    )
```

```python
import functools

import jax
import jax.numpy as jnp
from jax import lax
from jax.experimental import pallas as pl
from jax.experimental.pallas import tpu as pltpu
from jax.sharding import PartitionSpec as P

CAP = 4
LANES = 128
JOINT = 1
AFTER_WAIT = (10**9, 10**7)
WIDE = 1024
PAD = 8
VMEM = pl.BlockSpec(memory_space=pltpu.VMEM)
HBM = pl.BlockSpec(memory_space=pltpu.HBM)
PARAMS = pltpu.CompilerParams(vmem_limit_bytes=32 * 2**20)


def dot(a, b, dims):
    return lax.dot_general(a, b, (dims, ((), ())), preferred_element_type=jnp.float32)


def in_hbm(*arrays):
    return [pltpu.with_memory_space_constraint(x, pltpu.HBM) for x in arrays]


def cost(flops, nbytes):
    return pl.CostEstimate(flops=flops, bytes_accessed=nbytes, transcendentals=0)


def paired(size):
    return size & (size - 1) == 0


def target(me, step, size):
    if paired(size):
        return me ^ ((size - step) % size)
    after = me + step
    return after % size if isinstance(me, int) else jnp.where(after >= size, after - size, after)


def source(me, step, size):
    if paired(size):
        return target(me, step, size)
    before = me - step
    return before % size if isinstance(me, int) else jnp.where(before < 0, before + size, before)


def reply(step, size):
    return step if paired(size) else -step % size


def apart(size):
    return [r for r in range(size) if r != JOINT]


def send(value, axis, step, give=target):
    size = lax.axis_size(axis)
    return lax.ppermute(value, axis, [(i, give(i, step, size)) for i in range(size)])


def front_kernel(count, pieces, *refs):
    ids_hbm, gates_hbm, grad_hbm, hidden_hbm, weight_hbm = refs[:5]
    ids_ref, match_ref, weight_ref, hidden_ref = refs[5:9]
    sends = refs[9 : 9 + count]
    products = refs[9 + count : 8 + 2 * count]
    gates_ref, grad_ref, saved_ref, total_ref, sems = refs[8 + 2 * count :]
    units, width = weight_ref.shape
    top, tokens = ids_ref.shape
    pairs = [(ids_hbm, ids_ref), (gates_hbm, gates_ref), (hidden_hbm.at[0, 0], saved_ref)]
    half = tokens // 2
    for p in range(2):
        part = pl.ds(p * half, half)
        pairs.append((grad_hbm.at[part], grad_ref.at[part]))
    half = units // (2 * pieces)
    for p in range(2 * pieces):
        part = pl.ds(p * half, half)
        pairs.append((weight_hbm.at[0, part], weight_ref.at[part]))
    copies = [pltpu.make_async_copy(*pair, sems.at[n]) for n, pair in enumerate(pairs)]
    for copy in copies:
        copy.start()
    me = lax.axis_index("expert")
    rows = count * PAD
    row = lax.broadcasted_iota(jnp.int32, (rows, tokens), 0)
    expert = target(me, row // PAD, count)
    place = row % PAD
    earlier = lax.broadcasted_iota(jnp.int32, (tokens, tokens), 0)
    later = lax.broadcasted_iota(jnp.int32, (tokens, tokens), 1)
    order = (earlier < later).astype(jnp.bfloat16)
    for copy in copies[:3]:
        copy.wait()
    ids = ids_ref[...]
    gates = gates_ref[...].astype(jnp.float32)
    member = jnp.zeros((rows, tokens), jnp.float32)
    gate = jnp.zeros((rows, tokens), jnp.float32)
    for k in range(top):
        hit = ids[k : k + 1, :] == expert
        member = jnp.where(hit, 1.0, member)
        gate = jnp.where(hit, gates[k : k + 1, :], gate)
    before = dot(member.astype(jnp.bfloat16), order, ((1,), (0,)))
    taken = (member > 0) & (before == place.astype(jnp.float32)) & (place < CAP)
    match = taken.astype(jnp.float32)
    match_ref[...] = match
    slot_gate = jnp.sum(match * gate, axis=1, keepdims=True)
    match = match.astype(jnp.bfloat16)

    slots = count * CAP
    saved = saved_ref[...]
    hidden_ref[...] = dot(slot_order(count), saved, ((1,), (0,))).astype(jnp.bfloat16)
    here = lax.broadcasted_iota(jnp.int32, (rows, slots), 0)
    there = lax.broadcasted_iota(jnp.int32, (rows, slots), 1)
    chosen = (here % PAD < CAP) & (there == target(me, here // PAD, count) * CAP + here % PAD)
    hidden = dot(chosen.astype(jnp.bfloat16), saved, ((1,), (0,))).astype(jnp.bfloat16)

    for copy in copies[3:5]:
        copy.wait()
    for r in range(count):
        part = slice(r * PAD, r * PAD + CAP)
        gate = jnp.broadcast_to(slot_gate[part], (CAP, LANES)).astype(jnp.bfloat16)
        sends[r][:, width : width + LANES] = gate
    wide = min(width, WIDE)
    for begin in range(0, width, wide):
        part = slice(begin, begin + wide)
        picked = dot(match, grad_ref[:, part], ((1,), (0,)))
        for r in range(count):
            sends[r][:, part] = picked[r * PAD : r * PAD + CAP].astype(jnp.bfloat16)
    block = units // pieces
    for p in range(pieces):
        for copy in copies[5 + 2 * p : 7 + 2 * p]:
            copy.wait()
        rows = slice(p * block, (p + 1) * block)
        for begin in range(0, width, wide):
            part = slice(begin, begin + wide)
            term = dot(hidden[:, rows], weight_ref[rows, part], ((1,), (0,)))
            if p > 0:
                term = total_ref[:, part] + term
            if p < pieces - 1:
                total_ref[:, part] = term
                continue
            for product_ref, r in zip(products, apart(count)):
                product_ref[:, part] = term[r * PAD : r * PAD + CAP].astype(jnp.bfloat16)
            begin += width + LANES
            joint = term[JOINT * PAD : JOINT * PAD + CAP].astype(jnp.bfloat16)
            sends[JOINT][:, begin : begin + wide] = joint


def slot_order(count):
    me = lax.axis_index("expert")
    slots = count * CAP
    here = lax.broadcasted_iota(jnp.int32, (slots, slots), 0)
    saved = lax.broadcasted_iota(jnp.int32, (slots, slots), 1)
    return (saved == source(me, here // CAP, count) * CAP + here % CAP).astype(jnp.bfloat16)


def slot_kernel(count, groups, hidden_ref, *refs):
    received = refs[:count]
    rows_ref, gate_ref = refs[count : count + 2]
    pays = refs[count + 2 : count + 2 + groups]
    wide_ref, weighted_ref = refs[count + 2 + groups :]
    width = rows_ref.shape[1]
    for r in range(count):
        row = received[r][:, : width + LANES]
        wide_ref[r * CAP : (r + 1) * CAP, :] = row.astype(jnp.float32)
    rows = wide_ref[:, :width]
    gate = wide_ref[:, width:]
    gate_ref[...] = gate
    rows_ref[...] = rows.astype(jnp.bfloat16)
    weighted_ref[...] = (gate[:, :1] * rows).astype(jnp.bfloat16)
    share = width // groups
    me = lax.axis_index("dp")
    for r in range(groups):
        group = target(me, r, groups)
        pays[r][:, :share] = weighted_ref[:, pl.ds(pl.multiple_of(group * share, share), share)]
        pays[r][:, share:] = hidden_ref[...]


def back_kernel(count, *refs):
    sent = refs[:count]
    joint_ref = refs[count]
    products = dict(zip(apart(count), refs[count + 1 : 2 * count]))
    back_ref = refs[2 * count]
    width = products[0].shape[1]
    for r in range(count):
        step = reply(r, count)
        if step != JOINT:
            theirs = products[step][...].astype(jnp.float32)
        else:
            theirs = joint_ref[:, joint_ref.shape[1] - width :].astype(jnp.float32)
        mine = sent[r][:, :width].astype(jnp.float32)
        back = jnp.sum(mine * theirs, axis=1, keepdims=True)
        back_ref[r * CAP : (r + 1) * CAP, :] = jnp.broadcast_to(back, (CAP, LANES))


def upstream_kernel(count, rows_ref, gate_ref, weight_ref, out_ref):
    upstream = dot(rows_ref[...], weight_ref[...], ((1,), (1,)))
    scaled = (gate_ref[:, :1] * upstream).astype(jnp.bfloat16)
    out_ref[...] = dot(slot_order(count), scaled, ((0,), (0,))).astype(jnp.bfloat16)


def down_kernel(groups, pieces, hidden_ref, match_ref, *refs):
    pays = refs[:groups]
    hidden_hbm, down_hbm, match_out, down_out, sems = refs[groups:]
    units, share = down_out.shape
    block = units // pieces
    slots = jnp.concatenate([pay_ref[...] for pay_ref in pays], axis=0)
    copies = []

    def write(values, destination):
        copies.append(pltpu.make_async_copy(values, destination, sems.at[len(copies)]))
        copies[-1].start()

    for p in range(pieces):
        part = slice(p * block, (p + 1) * block)
        hidden = slots[:, share + p * block : share + (p + 1) * block]
        down_out[part, :] = dot(hidden, slots[:, :share], ((0,), (0,)))
        part = pl.ds(p * block, block)
        write(down_out.at[part], down_hbm.at[0, part])
    write(hidden_ref, hidden_hbm.at[0, 0])
    match_out[...] = match_ref[...]
    for copy in copies:
        copy.wait()


def gate_kernel(count, ids_ref, match_ref, *refs):
    backs, out_ref = refs[:-1], refs[-1]
    me = lax.axis_index("expert")
    ids = ids_ref[...]
    back = backs[0][...]
    for ref in backs[1:]:
        back = back + ref[...]
    total = jnp.zeros(out_ref.shape, jnp.float32)
    for r in range(count):
        value = back[r * CAP : (r + 1) * CAP, :]
        match = match_ref[r * PAD : r * PAD + CAP, :]
        chosen = jnp.sum(jnp.where(match > 0, value, 0.0), axis=0, keepdims=True)
        total = total + jnp.where(ids == target(me, r, count), chosen, 0.0)
    out_ref[...] = total


def on_device(grad_out, expert_ids, gate_values, saved_hidden, down_weight):
    count = lax.axis_size("expert")
    groups = lax.axis_size("dp")
    tensors = lax.axis_size("tensor")
    tokens, width = grad_out.shape
    top = expert_ids.shape[1]
    units = down_weight.shape[1]
    slots = count * CAP
    share = width // groups
    pieces = units // LANES

    ids, match, weight, hidden, *rest = pl.pallas_call(
        functools.partial(front_kernel, count, pieces),
        out_shape=[
            jax.ShapeDtypeStruct((top, tokens), jnp.int32),
            jax.ShapeDtypeStruct((count * PAD, tokens), jnp.float32),
            jax.ShapeDtypeStruct((units, width), jnp.bfloat16),
            jax.ShapeDtypeStruct((slots, units), jnp.bfloat16),
        ]
        + [
            jax.ShapeDtypeStruct((CAP, width + LANES + width * (r == JOINT)), jnp.bfloat16)
            for r in range(count)
        ]
        + [jax.ShapeDtypeStruct((CAP, width), jnp.bfloat16)] * (count - 1),
        in_specs=[HBM] * 5,
        out_specs=[VMEM] * (3 + 2 * count),
        scratch_shapes=[
            pltpu.VMEM((top, tokens), jnp.bfloat16),
            pltpu.VMEM((tokens, width), jnp.bfloat16),
            pltpu.VMEM((slots, units), jnp.bfloat16),
            pltpu.VMEM((count * PAD, width), jnp.float32),
            pltpu.SemaphoreType.DMA((5 + 2 * pieces,)),
        ],
        compiler_params=PARAMS,
        cost_estimate=cost(2 * count * PAD * (tokens + units) * width, 2 * (tokens + units) * width),
        name="front",
    )(*in_hbm(expert_ids.T, gate_values.T, grad_out, saved_hidden, down_weight))
    sends, products = rest[:count], rest[count:]

    received = [sends[0]] + [send(sends[r], "expert", r) for r in range(1, count)]
    theirs = [products[0]] + [send(products[r - 1], "expert", r) for r in range(JOINT + 1, count)]

    rows, gate, *pays = pl.pallas_call(
        functools.partial(slot_kernel, count, groups),
        out_shape=[
            jax.ShapeDtypeStruct((slots, width), jnp.bfloat16),
            jax.ShapeDtypeStruct((slots, LANES), jnp.float32),
        ]
        + [jax.ShapeDtypeStruct((slots, share + units), jnp.bfloat16)] * groups,
        in_specs=[VMEM] * (1 + count),
        out_specs=[VMEM] * (2 + groups),
        scratch_shapes=[
            pltpu.VMEM((slots, width + LANES), jnp.float32),
            pltpu.VMEM((slots, width), jnp.bfloat16),
        ],
        compiler_params=PARAMS,
        cost_estimate=cost(4 * slots * width, 8 * slots * width),
        name="slots",
    )(hidden, *received)

    back = pl.pallas_call(
        functools.partial(back_kernel, count),
        out_shape=jax.ShapeDtypeStruct((slots, LANES), jnp.float32),
        in_specs=[VMEM] * (2 * count),
        out_specs=VMEM,
        compiler_params=PARAMS,
        cost_estimate=cost(*AFTER_WAIT),
        name="backs",
    )(*sends, received[JOINT], *theirs)

    others = [send(pays[r], "dp", r) for r in range(1, groups)]
    backs = [back] + [send(back, "tensor", r) for r in reversed(range(1, tensors))]

    hidden_grad = pl.pallas_call(
        functools.partial(upstream_kernel, count),
        out_shape=jax.ShapeDtypeStruct((slots, units), jnp.bfloat16),
        in_specs=[VMEM] * 3,
        out_specs=VMEM,
        compiler_params=PARAMS,
        cost_estimate=cost(2 * slots * units * width, 2 * units * width),
        name="upstream",
    )(rows, gate, weight)

    hidden_grad, down_grad, match = pl.pallas_call(
        functools.partial(down_kernel, groups, pieces),
        out_shape=[
            jax.ShapeDtypeStruct(saved_hidden.shape, jnp.bfloat16),
            jax.ShapeDtypeStruct((1, units, share), jnp.float32),
            jax.ShapeDtypeStruct(match.shape, jnp.float32),
        ],
        in_specs=[VMEM] * (2 + groups),
        out_specs=[HBM, HBM, VMEM],
        scratch_shapes=[
            pltpu.VMEM((units, share), jnp.float32),
            pltpu.SemaphoreType.DMA((pieces + 1,)),
        ],
        compiler_params=PARAMS,
        cost_estimate=cost(2 * slots * units * share, 4 * units * share),
        name="down",
    )(hidden_grad, match, pays[0], *others)

    gate_grad = pl.pallas_call(
        functools.partial(gate_kernel, count),
        out_shape=jax.ShapeDtypeStruct(ids.shape, jnp.float32),
        in_specs=[VMEM] * (2 + tensors),
        out_specs=VMEM,
        compiler_params=PARAMS,
        cost_estimate=cost(slots * tokens, 4 * slots * tokens),
        name="gates",
    )(ids, match, *backs)
    return (gate_grad.T, hidden_grad, down_grad)


def solution(mesh):
    return jax.shard_map(
        on_device,
        mesh=mesh,
        in_specs=(
            P(("dp", "expert"), None),
            P(("dp", "expert"), None),
            P(("dp", "expert"), None),
            P("dp", "expert", None, "tensor"),
            P("expert", "tensor", None),
        ),
        out_specs=(
            P(("dp", "expert"), None),
            P("dp", "expert", None, "tensor"),
            P("expert", "tensor", "dp"),
        ),
        check_vma=False,
    )
```

```python
import functools

import jax
import jax.numpy as jnp
from jax import lax
from jax.experimental import pallas as pl
from jax.experimental.pallas import tpu as pltpu
from jax.sharding import PartitionSpec as P

CAP = 4
LANES = 128
JOINT = 1
AFTER_WAIT = (10**9, 10**7)
DEEP = 256
WIDE = 1024
PAD = 8
VMEM = pl.BlockSpec(memory_space=pltpu.VMEM)
HBM = pl.BlockSpec(memory_space=pltpu.HBM)
PARAMS = pltpu.CompilerParams(vmem_limit_bytes=32 * 2**20)


def dot(a, b, dims):
    return lax.dot_general(a, b, (dims, ((), ())), preferred_element_type=jnp.float32)


def in_hbm(*arrays):
    return [pltpu.with_memory_space_constraint(x, pltpu.HBM) for x in arrays]


def cost(flops, nbytes):
    return pl.CostEstimate(flops=flops, bytes_accessed=nbytes, transcendentals=0)


def paired(size):
    return size & (size - 1) == 0


def target(me, step, size):
    if paired(size):
        return me ^ ((size - step) % size)
    after = me + step
    return after % size if isinstance(me, int) else jnp.where(after >= size, after - size, after)


def source(me, step, size):
    if paired(size):
        return target(me, step, size)
    before = me - step
    return before % size if isinstance(me, int) else jnp.where(before < 0, before + size, before)


def reply(step, size):
    return step if paired(size) else -step % size


def apart(size):
    return [r for r in range(size) if r != JOINT]


def send(value, axis, step, give=target):
    size = lax.axis_size(axis)
    return lax.ppermute(value, axis, [(i, give(i, step, size)) for i in range(size)])


def front_kernel(count, *refs):
    ids_hbm, gates_hbm, grad_hbm, hidden_hbm, weight_hbm = refs[:5]
    ids_ref, match_ref, stack_ref, hidden_ref = refs[5:9]
    sends = refs[9 : 9 + count]
    products = refs[9 + count : 8 + 2 * count]
    gates_ref, saved_ref, total_ref, sems = refs[8 + 2 * count :]
    depth, width = stack_ref.shape
    top, tokens = ids_ref.shape
    pairs = [(ids_hbm, ids_ref), (gates_hbm, gates_ref), (hidden_hbm.at[0, 0], saved_ref)]
    pairs.append((grad_hbm, stack_ref.at[pl.ds(0, tokens)]))
    for begin in range(0, depth - tokens, LANES):
        part = stack_ref.at[pl.ds(tokens + begin, LANES)]
        pairs.append((weight_hbm.at[0, pl.ds(begin, LANES)], part))
    copies = [pltpu.make_async_copy(*pair, sems.at[n]) for n, pair in enumerate(pairs)]
    for copy in copies:
        copy.start()
    me = lax.axis_index("expert")
    rows = count * PAD
    row = lax.broadcasted_iota(jnp.int32, (rows, tokens), 0)
    expert = target(me, row // PAD, count)
    place = row % PAD
    earlier = lax.broadcasted_iota(jnp.int32, (tokens, tokens), 0)
    later = lax.broadcasted_iota(jnp.int32, (tokens, tokens), 1)
    order = (earlier < later).astype(jnp.bfloat16)
    for copy in copies[:3]:
        copy.wait()
    ids = ids_ref[...]
    gates = gates_ref[...].astype(jnp.float32)
    member = jnp.zeros((rows, tokens), jnp.float32)
    gate = jnp.zeros((rows, tokens), jnp.float32)
    for k in range(top):
        hit = ids[k : k + 1, :] == expert
        member = jnp.where(hit, 1.0, member)
        gate = jnp.where(hit, gates[k : k + 1, :], gate)
    before = dot(member.astype(jnp.bfloat16), order, ((1,), (0,)))
    taken = (member > 0) & (before == place.astype(jnp.float32)) & (place < CAP)
    match = taken.astype(jnp.float32)
    match_ref[...] = match
    slot_gate = jnp.sum(match * gate, axis=1, keepdims=True)
    match = match.astype(jnp.bfloat16)

    slots = count * CAP
    saved = saved_ref[...]
    hidden_ref[...] = dot(slot_order(count), saved, ((1,), (0,))).astype(jnp.bfloat16)
    here = lax.broadcasted_iota(jnp.int32, (rows, slots), 0)
    there = lax.broadcasted_iota(jnp.int32, (rows, slots), 1)
    chosen = (here % PAD < CAP) & (there == target(me, here // PAD, count) * CAP + here % PAD)
    hidden = dot(chosen.astype(jnp.bfloat16), saved, ((1,), (0,))).astype(jnp.bfloat16)

    for r in range(count):
        part = slice(r * PAD, r * PAD + CAP)
        gate = jnp.broadcast_to(slot_gate[part], (CAP, LANES)).astype(jnp.bfloat16)
        sends[r][:, width : width + LANES] = gate
    above = jnp.concatenate([match, jnp.zeros(hidden.shape, jnp.bfloat16)], axis=1)
    below = jnp.concatenate([jnp.zeros(match.shape, jnp.bfloat16), hidden], axis=1)
    left = jnp.concatenate([above, below], axis=0)
    wide = min(width, WIDE)
    arrived = copies[3:]
    for start in range(0, depth, DEEP):
        lines = slice(start, start + DEEP)
        while arrived and (len(copies) - len(arrived) - 3) * LANES < start + DEEP:
            arrived[0].wait()
            arrived = arrived[1:]
        for begin in range(0, width, wide):
            part = slice(begin, begin + wide)
            if start == 0:
                term = dot(left[:, lines], stack_ref[lines, part], ((1,), (0,)))
                for r in range(count):
                    sends[r][:, part] = term[r * PAD : r * PAD + CAP].astype(jnp.bfloat16)
                total_ref[:, part] = term[rows:]
                continue
            term = dot(below[:, lines], stack_ref[lines, part], ((1,), (0,)))
            term = total_ref[:, part] + term
            if start + DEEP < depth:
                total_ref[:, part] = term
                continue
            for product_ref, r in zip(products, apart(count)):
                product_ref[:, part] = term[r * PAD : r * PAD + CAP].astype(jnp.bfloat16)
            begin += width + LANES
            joint = term[JOINT * PAD : JOINT * PAD + CAP].astype(jnp.bfloat16)
            sends[JOINT][:, begin : begin + wide] = joint


def slot_order(count):
    me = lax.axis_index("expert")
    slots = count * CAP
    here = lax.broadcasted_iota(jnp.int32, (slots, slots), 0)
    saved = lax.broadcasted_iota(jnp.int32, (slots, slots), 1)
    return (saved == source(me, here // CAP, count) * CAP + here % CAP).astype(jnp.bfloat16)


def slot_kernel(count, groups, hidden_ref, *refs):
    received = refs[:count]
    rows_ref, gate_ref = refs[count : count + 2]
    pays = refs[count + 2 : count + 2 + groups]
    wide_ref, weighted_ref = refs[count + 2 + groups :]
    width = rows_ref.shape[1]
    for r in range(count):
        row = received[r][:, : width + LANES]
        wide_ref[r * CAP : (r + 1) * CAP, :] = row.astype(jnp.float32)
    rows = wide_ref[:, :width]
    gate = wide_ref[:, width:]
    gate_ref[...] = gate
    rows_ref[...] = rows.astype(jnp.bfloat16)
    weighted_ref[...] = (gate[:, :1] * rows).astype(jnp.bfloat16)
    share = width // groups
    me = lax.axis_index("dp")
    for r in range(groups):
        group = target(me, r, groups)
        pays[r][:, :share] = weighted_ref[:, pl.ds(pl.multiple_of(group * share, share), share)]
        pays[r][:, share:] = hidden_ref[...]


def back_kernel(count, *refs):
    sent = refs[:count]
    joint_ref = refs[count]
    products = dict(zip(apart(count), refs[count + 1 : 2 * count]))
    back_ref = refs[2 * count]
    width = products[0].shape[1]
    for r in range(count):
        step = reply(r, count)
        if step != JOINT:
            theirs = products[step][...].astype(jnp.float32)
        else:
            theirs = joint_ref[:, joint_ref.shape[1] - width :].astype(jnp.float32)
        mine = sent[r][:, :width].astype(jnp.float32)
        back = jnp.sum(mine * theirs, axis=1, keepdims=True)
        back_ref[r * CAP : (r + 1) * CAP, :] = jnp.broadcast_to(back, (CAP, LANES))


def upstream_kernel(count, rows_ref, gate_ref, weight_ref, out_ref):
    first = weight_ref.shape[0] - out_ref.shape[1]
    upstream = dot(rows_ref[...], weight_ref[first:, :], ((1,), (1,)))
    scaled = (gate_ref[:, :1] * upstream).astype(jnp.bfloat16)
    out_ref[...] = dot(slot_order(count), scaled, ((0,), (0,))).astype(jnp.bfloat16)


def down_kernel(groups, pieces, hidden_ref, match_ref, *refs):
    pays = refs[:groups]
    hidden_hbm, down_hbm, match_out, down_out, sems = refs[groups:]
    units, share = down_out.shape
    block = units // pieces
    slots = jnp.concatenate([pay_ref[...] for pay_ref in pays], axis=0)
    copies = []

    def write(values, destination):
        copies.append(pltpu.make_async_copy(values, destination, sems.at[len(copies)]))
        copies[-1].start()

    for p in range(pieces):
        part = slice(p * block, (p + 1) * block)
        hidden = slots[:, share + p * block : share + (p + 1) * block]
        down_out[part, :] = dot(hidden, slots[:, :share], ((0,), (0,)))
        part = pl.ds(p * block, block)
        write(down_out.at[part], down_hbm.at[0, part])
    write(hidden_ref, hidden_hbm.at[0, 0])
    match_out[...] = match_ref[...]
    for copy in copies:
        copy.wait()


def gate_kernel(count, ids_ref, match_ref, *refs):
    backs, out_ref = refs[:-1], refs[-1]
    me = lax.axis_index("expert")
    ids = ids_ref[...]
    back = backs[0][...]
    for ref in backs[1:]:
        back = back + ref[...]
    total = jnp.zeros(out_ref.shape, jnp.float32)
    for r in range(count):
        value = back[r * CAP : (r + 1) * CAP, :]
        match = match_ref[r * PAD : r * PAD + CAP, :]
        chosen = jnp.sum(jnp.where(match > 0, value, 0.0), axis=0, keepdims=True)
        total = total + jnp.where(ids == target(me, r, count), chosen, 0.0)
    out_ref[...] = total


def on_device(grad_out, expert_ids, gate_values, saved_hidden, down_weight):
    count = lax.axis_size("expert")
    groups = lax.axis_size("dp")
    tensors = lax.axis_size("tensor")
    tokens, width = grad_out.shape
    top = expert_ids.shape[1]
    units = down_weight.shape[1]
    slots = count * CAP
    share = width // groups
    pieces = units // LANES

    ids, match, weight, hidden, *rest = pl.pallas_call(
        functools.partial(front_kernel, count),
        out_shape=[
            jax.ShapeDtypeStruct((top, tokens), jnp.int32),
            jax.ShapeDtypeStruct((count * PAD, tokens), jnp.float32),
            jax.ShapeDtypeStruct((tokens + units, width), jnp.bfloat16),
            jax.ShapeDtypeStruct((slots, units), jnp.bfloat16),
        ]
        + [
            jax.ShapeDtypeStruct((CAP, width + LANES + width * (r == JOINT)), jnp.bfloat16)
            for r in range(count)
        ]
        + [jax.ShapeDtypeStruct((CAP, width), jnp.bfloat16)] * (count - 1),
        in_specs=[HBM] * 5,
        out_specs=[VMEM] * (3 + 2 * count),
        scratch_shapes=[
            pltpu.VMEM((top, tokens), jnp.bfloat16),
            pltpu.VMEM((slots, units), jnp.bfloat16),
            pltpu.VMEM((count * PAD, width), jnp.float32),
            pltpu.SemaphoreType.DMA((4 + pieces,)),
        ],
        compiler_params=PARAMS,
        cost_estimate=cost(2 * count * PAD * (tokens + units) * width, 2 * (tokens + units) * width),
        name="front",
    )(*in_hbm(expert_ids.T, gate_values.T, grad_out, saved_hidden, down_weight))
    sends, products = rest[:count], rest[count:]

    received = [sends[0]] + [send(sends[r], "expert", r) for r in range(1, count)]
    theirs = [products[0]] + [send(products[r - 1], "expert", r) for r in range(JOINT + 1, count)]

    rows, gate, *pays = pl.pallas_call(
        functools.partial(slot_kernel, count, groups),
        out_shape=[
            jax.ShapeDtypeStruct((slots, width), jnp.bfloat16),
            jax.ShapeDtypeStruct((slots, LANES), jnp.float32),
        ]
        + [jax.ShapeDtypeStruct((slots, share + units), jnp.bfloat16)] * groups,
        in_specs=[VMEM] * (1 + count),
        out_specs=[VMEM] * (2 + groups),
        scratch_shapes=[
            pltpu.VMEM((slots, width + LANES), jnp.float32),
            pltpu.VMEM((slots, width), jnp.bfloat16),
        ],
        compiler_params=PARAMS,
        cost_estimate=cost(4 * slots * width, 8 * slots * width),
        name="slots",
    )(hidden, *received)

    back = pl.pallas_call(
        functools.partial(back_kernel, count),
        out_shape=jax.ShapeDtypeStruct((slots, LANES), jnp.float32),
        in_specs=[VMEM] * (2 * count),
        out_specs=VMEM,
        compiler_params=PARAMS,
        cost_estimate=cost(*AFTER_WAIT),
        name="backs",
    )(*sends, received[JOINT], *theirs)

    others = [send(pays[r], "dp", r) for r in range(1, groups)]
    backs = [back] + [send(back, "tensor", r) for r in reversed(range(1, tensors))]

    hidden_grad = pl.pallas_call(
        functools.partial(upstream_kernel, count),
        out_shape=jax.ShapeDtypeStruct((slots, units), jnp.bfloat16),
        in_specs=[VMEM] * 3,
        out_specs=VMEM,
        compiler_params=PARAMS,
        cost_estimate=cost(2 * slots * units * width, 2 * units * width),
        name="upstream",
    )(rows, gate, weight)

    hidden_grad, down_grad, match = pl.pallas_call(
        functools.partial(down_kernel, groups, pieces),
        out_shape=[
            jax.ShapeDtypeStruct(saved_hidden.shape, jnp.bfloat16),
            jax.ShapeDtypeStruct((1, units, share), jnp.float32),
            jax.ShapeDtypeStruct(match.shape, jnp.float32),
        ],
        in_specs=[VMEM] * (2 + groups),
        out_specs=[HBM, HBM, VMEM],
        scratch_shapes=[
            pltpu.VMEM((units, share), jnp.float32),
            pltpu.SemaphoreType.DMA((pieces + 1,)),
        ],
        compiler_params=PARAMS,
        cost_estimate=cost(2 * slots * units * share, 4 * units * share),
        name="down",
    )(hidden_grad, match, pays[0], *others)

    gate_grad = pl.pallas_call(
        functools.partial(gate_kernel, count),
        out_shape=jax.ShapeDtypeStruct(ids.shape, jnp.float32),
        in_specs=[VMEM] * (2 + tensors),
        out_specs=VMEM,
        compiler_params=PARAMS,
        cost_estimate=cost(slots * tokens, 4 * slots * tokens),
        name="gates",
    )(ids, match, *backs)
    return (gate_grad.T, hidden_grad, down_grad)


def solution(mesh):
    return jax.shard_map(
        on_device,
        mesh=mesh,
        in_specs=(
            P(("dp", "expert"), None),
            P(("dp", "expert"), None),
            P(("dp", "expert"), None),
            P("dp", "expert", None, "tensor"),
            P("expert", "tensor", None),
        ),
        out_specs=(
            P(("dp", "expert"), None),
            P("dp", "expert", None, "tensor"),
            P("expert", "tensor", "dp"),
        ),
        check_vma=False,
    )
```

```python
import functools

import jax
import jax.numpy as jnp
from jax import lax
from jax.experimental import pallas as pl
from jax.experimental.pallas import tpu as pltpu
from jax.sharding import PartitionSpec as P

CAP = 4
LANES = 128
JOINT = 1
AFTER_WAIT = (10**9, 10**7)
WIDE = 1024
PAD = 8
VMEM = pl.BlockSpec(memory_space=pltpu.VMEM)
HBM = pl.BlockSpec(memory_space=pltpu.HBM)
PARAMS = pltpu.CompilerParams(vmem_limit_bytes=32 * 2**20)


def dot(a, b, dims):
    return lax.dot_general(a, b, (dims, ((), ())), preferred_element_type=jnp.float32)


def in_hbm(*arrays):
    return [pltpu.with_memory_space_constraint(x, pltpu.HBM) for x in arrays]


def cost(flops, nbytes):
    return pl.CostEstimate(flops=flops, bytes_accessed=nbytes, transcendentals=0)


def paired(size):
    return size & (size - 1) == 0


def target(me, step, size):
    if paired(size):
        return me ^ ((size - step) % size)
    after = me + step
    return after % size if isinstance(me, int) else jnp.where(after >= size, after - size, after)


def source(me, step, size):
    if paired(size):
        return target(me, step, size)
    before = me - step
    return before % size if isinstance(me, int) else jnp.where(before < 0, before + size, before)


def reply(step, size):
    return step if paired(size) else -step % size


def apart(size):
    return [r for r in range(size) if r != JOINT]


def send(value, axis, step, give=target):
    size = lax.axis_size(axis)
    return lax.ppermute(value, axis, [(i, give(i, step, size)) for i in range(size)])


def front_kernel(count, *refs):
    ids_hbm, gates_hbm, grad_hbm, hidden_hbm, weight_hbm = refs[:5]
    ids_ref, match_ref, weight_ref, hidden_ref = refs[5:9]
    sends = refs[9 : 9 + count]
    products = refs[9 + count : 8 + 2 * count]
    gates_ref, grad_ref, saved_ref, total_ref, sems = refs[8 + 2 * count :]
    units, width = weight_ref.shape
    top, tokens = ids_ref.shape
    pairs = [(ids_hbm, ids_ref), (gates_hbm, gates_ref), (hidden_hbm.at[0, 0], saved_ref)]
    half = tokens // 2
    for p in range(2):
        part = pl.ds(p * half, half)
        pairs.append((grad_hbm.at[part], grad_ref.at[part]))
    cuts = cuts_of(units)
    for start, end in zip(cuts, cuts[1:]):
        part = pl.ds(start, end - start)
        pairs.append((weight_hbm.at[0, part], weight_ref.at[part]))
    copies = [pltpu.make_async_copy(*pair, sems.at[n]) for n, pair in enumerate(pairs)]
    for copy in copies:
        copy.start()
    me = lax.axis_index("expert")
    rows = count * PAD
    row = lax.broadcasted_iota(jnp.int32, (rows, tokens), 0)
    expert = target(me, row // PAD, count)
    place = row % PAD
    earlier = lax.broadcasted_iota(jnp.int32, (tokens, tokens), 0)
    later = lax.broadcasted_iota(jnp.int32, (tokens, tokens), 1)
    order = (earlier < later).astype(jnp.bfloat16)
    for copy in copies[:3]:
        copy.wait()
    ids = ids_ref[...]
    gates = gates_ref[...].astype(jnp.float32)
    member = jnp.zeros((rows, tokens), jnp.float32)
    gate = jnp.zeros((rows, tokens), jnp.float32)
    for k in range(top):
        hit = ids[k : k + 1, :] == expert
        member = jnp.where(hit, 1.0, member)
        gate = jnp.where(hit, gates[k : k + 1, :], gate)
    before = dot(member.astype(jnp.bfloat16), order, ((1,), (0,)))
    taken = (member > 0) & (before == place.astype(jnp.float32)) & (place < CAP)
    match = taken.astype(jnp.float32)
    match_ref[...] = match
    slot_gate = jnp.sum(match * gate, axis=1, keepdims=True)
    match = match.astype(jnp.bfloat16)

    slots = count * CAP
    saved = saved_ref[...]
    hidden_ref[...] = dot(slot_order(count), saved, ((1,), (0,))).astype(jnp.bfloat16)
    here = lax.broadcasted_iota(jnp.int32, (rows, slots), 0)
    there = lax.broadcasted_iota(jnp.int32, (rows, slots), 1)
    chosen = (here % PAD < CAP) & (there == target(me, here // PAD, count) * CAP + here % PAD)
    hidden = dot(chosen.astype(jnp.bfloat16), saved, ((1,), (0,))).astype(jnp.bfloat16)

    for copy in copies[3:5]:
        copy.wait()
    for r in range(count):
        part = slice(r * PAD, r * PAD + CAP)
        gate = jnp.broadcast_to(slot_gate[part], (CAP, LANES)).astype(jnp.bfloat16)
        sends[r][:, width : width + LANES] = gate
    wide = min(width, WIDE)
    for begin in range(0, width, wide):
        part = slice(begin, begin + wide)
        picked = dot(match, grad_ref[:, part], ((1,), (0,)))
        for r in range(count):
            sends[r][:, part] = picked[r * PAD : r * PAD + CAP].astype(jnp.bfloat16)
    for p, (start, end) in enumerate(zip(cuts, cuts[1:])):
        copies[5 + p].wait()
        rows = slice(start, end)
        for begin in range(0, width, wide):
            part = slice(begin, begin + wide)
            term = dot(hidden[:, rows], weight_ref[rows, part], ((1,), (0,)))
            if p > 0:
                term = total_ref[:, part] + term
            if end < units:
                total_ref[:, part] = term
                continue
            for product_ref, r in zip(products, apart(count)):
                product_ref[:, part] = term[r * PAD : r * PAD + CAP].astype(jnp.bfloat16)
            begin += width + LANES
            joint = term[JOINT * PAD : JOINT * PAD + CAP].astype(jnp.bfloat16)
            sends[JOINT][:, begin : begin + wide] = joint


def cuts_of(units):
    return [*range(0, units, LANES), units - LANES // 2, units]


def slot_order(count):
    me = lax.axis_index("expert")
    slots = count * CAP
    here = lax.broadcasted_iota(jnp.int32, (slots, slots), 0)
    saved = lax.broadcasted_iota(jnp.int32, (slots, slots), 1)
    return (saved == source(me, here // CAP, count) * CAP + here % CAP).astype(jnp.bfloat16)


def slot_kernel(count, groups, hidden_ref, *refs):
    received = refs[:count]
    rows_ref, gate_ref = refs[count : count + 2]
    pays = refs[count + 2 : count + 2 + groups]
    wide_ref, weighted_ref = refs[count + 2 + groups :]
    width = rows_ref.shape[1]
    for r in range(count):
        row = received[r][:, : width + LANES]
        wide_ref[r * CAP : (r + 1) * CAP, :] = row.astype(jnp.float32)
    rows = wide_ref[:, :width]
    gate = wide_ref[:, width:]
    gate_ref[...] = gate
    rows_ref[...] = rows.astype(jnp.bfloat16)
    weighted_ref[...] = (gate[:, :1] * rows).astype(jnp.bfloat16)
    share = width // groups
    me = lax.axis_index("dp")
    for r in range(groups):
        group = target(me, r, groups)
        pays[r][:, :share] = weighted_ref[:, pl.ds(pl.multiple_of(group * share, share), share)]
        pays[r][:, share:] = hidden_ref[...]


def back_kernel(count, *refs):
    sent = refs[:count]
    joint_ref = refs[count]
    products = dict(zip(apart(count), refs[count + 1 : 2 * count]))
    back_ref = refs[2 * count]
    width = products[0].shape[1]
    for r in range(count):
        step = reply(r, count)
        if step != JOINT:
            theirs = products[step][...].astype(jnp.float32)
        else:
            theirs = joint_ref[:, joint_ref.shape[1] - width :].astype(jnp.float32)
        mine = sent[r][:, :width].astype(jnp.float32)
        back = jnp.sum(mine * theirs, axis=1, keepdims=True)
        back_ref[r * CAP : (r + 1) * CAP, :] = jnp.broadcast_to(back, (CAP, LANES))


def upstream_kernel(count, rows_ref, gate_ref, weight_ref, out_ref):
    upstream = dot(rows_ref[...], weight_ref[...], ((1,), (1,)))
    scaled = (gate_ref[:, :1] * upstream).astype(jnp.bfloat16)
    out_ref[...] = dot(slot_order(count), scaled, ((0,), (0,))).astype(jnp.bfloat16)


def down_kernel(groups, hidden_ref, match_ref, *refs):
    pays = refs[:groups]
    hidden_hbm, down_hbm, match_out, down_out, sems = refs[groups:]
    units, share = down_out.shape
    slots = jnp.concatenate([pay_ref[...] for pay_ref in pays], axis=0)
    copies = []

    def write(values, destination):
        copies.append(pltpu.make_async_copy(values, destination, sems.at[len(copies)]))
        copies[-1].start()

    cuts = [units - cut for cut in reversed(cuts_of(units))]
    for start, end in zip(cuts, cuts[1:]):
        hidden = slots[:, share + start : share + end]
        down_out[start:end, :] = dot(hidden, slots[:, :share], ((0,), (0,)))
        part = pl.ds(start, end - start)
        write(down_out.at[part], down_hbm.at[0, part])
    write(hidden_ref, hidden_hbm.at[0, 0])
    match_out[...] = match_ref[...]
    for copy in copies:
        copy.wait()


def gate_kernel(count, ids_ref, match_ref, *refs):
    backs, out_ref = refs[:-1], refs[-1]
    me = lax.axis_index("expert")
    ids = ids_ref[...]
    back = backs[0][...]
    for ref in backs[1:]:
        back = back + ref[...]
    total = jnp.zeros(out_ref.shape, jnp.float32)
    for r in range(count):
        value = back[r * CAP : (r + 1) * CAP, :]
        match = match_ref[r * PAD : r * PAD + CAP, :]
        chosen = jnp.sum(jnp.where(match > 0, value, 0.0), axis=0, keepdims=True)
        total = total + jnp.where(ids == target(me, r, count), chosen, 0.0)
    out_ref[...] = total


def on_device(grad_out, expert_ids, gate_values, saved_hidden, down_weight):
    count = lax.axis_size("expert")
    groups = lax.axis_size("dp")
    tensors = lax.axis_size("tensor")
    tokens, width = grad_out.shape
    top = expert_ids.shape[1]
    units = down_weight.shape[1]
    slots = count * CAP
    share = width // groups

    ids, match, weight, hidden, *rest = pl.pallas_call(
        functools.partial(front_kernel, count),
        out_shape=[
            jax.ShapeDtypeStruct((top, tokens), jnp.int32),
            jax.ShapeDtypeStruct((count * PAD, tokens), jnp.float32),
            jax.ShapeDtypeStruct((units, width), jnp.bfloat16),
            jax.ShapeDtypeStruct((slots, units), jnp.bfloat16),
        ]
        + [
            jax.ShapeDtypeStruct((CAP, width + LANES + width * (r == JOINT)), jnp.bfloat16)
            for r in range(count)
        ]
        + [jax.ShapeDtypeStruct((CAP, width), jnp.bfloat16)] * (count - 1),
        in_specs=[HBM] * 5,
        out_specs=[VMEM] * (3 + 2 * count),
        scratch_shapes=[
            pltpu.VMEM((top, tokens), jnp.bfloat16),
            pltpu.VMEM((tokens, width), jnp.bfloat16),
            pltpu.VMEM((slots, units), jnp.bfloat16),
            pltpu.VMEM((count * PAD, width), jnp.float32),
            pltpu.SemaphoreType.DMA((4 + len(cuts_of(units)),)),
        ],
        compiler_params=PARAMS,
        cost_estimate=cost(2 * count * PAD * (tokens + units) * width, 2 * (tokens + units) * width),
        name="front",
    )(*in_hbm(expert_ids.T, gate_values.T, grad_out, saved_hidden, down_weight))
    sends, products = rest[:count], rest[count:]

    received = [sends[0]] + [send(sends[r], "expert", r) for r in range(1, count)]
    theirs = [products[0]] + [send(products[r - 1], "expert", r) for r in range(JOINT + 1, count)]

    rows, gate, *pays = pl.pallas_call(
        functools.partial(slot_kernel, count, groups),
        out_shape=[
            jax.ShapeDtypeStruct((slots, width), jnp.bfloat16),
            jax.ShapeDtypeStruct((slots, LANES), jnp.float32),
        ]
        + [jax.ShapeDtypeStruct((slots, share + units), jnp.bfloat16)] * groups,
        in_specs=[VMEM] * (1 + count),
        out_specs=[VMEM] * (2 + groups),
        scratch_shapes=[
            pltpu.VMEM((slots, width + LANES), jnp.float32),
            pltpu.VMEM((slots, width), jnp.bfloat16),
        ],
        compiler_params=PARAMS,
        cost_estimate=cost(4 * slots * width, 8 * slots * width),
        name="slots",
    )(hidden, *received)

    back = pl.pallas_call(
        functools.partial(back_kernel, count),
        out_shape=jax.ShapeDtypeStruct((slots, LANES), jnp.float32),
        in_specs=[VMEM] * (2 * count),
        out_specs=VMEM,
        compiler_params=PARAMS,
        cost_estimate=cost(*AFTER_WAIT),
        name="backs",
    )(*sends, received[JOINT], *theirs)

    others = [send(pays[r], "dp", r) for r in range(1, groups)]
    backs = [back] + [send(back, "tensor", r) for r in reversed(range(1, tensors))]

    hidden_grad = pl.pallas_call(
        functools.partial(upstream_kernel, count),
        out_shape=jax.ShapeDtypeStruct((slots, units), jnp.bfloat16),
        in_specs=[VMEM] * 3,
        out_specs=VMEM,
        compiler_params=PARAMS,
        cost_estimate=cost(2 * slots * units * width, 2 * units * width),
        name="upstream",
    )(rows, gate, weight)

    hidden_grad, down_grad, match = pl.pallas_call(
        functools.partial(down_kernel, groups),
        out_shape=[
            jax.ShapeDtypeStruct(saved_hidden.shape, jnp.bfloat16),
            jax.ShapeDtypeStruct((1, units, share), jnp.float32),
            jax.ShapeDtypeStruct(match.shape, jnp.float32),
        ],
        in_specs=[VMEM] * (2 + groups),
        out_specs=[HBM, HBM, VMEM],
        scratch_shapes=[
            pltpu.VMEM((units, share), jnp.float32),
            pltpu.SemaphoreType.DMA((len(cuts_of(units)),)),
        ],
        compiler_params=PARAMS,
        cost_estimate=cost(2 * slots * units * share, 4 * units * share),
        name="down",
    )(hidden_grad, match, pays[0], *others)

    gate_grad = pl.pallas_call(
        functools.partial(gate_kernel, count),
        out_shape=jax.ShapeDtypeStruct(ids.shape, jnp.float32),
        in_specs=[VMEM] * (2 + tensors),
        out_specs=VMEM,
        compiler_params=PARAMS,
        cost_estimate=cost(slots * tokens, 4 * slots * tokens),
        name="gates",
    )(ids, match, *backs)
    return (gate_grad.T, hidden_grad, down_grad)


def solution(mesh):
    return jax.shard_map(
        on_device,
        mesh=mesh,
        in_specs=(
            P(("dp", "expert"), None),
            P(("dp", "expert"), None),
            P(("dp", "expert"), None),
            P("dp", "expert", None, "tensor"),
            P("expert", "tensor", None),
        ),
        out_specs=(
            P(("dp", "expert"), None),
            P("dp", "expert", None, "tensor"),
            P("expert", "tensor", "dp"),
        ),
        check_vma=False,
    )
```

```python
import functools

import jax
import jax.numpy as jnp
from jax import lax
from jax.experimental import pallas as pl
from jax.experimental.pallas import tpu as pltpu
from jax.sharding import PartitionSpec as P

CAP = 4
LANES = 128
JOINT = 1
AFTER_WAIT = (10**9, 10**7)
WIDE = 1024
PAD = 8
VMEM = pl.BlockSpec(memory_space=pltpu.VMEM)
HBM = pl.BlockSpec(memory_space=pltpu.HBM)
PARAMS = pltpu.CompilerParams(vmem_limit_bytes=32 * 2**20)


def dot(a, b, dims):
    return lax.dot_general(a, b, (dims, ((), ())), preferred_element_type=jnp.float32)


def in_hbm(*arrays):
    return [pltpu.with_memory_space_constraint(x, pltpu.HBM) for x in arrays]


def cost(flops, nbytes):
    return pl.CostEstimate(flops=flops, bytes_accessed=nbytes, transcendentals=0)


def paired(size):
    return size & (size - 1) == 0


def target(me, step, size):
    if paired(size):
        return me ^ ((size - step) % size)
    after = me + step
    return after % size if isinstance(me, int) else jnp.where(after >= size, after - size, after)


def source(me, step, size):
    if paired(size):
        return target(me, step, size)
    before = me - step
    return before % size if isinstance(me, int) else jnp.where(before < 0, before + size, before)


def reply(step, size):
    return step if paired(size) else -step % size


def apart(size):
    return [r for r in range(size) if r != JOINT]


def send(value, axis, step, give=target):
    size = lax.axis_size(axis)
    return lax.ppermute(value, axis, [(i, give(i, step, size)) for i in range(size)])


def front_kernel(count, pieces, *refs):
    ids_hbm, gates_hbm, grad_hbm, hidden_hbm, weight_hbm = refs[:5]
    ids_ref, match_ref, weight_ref, hidden_ref = refs[5:9]
    sends = refs[9 : 9 + count]
    products = refs[9 + count : 8 + 2 * count]
    gates_ref, grad_ref, saved_ref, total_ref, sems = refs[8 + 2 * count :]
    units, width = weight_ref.shape
    top, tokens = ids_ref.shape
    pairs = [(ids_hbm, ids_ref), (gates_hbm, gates_ref), (hidden_hbm.at[0, 0], saved_ref)]
    half = tokens // 2
    for p in range(2):
        part = pl.ds(p * half, half)
        pairs.append((grad_hbm.at[part], grad_ref.at[part]))
    half = units // (2 * pieces)
    for p in range(2 * pieces):
        part = pl.ds(p * half, half)
        pairs.append((weight_hbm.at[0, part], weight_ref.at[part]))
    copies = [pltpu.make_async_copy(*pair, sems.at[n]) for n, pair in enumerate(pairs)]
    for copy in copies:
        copy.start()
    me = lax.axis_index("expert")
    rows = count * PAD
    row = lax.broadcasted_iota(jnp.int32, (rows, tokens), 0)
    expert = target(me, row // PAD, count)
    place = row % PAD
    earlier = lax.broadcasted_iota(jnp.int32, (tokens, tokens), 0)
    later = lax.broadcasted_iota(jnp.int32, (tokens, tokens), 1)
    order = (earlier < later).astype(jnp.bfloat16)
    for copy in copies[:3]:
        copy.wait()
    ids = ids_ref[...]
    gates = gates_ref[...].astype(jnp.float32)
    member = jnp.zeros((rows, tokens), jnp.float32)
    gate = jnp.zeros((rows, tokens), jnp.float32)
    for k in range(top):
        hit = ids[k : k + 1, :] == expert
        member = jnp.where(hit, 1.0, member)
        gate = jnp.where(hit, gates[k : k + 1, :], gate)
    before = dot(member.astype(jnp.bfloat16), order, ((1,), (0,)))
    taken = (member > 0) & (before == place.astype(jnp.float32)) & (place < CAP)
    match = taken.astype(jnp.float32)
    match_ref[...] = match
    slot_gate = jnp.sum(match * gate, axis=1, keepdims=True)
    match = match.astype(jnp.bfloat16)

    slots = count * CAP
    saved = saved_ref[...]
    hidden_ref[...] = dot(slot_order(count), saved, ((1,), (0,))).astype(jnp.bfloat16)
    here = lax.broadcasted_iota(jnp.int32, (rows, slots), 0)
    there = lax.broadcasted_iota(jnp.int32, (rows, slots), 1)
    chosen = (here % PAD < CAP) & (there == target(me, here // PAD, count) * CAP + here % PAD)
    hidden = dot(chosen.astype(jnp.bfloat16), saved, ((1,), (0,))).astype(jnp.bfloat16)

    for copy in copies[3:5]:
        copy.wait()
    for r in range(count):
        part = slice(r * PAD, r * PAD + CAP)
        gate = jnp.broadcast_to(slot_gate[part], (CAP, LANES)).astype(jnp.bfloat16)
        sends[r][:, width : width + LANES] = gate
    wide = min(width, WIDE)
    for begin in range(0, width, wide):
        part = slice(begin, begin + wide)
        picked = dot(match, grad_ref[:, part], ((1,), (0,)))
        for r in range(count):
            sends[r][:, part] = picked[r * PAD : r * PAD + CAP].astype(jnp.bfloat16)
    block = units // pieces
    for p in range(pieces):
        for copy in copies[5 + 2 * p : 7 + 2 * p]:
            copy.wait()
        rows = slice(p * block, (p + 1) * block)
        for begin in range(0, width, wide):
            part = slice(begin, begin + wide)
            term = dot(hidden[:, rows], weight_ref[rows, part], ((1,), (0,)))
            if p > 0:
                term = total_ref[:, part] + term
            if p < pieces - 1:
                total_ref[:, part] = term
                continue
            for product_ref, r in zip(products, apart(count)):
                product_ref[:, part] = term[r * PAD : r * PAD + CAP].astype(jnp.bfloat16)
            begin += width + LANES
            joint = term[JOINT * PAD : JOINT * PAD + CAP].astype(jnp.bfloat16)
            sends[JOINT][:, begin : begin + wide] = joint


def slot_order(count):
    me = lax.axis_index("expert")
    slots = count * CAP
    here = lax.broadcasted_iota(jnp.int32, (slots, slots), 0)
    saved = lax.broadcasted_iota(jnp.int32, (slots, slots), 1)
    return (saved == source(me, here // CAP, count) * CAP + here % CAP).astype(jnp.bfloat16)


def slot_kernel(count, groups, hidden_ref, *refs):
    received = refs[:count]
    rows_ref, gate_ref = refs[count : count + 2]
    pays = refs[count + 2 : count + 2 + groups]
    wide_ref, weighted_ref = refs[count + 2 + groups :]
    width = rows_ref.shape[1]
    for r in range(count):
        row = received[r][:, : width + LANES]
        wide_ref[r * CAP : (r + 1) * CAP, :] = row.astype(jnp.float32)
    slots = count * CAP
    rows = wide_ref[:slots, :width]
    gate = wide_ref[:slots, width:]
    gate_ref[...] = gate
    rows_ref[...] = rows.astype(jnp.bfloat16)
    weighted_ref[...] = (gate[:, :1] * rows).astype(jnp.bfloat16)
    share = width // groups
    me = lax.axis_index("dp")
    for r in range(groups):
        group = target(me, r, groups)
        pays[r][:, :share] = weighted_ref[:, pl.ds(pl.multiple_of(group * share, share), share)]
        pays[r][:, share:] = hidden_ref[...]


def back_kernel(count, *refs):
    sent = refs[:count]
    joint_ref = refs[count]
    products = dict(zip(apart(count), refs[count + 1 : 2 * count]))
    out_ref, back_ref = refs[2 * count :]
    width = products[0].shape[1]
    for r in range(count):
        step = reply(r, count)
        if step != JOINT:
            theirs = products[step][...].astype(jnp.float32)
        else:
            theirs = joint_ref[:, joint_ref.shape[1] - width :].astype(jnp.float32)
        mine = sent[r][:, :width].astype(jnp.float32)
        back = jnp.sum(mine * theirs, axis=1, keepdims=True)
        back_ref[r * CAP : (r + 1) * CAP, :] = jnp.broadcast_to(back, (CAP, LANES))
    out_ref[...] = back_ref[: count * CAP, :]


def upstream_part(rows_ref, weight_ref, begin, end):
    return dot(rows_ref[:, begin:end], weight_ref[:, begin:end], ((1,), (1,)))


def upstream_kernel(split, rows_ref, weight_ref, out_ref):
    out_ref[...] = upstream_part(rows_ref, weight_ref, 0, split)


def down_kernel(count, groups, pieces, split, part_ref, rows_ref, gate_ref, weight_ref, match_ref, *refs):
    pays = refs[:groups]
    hidden_hbm, down_hbm, match_out, hidden_out, down_out, sems = refs[groups:]
    units, share = down_out.shape
    block = units // pieces
    slots = jnp.concatenate([pay_ref[...] for pay_ref in pays], axis=0)
    copies = []

    def write(values, destination):
        copies.append(pltpu.make_async_copy(values, destination, sems.at[len(copies)]))
        copies[-1].start()

    for p in range(pieces):
        part = slice(p * block, (p + 1) * block)
        hidden = slots[:, share + p * block : share + (p + 1) * block]
        down_out[part, :] = dot(hidden, slots[:, :share], ((0,), (0,)))
        part = pl.ds(p * block, block)
        write(down_out.at[part], down_hbm.at[0, part])
    upstream = part_ref[...] + upstream_part(rows_ref, weight_ref, split, weight_ref.shape[1])
    scaled = (gate_ref[:, :1] * upstream).astype(jnp.bfloat16)
    hidden_out[...] = dot(slot_order(count), scaled, ((0,), (0,))).astype(jnp.bfloat16)
    write(hidden_out, hidden_hbm.at[0, 0])
    match_out[...] = match_ref[...]
    for copy in copies:
        copy.wait()


def gate_kernel(count, ids_ref, match_ref, *refs):
    backs, out_ref = refs[:-1], refs[-1]
    me = lax.axis_index("expert")
    ids = ids_ref[...]
    back = backs[0][...]
    for ref in backs[1:]:
        back = back + ref[...]
    total = jnp.zeros(out_ref.shape, jnp.float32)
    for r in range(count):
        value = back[r * CAP : (r + 1) * CAP, :]
        match = match_ref[r * PAD : r * PAD + CAP, :]
        chosen = jnp.sum(jnp.where(match > 0, value, 0.0), axis=0, keepdims=True)
        total = total + jnp.where(ids == target(me, r, count), chosen, 0.0)
    out_ref[...] = total


def on_device(grad_out, expert_ids, gate_values, saved_hidden, down_weight):
    count = lax.axis_size("expert")
    groups = lax.axis_size("dp")
    tensors = lax.axis_size("tensor")
    tokens, width = grad_out.shape
    top = expert_ids.shape[1]
    units = down_weight.shape[1]
    slots = count * CAP
    share = width // groups
    pieces = units // LANES

    ids, match, weight, hidden, *rest = pl.pallas_call(
        functools.partial(front_kernel, count, pieces),
        out_shape=[
            jax.ShapeDtypeStruct((top, tokens), jnp.int32),
            jax.ShapeDtypeStruct((count * PAD, tokens), jnp.float32),
            jax.ShapeDtypeStruct((units, width), jnp.bfloat16),
            jax.ShapeDtypeStruct((slots, units), jnp.bfloat16),
        ]
        + [
            jax.ShapeDtypeStruct((CAP, width + LANES + width * (r == JOINT)), jnp.bfloat16)
            for r in range(count)
        ]
        + [jax.ShapeDtypeStruct((CAP, width), jnp.bfloat16)] * (count - 1),
        in_specs=[HBM] * 5,
        out_specs=[VMEM] * (3 + 2 * count),
        scratch_shapes=[
            pltpu.VMEM((top, tokens), jnp.bfloat16),
            pltpu.VMEM((tokens, width), jnp.bfloat16),
            pltpu.VMEM((slots, units), jnp.bfloat16),
            pltpu.VMEM((count * PAD, width), jnp.float32),
            pltpu.SemaphoreType.DMA((5 + 2 * pieces,)),
        ],
        compiler_params=PARAMS,
        cost_estimate=cost(2 * count * PAD * (tokens + units) * width, 2 * (tokens + units) * width),
        name="front",
    )(*in_hbm(expert_ids.T, gate_values.T, grad_out, saved_hidden, down_weight))
    sends, products = rest[:count], rest[count:]

    received = [sends[0]] + [send(sends[r], "expert", r) for r in range(1, count)]
    theirs = [products[0]] + [send(products[r - 1], "expert", r) for r in range(JOINT + 1, count)]

    rows, gate, *pays = pl.pallas_call(
        functools.partial(slot_kernel, count, groups),
        out_shape=[
            jax.ShapeDtypeStruct((slots, width), jnp.bfloat16),
            jax.ShapeDtypeStruct((slots, LANES), jnp.float32),
        ]
        + [jax.ShapeDtypeStruct((slots, share + units), jnp.bfloat16)] * groups,
        in_specs=[VMEM] * (1 + count),
        out_specs=[VMEM] * (2 + groups),
        scratch_shapes=[
            pltpu.VMEM((slots + PAD, width + LANES), jnp.float32),
            pltpu.VMEM((slots, width), jnp.bfloat16),
        ],
        compiler_params=PARAMS,
        cost_estimate=cost(4 * slots * width, 8 * slots * width),
        name="slots",
    )(hidden, *received)

    back = pl.pallas_call(
        functools.partial(back_kernel, count),
        out_shape=jax.ShapeDtypeStruct((slots, LANES), jnp.float32),
        in_specs=[VMEM] * (2 * count),
        out_specs=VMEM,
        scratch_shapes=[pltpu.VMEM((slots + PAD, LANES), jnp.float32)],
        compiler_params=PARAMS,
        cost_estimate=cost(*AFTER_WAIT),
        name="backs",
    )(*sends, received[JOINT], *theirs)

    others = [send(pays[r], "dp", r) for r in range(1, groups)]
    backs = [back] + [send(back, "tensor", r) for r in reversed(range(1, tensors))]

    split = width * 3 // 4
    upstream = pl.pallas_call(
        functools.partial(upstream_kernel, split),
        out_shape=jax.ShapeDtypeStruct((slots, units), jnp.float32),
        in_specs=[VMEM] * 2,
        out_specs=VMEM,
        compiler_params=PARAMS,
        cost_estimate=cost(2 * slots * units * split, 2 * units * split),
        name="upstream",
    )(rows, weight)

    hidden_grad, down_grad, match = pl.pallas_call(
        functools.partial(down_kernel, count, groups, pieces, split),
        out_shape=[
            jax.ShapeDtypeStruct(saved_hidden.shape, jnp.bfloat16),
            jax.ShapeDtypeStruct((1, units, share), jnp.float32),
            jax.ShapeDtypeStruct(match.shape, jnp.float32),
        ],
        in_specs=[VMEM] * (5 + groups),
        out_specs=[HBM, HBM, VMEM],
        scratch_shapes=[
            pltpu.VMEM((slots, units), jnp.bfloat16),
            pltpu.VMEM((units, share), jnp.float32),
            pltpu.SemaphoreType.DMA((pieces + 1,)),
        ],
        compiler_params=PARAMS,
        cost_estimate=cost(2 * slots * units * share, 4 * units * share),
        name="down",
    )(upstream, rows, gate, weight, match, pays[0], *others)

    gate_grad = pl.pallas_call(
        functools.partial(gate_kernel, count),
        out_shape=jax.ShapeDtypeStruct(ids.shape, jnp.float32),
        in_specs=[VMEM] * (2 + tensors),
        out_specs=VMEM,
        compiler_params=PARAMS,
        cost_estimate=cost(slots * tokens, 4 * slots * tokens),
        name="gates",
    )(ids, match, *backs)
    return (gate_grad.T, hidden_grad, down_grad)


def solution(mesh):
    return jax.shard_map(
        on_device,
        mesh=mesh,
        in_specs=(
            P(("dp", "expert"), None),
            P(("dp", "expert"), None),
            P(("dp", "expert"), None),
            P("dp", "expert", None, "tensor"),
            P("expert", "tensor", None),
        ),
        out_specs=(
            P(("dp", "expert"), None),
            P("dp", "expert", None, "tensor"),
            P("expert", "tensor", "dp"),
        ),
        check_vma=False,
    )
```

```python
import functools

import jax
import jax.numpy as jnp
from jax import lax
from jax.experimental import pallas as pl
from jax.experimental.pallas import tpu as pltpu
from jax.sharding import PartitionSpec as P

CAP = 4
LANES = 128
AFTER_WAIT = (10**9, 10**7)
WIDE = 1024
PAD = 8
VMEM = pl.BlockSpec(memory_space=pltpu.VMEM)
HBM = pl.BlockSpec(memory_space=pltpu.HBM)
PARAMS = pltpu.CompilerParams(vmem_limit_bytes=32 * 2**20)


def dot(a, b, dims):
    return lax.dot_general(a, b, (dims, ((), ())), preferred_element_type=jnp.float32)


def in_hbm(*arrays):
    return [pltpu.with_memory_space_constraint(x, pltpu.HBM) for x in arrays]


def cost(flops, nbytes):
    return pl.CostEstimate(flops=flops, bytes_accessed=nbytes, transcendentals=0)


def paired(size):
    return size & (size - 1) == 0


def target(me, step, size):
    if paired(size):
        return me ^ ((size - step) % size)
    after = me + step
    return after % size if isinstance(me, int) else jnp.where(after >= size, after - size, after)


def source(me, step, size):
    if paired(size):
        return target(me, step, size)
    before = me - step
    return before % size if isinstance(me, int) else jnp.where(before < 0, before + size, before)


def reply(step, size):
    return step if paired(size) else -step % size


def apart(size):
    return [r for r in range(size) if r not in (1, size - 1)]


def send(value, axis, step, give=target):
    size = lax.axis_size(axis)
    return lax.ppermute(value, axis, [(i, give(i, step, size)) for i in range(size)])


def front_kernel(count, groups, pieces, *refs):
    ids_hbm, gates_hbm, grad_hbm, hidden_hbm, weight_hbm = refs[:5]
    ids_ref, match_ref, weight_ref, hidden_ref = refs[5:9]
    sends = refs[9 : 9 + count]
    products = dict(zip(apart(count), refs[9 + count :]))
    early = refs[-4 - groups : -5]
    gates_ref, grad_ref, saved_ref, total_ref, sems = refs[-5:]
    units, width = weight_ref.shape
    top, tokens = ids_ref.shape
    pairs = [(ids_hbm, ids_ref), (gates_hbm, gates_ref), (hidden_hbm.at[0, 0], saved_ref)]
    half = tokens // 2
    for p in range(2):
        part = pl.ds(p * half, half)
        pairs.append((grad_hbm.at[part], grad_ref.at[part]))
    half = units // (2 * pieces)
    for p in range(2 * pieces):
        part = pl.ds(p * half, half)
        pairs.append((weight_hbm.at[0, part], weight_ref.at[part]))
    copies = [pltpu.make_async_copy(*pair, sems.at[n]) for n, pair in enumerate(pairs)]
    for copy in copies:
        copy.start()
    me = lax.axis_index("expert")
    rows = count * PAD
    row = lax.broadcasted_iota(jnp.int32, (rows, tokens), 0)
    expert = target(me, row // PAD, count)
    place = row % PAD
    earlier = lax.broadcasted_iota(jnp.int32, (tokens, tokens), 0)
    later = lax.broadcasted_iota(jnp.int32, (tokens, tokens), 1)
    order = (earlier < later).astype(jnp.bfloat16)
    for copy in copies[:3]:
        copy.wait()
    ids = ids_ref[...]
    gates = gates_ref[...].astype(jnp.float32)
    member = jnp.zeros((rows, tokens), jnp.float32)
    gate = jnp.zeros((rows, tokens), jnp.float32)
    for k in range(top):
        hit = ids[k : k + 1, :] == expert
        member = jnp.where(hit, 1.0, member)
        gate = jnp.where(hit, gates[k : k + 1, :], gate)
    before = dot(member.astype(jnp.bfloat16), order, ((1,), (0,)))
    taken = (member > 0) & (before == place.astype(jnp.float32)) & (place < CAP)
    match = taken.astype(jnp.float32)
    match_ref[...] = match
    slot_gate = jnp.sum(match * gate, axis=1, keepdims=True)
    match = match.astype(jnp.bfloat16)

    slots = count * CAP
    saved = saved_ref[...]
    hidden_ref[...] = dot(slot_order(count), saved, ((1,), (0,))).astype(jnp.bfloat16)
    spread = dot(slot_order(count, PAD), saved, ((1,), (0,)))
    here = lax.broadcasted_iota(jnp.int32, (rows, slots), 0)
    there = lax.broadcasted_iota(jnp.int32, (rows, slots), 1)
    chosen = (here % PAD < CAP) & (there == target(me, here // PAD, count) * CAP + here % PAD)
    hidden = dot(chosen.astype(jnp.bfloat16), saved, ((1,), (0,))).astype(jnp.bfloat16)

    for copy in copies[3:5]:
        copy.wait()
    for r in range(count):
        part = slice(r * PAD, r * PAD + CAP)
        gate = jnp.broadcast_to(slot_gate[part], (CAP, LANES)).astype(jnp.bfloat16)
        sends[r][:, width : width + LANES] = gate
    wide = min(width, WIDE)
    for begin in range(0, width, wide):
        part = slice(begin, begin + wide)
        picked = dot(match, grad_ref[:, part], ((1,), (0,)))
        for r in range(count):
            sends[r][:, part] = picked[r * PAD : r * PAD + CAP].astype(jnp.bfloat16)
        total_ref[:PAD, part] = picked[:PAD]
    share = width // groups
    group = lax.axis_index("dp")
    for r, early_ref in enumerate(early, 1):
        begin = pl.multiple_of(target(group, r, groups) * share, share)
        weighted = slot_gate[:CAP] * total_ref[:CAP, pl.ds(begin, share)]
        early_ref[:, :share] = weighted.astype(jnp.bfloat16)
        for k in range(count):
            part = slice(share + k * units, share + (k + 1) * units)
            early_ref[:, part] = spread[k * PAD : k * PAD + CAP].astype(jnp.bfloat16)
    block = units // pieces
    for p in range(pieces):
        for copy in copies[5 + 2 * p : 7 + 2 * p]:
            copy.wait()
        rows = slice(p * block, (p + 1) * block)
        for begin in range(0, width, wide):
            part = slice(begin, begin + wide)
            term = dot(hidden[:, rows], weight_ref[rows, part], ((1,), (0,)))
            if p > 0:
                term = total_ref[:, part] + term
            if p < pieces - 1:
                total_ref[:, part] = term
                continue
            for r in range(count):
                product = term[r * PAD : r * PAD + CAP].astype(jnp.bfloat16)
                if r in products:
                    products[r][:, part] = product
                else:
                    joint = slice(width + LANES + begin, width + LANES + begin + wide)
                    sends[r][:, joint] = product


def slot_order(count, lines=CAP):
    me = lax.axis_index("expert")
    here = lax.broadcasted_iota(jnp.int32, (count * lines, count * CAP), 0)
    saved = lax.broadcasted_iota(jnp.int32, (count * lines, count * CAP), 1)
    place = here % lines
    block = source(me, here // lines, count)
    return ((saved == block * CAP + place) & (place < CAP)).astype(jnp.bfloat16)


def slot_kernel(count, groups, hidden_ref, *refs):
    received = refs[:count]
    rows_ref, gate_ref, own_ref = refs[count : count + 3]
    lates = refs[count + 3 : count + 2 + groups]
    wide_ref, spread_ref = refs[count + 2 + groups :]
    width = rows_ref.shape[1]
    share = width // groups
    slots = count * CAP
    for r in range(count):
        row = received[r][:, : width + LANES].astype(jnp.float32)
        wide_ref[r * CAP : (r + 1) * CAP, :] = row
        spread_ref[r * PAD : r * PAD + CAP, :] = row[:, width : width + 1] * row[:, :width]
    rows = wide_ref[:slots, :width]
    gate = wide_ref[:slots, width:]
    gate_ref[...] = gate
    rows_ref[...] = rows.astype(jnp.bfloat16)
    me = lax.axis_index("dp")
    for r, late_ref in enumerate(lates, 1):
        begin = pl.multiple_of(target(me, r, groups) * share, share)
        for k in range(1, count):
            late = spread_ref[k * PAD : k * PAD + CAP, pl.ds(begin, share)]
            late_ref[:, (k - 1) * share : k * share] = late.astype(jnp.bfloat16)
    weighted = gate[:, :1] * wide_ref[:slots, pl.ds(pl.multiple_of(me * share, share), share)]
    own_ref[:, :share] = weighted.astype(jnp.bfloat16)
    own_ref[:, share:] = hidden_ref[...]


def back_kernel(count, groups, *refs):
    sent, refs = refs[:count], refs[count:]
    received, refs = dict(enumerate(refs[: count - 1], 1)), refs[count - 1 :]
    received.update(zip(apart(count), refs))
    refs = refs[len(apart(count)) :]
    early, refs = refs[: groups - 1], refs[groups - 1 :]
    out_ref, hiddens = refs[0], refs[1:groups]
    back_ref, units_ref = refs[groups:]
    width = received[0].shape[1]
    for r in range(count):
        ref = received[reply(r, count)]
        theirs = ref[:, ref.shape[1] - width :].astype(jnp.float32)
        mine = sent[r][:, :width].astype(jnp.float32)
        back = jnp.sum(mine * theirs, axis=1, keepdims=True)
        back_ref[r * CAP : (r + 1) * CAP, :] = jnp.broadcast_to(back, (CAP, LANES))
    slots, units = count * CAP, units_ref.shape[1]
    out_ref[...] = back_ref[:slots, :]
    for early_ref, hidden_ref in zip(early, hiddens):
        share = early_ref.shape[1] - count * units
        for k in range(count):
            part = early_ref[:, share + k * units : share + (k + 1) * units]
            units_ref[k * CAP : (k + 1) * CAP, :] = part.astype(jnp.float32)
        hidden_ref[...] = units_ref[:slots, :].astype(jnp.bfloat16)


def upstream_part(rows_ref, weight_ref, begin, end):
    return dot(rows_ref[:, begin:end], weight_ref[:, begin:end], ((1,), (1,)))


def upstream_kernel(split, rows_ref, weight_ref, out_ref):
    out_ref[...] = upstream_part(rows_ref, weight_ref, 0, split)


def down_kernel(count, groups, pieces, split, part_ref, rows_ref, gate_ref, weight_ref, match_ref, *refs):
    others = groups - 1
    own_ref, early, refs = refs[0], refs[1:groups], refs[groups:]
    lates, hiddens, refs = refs[:others], refs[others : 2 * others], refs[2 * others :]
    hidden_hbm, down_hbm, match_out, hidden_out, down_out, wide_ref, sems = refs
    units, share = down_out.shape
    block = units // pieces
    rows, hidden = [own_ref[:, :share]], [own_ref[:, share:]]
    for early_ref, late_ref, hidden_ref in zip(early, lates, hiddens):
        wide_ref[:CAP, :] = early_ref[:, :share].astype(jnp.float32)
        for k in range(1, count):
            late = late_ref[:, (k - 1) * share : k * share].astype(jnp.float32)
            wide_ref[k * CAP : (k + 1) * CAP, :] = late
        rows.append(wide_ref[: count * CAP, :].astype(jnp.bfloat16))
        hidden.append(hidden_ref[...])
    rows, hidden = jnp.concatenate(rows, axis=0), jnp.concatenate(hidden, axis=0)
    copies = []

    def write(values, destination):
        copies.append(pltpu.make_async_copy(values, destination, sems.at[len(copies)]))
        copies[-1].start()

    for p in range(pieces):
        part = slice(p * block, (p + 1) * block)
        down_out[part, :] = dot(hidden[:, part], rows, ((0,), (0,)))
        part = pl.ds(p * block, block)
        write(down_out.at[part], down_hbm.at[0, part])
    upstream = part_ref[...] + upstream_part(rows_ref, weight_ref, split, weight_ref.shape[1])
    scaled = (gate_ref[:, :1] * upstream).astype(jnp.bfloat16)
    hidden_out[...] = dot(slot_order(count), scaled, ((0,), (0,))).astype(jnp.bfloat16)
    write(hidden_out, hidden_hbm.at[0, 0])
    match_out[...] = match_ref[...]
    for copy in copies:
        copy.wait()


def gate_kernel(count, ids_ref, match_ref, *refs):
    backs, out_ref = refs[:-1], refs[-1]
    me = lax.axis_index("expert")
    ids = ids_ref[...]
    back = backs[0][...]
    for ref in backs[1:]:
        back = back + ref[...]
    total = jnp.zeros(out_ref.shape, jnp.float32)
    for r in range(count):
        value = back[r * CAP : (r + 1) * CAP, :]
        match = match_ref[r * PAD : r * PAD + CAP, :]
        chosen = jnp.sum(jnp.where(match > 0, value, 0.0), axis=0, keepdims=True)
        total = total + jnp.where(ids == target(me, r, count), chosen, 0.0)
    out_ref[...] = total


def on_device(grad_out, expert_ids, gate_values, saved_hidden, down_weight):
    count = lax.axis_size("expert")
    groups = lax.axis_size("dp")
    tensors = lax.axis_size("tensor")
    tokens, width = grad_out.shape
    top = expert_ids.shape[1]
    units = down_weight.shape[1]
    slots = count * CAP
    share = width // groups
    pieces = units // LANES

    ids, match, weight, hidden, *rest = pl.pallas_call(
        functools.partial(front_kernel, count, groups, pieces),
        out_shape=[
            jax.ShapeDtypeStruct((top, tokens), jnp.int32),
            jax.ShapeDtypeStruct((count * PAD, tokens), jnp.float32),
            jax.ShapeDtypeStruct((units, width), jnp.bfloat16),
            jax.ShapeDtypeStruct((slots, units), jnp.bfloat16),
        ]
        + [
            jax.ShapeDtypeStruct((CAP, width + LANES + width * (r not in apart(count))), jnp.bfloat16)
            for r in range(count)
        ]
        + [jax.ShapeDtypeStruct((CAP, width), jnp.bfloat16)] * len(apart(count))
        + [jax.ShapeDtypeStruct((CAP, share + count * units), jnp.bfloat16)] * (groups - 1),
        in_specs=[HBM] * 5,
        out_specs=[VMEM] * (3 + count + len(apart(count)) + groups),
        scratch_shapes=[
            pltpu.VMEM((top, tokens), jnp.bfloat16),
            pltpu.VMEM((tokens, width), jnp.bfloat16),
            pltpu.VMEM((slots, units), jnp.bfloat16),
            pltpu.VMEM((count * PAD, width), jnp.float32),
            pltpu.SemaphoreType.DMA((5 + 2 * pieces,)),
        ],
        compiler_params=PARAMS,
        cost_estimate=cost(2 * count * PAD * (tokens + units) * width, 2 * (tokens + units) * width),
        name="front",
    )(*in_hbm(expert_ids.T, gate_values.T, grad_out, saved_hidden, down_weight))
    sends, rest = rest[:count], rest[count:]
    products, early = rest[: len(apart(count))], rest[len(apart(count)) :]

    received = [sends[0]] + [send(sends[r], "expert", r) for r in range(1, count)]
    theirs = [products[0]]
    theirs += [send(x, "expert", r) for r, x in zip(apart(count)[1:], products[1:])]
    early = [send(x, "dp", r) for r, x in enumerate(early, 1)]

    rows, gate, own, *lates = pl.pallas_call(
        functools.partial(slot_kernel, count, groups),
        out_shape=[
            jax.ShapeDtypeStruct((slots, width), jnp.bfloat16),
            jax.ShapeDtypeStruct((slots, LANES), jnp.float32),
            jax.ShapeDtypeStruct((slots, share + units), jnp.bfloat16),
        ]
        + [jax.ShapeDtypeStruct((CAP, (count - 1) * share), jnp.bfloat16)] * (groups - 1),
        in_specs=[VMEM] * (1 + count),
        out_specs=[VMEM] * (2 + groups),
        scratch_shapes=[
            pltpu.VMEM((slots + PAD, width + LANES), jnp.float32),
            pltpu.VMEM((count * PAD, width), jnp.float32),
        ],
        compiler_params=PARAMS,
        cost_estimate=cost(4 * slots * width, 8 * slots * width),
        name="slots",
    )(hidden, *received)

    back, *hiddens = pl.pallas_call(
        functools.partial(back_kernel, count, groups),
        out_shape=[jax.ShapeDtypeStruct((slots, LANES), jnp.float32)]
        + [jax.ShapeDtypeStruct((slots, units), jnp.bfloat16)] * (groups - 1),
        in_specs=[VMEM] * (2 * count - 2 + len(apart(count)) + groups),
        out_specs=[VMEM] * groups,
        scratch_shapes=[
            pltpu.VMEM((slots + PAD, LANES), jnp.float32),
            pltpu.VMEM((slots + PAD, units), jnp.float32),
        ],
        compiler_params=PARAMS,
        cost_estimate=cost(*AFTER_WAIT),
        name="backs",
    )(*sends, *received[1:], *theirs, *early)

    lates = [send(x, "dp", r) for r, x in enumerate(lates, 1)]
    backs = [back] + [send(back, "tensor", r) for r in range(1, tensors)]

    split = width * 3 // 8
    upstream = pl.pallas_call(
        functools.partial(upstream_kernel, split),
        out_shape=jax.ShapeDtypeStruct((slots, units), jnp.float32),
        in_specs=[VMEM] * 2,
        out_specs=VMEM,
        compiler_params=PARAMS,
        cost_estimate=cost(2 * slots * units * split, 2 * units * split),
        name="upstream",
    )(rows, weight)

    hidden_grad, down_grad, match = pl.pallas_call(
        functools.partial(down_kernel, count, groups, pieces, split),
        out_shape=[
            jax.ShapeDtypeStruct(saved_hidden.shape, jnp.bfloat16),
            jax.ShapeDtypeStruct((1, units, share), jnp.float32),
            jax.ShapeDtypeStruct(match.shape, jnp.float32),
        ],
        in_specs=[VMEM] * (3 + 3 * groups),
        out_specs=[HBM, HBM, VMEM],
        scratch_shapes=[
            pltpu.VMEM((slots, units), jnp.bfloat16),
            pltpu.VMEM((units, share), jnp.float32),
            pltpu.VMEM((slots + PAD, share), jnp.float32),
            pltpu.SemaphoreType.DMA((pieces + 1,)),
        ],
        compiler_params=PARAMS,
        cost_estimate=cost(2 * slots * units * share, 4 * units * share),
        name="down",
    )(upstream, rows, gate, weight, match, own, *early, *lates, *hiddens)

    gate_grad = pl.pallas_call(
        functools.partial(gate_kernel, count),
        out_shape=jax.ShapeDtypeStruct(ids.shape, jnp.float32),
        in_specs=[VMEM] * (2 + tensors),
        out_specs=VMEM,
        compiler_params=PARAMS,
        cost_estimate=cost(slots * tokens, 4 * slots * tokens),
        name="gates",
    )(ids, match, *backs)
    return (gate_grad.T, hidden_grad, down_grad)


def solution(mesh):
    return jax.shard_map(
        on_device,
        mesh=mesh,
        in_specs=(
            P(("dp", "expert"), None),
            P(("dp", "expert"), None),
            P(("dp", "expert"), None),
            P("dp", "expert", None, "tensor"),
            P("expert", "tensor", None),
        ),
        out_specs=(
            P(("dp", "expert"), None),
            P("dp", "expert", None, "tensor"),
            P("expert", "tensor", "dp"),
        ),
        check_vma=False,
    )
```

```python
import functools

import jax
import jax.numpy as jnp
from jax import lax
from jax.experimental import pallas as pl
from jax.experimental.pallas import tpu as pltpu
from jax.sharding import PartitionSpec as P

CAP = 4
LANES = 128
AFTER_WAIT = (3 * 10**8, 3 * 10**6)
WIDE = 1024
PAD = 8
VMEM = pl.BlockSpec(memory_space=pltpu.VMEM)
HBM = pl.BlockSpec(memory_space=pltpu.HBM)
PARAMS = pltpu.CompilerParams(vmem_limit_bytes=32 * 2**20)


def dot(a, b, dims):
    return lax.dot_general(a, b, (dims, ((), ())), preferred_element_type=jnp.float32)


def in_hbm(*arrays):
    return [pltpu.with_memory_space_constraint(x, pltpu.HBM) for x in arrays]


def cost(flops, nbytes):
    return pl.CostEstimate(flops=flops, bytes_accessed=nbytes, transcendentals=0)


def paired(size):
    return size & (size - 1) == 0


def target(me, step, size):
    if paired(size):
        return me ^ ((size - step) % size)
    after = me + step
    return after % size if isinstance(me, int) else jnp.where(after >= size, after - size, after)


def source(me, step, size):
    if paired(size):
        return target(me, step, size)
    before = me - step
    return before % size if isinstance(me, int) else jnp.where(before < 0, before + size, before)


def reply(step, size):
    return step if paired(size) else -step % size


def apart(size):
    return [r for r in range(size) if r not in (1, size - 1)]


def send(value, axis, step, give=target):
    size = lax.axis_size(axis)
    return lax.ppermute(value, axis, [(i, give(i, step, size)) for i in range(size)])


def front_kernel(count, pieces, *refs):
    ids_hbm, gates_hbm, grad_hbm, hidden_hbm, weight_hbm = refs[:5]
    ids_ref, match_ref, weight_ref, hidden_ref = refs[5:9]
    sends = refs[9 : 9 + count]
    products = dict(zip(apart(count), refs[9 + count :]))
    spread_ref, gates_ref, grad_ref, saved_ref, total_ref, sems = refs[-6:]
    units, width = weight_ref.shape
    top, tokens = ids_ref.shape
    pairs = [(ids_hbm, ids_ref), (gates_hbm, gates_ref), (hidden_hbm.at[0, 0], saved_ref)]
    half = tokens // 2
    for p in range(2):
        part = pl.ds(p * half, half)
        pairs.append((grad_hbm.at[part], grad_ref.at[part]))
    half = units // (2 * pieces)
    for p in range(2 * pieces):
        part = pl.ds(p * half, half)
        pairs.append((weight_hbm.at[0, part], weight_ref.at[part]))
    copies = [pltpu.make_async_copy(*pair, sems.at[n]) for n, pair in enumerate(pairs)]
    for copy in copies:
        copy.start()
    me = lax.axis_index("expert")
    rows = count * PAD
    row = lax.broadcasted_iota(jnp.int32, (rows, tokens), 0)
    expert = target(me, row // PAD, count)
    place = row % PAD
    earlier = lax.broadcasted_iota(jnp.int32, (tokens, tokens), 0)
    later = lax.broadcasted_iota(jnp.int32, (tokens, tokens), 1)
    order = (earlier < later).astype(jnp.bfloat16)
    for copy in copies[:3]:
        copy.wait()
    ids = ids_ref[...]
    gates = gates_ref[...].astype(jnp.float32)
    member = jnp.zeros((rows, tokens), jnp.float32)
    gate = jnp.zeros((rows, tokens), jnp.float32)
    for k in range(top):
        hit = ids[k : k + 1, :] == expert
        member = jnp.where(hit, 1.0, member)
        gate = jnp.where(hit, gates[k : k + 1, :], gate)
    before = dot(member.astype(jnp.bfloat16), order, ((1,), (0,)))
    taken = (member > 0) & (before == place.astype(jnp.float32)) & (place < CAP)
    match = taken.astype(jnp.float32)
    match_ref[...] = match
    slot_gate = jnp.sum(match * gate, axis=1, keepdims=True)
    match = match.astype(jnp.bfloat16)

    slots = count * CAP
    saved = saved_ref[...]
    hidden_ref[...] = dot(slot_order(count), saved, ((1,), (0,))).astype(jnp.bfloat16)
    spread = dot(slot_order(count, PAD), saved, ((1,), (0,)))
    here = lax.broadcasted_iota(jnp.int32, (rows, slots), 0)
    there = lax.broadcasted_iota(jnp.int32, (rows, slots), 1)
    chosen = (here % PAD < CAP) & (there == target(me, here // PAD, count) * CAP + here % PAD)
    hidden = dot(chosen.astype(jnp.bfloat16), saved, ((1,), (0,))).astype(jnp.bfloat16)

    for copy in copies[3:5]:
        copy.wait()
    for r in range(count):
        part = slice(r * PAD, r * PAD + CAP)
        gate = jnp.broadcast_to(slot_gate[part], (CAP, LANES)).astype(jnp.bfloat16)
        sends[r][:, width : width + LANES] = gate
    wide = min(width, WIDE)
    for begin in range(0, width, wide):
        part = slice(begin, begin + wide)
        picked = dot(match, grad_ref[:, part], ((1,), (0,)))
        for r in range(count):
            sends[r][:, part] = picked[r * PAD : r * PAD + CAP].astype(jnp.bfloat16)
    for k in range(count):
        hidden_of = spread[k * PAD : k * PAD + CAP].astype(jnp.bfloat16)
        spread_ref[:, k * units : (k + 1) * units] = hidden_of
    block = units // pieces
    for p in range(pieces):
        for copy in copies[5 + 2 * p : 7 + 2 * p]:
            copy.wait()
        rows = slice(p * block, (p + 1) * block)
        for begin in range(0, width, wide):
            part = slice(begin, begin + wide)
            term = dot(hidden[:, rows], weight_ref[rows, part], ((1,), (0,)))
            if p > 0:
                term = total_ref[:, part] + term
            if p < pieces - 1:
                total_ref[:, part] = term
                continue
            for r in range(count):
                product = term[r * PAD : r * PAD + CAP].astype(jnp.bfloat16)
                if r in products:
                    products[r][:, part] = product
                else:
                    joint = slice(width + LANES + begin, width + LANES + begin + wide)
                    sends[r][:, joint] = product


def slot_order(count, lines=CAP):
    me = lax.axis_index("expert")
    here = lax.broadcasted_iota(jnp.int32, (count * lines, count * CAP), 0)
    saved = lax.broadcasted_iota(jnp.int32, (count * lines, count * CAP), 1)
    place = here % lines
    block = source(me, here // lines, count)
    return ((saved == block * CAP + place) & (place < CAP)).astype(jnp.bfloat16)


def early_kernel(groups, spread_ref, *refs):
    received, early, row_ref = refs[: -groups], refs[-groups:-1], refs[-1]
    width = row_ref.shape[1]
    share = width // groups
    me = lax.axis_index("dp")
    for n, ref in enumerate(received):
        row = ref[:, : width + LANES].astype(jnp.float32)
        row_ref[:CAP, :] = row[:, width : width + 1] * row[:, :width]
        for r, early_ref in enumerate(early, 1):
            begin = pl.multiple_of(target(me, r, groups) * share, share)
            part = row_ref[:CAP, pl.ds(begin, share)].astype(jnp.bfloat16)
            early_ref[:, n * share : (n + 1) * share] = part
    for early_ref in early:
        early_ref[:, len(received) * share :] = spread_ref[...]


def slot_kernel(count, groups, hidden_ref, *refs):
    received = refs[:count]
    rows_ref, gate_ref, own_ref = refs[count : count + 3]
    lates = refs[count + 3 : count + 2 + groups]
    wide_ref, spread_ref = refs[count + 2 + groups :]
    width = rows_ref.shape[1]
    share = width // groups
    slots = count * CAP
    for r in range(count):
        row = received[r][:, : width + LANES].astype(jnp.float32)
        wide_ref[r * CAP : (r + 1) * CAP, :] = row
        spread_ref[r * PAD : r * PAD + CAP, :] = row[:, width : width + 1] * row[:, :width]
    rows = wide_ref[:slots, :width]
    gate = wide_ref[:slots, width:]
    gate_ref[...] = gate
    rows_ref[...] = rows.astype(jnp.bfloat16)
    me = lax.axis_index("dp")
    for r, late_ref in enumerate(lates, 1):
        begin = pl.multiple_of(target(me, r, groups) * share, share)
        for n, k in enumerate(apart(count)[1:]):
            late = spread_ref[k * PAD : k * PAD + CAP, pl.ds(begin, share)]
            late_ref[:, n * share : (n + 1) * share] = late.astype(jnp.bfloat16)
    weighted = gate[:, :1] * wide_ref[:slots, pl.ds(pl.multiple_of(me * share, share), share)]
    own_ref[:, :share] = weighted.astype(jnp.bfloat16)
    own_ref[:, share:] = hidden_ref[...]


def back_kernel(count, *refs):
    sent, refs = refs[:count], refs[count:]
    received, refs = dict(enumerate(refs[: count - 1], 1)), refs[count - 1 :]
    received.update(zip(apart(count), refs))
    out_ref, back_ref = refs[-2:]
    width = received[0].shape[1]
    for r in range(count):
        ref = received[reply(r, count)]
        theirs = ref[:, ref.shape[1] - width :].astype(jnp.float32)
        mine = sent[r][:, :width].astype(jnp.float32)
        back = jnp.sum(mine * theirs, axis=1, keepdims=True)
        back_ref[r * CAP : (r + 1) * CAP, :] = jnp.broadcast_to(back, (CAP, LANES))
    out_ref[...] = back_ref[: count * CAP, :]


def upstream_part(rows_ref, weight_ref, begin, end):
    return dot(rows_ref[:, begin:end], weight_ref[:, begin:end], ((1,), (1,)))


def upstream_kernel(count, split, rows_ref, weight_ref, *refs):
    others = (len(refs) - 3) // 3
    early, out_ref, refs = refs[:others], refs[others], refs[others + 1 :]
    wides, hiddens, (units_ref, row_ref) = refs[:others], refs[others : 2 * others], refs[2 * others :]
    units, share = units_ref.shape[1], row_ref.shape[1]
    first = [0, 1, count - 1]
    for early_ref, wide_ref, hidden_ref in zip(early, wides, hiddens):
        for n, k in enumerate(first):
            part = early_ref[:, n * share : (n + 1) * share]
            wide_ref[k * CAP : (k + 1) * CAP, :] = part.astype(jnp.float32)
        begin = len(first) * share
        for k in range(count):
            part = early_ref[:, begin + k * units : begin + (k + 1) * units]
            units_ref[k * CAP : (k + 1) * CAP, :] = part.astype(jnp.float32)
        hidden_ref[...] = units_ref[: count * CAP, :].astype(jnp.bfloat16)
    out_ref[...] = upstream_part(rows_ref, weight_ref, 0, split)


def down_kernel(count, groups, pieces, split, part_ref, rows_ref, gate_ref, weight_ref, match_ref, *refs):
    others = groups - 1
    own_ref, wides, refs = refs[0], refs[1:groups], refs[groups:]
    lates, hiddens, refs = refs[:others], refs[others : 2 * others], refs[2 * others :]
    hidden_hbm, down_hbm, match_out, hidden_out, down_out, all_ref, sems = refs
    units, share = down_out.shape
    block = units // pieces
    rows, hidden = [own_ref[:, :share]], [own_ref[:, share:]]
    for wide_ref, late_ref, hidden_ref in zip(wides, lates, hiddens):
        all_ref[...] = wide_ref[...]
        for n, k in enumerate(apart(count)[1:]):
            late = late_ref[:, n * share : (n + 1) * share].astype(jnp.float32)
            all_ref[k * CAP : (k + 1) * CAP, :] = late
        rows.append(all_ref[: count * CAP, :].astype(jnp.bfloat16))
        hidden.append(hidden_ref[...])
    rows, hidden = jnp.concatenate(rows, axis=0), jnp.concatenate(hidden, axis=0)
    copies = []

    def write(values, destination):
        copies.append(pltpu.make_async_copy(values, destination, sems.at[len(copies)]))
        copies[-1].start()

    for p in range(pieces):
        part = slice(p * block, (p + 1) * block)
        down_out[part, :] = dot(hidden[:, part], rows, ((0,), (0,)))
        part = pl.ds(p * block, block)
        write(down_out.at[part], down_hbm.at[0, part])
    upstream = part_ref[...] + upstream_part(rows_ref, weight_ref, split, weight_ref.shape[1])
    scaled = (gate_ref[:, :1] * upstream).astype(jnp.bfloat16)
    hidden_out[...] = dot(slot_order(count), scaled, ((0,), (0,))).astype(jnp.bfloat16)
    write(hidden_out, hidden_hbm.at[0, 0])
    match_out[...] = match_ref[...]
    for copy in copies:
        copy.wait()


def gate_kernel(count, ids_ref, match_ref, *refs):
    backs, out_ref = refs[:-1], refs[-1]
    me = lax.axis_index("expert")
    ids = ids_ref[...]
    back = backs[0][...]
    for ref in backs[1:]:
        back = back + ref[...]
    total = jnp.zeros(out_ref.shape, jnp.float32)
    for r in range(count):
        value = back[r * CAP : (r + 1) * CAP, :]
        match = match_ref[r * PAD : r * PAD + CAP, :]
        chosen = jnp.sum(jnp.where(match > 0, value, 0.0), axis=0, keepdims=True)
        total = total + jnp.where(ids == target(me, r, count), chosen, 0.0)
    out_ref[...] = total


def on_device(grad_out, expert_ids, gate_values, saved_hidden, down_weight):
    count = lax.axis_size("expert")
    groups = lax.axis_size("dp")
    tensors = lax.axis_size("tensor")
    tokens, width = grad_out.shape
    top = expert_ids.shape[1]
    units = down_weight.shape[1]
    slots = count * CAP
    share = width // groups
    pieces = units // LANES

    ids, match, weight, hidden, *rest = pl.pallas_call(
        functools.partial(front_kernel, count, pieces),
        out_shape=[
            jax.ShapeDtypeStruct((top, tokens), jnp.int32),
            jax.ShapeDtypeStruct((count * PAD, tokens), jnp.float32),
            jax.ShapeDtypeStruct((units, width), jnp.bfloat16),
            jax.ShapeDtypeStruct((slots, units), jnp.bfloat16),
        ]
        + [
            jax.ShapeDtypeStruct((CAP, width + LANES + width * (r not in apart(count))), jnp.bfloat16)
            for r in range(count)
        ]
        + [jax.ShapeDtypeStruct((CAP, width), jnp.bfloat16)] * len(apart(count))
        + [jax.ShapeDtypeStruct((CAP, count * units), jnp.bfloat16)],
        in_specs=[HBM] * 5,
        out_specs=[VMEM] * (5 + count + len(apart(count))),
        scratch_shapes=[
            pltpu.VMEM((top, tokens), jnp.bfloat16),
            pltpu.VMEM((tokens, width), jnp.bfloat16),
            pltpu.VMEM((slots, units), jnp.bfloat16),
            pltpu.VMEM((count * PAD, width), jnp.float32),
            pltpu.SemaphoreType.DMA((5 + 2 * pieces,)),
        ],
        compiler_params=PARAMS,
        cost_estimate=cost(2 * count * PAD * (tokens + units) * width, 2 * (tokens + units) * width),
        name="front",
    )(*in_hbm(expert_ids.T, gate_values.T, grad_out, saved_hidden, down_weight))
    sends, rest = rest[:count], rest[count:]
    products, spread = rest[:-1], rest[-1]

    received = [sends[0]] + [send(sends[r], "expert", r) for r in range(1, count)]
    theirs = [products[0]]
    theirs += [send(x, "expert", r) for r, x in zip(apart(count)[1:], products[1:])]
    first, middle = [0, 1, count - 1], apart(count)[1:]
    early = pl.pallas_call(
        functools.partial(early_kernel, groups),
        out_shape=[jax.ShapeDtypeStruct((CAP, len(first) * share + count * units), jnp.bfloat16)]
        * (groups - 1),
        in_specs=[VMEM] * (1 + len(first)),
        out_specs=[VMEM] * (groups - 1),
        scratch_shapes=[pltpu.VMEM((PAD, width), jnp.float32)],
        compiler_params=PARAMS,
        cost_estimate=cost(len(first) * CAP * width, 4 * len(first) * CAP * width),
        name="early",
    )(spread, *[received[r] for r in first])
    early = [send(x, "dp", r) for r, x in enumerate(early, 1)]

    rows, gate, own, *lates = pl.pallas_call(
        functools.partial(slot_kernel, count, groups),
        out_shape=[
            jax.ShapeDtypeStruct((slots, width), jnp.bfloat16),
            jax.ShapeDtypeStruct((slots, LANES), jnp.float32),
            jax.ShapeDtypeStruct((slots, share + units), jnp.bfloat16),
        ]
        + [jax.ShapeDtypeStruct((CAP, len(middle) * share), jnp.bfloat16)] * (groups - 1),
        in_specs=[VMEM] * (1 + count),
        out_specs=[VMEM] * (2 + groups),
        scratch_shapes=[
            pltpu.VMEM((slots + PAD, width + LANES), jnp.float32),
            pltpu.VMEM((count * PAD, width), jnp.float32),
        ],
        compiler_params=PARAMS,
        cost_estimate=cost(4 * slots * width, 8 * slots * width),
        name="slots",
    )(hidden, *received)

    back = pl.pallas_call(
        functools.partial(back_kernel, count),
        out_shape=jax.ShapeDtypeStruct((slots, LANES), jnp.float32),
        in_specs=[VMEM] * (2 * count - 1 + len(apart(count))),
        out_specs=VMEM,
        scratch_shapes=[pltpu.VMEM((slots + PAD, LANES), jnp.float32)],
        compiler_params=PARAMS,
        cost_estimate=cost(*AFTER_WAIT),
        name="backs",
    )(*sends, *received[1:], *theirs)

    lates = [send(x, "dp", r) for r, x in enumerate(lates, 1)]
    backs = [back] + [send(back, "tensor", r) for r in reversed(range(1, tensors))]

    split = width // 8
    upstream, *rest = pl.pallas_call(
        functools.partial(upstream_kernel, count, split),
        out_shape=[jax.ShapeDtypeStruct((slots, units), jnp.float32)]
        + [jax.ShapeDtypeStruct((slots + PAD, share), jnp.float32)] * (groups - 1)
        + [jax.ShapeDtypeStruct((slots, units), jnp.bfloat16)] * (groups - 1),
        in_specs=[VMEM] * (1 + groups),
        out_specs=[VMEM] * (2 * groups - 1),
        scratch_shapes=[
            pltpu.VMEM((slots + PAD, units), jnp.float32),
            pltpu.VMEM((PAD, share), jnp.float32),
        ],
        compiler_params=PARAMS,
        cost_estimate=cost(2 * slots * units * split, 2 * units * split),
        name="upstream",
    )(rows, weight, *early)
    wides, hiddens = rest[: groups - 1], rest[groups - 1 :]

    hidden_grad, down_grad, match = pl.pallas_call(
        functools.partial(down_kernel, count, groups, pieces, split),
        out_shape=[
            jax.ShapeDtypeStruct(saved_hidden.shape, jnp.bfloat16),
            jax.ShapeDtypeStruct((1, units, share), jnp.float32),
            jax.ShapeDtypeStruct(match.shape, jnp.float32),
        ],
        in_specs=[VMEM] * (3 + 3 * groups),
        out_specs=[HBM, HBM, VMEM],
        scratch_shapes=[
            pltpu.VMEM((slots, units), jnp.bfloat16),
            pltpu.VMEM((units, share), jnp.float32),
            pltpu.VMEM((slots + PAD, share), jnp.float32),
            pltpu.SemaphoreType.DMA((pieces + 1,)),
        ],
        compiler_params=PARAMS,
        cost_estimate=cost(2 * slots * units * share, 4 * units * share),
        name="down",
    )(upstream, rows, gate, weight, match, own, *wides, *lates, *hiddens)

    gate_grad = pl.pallas_call(
        functools.partial(gate_kernel, count),
        out_shape=jax.ShapeDtypeStruct(ids.shape, jnp.float32),
        in_specs=[VMEM] * (2 + tensors),
        out_specs=VMEM,
        compiler_params=PARAMS,
        cost_estimate=cost(slots * tokens, 4 * slots * tokens),
        name="gates",
    )(ids, match, *backs)
    return (gate_grad.T, hidden_grad, down_grad)


def solution(mesh):
    return jax.shard_map(
        on_device,
        mesh=mesh,
        in_specs=(
            P(("dp", "expert"), None),
            P(("dp", "expert"), None),
            P(("dp", "expert"), None),
            P("dp", "expert", None, "tensor"),
            P("expert", "tensor", None),
        ),
        out_specs=(
            P(("dp", "expert"), None),
            P("dp", "expert", None, "tensor"),
            P("expert", "tensor", "dp"),
        ),
        check_vma=False,
    )
```

```python
import functools

import jax
import jax.numpy as jnp
from jax import lax
from jax.experimental import pallas as pl
from jax.experimental.pallas import tpu as pltpu
from jax.sharding import PartitionSpec as P

CAP = 4
LANES = 128
AFTER_WAIT = (10**9, 10**7)
WIDE = 1024
PAD = 8
VMEM = pl.BlockSpec(memory_space=pltpu.VMEM)
HBM = pl.BlockSpec(memory_space=pltpu.HBM)
PARAMS = pltpu.CompilerParams(vmem_limit_bytes=32 * 2**20)


def dot(a, b, dims):
    return lax.dot_general(a, b, (dims, ((), ())), preferred_element_type=jnp.float32)


def in_hbm(*arrays):
    return [pltpu.with_memory_space_constraint(x, pltpu.HBM) for x in arrays]


def cost(flops, nbytes):
    return pl.CostEstimate(flops=flops, bytes_accessed=nbytes, transcendentals=0)


def paired(size):
    return size & (size - 1) == 0


def target(me, step, size):
    if paired(size):
        return me ^ ((size - step) % size)
    after = me + step
    return after % size if isinstance(me, int) else jnp.where(after >= size, after - size, after)


def source(me, step, size):
    if paired(size):
        return target(me, step, size)
    before = me - step
    return before % size if isinstance(me, int) else jnp.where(before < 0, before + size, before)


def reply(step, size):
    return step if paired(size) else -step % size


def apart(size):
    return [r for r in range(size) if r not in (1, size - 1)]


def send(value, axis, step, give=target):
    size = lax.axis_size(axis)
    return lax.ppermute(value, axis, [(i, give(i, step, size)) for i in range(size)])


def front_kernel(count, groups, pieces, *refs):
    ids_hbm, gates_hbm, grad_hbm, hidden_hbm, weight_hbm = refs[:5]
    ids_ref, match_ref, weight_ref, hidden_ref = refs[5:9]
    sends = refs[9 : 9 + count]
    products = dict(zip(apart(count), refs[9 + count :]))
    early = refs[-4 - groups : -5]
    gates_ref, grad_ref, saved_ref, total_ref, sems = refs[-5:]
    units, width = weight_ref.shape
    top, tokens = ids_ref.shape
    pairs = [(ids_hbm, ids_ref), (gates_hbm, gates_ref), (hidden_hbm.at[0, 0], saved_ref)]
    half = tokens // 2
    for p in range(2):
        part = pl.ds(p * half, half)
        pairs.append((grad_hbm.at[part], grad_ref.at[part]))
    half = units // (2 * pieces)
    for p in range(2 * pieces):
        part = pl.ds(p * half, half)
        pairs.append((weight_hbm.at[0, part], weight_ref.at[part]))
    copies = [pltpu.make_async_copy(*pair, sems.at[n]) for n, pair in enumerate(pairs)]
    for copy in copies:
        copy.start()
    me = lax.axis_index("expert")
    rows = count * PAD
    row = lax.broadcasted_iota(jnp.int32, (rows, tokens), 0)
    expert = target(me, row // PAD, count)
    place = row % PAD
    earlier = lax.broadcasted_iota(jnp.int32, (tokens, tokens), 0)
    later = lax.broadcasted_iota(jnp.int32, (tokens, tokens), 1)
    order = (earlier < later).astype(jnp.bfloat16)
    for copy in copies[:3]:
        copy.wait()
    ids = ids_ref[...]
    gates = gates_ref[...].astype(jnp.float32)
    member = jnp.zeros((rows, tokens), jnp.float32)
    gate = jnp.zeros((rows, tokens), jnp.float32)
    for k in range(top):
        hit = ids[k : k + 1, :] == expert
        member = jnp.where(hit, 1.0, member)
        gate = jnp.where(hit, gates[k : k + 1, :], gate)
    before = dot(member.astype(jnp.bfloat16), order, ((1,), (0,)))
    taken = (member > 0) & (before == place.astype(jnp.float32)) & (place < CAP)
    match = taken.astype(jnp.float32)
    match_ref[...] = match
    slot_gate = jnp.sum(match * gate, axis=1, keepdims=True)
    match = match.astype(jnp.bfloat16)

    slots = count * CAP
    saved = saved_ref[...]
    hidden_ref[...] = dot(slot_order(count), saved, ((1,), (0,))).astype(jnp.bfloat16)
    spread = dot(slot_order(count, PAD), saved, ((1,), (0,)))
    here = lax.broadcasted_iota(jnp.int32, (rows, slots), 0)
    there = lax.broadcasted_iota(jnp.int32, (rows, slots), 1)
    chosen = (here % PAD < CAP) & (there == target(me, here // PAD, count) * CAP + here % PAD)
    hidden = dot(chosen.astype(jnp.bfloat16), saved, ((1,), (0,))).astype(jnp.bfloat16)

    for copy in copies[3:5]:
        copy.wait()
    for r in range(count):
        part = slice(r * PAD, r * PAD + CAP)
        gate = jnp.broadcast_to(slot_gate[part], (CAP, LANES)).astype(jnp.bfloat16)
        sends[r][:, width : width + LANES] = gate
    wide = min(width, WIDE)
    for begin in range(0, width, wide):
        part = slice(begin, begin + wide)
        picked = dot(match, grad_ref[:, part], ((1,), (0,)))
        for r in range(count):
            sends[r][:, part] = picked[r * PAD : r * PAD + CAP].astype(jnp.bfloat16)
        total_ref[:PAD, part] = picked[:PAD]
    share = width // groups
    group = lax.axis_index("dp")
    for r, early_ref in enumerate(early, 1):
        begin = pl.multiple_of(target(group, r, groups) * share, share)
        weighted = slot_gate[:CAP] * total_ref[:CAP, pl.ds(begin, share)]
        early_ref[:, :share] = weighted.astype(jnp.bfloat16)
        for k in range(count):
            part = slice(share + k * units, share + (k + 1) * units)
            early_ref[:, part] = spread[k * PAD : k * PAD + CAP].astype(jnp.bfloat16)
    block = units // pieces
    for p in range(pieces):
        for copy in copies[5 + 2 * p : 7 + 2 * p]:
            copy.wait()
        rows = slice(p * block, (p + 1) * block)
        for begin in range(0, width, wide):
            part = slice(begin, begin + wide)
            term = dot(hidden[:, rows], weight_ref[rows, part], ((1,), (0,)))
            if p > 0:
                term = total_ref[:, part] + term
            if p < pieces - 1:
                total_ref[:, part] = term
                continue
            for r in range(count):
                product = term[r * PAD : r * PAD + CAP].astype(jnp.bfloat16)
                if r in products:
                    products[r][:, part] = product
                else:
                    joint = slice(width + LANES + begin, width + LANES + begin + wide)
                    sends[r][:, joint] = product


def slot_order(count, lines=CAP):
    me = lax.axis_index("expert")
    here = lax.broadcasted_iota(jnp.int32, (count * lines, count * CAP), 0)
    saved = lax.broadcasted_iota(jnp.int32, (count * lines, count * CAP), 1)
    place = here % lines
    block = source(me, here // lines, count)
    return ((saved == block * CAP + place) & (place < CAP)).astype(jnp.bfloat16)


def late_kernel(count, groups, *refs):
    received, lates, weighted_ref = refs[: count - 1], refs[count - 1 : -1], refs[-1]
    width = weighted_ref.shape[1]
    share = width // groups
    me = lax.axis_index("dp")
    for k in range(1, count):
        row = received[k - 1][:, : width + LANES].astype(jnp.float32)
        part = slice(k * PAD, k * PAD + CAP)
        weighted_ref[part, :] = row[:, width : width + 1] * row[:, :width]
        for r, late_ref in enumerate(lates, 1):
            begin = pl.multiple_of(target(me, r, groups) * share, share)
            late = weighted_ref[part, pl.ds(begin, share)].astype(jnp.bfloat16)
            late_ref[:, (k - 1) * share : k * share] = late


def slot_kernel(count, groups, hidden_ref, *refs):
    received = refs[:count]
    rows_ref, gate_ref, own_ref, wide_ref = refs[count:]
    width = rows_ref.shape[1]
    share = width // groups
    slots = count * CAP
    for r in range(count):
        row = received[r][:, : width + LANES].astype(jnp.float32)
        wide_ref[r * CAP : (r + 1) * CAP, :] = row
    gate = wide_ref[:slots, width:]
    gate_ref[...] = gate
    rows_ref[...] = wide_ref[:slots, :width].astype(jnp.bfloat16)
    begin = pl.multiple_of(lax.axis_index("dp") * share, share)
    weighted = gate[:, :1] * wide_ref[:slots, pl.ds(begin, share)]
    own_ref[:, :share] = weighted.astype(jnp.bfloat16)
    own_ref[:, share:] = hidden_ref[...]


def back_kernel(count, groups, *refs):
    sent, refs = refs[:count], refs[count:]
    received, refs = dict(enumerate(refs[: count - 1], 1)), refs[count - 1 :]
    received.update(zip(apart(count), refs))
    refs = refs[len(apart(count)) :]
    early, refs = refs[: groups - 1], refs[groups - 1 :]
    out_ref, hiddens = refs[0], refs[1:groups]
    back_ref, units_ref = refs[groups:]
    width = received[0].shape[1]
    for r in range(count):
        ref = received[reply(r, count)]
        theirs = ref[:, ref.shape[1] - width :].astype(jnp.float32)
        mine = sent[r][:, :width].astype(jnp.float32)
        back = jnp.sum(mine * theirs, axis=1, keepdims=True)
        back_ref[r * CAP : (r + 1) * CAP, :] = jnp.broadcast_to(back, (CAP, LANES))
    slots, units = count * CAP, units_ref.shape[1]
    out_ref[...] = back_ref[:slots, :]
    for early_ref, hidden_ref in zip(early, hiddens):
        share = early_ref.shape[1] - count * units
        for k in range(count):
            part = early_ref[:, share + k * units : share + (k + 1) * units]
            units_ref[k * CAP : (k + 1) * CAP, :] = part.astype(jnp.float32)
        hidden_ref[...] = units_ref[:slots, :].astype(jnp.bfloat16)


def upstream_part(rows_ref, weight_ref, begin, end):
    return dot(rows_ref[:, begin:end], weight_ref[:, begin:end], ((1,), (1,)))


def upstream_kernel(split, rows_ref, weight_ref, out_ref):
    out_ref[...] = upstream_part(rows_ref, weight_ref, 0, split)


def down_kernel(count, groups, pieces, split, part_ref, rows_ref, gate_ref, weight_ref, match_ref, *refs):
    others = groups - 1
    own_ref, early, refs = refs[0], refs[1:groups], refs[groups:]
    lates, hiddens, refs = refs[:others], refs[others : 2 * others], refs[2 * others :]
    hidden_hbm, down_hbm, match_out, hidden_out, down_out, wide_ref, sems = refs
    units, share = down_out.shape
    block = units // pieces
    rows, hidden = [own_ref[:, :share]], [own_ref[:, share:]]
    for early_ref, late_ref, hidden_ref in zip(early, lates, hiddens):
        wide_ref[:CAP, :] = early_ref[:, :share].astype(jnp.float32)
        for k in range(1, count):
            late = late_ref[:, (k - 1) * share : k * share].astype(jnp.float32)
            wide_ref[k * CAP : (k + 1) * CAP, :] = late
        rows.append(wide_ref[: count * CAP, :].astype(jnp.bfloat16))
        hidden.append(hidden_ref[...])
    rows, hidden = jnp.concatenate(rows, axis=0), jnp.concatenate(hidden, axis=0)
    copies = []

    def write(values, destination):
        copies.append(pltpu.make_async_copy(values, destination, sems.at[len(copies)]))
        copies[-1].start()

    cuts = [0, block // 2, *range(block, units + 1, block)]
    for start, end in zip(cuts, cuts[1:]):
        part = slice(start, end)
        down_out[part, :] = dot(hidden[:, part], rows, ((0,), (0,)))
        part = pl.ds(start, end - start)
        write(down_out.at[part], down_hbm.at[0, part])
    upstream = part_ref[...] + upstream_part(rows_ref, weight_ref, split, weight_ref.shape[1])
    scaled = (gate_ref[:, :1] * upstream).astype(jnp.bfloat16)
    hidden_out[...] = dot(slot_order(count), scaled, ((0,), (0,))).astype(jnp.bfloat16)
    write(hidden_out, hidden_hbm.at[0, 0])
    match_out[...] = match_ref[...]
    for copy in copies:
        copy.wait()


def gate_kernel(count, ids_ref, match_ref, *refs):
    backs, out_ref = refs[:-1], refs[-1]
    me = lax.axis_index("expert")
    ids = ids_ref[...]
    back = backs[0][...]
    for ref in backs[1:]:
        back = back + ref[...]
    total = jnp.zeros(out_ref.shape, jnp.float32)
    for r in range(count):
        value = back[r * CAP : (r + 1) * CAP, :]
        match = match_ref[r * PAD : r * PAD + CAP, :]
        chosen = jnp.sum(jnp.where(match > 0, value, 0.0), axis=0, keepdims=True)
        total = total + jnp.where(ids == target(me, r, count), chosen, 0.0)
    out_ref[...] = total


def on_device(grad_out, expert_ids, gate_values, saved_hidden, down_weight):
    count = lax.axis_size("expert")
    groups = lax.axis_size("dp")
    tensors = lax.axis_size("tensor")
    tokens, width = grad_out.shape
    top = expert_ids.shape[1]
    units = down_weight.shape[1]
    slots = count * CAP
    share = width // groups
    pieces = units // LANES

    ids, match, weight, hidden, *rest = pl.pallas_call(
        functools.partial(front_kernel, count, groups, pieces),
        out_shape=[
            jax.ShapeDtypeStruct((top, tokens), jnp.int32),
            jax.ShapeDtypeStruct((count * PAD, tokens), jnp.float32),
            jax.ShapeDtypeStruct((units, width), jnp.bfloat16),
            jax.ShapeDtypeStruct((slots, units), jnp.bfloat16),
        ]
        + [
            jax.ShapeDtypeStruct((CAP, width + LANES + width * (r not in apart(count))), jnp.bfloat16)
            for r in range(count)
        ]
        + [jax.ShapeDtypeStruct((CAP, width), jnp.bfloat16)] * len(apart(count))
        + [jax.ShapeDtypeStruct((CAP, share + count * units), jnp.bfloat16)] * (groups - 1),
        in_specs=[HBM] * 5,
        out_specs=[VMEM] * (3 + count + len(apart(count)) + groups),
        scratch_shapes=[
            pltpu.VMEM((top, tokens), jnp.bfloat16),
            pltpu.VMEM((tokens, width), jnp.bfloat16),
            pltpu.VMEM((slots, units), jnp.bfloat16),
            pltpu.VMEM((count * PAD, width), jnp.float32),
            pltpu.SemaphoreType.DMA((5 + 2 * pieces,)),
        ],
        compiler_params=PARAMS,
        cost_estimate=cost(2 * count * PAD * (tokens + units) * width, 2 * (tokens + units) * width),
        name="front",
    )(*in_hbm(expert_ids.T, gate_values.T, grad_out, saved_hidden, down_weight))
    sends, rest = rest[:count], rest[count:]
    products, early = rest[: len(apart(count))], rest[len(apart(count)) :]

    received = [sends[0]] + [send(sends[r], "expert", r) for r in range(1, count)]
    theirs = [products[0]]
    theirs += [send(x, "expert", r) for r, x in zip(apart(count)[1:], products[1:])]
    early = [send(x, "dp", r) for r, x in enumerate(early, 1)]

    lates = pl.pallas_call(
        functools.partial(late_kernel, count, groups),
        out_shape=[jax.ShapeDtypeStruct((CAP, (count - 1) * share), jnp.bfloat16)] * (groups - 1),
        in_specs=[VMEM] * (count - 1),
        out_specs=[VMEM] * (groups - 1),
        scratch_shapes=[pltpu.VMEM((count * PAD, width), jnp.float32)],
        compiler_params=PARAMS,
        cost_estimate=cost(2 * slots * width, 4 * slots * width),
        name="late",
    )(*received[1:])

    rows, gate, own = pl.pallas_call(
        functools.partial(slot_kernel, count, groups),
        out_shape=[
            jax.ShapeDtypeStruct((slots, width), jnp.bfloat16),
            jax.ShapeDtypeStruct((slots, LANES), jnp.float32),
            jax.ShapeDtypeStruct((slots, share + units), jnp.bfloat16),
        ],
        in_specs=[VMEM] * (1 + count),
        out_specs=[VMEM] * 3,
        scratch_shapes=[pltpu.VMEM((slots + PAD, width + LANES), jnp.float32)],
        compiler_params=PARAMS,
        cost_estimate=cost(4 * slots * width, 8 * slots * width),
        name="slots",
    )(hidden, *received)

    back, *hiddens = pl.pallas_call(
        functools.partial(back_kernel, count, groups),
        out_shape=[jax.ShapeDtypeStruct((slots, LANES), jnp.float32)]
        + [jax.ShapeDtypeStruct((slots, units), jnp.bfloat16)] * (groups - 1),
        in_specs=[VMEM] * (2 * count - 2 + len(apart(count)) + groups),
        out_specs=[VMEM] * groups,
        scratch_shapes=[
            pltpu.VMEM((slots + PAD, LANES), jnp.float32),
            pltpu.VMEM((slots + PAD, units), jnp.float32),
        ],
        compiler_params=PARAMS,
        cost_estimate=cost(*AFTER_WAIT),
        name="backs",
    )(*sends, *received[1:], *theirs, *early)

    lates = [send(x, "dp", r) for r, x in enumerate(lates, 1)]
    backs = [back] + [send(back, "tensor", r) for r in range(1, tensors)]

    split = width * 3 // 8
    upstream = pl.pallas_call(
        functools.partial(upstream_kernel, split),
        out_shape=jax.ShapeDtypeStruct((slots, units), jnp.float32),
        in_specs=[VMEM] * 2,
        out_specs=VMEM,
        compiler_params=PARAMS,
        cost_estimate=cost(2 * slots * units * split, 2 * units * split),
        name="upstream",
    )(rows, weight)

    hidden_grad, down_grad, match = pl.pallas_call(
        functools.partial(down_kernel, count, groups, pieces, split),
        out_shape=[
            jax.ShapeDtypeStruct(saved_hidden.shape, jnp.bfloat16),
            jax.ShapeDtypeStruct((1, units, share), jnp.float32),
            jax.ShapeDtypeStruct(match.shape, jnp.float32),
        ],
        in_specs=[VMEM] * (3 + 3 * groups),
        out_specs=[HBM, HBM, VMEM],
        scratch_shapes=[
            pltpu.VMEM((slots, units), jnp.bfloat16),
            pltpu.VMEM((units, share), jnp.float32),
            pltpu.VMEM((slots + PAD, share), jnp.float32),
            pltpu.SemaphoreType.DMA((pieces + 2,)),
        ],
        compiler_params=PARAMS,
        cost_estimate=cost(2 * slots * units * share, 4 * units * share),
        name="down",
    )(upstream, rows, gate, weight, match, own, *early, *lates, *hiddens)

    gate_grad = pl.pallas_call(
        functools.partial(gate_kernel, count),
        out_shape=jax.ShapeDtypeStruct(ids.shape, jnp.float32),
        in_specs=[VMEM] * (2 + tensors),
        out_specs=VMEM,
        compiler_params=PARAMS,
        cost_estimate=cost(slots * tokens, 4 * slots * tokens),
        name="gates",
    )(ids, match, *backs)
    return (gate_grad.T, hidden_grad, down_grad)


def solution(mesh):
    return jax.shard_map(
        on_device,
        mesh=mesh,
        in_specs=(
            P(("dp", "expert"), None),
            P(("dp", "expert"), None),
            P(("dp", "expert"), None),
            P("dp", "expert", None, "tensor"),
            P("expert", "tensor", None),
        ),
        out_specs=(
            P(("dp", "expert"), None),
            P("dp", "expert", None, "tensor"),
            P("expert", "tensor", "dp"),
        ),
        check_vma=False,
    )
```

```python
import functools

import jax
import jax.numpy as jnp
from jax import lax
from jax.experimental import pallas as pl
from jax.experimental.pallas import tpu as pltpu
from jax.sharding import PartitionSpec as P

CAP = 4
LANES = 128
AFTER_WAIT = (10**9, 10**7)
WIDE = 1024
PAD = 8
VMEM = pl.BlockSpec(memory_space=pltpu.VMEM)
HBM = pl.BlockSpec(memory_space=pltpu.HBM)
PARAMS = pltpu.CompilerParams(vmem_limit_bytes=32 * 2**20)


def dot(a, b, dims):
    return lax.dot_general(a, b, (dims, ((), ())), preferred_element_type=jnp.float32)


def in_hbm(*arrays):
    return [pltpu.with_memory_space_constraint(x, pltpu.HBM) for x in arrays]


def cost(flops, nbytes):
    return pl.CostEstimate(flops=flops, bytes_accessed=nbytes, transcendentals=0)


def paired(size):
    return size & (size - 1) == 0


def target(me, step, size):
    if paired(size):
        return me ^ ((size - step) % size)
    after = me + step
    return after % size if isinstance(me, int) else jnp.where(after >= size, after - size, after)


def source(me, step, size):
    if paired(size):
        return target(me, step, size)
    before = me - step
    return before % size if isinstance(me, int) else jnp.where(before < 0, before + size, before)


def reply(step, size):
    return step if paired(size) else -step % size


def apart(size):
    return [r for r in range(size) if r not in (1, size - 1)]


def send(value, axis, step, give=target):
    size = lax.axis_size(axis)
    return lax.ppermute(value, axis, [(i, give(i, step, size)) for i in range(size)])


def front_kernel(count, groups, pieces, *refs):
    ids_hbm, gates_hbm, grad_hbm, hidden_hbm, weight_hbm = refs[:5]
    hits_ref, match_ref, weight_ref, hidden_ref = refs[5:9]
    sends = refs[9 : 9 + count]
    products = dict(zip(apart(count), refs[9 + count :]))
    early = refs[-5 - groups : -6]
    ids_ref, gates_ref, grad_ref, saved_ref, total_ref, sems = refs[-6:]
    units, width = weight_ref.shape
    top, tokens = ids_ref.shape
    pairs = [(ids_hbm, ids_ref), (gates_hbm, gates_ref), (hidden_hbm.at[0, 0], saved_ref)]
    half = tokens // 2
    for p in range(2):
        part = pl.ds(p * half, half)
        pairs.append((grad_hbm.at[part], grad_ref.at[part]))
    half = units // (2 * pieces)
    for p in range(2 * pieces):
        part = pl.ds(p * half, half)
        pairs.append((weight_hbm.at[0, part], weight_ref.at[part]))
    copies = [pltpu.make_async_copy(*pair, sems.at[n]) for n, pair in enumerate(pairs)]
    for copy in copies:
        copy.start()
    me = lax.axis_index("expert")
    rows = count * PAD
    row = lax.broadcasted_iota(jnp.int32, (rows, tokens), 0)
    expert = target(me, row // PAD, count)
    place = row % PAD
    earlier = lax.broadcasted_iota(jnp.int32, (tokens, tokens), 0)
    later = lax.broadcasted_iota(jnp.int32, (tokens, tokens), 1)
    order = (earlier < later).astype(jnp.bfloat16)
    for copy in copies[:3]:
        copy.wait()
    ids = ids_ref[...]
    gates = gates_ref[...].astype(jnp.float32)
    member = jnp.zeros((rows, tokens), jnp.float32)
    gate = jnp.zeros((rows, tokens), jnp.float32)
    for k in range(top):
        hit = ids[k : k + 1, :] == expert
        member = jnp.where(hit, 1.0, member)
        gate = jnp.where(hit, gates[k : k + 1, :], gate)
    for r in range(count):
        hits_ref[r] = (ids == target(me, r, count)).astype(jnp.float32)
    before = dot(member.astype(jnp.bfloat16), order, ((1,), (0,)))
    taken = (member > 0) & (before == place.astype(jnp.float32)) & (place < CAP)
    match = taken.astype(jnp.float32)
    match_ref[...] = match
    slot_gate = jnp.sum(match * gate, axis=1, keepdims=True)
    match = match.astype(jnp.bfloat16)

    slots = count * CAP
    saved = saved_ref[...]
    hidden_ref[...] = dot(slot_order(count), saved, ((1,), (0,))).astype(jnp.bfloat16)
    spread = dot(slot_order(count, PAD), saved, ((1,), (0,)))
    here = lax.broadcasted_iota(jnp.int32, (rows, slots), 0)
    there = lax.broadcasted_iota(jnp.int32, (rows, slots), 1)
    chosen = (here % PAD < CAP) & (there == target(me, here // PAD, count) * CAP + here % PAD)
    hidden = dot(chosen.astype(jnp.bfloat16), saved, ((1,), (0,))).astype(jnp.bfloat16)

    for copy in copies[3:5]:
        copy.wait()
    for r in range(count):
        part = slice(r * PAD, r * PAD + CAP)
        gate = jnp.broadcast_to(slot_gate[part], (CAP, LANES)).astype(jnp.bfloat16)
        sends[r][:, width : width + LANES] = gate
    wide = min(width, WIDE)
    for begin in range(0, width, wide):
        part = slice(begin, begin + wide)
        picked = dot(match, grad_ref[:, part], ((1,), (0,)))
        for r in range(count):
            sends[r][:, part] = picked[r * PAD : r * PAD + CAP].astype(jnp.bfloat16)
        total_ref[:PAD, part] = picked[:PAD]
    share = width // groups
    group = lax.axis_index("dp")
    for r, early_ref in enumerate(early, 1):
        begin = pl.multiple_of(target(group, r, groups) * share, share)
        weighted = slot_gate[:CAP] * total_ref[:CAP, pl.ds(begin, share)]
        early_ref[:, :share] = weighted.astype(jnp.bfloat16)
        for k in range(count):
            part = slice(share + k * units, share + (k + 1) * units)
            early_ref[:, part] = spread[k * PAD : k * PAD + CAP].astype(jnp.bfloat16)
    block = units // pieces
    for p in range(pieces):
        for copy in copies[5 + 2 * p : 7 + 2 * p]:
            copy.wait()
        rows = slice(p * block, (p + 1) * block)
        for begin in range(0, width, wide):
            part = slice(begin, begin + wide)
            term = dot(hidden[:, rows], weight_ref[rows, part], ((1,), (0,)))
            if p > 0:
                term = total_ref[:, part] + term
            if p < pieces - 1:
                total_ref[:, part] = term
                continue
            for r in range(count):
                product = term[r * PAD : r * PAD + CAP].astype(jnp.bfloat16)
                if r in products:
                    products[r][:, part] = product
                else:
                    joint = slice(width + LANES + begin, width + LANES + begin + wide)
                    sends[r][:, joint] = product


def slot_order(count, lines=CAP):
    me = lax.axis_index("expert")
    here = lax.broadcasted_iota(jnp.int32, (count * lines, count * CAP), 0)
    saved = lax.broadcasted_iota(jnp.int32, (count * lines, count * CAP), 1)
    place = here % lines
    block = source(me, here // lines, count)
    return ((saved == block * CAP + place) & (place < CAP)).astype(jnp.bfloat16)


def late_kernel(count, groups, *refs):
    received, lates, weighted_ref = refs[: count - 1], refs[count - 1 : -1], refs[-1]
    width = weighted_ref.shape[1]
    share = width // groups
    me = lax.axis_index("dp")
    for k in range(1, count):
        row = received[k - 1][:, : width + LANES].astype(jnp.float32)
        part = slice(k * PAD, k * PAD + CAP)
        weighted_ref[part, :] = row[:, width : width + 1] * row[:, :width]
        for r, late_ref in enumerate(lates, 1):
            begin = pl.multiple_of(target(me, r, groups) * share, share)
            late = weighted_ref[part, pl.ds(begin, share)].astype(jnp.bfloat16)
            late_ref[:, (k - 1) * share : k * share] = late


def slot_kernel(count, groups, hidden_ref, *refs):
    received = refs[:count]
    rows_ref, gate_ref, own_ref, wide_ref = refs[count:]
    width = rows_ref.shape[1]
    share = width // groups
    slots = count * CAP
    for r in range(count):
        row = received[r][:, : width + LANES].astype(jnp.float32)
        wide_ref[r * CAP : (r + 1) * CAP, :] = row
    gate = wide_ref[:slots, width:]
    gate_ref[...] = gate
    rows_ref[...] = wide_ref[:slots, :width].astype(jnp.bfloat16)
    begin = pl.multiple_of(lax.axis_index("dp") * share, share)
    weighted = gate[:, :1] * wide_ref[:slots, pl.ds(begin, share)]
    own_ref[:, :share] = weighted.astype(jnp.bfloat16)
    own_ref[:, share:] = hidden_ref[...]


def back_kernel(count, groups, *refs):
    sent, refs = refs[:count], refs[count:]
    received, refs = dict(enumerate(refs[: count - 1], 1)), refs[count - 1 :]
    received.update(zip(apart(count), refs))
    refs = refs[len(apart(count)) :]
    early, refs = refs[: groups - 1], refs[groups - 1 :]
    out_ref, hiddens = refs[0], refs[1:groups]
    back_ref, units_ref = refs[groups:]
    width = received[0].shape[1]
    for r in range(count):
        ref = received[reply(r, count)]
        theirs = ref[:, ref.shape[1] - width :].astype(jnp.float32)
        mine = sent[r][:, :width].astype(jnp.float32)
        back = jnp.sum(mine * theirs, axis=1, keepdims=True)
        back_ref[r * CAP : (r + 1) * CAP, :] = jnp.broadcast_to(back, (CAP, LANES))
    slots, units = count * CAP, units_ref.shape[1]
    out_ref[...] = back_ref[:slots, :]
    for early_ref, hidden_ref in zip(early, hiddens):
        share = early_ref.shape[1] - count * units
        for k in range(count):
            part = early_ref[:, share + k * units : share + (k + 1) * units]
            units_ref[k * CAP : (k + 1) * CAP, :] = part.astype(jnp.float32)
        hidden_ref[...] = units_ref[:slots, :].astype(jnp.bfloat16)


def upstream_part(rows_ref, weight_ref, begin, end):
    return dot(rows_ref[:, begin:end], weight_ref[:, begin:end], ((1,), (1,)))


def upstream_kernel(split, rows_ref, weight_ref, out_ref):
    out_ref[...] = upstream_part(rows_ref, weight_ref, 0, split)


def down_kernel(count, groups, pieces, split, part_ref, rows_ref, gate_ref, weight_ref, match_ref, *refs):
    others = groups - 1
    own_ref, early, refs = refs[0], refs[1:groups], refs[groups:]
    lates, hiddens, refs = refs[:others], refs[others : 2 * others], refs[2 * others :]
    hidden_hbm, down_hbm, match_out, hidden_out, down_out, wide_ref, sems = refs
    units, share = down_out.shape
    block = units // pieces
    rows, hidden = [own_ref[:, :share]], [own_ref[:, share:]]
    for early_ref, late_ref, hidden_ref in zip(early, lates, hiddens):
        wide_ref[:CAP, :] = early_ref[:, :share].astype(jnp.float32)
        for k in range(1, count):
            late = late_ref[:, (k - 1) * share : k * share].astype(jnp.float32)
            wide_ref[k * CAP : (k + 1) * CAP, :] = late
        rows.append(wide_ref[: count * CAP, :].astype(jnp.bfloat16))
        hidden.append(hidden_ref[...])
    rows, hidden = jnp.concatenate(rows, axis=0), jnp.concatenate(hidden, axis=0)
    copies = []

    def write(values, destination):
        copies.append(pltpu.make_async_copy(values, destination, sems.at[len(copies)]))
        copies[-1].start()

    cuts = [0, block // 2, *range(block, units + 1, block)]
    for start, end in zip(cuts, cuts[1:]):
        part = slice(start, end)
        down_out[part, :] = dot(hidden[:, part], rows, ((0,), (0,)))
        part = pl.ds(start, end - start)
        write(down_out.at[part], down_hbm.at[0, part])
    upstream = part_ref[...] + upstream_part(rows_ref, weight_ref, split, weight_ref.shape[1])
    scaled = (gate_ref[:, :1] * upstream).astype(jnp.bfloat16)
    hidden_out[...] = dot(slot_order(count), scaled, ((0,), (0,))).astype(jnp.bfloat16)
    write(hidden_out, hidden_hbm.at[0, 0])
    match_out[...] = match_ref[...]
    for copy in copies:
        copy.wait()


def on_device(grad_out, expert_ids, gate_values, saved_hidden, down_weight):
    count = lax.axis_size("expert")
    groups = lax.axis_size("dp")
    tensors = lax.axis_size("tensor")
    tokens, width = grad_out.shape
    top = expert_ids.shape[1]
    units = down_weight.shape[1]
    slots = count * CAP
    share = width // groups
    pieces = units // LANES

    hits, match, weight, hidden, *rest = pl.pallas_call(
        functools.partial(front_kernel, count, groups, pieces),
        out_shape=[
            jax.ShapeDtypeStruct((count, top, tokens), jnp.float32),
            jax.ShapeDtypeStruct((count * PAD, tokens), jnp.float32),
            jax.ShapeDtypeStruct((units, width), jnp.bfloat16),
            jax.ShapeDtypeStruct((slots, units), jnp.bfloat16),
        ]
        + [
            jax.ShapeDtypeStruct((CAP, width + LANES + width * (r not in apart(count))), jnp.bfloat16)
            for r in range(count)
        ]
        + [jax.ShapeDtypeStruct((CAP, width), jnp.bfloat16)] * len(apart(count))
        + [jax.ShapeDtypeStruct((CAP, share + count * units), jnp.bfloat16)] * (groups - 1),
        in_specs=[HBM] * 5,
        out_specs=[VMEM] * (3 + count + len(apart(count)) + groups),
        scratch_shapes=[
            pltpu.VMEM((top, tokens), jnp.int32),
            pltpu.VMEM((top, tokens), jnp.bfloat16),
            pltpu.VMEM((tokens, width), jnp.bfloat16),
            pltpu.VMEM((slots, units), jnp.bfloat16),
            pltpu.VMEM((count * PAD, width), jnp.float32),
            pltpu.SemaphoreType.DMA((5 + 2 * pieces,)),
        ],
        compiler_params=PARAMS,
        cost_estimate=cost(2 * count * PAD * (tokens + units) * width, 2 * (tokens + units) * width),
        name="front",
    )(*in_hbm(expert_ids.T, gate_values.T, grad_out, saved_hidden, down_weight))
    sends, rest = rest[:count], rest[count:]
    products, early = rest[: len(apart(count))], rest[len(apart(count)) :]

    received = [sends[0]] + [send(sends[r], "expert", r) for r in range(1, count)]
    theirs = [products[0]]
    theirs += [send(x, "expert", r) for r, x in zip(apart(count)[1:], products[1:])]
    early = [send(x, "dp", r) for r, x in enumerate(early, 1)]

    lates = pl.pallas_call(
        functools.partial(late_kernel, count, groups),
        out_shape=[jax.ShapeDtypeStruct((CAP, (count - 1) * share), jnp.bfloat16)] * (groups - 1),
        in_specs=[VMEM] * (count - 1),
        out_specs=[VMEM] * (groups - 1),
        scratch_shapes=[pltpu.VMEM((count * PAD, width), jnp.float32)],
        compiler_params=PARAMS,
        cost_estimate=cost(2 * slots * width, 4 * slots * width),
        name="late",
    )(*received[1:])

    rows, gate, own = pl.pallas_call(
        functools.partial(slot_kernel, count, groups),
        out_shape=[
            jax.ShapeDtypeStruct((slots, width), jnp.bfloat16),
            jax.ShapeDtypeStruct((slots, LANES), jnp.float32),
            jax.ShapeDtypeStruct((slots, share + units), jnp.bfloat16),
        ],
        in_specs=[VMEM] * (1 + count),
        out_specs=[VMEM] * 3,
        scratch_shapes=[pltpu.VMEM((slots + PAD, width + LANES), jnp.float32)],
        compiler_params=PARAMS,
        cost_estimate=cost(4 * slots * width, 8 * slots * width),
        name="slots",
    )(hidden, *received)

    back, *hiddens = pl.pallas_call(
        functools.partial(back_kernel, count, groups),
        out_shape=[jax.ShapeDtypeStruct((slots, LANES), jnp.float32)]
        + [jax.ShapeDtypeStruct((slots, units), jnp.bfloat16)] * (groups - 1),
        in_specs=[VMEM] * (2 * count - 2 + len(apart(count)) + groups),
        out_specs=[VMEM] * groups,
        scratch_shapes=[
            pltpu.VMEM((slots + PAD, LANES), jnp.float32),
            pltpu.VMEM((slots + PAD, units), jnp.float32),
        ],
        compiler_params=PARAMS,
        cost_estimate=cost(*AFTER_WAIT),
        name="backs",
    )(*sends, *received[1:], *theirs, *early)

    lates = [send(x, "dp", r) for r, x in enumerate(lates, 1)]
    backs = [back] + [send(back, "tensor", r) for r in range(1, tensors)]

    split = width * 3 // 8
    upstream = pl.pallas_call(
        functools.partial(upstream_kernel, split),
        out_shape=jax.ShapeDtypeStruct((slots, units), jnp.float32),
        in_specs=[VMEM] * 2,
        out_specs=VMEM,
        compiler_params=PARAMS,
        cost_estimate=cost(2 * slots * units * split, 2 * units * split),
        name="upstream",
    )(rows, weight)

    hidden_grad, down_grad, match = pl.pallas_call(
        functools.partial(down_kernel, count, groups, pieces, split),
        out_shape=[
            jax.ShapeDtypeStruct(saved_hidden.shape, jnp.bfloat16),
            jax.ShapeDtypeStruct((1, units, share), jnp.float32),
            jax.ShapeDtypeStruct(match.shape, jnp.float32),
        ],
        in_specs=[VMEM] * (3 + 3 * groups),
        out_specs=[HBM, HBM, VMEM],
        scratch_shapes=[
            pltpu.VMEM((slots, units), jnp.bfloat16),
            pltpu.VMEM((units, share), jnp.float32),
            pltpu.VMEM((slots + PAD, share), jnp.float32),
            pltpu.SemaphoreType.DMA((pieces + 2,)),
        ],
        compiler_params=PARAMS,
        cost_estimate=cost(2 * slots * units * share, 4 * units * share),
        name="down",
    )(upstream, rows, gate, weight, match, own, *early, *lates, *hiddens)

    match, backs = lax.optimization_barrier((match, backs))
    back = sum(backs[1:], backs[0]).reshape(count, CAP, tokens)
    taken = match.reshape(count, PAD, tokens)[:, :CAP]
    chosen = jnp.sum(jnp.where(taken > 0, back, 0.0), axis=1)
    gate_grad = jnp.sum(jnp.where(hits > 0, chosen[:, None, :], 0.0), axis=0)
    return (gate_grad.T, hidden_grad, down_grad)


def solution(mesh):
    return jax.shard_map(
        on_device,
        mesh=mesh,
        in_specs=(
            P(("dp", "expert"), None),
            P(("dp", "expert"), None),
            P(("dp", "expert"), None),
            P("dp", "expert", None, "tensor"),
            P("expert", "tensor", None),
        ),
        out_specs=(
            P(("dp", "expert"), None),
            P("dp", "expert", None, "tensor"),
            P("expert", "tensor", "dp"),
        ),
        check_vma=False,
    )
```

```python
import functools

import jax
import jax.numpy as jnp
from jax import lax
from jax.experimental import pallas as pl
from jax.experimental.pallas import tpu as pltpu
from jax.sharding import PartitionSpec as P

CAP = 4
LANES = 128
AFTER_WAIT = (10**9, 10**7)
WIDE = 1024
PAD = 8
VMEM = pl.BlockSpec(memory_space=pltpu.VMEM)
HBM = pl.BlockSpec(memory_space=pltpu.HBM)
PARAMS = pltpu.CompilerParams(vmem_limit_bytes=32 * 2**20)


def dot(a, b, dims):
    return lax.dot_general(a, b, (dims, ((), ())), preferred_element_type=jnp.float32)


def in_hbm(*arrays):
    return [pltpu.with_memory_space_constraint(x, pltpu.HBM) for x in arrays]


def cost(flops, nbytes):
    return pl.CostEstimate(flops=flops, bytes_accessed=nbytes, transcendentals=0)


def paired(size):
    return size & (size - 1) == 0


def target(me, step, size):
    if paired(size):
        return me ^ ((size - step) % size)
    after = me + step
    return after % size if isinstance(me, int) else jnp.where(after >= size, after - size, after)


def source(me, step, size):
    if paired(size):
        return target(me, step, size)
    before = me - step
    return before % size if isinstance(me, int) else jnp.where(before < 0, before + size, before)


def reply(step, size):
    return step if paired(size) else -step % size


def apart(size):
    return [r for r in range(size) if r not in (1, size - 1)]


def send(value, axis, step, give=target):
    size = lax.axis_size(axis)
    return lax.ppermute(value, axis, [(i, give(i, step, size)) for i in range(size)])


def front_kernel(count, groups, pieces, *refs):
    ids_hbm, gates_hbm, grad_hbm, hidden_hbm, weight_hbm = refs[:5]
    hits_ref, match_ref, weight_ref, hidden_ref = refs[5:9]
    sends = refs[9 : 9 + count]
    products = dict(zip(apart(count), refs[9 + count :]))
    early = refs[-5 - groups : -6]
    ids_ref, gates_ref, grad_ref, saved_ref, total_ref, sems = refs[-6:]
    units, width = weight_ref.shape
    top, tokens = ids_ref.shape
    pairs = [(ids_hbm, ids_ref), (gates_hbm, gates_ref), (hidden_hbm.at[0, 0], saved_ref)]
    pairs.append((grad_hbm, grad_ref))
    block = units // pieces
    for p in range(pieces):
        part = pl.ds(p * block, block)
        pairs.append((weight_hbm.at[0, part], weight_ref.at[part]))
    copies = [pltpu.make_async_copy(*pair, sems.at[n]) for n, pair in enumerate(pairs)]
    for copy in copies:
        copy.start()
    me = lax.axis_index("expert")
    rows = count * PAD
    row = lax.broadcasted_iota(jnp.int32, (rows, tokens), 0)
    expert = target(me, row // PAD, count)
    place = row % PAD
    earlier = lax.broadcasted_iota(jnp.int32, (tokens, tokens), 0)
    later = lax.broadcasted_iota(jnp.int32, (tokens, tokens), 1)
    order = (earlier < later).astype(jnp.bfloat16)
    for copy in copies[:3]:
        copy.wait()
    ids = ids_ref[...]
    gates = gates_ref[...].astype(jnp.float32)
    member = jnp.zeros((rows, tokens), jnp.float32)
    gate = jnp.zeros((rows, tokens), jnp.float32)
    for k in range(top):
        hit = ids[k : k + 1, :] == expert
        member = jnp.where(hit, 1.0, member)
        gate = jnp.where(hit, gates[k : k + 1, :], gate)
    for r in range(count):
        hits_ref[r] = (ids == target(me, r, count)).astype(jnp.float32)
    before = dot(member.astype(jnp.bfloat16), order, ((1,), (0,)))
    taken = (member > 0) & (before == place.astype(jnp.float32)) & (place < CAP)
    match = taken.astype(jnp.float32)
    match_ref[...] = match
    slot_gate = jnp.sum(match * gate, axis=1, keepdims=True)
    match = match.astype(jnp.bfloat16)

    slots = count * CAP
    saved = saved_ref[...]
    hidden_ref[...] = dot(slot_order(count), saved, ((1,), (0,))).astype(jnp.bfloat16)
    spread = dot(slot_order(count, PAD), saved, ((1,), (0,)))
    here = lax.broadcasted_iota(jnp.int32, (rows, slots), 0)
    there = lax.broadcasted_iota(jnp.int32, (rows, slots), 1)
    chosen = (here % PAD < CAP) & (there == target(me, here // PAD, count) * CAP + here % PAD)
    hidden = dot(chosen.astype(jnp.bfloat16), saved, ((1,), (0,))).astype(jnp.bfloat16)

    copies[3].wait()
    for r in range(count):
        part = slice(r * PAD, r * PAD + CAP)
        gate = jnp.broadcast_to(slot_gate[part], (CAP, LANES)).astype(jnp.bfloat16)
        sends[r][:, width : width + LANES] = gate
    wide = min(width, WIDE)
    for begin in range(0, width, wide):
        part = slice(begin, begin + wide)
        picked = dot(match, grad_ref[:, part], ((1,), (0,)))
        for r in range(count):
            sends[r][:, part] = picked[r * PAD : r * PAD + CAP].astype(jnp.bfloat16)
        total_ref[:PAD, part] = picked[:PAD]
    share = width // groups
    group = lax.axis_index("dp")
    for r, early_ref in enumerate(early, 1):
        begin = pl.multiple_of(target(group, r, groups) * share, share)
        weighted = slot_gate[:CAP] * total_ref[:CAP, pl.ds(begin, share)]
        early_ref[:, :share] = weighted.astype(jnp.bfloat16)
        for k in range(count):
            part = slice(share + k * units, share + (k + 1) * units)
            early_ref[:, part] = spread[k * PAD : k * PAD + CAP].astype(jnp.bfloat16)
    for p in range(pieces):
        copies[4 + p].wait()
        rows = slice(p * block, (p + 1) * block)
        for begin in range(0, width, wide):
            part = slice(begin, begin + wide)
            term = dot(hidden[:, rows], weight_ref[rows, part], ((1,), (0,)))
            if p > 0:
                term = total_ref[:, part] + term
            if p < pieces - 1:
                total_ref[:, part] = term
                continue
            for r in range(count):
                product = term[r * PAD : r * PAD + CAP].astype(jnp.bfloat16)
                if r in products:
                    products[r][:, part] = product
                else:
                    joint = slice(width + LANES + begin, width + LANES + begin + wide)
                    sends[r][:, joint] = product


def slot_order(count, lines=CAP):
    me = lax.axis_index("expert")
    here = lax.broadcasted_iota(jnp.int32, (count * lines, count * CAP), 0)
    saved = lax.broadcasted_iota(jnp.int32, (count * lines, count * CAP), 1)
    place = here % lines
    block = source(me, here // lines, count)
    return ((saved == block * CAP + place) & (place < CAP)).astype(jnp.bfloat16)


def late_kernel(count, groups, *refs):
    received, lates, weighted_ref = refs[: count - 1], refs[count - 1 : -1], refs[-1]
    width = weighted_ref.shape[1]
    share = width // groups
    me = lax.axis_index("dp")
    for k in range(1, count):
        row = received[k - 1][:, : width + LANES].astype(jnp.float32)
        part = slice(k * PAD, k * PAD + CAP)
        weighted_ref[part, :] = row[:, width : width + 1] * row[:, :width]
        for r, late_ref in enumerate(lates, 1):
            begin = pl.multiple_of(target(me, r, groups) * share, share)
            late = weighted_ref[part, pl.ds(begin, share)].astype(jnp.bfloat16)
            late_ref[:, (k - 1) * share : k * share] = late


def slot_kernel(count, groups, hidden_ref, *refs):
    received = refs[:count]
    rows_ref, gate_ref, own_ref, wide_ref = refs[count:]
    width = rows_ref.shape[1]
    share = width // groups
    slots = count * CAP
    for r in range(count):
        row = received[r][:, : width + LANES].astype(jnp.float32)
        wide_ref[r * CAP : (r + 1) * CAP, :] = row
    gate = wide_ref[:slots, width:]
    gate_ref[...] = gate
    rows_ref[...] = wide_ref[:slots, :width].astype(jnp.bfloat16)
    begin = pl.multiple_of(lax.axis_index("dp") * share, share)
    weighted = gate[:, :1] * wide_ref[:slots, pl.ds(begin, share)]
    own_ref[:, :share] = weighted.astype(jnp.bfloat16)
    own_ref[:, share:] = hidden_ref[...]


def back_kernel(count, groups, *refs):
    sent, refs = refs[:count], refs[count:]
    received, refs = dict(enumerate(refs[: count - 1], 1)), refs[count - 1 :]
    received.update(zip(apart(count), refs))
    refs = refs[len(apart(count)) :]
    early, refs = refs[: groups - 1], refs[groups - 1 :]
    out_ref, hiddens = refs[0], refs[1:groups]
    back_ref, units_ref = refs[groups:]
    width = received[0].shape[1]
    for r in range(count):
        ref = received[reply(r, count)]
        theirs = ref[:, ref.shape[1] - width :].astype(jnp.float32)
        mine = sent[r][:, :width].astype(jnp.float32)
        back = jnp.sum(mine * theirs, axis=1, keepdims=True)
        back_ref[r * CAP : (r + 1) * CAP, :] = jnp.broadcast_to(back, (CAP, LANES))
    slots, units = count * CAP, units_ref.shape[1]
    out_ref[...] = back_ref[:slots, :]
    for early_ref, hidden_ref in zip(early, hiddens):
        share = early_ref.shape[1] - count * units
        for k in range(count):
            part = early_ref[:, share + k * units : share + (k + 1) * units]
            units_ref[k * CAP : (k + 1) * CAP, :] = part.astype(jnp.float32)
        hidden_ref[...] = units_ref[:slots, :].astype(jnp.bfloat16)


def upstream_part(rows_ref, weight_ref, begin, end):
    return dot(rows_ref[:, begin:end], weight_ref[:, begin:end], ((1,), (1,)))


def upstream_kernel(split, rows_ref, weight_ref, out_ref):
    out_ref[...] = upstream_part(rows_ref, weight_ref, 0, split)


def down_kernel(count, groups, pieces, split, part_ref, rows_ref, gate_ref, weight_ref, match_ref, *refs):
    others = groups - 1
    own_ref, early, refs = refs[0], refs[1:groups], refs[groups:]
    lates, hiddens, refs = refs[:others], refs[others : 2 * others], refs[2 * others :]
    hidden_hbm, down_hbm, match_out, hidden_out, down_out, wide_ref, sems = refs
    units, share = down_out.shape
    block = units // pieces
    rows, hidden = [own_ref[:, :share]], [own_ref[:, share:]]
    for early_ref, late_ref, hidden_ref in zip(early, lates, hiddens):
        wide_ref[:CAP, :] = early_ref[:, :share].astype(jnp.float32)
        for k in range(1, count):
            late = late_ref[:, (k - 1) * share : k * share].astype(jnp.float32)
            wide_ref[k * CAP : (k + 1) * CAP, :] = late
        rows.append(wide_ref[: count * CAP, :].astype(jnp.bfloat16))
        hidden.append(hidden_ref[...])
    rows, hidden = jnp.concatenate(rows, axis=0), jnp.concatenate(hidden, axis=0)
    copies = []

    def write(values, destination):
        copies.append(pltpu.make_async_copy(values, destination, sems.at[len(copies)]))
        copies[-1].start()

    cuts = [0, block // 2, *range(block, units + 1, block)]
    for start, end in zip(cuts, cuts[1:]):
        part = slice(start, end)
        down_out[part, :] = dot(hidden[:, part], rows, ((0,), (0,)))
        part = pl.ds(start, end - start)
        write(down_out.at[part], down_hbm.at[0, part])
    upstream = part_ref[...] + upstream_part(rows_ref, weight_ref, split, weight_ref.shape[1])
    scaled = (gate_ref[:, :1] * upstream).astype(jnp.bfloat16)
    hidden_out[...] = dot(slot_order(count), scaled, ((0,), (0,))).astype(jnp.bfloat16)
    write(hidden_out, hidden_hbm.at[0, 0])
    match_out[...] = match_ref[...]
    for copy in copies:
        copy.wait()


def on_device(grad_out, expert_ids, gate_values, saved_hidden, down_weight):
    count = lax.axis_size("expert")
    groups = lax.axis_size("dp")
    tensors = lax.axis_size("tensor")
    tokens, width = grad_out.shape
    top = expert_ids.shape[1]
    units = down_weight.shape[1]
    slots = count * CAP
    share = width // groups
    pieces = units // LANES

    hits, match, weight, hidden, *rest = pl.pallas_call(
        functools.partial(front_kernel, count, groups, pieces),
        out_shape=[
            jax.ShapeDtypeStruct((count, top, tokens), jnp.float32),
            jax.ShapeDtypeStruct((count * PAD, tokens), jnp.float32),
            jax.ShapeDtypeStruct((units, width), jnp.bfloat16),
            jax.ShapeDtypeStruct((slots, units), jnp.bfloat16),
        ]
        + [
            jax.ShapeDtypeStruct((CAP, width + LANES + width * (r not in apart(count))), jnp.bfloat16)
            for r in range(count)
        ]
        + [jax.ShapeDtypeStruct((CAP, width), jnp.bfloat16)] * len(apart(count))
        + [jax.ShapeDtypeStruct((CAP, share + count * units), jnp.bfloat16)] * (groups - 1),
        in_specs=[HBM] * 5,
        out_specs=[VMEM] * (3 + count + len(apart(count)) + groups),
        scratch_shapes=[
            pltpu.VMEM((top, tokens), jnp.int32),
            pltpu.VMEM((top, tokens), jnp.bfloat16),
            pltpu.VMEM((tokens, width), jnp.bfloat16),
            pltpu.VMEM((slots, units), jnp.bfloat16),
            pltpu.VMEM((count * PAD, width), jnp.float32),
            pltpu.SemaphoreType.DMA((4 + pieces,)),
        ],
        compiler_params=PARAMS,
        cost_estimate=cost(2 * count * PAD * (tokens + units) * width, 2 * (tokens + units) * width),
        name="front",
    )(*in_hbm(expert_ids.T, gate_values.T, grad_out, saved_hidden, down_weight))
    sends, rest = rest[:count], rest[count:]
    products, early = rest[: len(apart(count))], rest[len(apart(count)) :]

    received = [sends[0]] + [send(sends[r], "expert", r) for r in range(1, count)]
    theirs = [products[0]]
    theirs += [send(x, "expert", r) for r, x in zip(apart(count)[1:], products[1:])]
    early = [send(x, "dp", r) for r, x in enumerate(early, 1)]

    lates = pl.pallas_call(
        functools.partial(late_kernel, count, groups),
        out_shape=[jax.ShapeDtypeStruct((CAP, (count - 1) * share), jnp.bfloat16)] * (groups - 1),
        in_specs=[VMEM] * (count - 1),
        out_specs=[VMEM] * (groups - 1),
        scratch_shapes=[pltpu.VMEM((count * PAD, width), jnp.float32)],
        compiler_params=PARAMS,
        cost_estimate=cost(2 * slots * width, 4 * slots * width),
        name="late",
    )(*received[1:])

    rows, gate, own = pl.pallas_call(
        functools.partial(slot_kernel, count, groups),
        out_shape=[
            jax.ShapeDtypeStruct((slots, width), jnp.bfloat16),
            jax.ShapeDtypeStruct((slots, LANES), jnp.float32),
            jax.ShapeDtypeStruct((slots, share + units), jnp.bfloat16),
        ],
        in_specs=[VMEM] * (1 + count),
        out_specs=[VMEM] * 3,
        scratch_shapes=[pltpu.VMEM((slots + PAD, width + LANES), jnp.float32)],
        compiler_params=PARAMS,
        cost_estimate=cost(4 * slots * width, 8 * slots * width),
        name="slots",
    )(hidden, *received)

    back, *hiddens = pl.pallas_call(
        functools.partial(back_kernel, count, groups),
        out_shape=[jax.ShapeDtypeStruct((slots, LANES), jnp.float32)]
        + [jax.ShapeDtypeStruct((slots, units), jnp.bfloat16)] * (groups - 1),
        in_specs=[VMEM] * (2 * count - 2 + len(apart(count)) + groups),
        out_specs=[VMEM] * groups,
        scratch_shapes=[
            pltpu.VMEM((slots + PAD, LANES), jnp.float32),
            pltpu.VMEM((slots + PAD, units), jnp.float32),
        ],
        compiler_params=PARAMS,
        cost_estimate=cost(*AFTER_WAIT),
        name="backs",
    )(*sends, *received[1:], *theirs, *early)

    lates = [send(x, "dp", r) for r, x in enumerate(lates, 1)]
    backs = [back] + [send(back, "tensor", r) for r in range(1, tensors)]

    split = width * 3 // 8
    upstream = pl.pallas_call(
        functools.partial(upstream_kernel, split),
        out_shape=jax.ShapeDtypeStruct((slots, units), jnp.float32),
        in_specs=[VMEM] * 2,
        out_specs=VMEM,
        compiler_params=PARAMS,
        cost_estimate=cost(2 * slots * units * split, 2 * units * split),
        name="upstream",
    )(rows, weight)

    hidden_grad, down_grad, match = pl.pallas_call(
        functools.partial(down_kernel, count, groups, pieces, split),
        out_shape=[
            jax.ShapeDtypeStruct(saved_hidden.shape, jnp.bfloat16),
            jax.ShapeDtypeStruct((1, units, share), jnp.float32),
            jax.ShapeDtypeStruct(match.shape, jnp.float32),
        ],
        in_specs=[VMEM] * (3 + 3 * groups),
        out_specs=[HBM, HBM, VMEM],
        scratch_shapes=[
            pltpu.VMEM((slots, units), jnp.bfloat16),
            pltpu.VMEM((units, share), jnp.float32),
            pltpu.VMEM((slots + PAD, share), jnp.float32),
            pltpu.SemaphoreType.DMA((pieces + 2,)),
        ],
        compiler_params=PARAMS,
        cost_estimate=cost(2 * slots * units * share, 4 * units * share),
        name="down",
    )(upstream, rows, gate, weight, match, own, *early, *lates, *hiddens)

    match, backs = lax.optimization_barrier((match, backs))
    back = sum(backs[1:], backs[0]).reshape(count, CAP, tokens)
    taken = match.reshape(count, PAD, tokens)[:, :CAP]
    chosen = jnp.sum(jnp.where(taken > 0, back, 0.0), axis=1)
    gate_grad = jnp.sum(jnp.where(hits > 0, chosen[:, None, :], 0.0), axis=0)
    return (gate_grad.T, hidden_grad, down_grad)


def solution(mesh):
    return jax.shard_map(
        on_device,
        mesh=mesh,
        in_specs=(
            P(("dp", "expert"), None),
            P(("dp", "expert"), None),
            P(("dp", "expert"), None),
            P("dp", "expert", None, "tensor"),
            P("expert", "tensor", None),
        ),
        out_specs=(
            P(("dp", "expert"), None),
            P("dp", "expert", None, "tensor"),
            P("expert", "tensor", "dp"),
        ),
        check_vma=False,
    )
```

```python
import functools

import jax
import jax.numpy as jnp
from jax import lax
from jax.experimental import pallas as pl
from jax.experimental.pallas import tpu as pltpu
from jax.sharding import PartitionSpec as P

CAP = 4
LANES = 128
AFTER_WAIT = (10**9, 10**7)
WIDE = 1024
PAD = 8
VMEM = pl.BlockSpec(memory_space=pltpu.VMEM)
HBM = pl.BlockSpec(memory_space=pltpu.HBM)
PARAMS = pltpu.CompilerParams(vmem_limit_bytes=32 * 2**20)


def dot(a, b, dims):
    return lax.dot_general(a, b, (dims, ((), ())), preferred_element_type=jnp.float32)


def in_hbm(*arrays):
    return [pltpu.with_memory_space_constraint(x, pltpu.HBM) for x in arrays]


def cost(flops, nbytes):
    return pl.CostEstimate(flops=flops, bytes_accessed=nbytes, transcendentals=0)


def paired(size):
    return size & (size - 1) == 0


def target(me, step, size):
    if paired(size):
        return me ^ ((size - step) % size)
    after = me + step
    return after % size if isinstance(me, int) else jnp.where(after >= size, after - size, after)


def source(me, step, size):
    if paired(size):
        return target(me, step, size)
    before = me - step
    return before % size if isinstance(me, int) else jnp.where(before < 0, before + size, before)


def reply(step, size):
    return step if paired(size) else -step % size


def apart(size):
    return [r for r in range(size) if r not in (1, size - 1)]


def send(value, axis, step, give=target):
    size = lax.axis_size(axis)
    return lax.ppermute(value, axis, [(i, give(i, step, size)) for i in range(size)])


def front_kernel(count, groups, pieces, *refs):
    ids_hbm, gates_hbm, grad_hbm, hidden_hbm, weight_hbm = refs[:5]
    hits_ref, match_ref, weight_ref, hidden_ref = refs[5:9]
    sends = refs[9 : 9 + count]
    products = dict(zip(apart(count), refs[9 + count :]))
    early = refs[-5 - groups : -6]
    ids_ref, gates_ref, grad_ref, saved_ref, total_ref, sems = refs[-6:]
    units, width = weight_ref.shape
    top, tokens = ids_ref.shape
    pairs = [(ids_hbm, ids_ref), (gates_hbm, gates_ref), (hidden_hbm.at[0, 0], saved_ref)]
    pairs.append((grad_hbm, grad_ref))
    block = units // pieces
    for p in range(pieces):
        part = pl.ds(p * block, block)
        pairs.append((weight_hbm.at[0, part], weight_ref.at[part]))
    copies = [pltpu.make_async_copy(*pair, sems.at[n]) for n, pair in enumerate(pairs)]
    for copy in copies:
        copy.start()
    me = lax.axis_index("expert")
    rows = count * PAD
    row = lax.broadcasted_iota(jnp.int32, (rows, tokens), 0)
    expert = target(me, row // PAD, count)
    place = row % PAD
    earlier = lax.broadcasted_iota(jnp.int32, (tokens, tokens), 0)
    later = lax.broadcasted_iota(jnp.int32, (tokens, tokens), 1)
    order = (earlier < later).astype(jnp.bfloat16)
    for copy in copies[:3]:
        copy.wait()
    ids = ids_ref[...]
    gates = gates_ref[...].astype(jnp.float32)
    member = jnp.zeros((rows, tokens), jnp.float32)
    gate = jnp.zeros((rows, tokens), jnp.float32)
    for k in range(top):
        hit = ids[k : k + 1, :] == expert
        member = jnp.where(hit, 1.0, member)
        gate = jnp.where(hit, gates[k : k + 1, :], gate)
    for r in range(count):
        hits_ref[r] = (ids == target(me, r, count)).astype(jnp.float32)
    before = dot(member.astype(jnp.bfloat16), order, ((1,), (0,)))
    taken = (member > 0) & (before == place.astype(jnp.float32)) & (place < CAP)
    match = taken.astype(jnp.float32)
    match_ref[...] = match
    slot_gate = jnp.sum(match * gate, axis=1, keepdims=True)
    match = match.astype(jnp.bfloat16)

    slots = count * CAP
    saved = saved_ref[...]
    hidden_ref[...] = dot(slot_order(count), saved, ((1,), (0,))).astype(jnp.bfloat16)
    spread = dot(slot_order(count, PAD), saved, ((1,), (0,)))
    here = lax.broadcasted_iota(jnp.int32, (rows, slots), 0)
    there = lax.broadcasted_iota(jnp.int32, (rows, slots), 1)
    chosen = (here % PAD < CAP) & (there == target(me, here // PAD, count) * CAP + here % PAD)
    hidden = dot(chosen.astype(jnp.bfloat16), saved, ((1,), (0,))).astype(jnp.bfloat16)

    copies[3].wait()
    for r in range(count):
        part = slice(r * PAD, r * PAD + CAP)
        gate = jnp.broadcast_to(slot_gate[part], (CAP, LANES)).astype(jnp.bfloat16)
        sends[r][:, width : width + LANES] = gate
    wide = min(width, WIDE)
    for begin in range(0, width, wide):
        part = slice(begin, begin + wide)
        picked = dot(match, grad_ref[:, part], ((1,), (0,)))
        for r in range(count):
            sends[r][:, part] = picked[r * PAD : r * PAD + CAP].astype(jnp.bfloat16)
        total_ref[:PAD, part] = picked[:PAD]
    share = width // groups
    group = lax.axis_index("dp")
    for r, early_ref in enumerate(early, 1):
        begin = pl.multiple_of(target(group, r, groups) * share, share)
        weighted = slot_gate[:CAP] * total_ref[:CAP, pl.ds(begin, share)]
        early_ref[:, :share] = weighted.astype(jnp.bfloat16)
        for k in range(count):
            part = slice(share + k * units, share + (k + 1) * units)
            early_ref[:, part] = spread[k * PAD : k * PAD + CAP].astype(jnp.bfloat16)
    for p in range(pieces):
        copies[4 + p].wait()
        rows = slice(p * block, (p + 1) * block)
        for begin in range(0, width, wide):
            part = slice(begin, begin + wide)
            term = dot(hidden[:, rows], weight_ref[rows, part], ((1,), (0,)))
            if p > 0:
                term = total_ref[:, part] + term
            if p < pieces - 1:
                total_ref[:, part] = term
                continue
            for r in range(count):
                product = term[r * PAD : r * PAD + CAP].astype(jnp.bfloat16)
                if r in products:
                    products[r][:, part] = product
                else:
                    joint = slice(width + LANES + begin, width + LANES + begin + wide)
                    sends[r][:, joint] = product


def slot_order(count, lines=CAP):
    me = lax.axis_index("expert")
    here = lax.broadcasted_iota(jnp.int32, (count * lines, count * CAP), 0)
    saved = lax.broadcasted_iota(jnp.int32, (count * lines, count * CAP), 1)
    place = here % lines
    block = source(me, here // lines, count)
    return ((saved == block * CAP + place) & (place < CAP)).astype(jnp.bfloat16)


def late_kernel(count, groups, *refs):
    received, lates = refs[: count - 1], refs[count - 1 :]
    share = lates[0].shape[1] // (count - 1)
    width = share * groups
    me = lax.axis_index("dp")
    for k in range(1, count):
        gate = received[k - 1][:, width : width + LANES].astype(jnp.float32)
        for r, late_ref in enumerate(lates, 1):
            begin = pl.multiple_of(target(me, r, groups) * share, share)
            row = received[k - 1][:, pl.ds(begin, share)].astype(jnp.float32)
            late_ref[:, (k - 1) * share : k * share] = (gate[:, :1] * row).astype(jnp.bfloat16)


def slot_kernel(count, groups, hidden_ref, *refs):
    received = refs[:count]
    rows_ref, gate_ref, own_ref, wide_ref = refs[count:]
    width = rows_ref.shape[1]
    share = width // groups
    slots = count * CAP
    for r in range(count):
        row = received[r][:, : width + LANES].astype(jnp.float32)
        wide_ref[r * CAP : (r + 1) * CAP, :] = row
    gate = wide_ref[:slots, width:]
    gate_ref[...] = gate
    rows_ref[...] = wide_ref[:slots, :width].astype(jnp.bfloat16)
    begin = pl.multiple_of(lax.axis_index("dp") * share, share)
    weighted = gate[:, :1] * wide_ref[:slots, pl.ds(begin, share)]
    own_ref[:, :share] = weighted.astype(jnp.bfloat16)
    own_ref[:, share:] = hidden_ref[...]


def back_kernel(count, groups, *refs):
    sent, refs = refs[:count], refs[count:]
    received, refs = dict(enumerate(refs[: count - 1], 1)), refs[count - 1 :]
    received.update(zip(apart(count), refs))
    refs = refs[len(apart(count)) :]
    early, refs = refs[: groups - 1], refs[groups - 1 :]
    out_ref, hiddens = refs[0], refs[1:groups]
    back_ref, units_ref = refs[groups:]
    width = received[0].shape[1]
    for r in range(count):
        ref = received[reply(r, count)]
        theirs = ref[:, ref.shape[1] - width :].astype(jnp.float32)
        mine = sent[r][:, :width].astype(jnp.float32)
        back = jnp.sum(mine * theirs, axis=1, keepdims=True)
        back_ref[r * CAP : (r + 1) * CAP, :] = jnp.broadcast_to(back, (CAP, LANES))
    slots, units = count * CAP, units_ref.shape[1]
    out_ref[...] = back_ref[:slots, :]
    for early_ref, hidden_ref in zip(early, hiddens):
        share = early_ref.shape[1] - count * units
        for k in range(count):
            part = early_ref[:, share + k * units : share + (k + 1) * units]
            units_ref[k * CAP : (k + 1) * CAP, :] = part.astype(jnp.float32)
        hidden_ref[...] = units_ref[:slots, :].astype(jnp.bfloat16)


def upstream_part(rows_ref, weight_ref, begin, end):
    return dot(rows_ref[:, begin:end], weight_ref[:, begin:end], ((1,), (1,)))


def upstream_kernel(split, rows_ref, weight_ref, out_ref):
    out_ref[...] = upstream_part(rows_ref, weight_ref, 0, split)


def down_kernel(count, groups, pieces, split, part_ref, rows_ref, gate_ref, weight_ref, match_ref, *refs):
    others = groups - 1
    own_ref, early, refs = refs[0], refs[1:groups], refs[groups:]
    lates, hiddens, refs = refs[:others], refs[others : 2 * others], refs[2 * others :]
    hidden_hbm, down_hbm, match_out, hidden_out, down_out, wide_ref, sems = refs
    units, share = down_out.shape
    block = units // pieces
    rows, hidden = [own_ref[:, :share]], [own_ref[:, share:]]
    for early_ref, late_ref, hidden_ref in zip(early, lates, hiddens):
        wide_ref[:CAP, :] = early_ref[:, :share].astype(jnp.float32)
        for k in range(1, count):
            late = late_ref[:, (k - 1) * share : k * share].astype(jnp.float32)
            wide_ref[k * CAP : (k + 1) * CAP, :] = late
        rows.append(wide_ref[: count * CAP, :].astype(jnp.bfloat16))
        hidden.append(hidden_ref[...])
    rows, hidden = jnp.concatenate(rows, axis=0), jnp.concatenate(hidden, axis=0)
    copies = []

    def write(values, destination):
        copies.append(pltpu.make_async_copy(values, destination, sems.at[len(copies)]))
        copies[-1].start()

    cuts = [0, block // 2, *range(block, units + 1, block)]
    for start, end in zip(cuts, cuts[1:]):
        part = slice(start, end)
        down_out[part, :] = dot(hidden[:, part], rows, ((0,), (0,)))
        part = pl.ds(start, end - start)
        write(down_out.at[part], down_hbm.at[0, part])
    upstream = part_ref[...] + upstream_part(rows_ref, weight_ref, split, weight_ref.shape[1])
    scaled = (gate_ref[:, :1] * upstream).astype(jnp.bfloat16)
    hidden_out[...] = dot(slot_order(count), scaled, ((0,), (0,))).astype(jnp.bfloat16)
    write(hidden_out, hidden_hbm.at[0, 0])
    match_out[...] = match_ref[...]
    for copy in copies:
        copy.wait()


def on_device(grad_out, expert_ids, gate_values, saved_hidden, down_weight):
    count = lax.axis_size("expert")
    groups = lax.axis_size("dp")
    tensors = lax.axis_size("tensor")
    tokens, width = grad_out.shape
    top = expert_ids.shape[1]
    units = down_weight.shape[1]
    slots = count * CAP
    share = width // groups
    pieces = units // LANES

    hits, match, weight, hidden, *rest = pl.pallas_call(
        functools.partial(front_kernel, count, groups, pieces),
        out_shape=[
            jax.ShapeDtypeStruct((count, top, tokens), jnp.float32),
            jax.ShapeDtypeStruct((count * PAD, tokens), jnp.float32),
            jax.ShapeDtypeStruct((units, width), jnp.bfloat16),
            jax.ShapeDtypeStruct((slots, units), jnp.bfloat16),
        ]
        + [
            jax.ShapeDtypeStruct((CAP, width + LANES + width * (r not in apart(count))), jnp.bfloat16)
            for r in range(count)
        ]
        + [jax.ShapeDtypeStruct((CAP, width), jnp.bfloat16)] * len(apart(count))
        + [jax.ShapeDtypeStruct((CAP, share + count * units), jnp.bfloat16)] * (groups - 1),
        in_specs=[HBM] * 5,
        out_specs=[VMEM] * (3 + count + len(apart(count)) + groups),
        scratch_shapes=[
            pltpu.VMEM((top, tokens), jnp.int32),
            pltpu.VMEM((top, tokens), jnp.bfloat16),
            pltpu.VMEM((tokens, width), jnp.bfloat16),
            pltpu.VMEM((slots, units), jnp.bfloat16),
            pltpu.VMEM((count * PAD, width), jnp.float32),
            pltpu.SemaphoreType.DMA((4 + pieces,)),
        ],
        compiler_params=PARAMS,
        cost_estimate=cost(2 * count * PAD * (tokens + units) * width, 2 * (tokens + units) * width),
        name="front",
    )(*in_hbm(expert_ids.T, gate_values.T, grad_out, saved_hidden, down_weight))
    sends, rest = rest[:count], rest[count:]
    products, early = rest[: len(apart(count))], rest[len(apart(count)) :]

    received = [sends[0]] + [send(sends[r], "expert", r) for r in range(1, count)]
    theirs = [products[0]]
    theirs += [send(x, "expert", r) for r, x in zip(apart(count)[1:], products[1:])]
    early = [send(x, "dp", r) for r, x in enumerate(early, 1)]

    lates = pl.pallas_call(
        functools.partial(late_kernel, count, groups),
        out_shape=[jax.ShapeDtypeStruct((CAP, (count - 1) * share), jnp.bfloat16)] * (groups - 1),
        in_specs=[VMEM] * (count - 1),
        out_specs=[VMEM] * (groups - 1),
        compiler_params=PARAMS,
        cost_estimate=cost(2 * slots * width, 4 * slots * width),
        name="late",
    )(*received[1:])

    rows, gate, own = pl.pallas_call(
        functools.partial(slot_kernel, count, groups),
        out_shape=[
            jax.ShapeDtypeStruct((slots, width), jnp.bfloat16),
            jax.ShapeDtypeStruct((slots, LANES), jnp.float32),
            jax.ShapeDtypeStruct((slots, share + units), jnp.bfloat16),
        ],
        in_specs=[VMEM] * (1 + count),
        out_specs=[VMEM] * 3,
        scratch_shapes=[pltpu.VMEM((slots + PAD, width + LANES), jnp.float32)],
        compiler_params=PARAMS,
        cost_estimate=cost(4 * slots * width, 8 * slots * width),
        name="slots",
    )(hidden, *received)

    back, *hiddens = pl.pallas_call(
        functools.partial(back_kernel, count, groups),
        out_shape=[jax.ShapeDtypeStruct((slots, LANES), jnp.float32)]
        + [jax.ShapeDtypeStruct((slots, units), jnp.bfloat16)] * (groups - 1),
        in_specs=[VMEM] * (2 * count - 2 + len(apart(count)) + groups),
        out_specs=[VMEM] * groups,
        scratch_shapes=[
            pltpu.VMEM((slots + PAD, LANES), jnp.float32),
            pltpu.VMEM((slots + PAD, units), jnp.float32),
        ],
        compiler_params=PARAMS,
        cost_estimate=cost(*AFTER_WAIT),
        name="backs",
    )(*sends, *received[1:], *theirs, *early)

    lates = [send(x, "dp", r) for r, x in enumerate(lates, 1)]
    backs = [back] + [send(back, "tensor", r) for r in range(1, tensors)]

    split = width * 3 // 8
    upstream = pl.pallas_call(
        functools.partial(upstream_kernel, split),
        out_shape=jax.ShapeDtypeStruct((slots, units), jnp.float32),
        in_specs=[VMEM] * 2,
        out_specs=VMEM,
        compiler_params=PARAMS,
        cost_estimate=cost(2 * slots * units * split, 2 * units * split),
        name="upstream",
    )(rows, weight)

    hidden_grad, down_grad, match = pl.pallas_call(
        functools.partial(down_kernel, count, groups, pieces, split),
        out_shape=[
            jax.ShapeDtypeStruct(saved_hidden.shape, jnp.bfloat16),
            jax.ShapeDtypeStruct((1, units, share), jnp.float32),
            jax.ShapeDtypeStruct(match.shape, jnp.float32),
        ],
        in_specs=[VMEM] * (3 + 3 * groups),
        out_specs=[HBM, HBM, VMEM],
        scratch_shapes=[
            pltpu.VMEM((slots, units), jnp.bfloat16),
            pltpu.VMEM((units, share), jnp.float32),
            pltpu.VMEM((slots + PAD, share), jnp.float32),
            pltpu.SemaphoreType.DMA((pieces + 2,)),
        ],
        compiler_params=PARAMS,
        cost_estimate=cost(2 * slots * units * share, 4 * units * share),
        name="down",
    )(upstream, rows, gate, weight, match, own, *early, *lates, *hiddens)

    match, backs = lax.optimization_barrier((match, backs))
    back = sum(backs[1:], backs[0]).reshape(count, CAP, tokens)
    taken = match.reshape(count, PAD, tokens)[:, :CAP]
    chosen = jnp.sum(jnp.where(taken > 0, back, 0.0), axis=1)
    gate_grad = jnp.sum(jnp.where(hits > 0, chosen[:, None, :], 0.0), axis=0)
    return (gate_grad.T, hidden_grad, down_grad)


def solution(mesh):
    return jax.shard_map(
        on_device,
        mesh=mesh,
        in_specs=(
            P(("dp", "expert"), None),
            P(("dp", "expert"), None),
            P(("dp", "expert"), None),
            P("dp", "expert", None, "tensor"),
            P("expert", "tensor", None),
        ),
        out_specs=(
            P(("dp", "expert"), None),
            P("dp", "expert", None, "tensor"),
            P("expert", "tensor", "dp"),
        ),
        check_vma=False,
    )
```
